32 devices in a mesh: tm: 8 (over y, x, core), head: 4 (over z).
Axes of the slice: x: 2, y: 2, z: 4, core: 2. Of those that a mesh axis runs over, the one named last changes fastest.
Arguments:
- frames: bfloat16 [32768, 144], P(('tm', 'head')), may hold values from -6 to 6
- lengths: int32 [8, 165], P('tm'), may hold values from 0 to 750, as said below
- first_gain: bfloat16 [144], replicated, may hold values from 0.25 to 1.75
- first_shift: bfloat16 [144], replicated, may hold values from -1.25 to 1.25
- first_up: bfloat16 [144, 576], replicated, may hold values from -0.5 to 0.5
- first_up_bias: bfloat16 [576], replicated, may hold values from -1.25 to 1.25
- first_down: bfloat16 [576, 144], replicated, may hold values from -0.25 to 0.25
- first_down_bias: bfloat16 [144], replicated, may hold values from -1.25 to 1.25
- mix_gain: bfloat16 [144], replicated, may hold values from 0.25 to 1.75
- mix_shift: bfloat16 [144], replicated, may hold values from -1.25 to 1.25
- mix_inputs: bfloat16 [144, 432], replicated, may hold values from -0.5 to 0.5
- position_bias: bfloat16 [4, 128], replicated, may hold values from -3 to 3
- mix_output: bfloat16 [144, 144], replicated, may hold values from -3 to 3
- mix_output_bias: bfloat16 [144], replicated, may hold values from -1.25 to 1.25
- filter_gain: bfloat16 [144], replicated, may hold values from 0.25 to 1.75
- filter_shift: bfloat16 [144], replicated, may hold values from -1.25 to 1.25
- pointwise_in: bfloat16 [144, 288], replicated, may hold values from -0.5 to 0.5
- pointwise_in_bias: bfloat16 [288], replicated, may hold values from -1.25 to 1.25
- depthwise_taps: bfloat16 [32, 144], replicated, may hold values from -1 to 1
- batch_gain: bfloat16 [144], replicated, may hold values from 0.25 to 1.75
- batch_shift: bfloat16 [144], replicated, may hold values from -1.25 to 1.25
- pointwise_out: bfloat16 [144, 144], replicated, may hold values from -0.5 to 0.5
- pointwise_out_bias: bfloat16 [144], replicated, may hold values from -1.25 to 1.25
- second_gain: bfloat16 [144], replicated, may hold values from 0.25 to 1.75
- second_shift: bfloat16 [144], replicated, may hold values from -1.25 to 1.25
- second_up: bfloat16 [144, 576], replicated, may hold values from -0.5 to 0.5
- second_up_bias: bfloat16 [576], replicated, may hold values from -1.25 to 1.25
- second_down: bfloat16 [576, 144], replicated, may hold values from -0.25 to 0.25
- second_down_bias: bfloat16 [144], replicated, may hold values from -1.25 to 1.25
- final_gain: bfloat16 [144], replicated, may hold values from 0.25 to 1.75
- final_shift: bfloat16 [144], replicated, may hold values from -1.25 to 1.25
- cotangent: bfloat16 [32768, 144], P(('tm', 'head')), may hold values from -6 to 6
Outputs:
- layer_output: bfloat16 [32768, 144], P(('tm', 'head'))
- frames_grad: float32 [32768, 144], P(('tm', 'head'))
- grad_first_gain: float32 [144], replicated
- grad_first_shift: float32 [144], replicated
- grad_first_up: float32 [144, 576], replicated
- grad_first_up_bias: float32 [576], replicated
- grad_first_down: float32 [576, 144], replicated
- grad_first_down_bias: float32 [144], replicated
- grad_mix_gain: float32 [144], replicated
- grad_mix_shift: float32 [144], replicated
- grad_mix_inputs: float32 [144, 432], replicated
- grad_position_bias: float32 [4, 128], replicated
- grad_mix_output: float32 [144, 144], replicated
- grad_mix_output_bias: float32 [144], replicated
- grad_filter_gain: float32 [144], replicated
- grad_filter_shift: float32 [144], replicated
- grad_pointwise_in: float32 [144, 288], replicated
- grad_pointwise_in_bias: float32 [288], replicated
- grad_depthwise_taps: float32 [32, 144], replicated
- grad_batch_gain: float32 [144], replicated
- grad_batch_shift: float32 [144], replicated
- grad_pointwise_out: float32 [144, 144], replicated
- grad_pointwise_out_bias: float32 [144], replicated
- grad_second_gain: float32 [144], replicated
- grad_second_shift: float32 [144], replicated
- grad_second_up: float32 [144, 576], replicated
- grad_second_up_bias: float32 [576], replicated
- grad_second_down: float32 [576, 144], replicated
- grad_second_down_bias: float32 [144], replicated
- grad_final_gain: float32 [144], replicated
- grad_final_shift: float32 [144], replicated
The draws below stay inside these ranges and needn't reach their ends.
Inputs may be any that keep to these rules, and one draw needn't show every extreme that they name: `lengths`: row g lists in order the utterances packed into group g from its first frame on; frames after the last utterance are padding, and slots after it are 0. Every row holds one utterance of 750 frames among its first two slots; the others have 25 to 75 frames, except the last one, which may be cut shorter. The last group has no padding.
All inputs are finite; a program needn't handle non-finite values.
Results may differ from the reference program's by a relative error of at most 0.017.
Values may be sent and summed in bfloat16 or wider, within the bound.
A program may use at most 128 MiB of HBM per device.

```python
import math
import jax
import jax.numpy as jnp
from jax import lax

D = 144
FF = 576
HEADS = 4
KER = 32
HEAD_DIM = 36
REL = 64
SHORT_LO = 25
SHORT_HI = 75
LONG = 750
GROUP_LEN = 4096
GROUPS = 8
TOKENS = 32768
UTTS = 165


def draw_lengths(key, part):
    key = jax.random.fold_in(key, 11)
    short_key, place_key = jax.random.split(key)
    shorts = jax.random.randint(short_key, (GROUPS, UTTS), SHORT_LO, SHORT_HI + 1, dtype=jnp.int32)
    long_slot = jax.random.randint(place_key, (GROUPS, 1), 0, 2, dtype=jnp.int32)
    slot_ids = jnp.arange(UTTS, dtype=jnp.int32)[None, :]
    drawn_len = jnp.where(slot_ids == long_slot, LONG, shorts).astype(jnp.int32)
    group_ids = jnp.arange(GROUPS, dtype=jnp.int32)
    spare_len = GROUP_LEN - LONG - SHORT_HI
    filled = GROUP_LEN - spare_len * (GROUPS - 1 - group_ids) // max(GROUPS - 1, 1)
    before = jnp.cumsum(drawn_len, axis=1, dtype=jnp.int32) - drawn_len
    return jnp.clip(filled[:, None] - before, 0, drawn_len).astype(jnp.int32)


def block_levels(own_key, shape, cuts, low, high):
    level = 1.0
    for position, blocks in cuts:
        steps = jax.random.uniform(jax.random.fold_in(jax.random.fold_in(own_key, 6), position), (blocks,), jnp.float32, low / len(cuts), high / len(cuts))
        level = level * jnp.repeat(jnp.exp(steps), shape[position] // blocks).reshape((-1,) + (1,) * (len(shape) - 1 - position))
    return level


def scatter_about(rng, dims, scale, reach, cuts=(), held_as=jnp.bfloat16):
    values = jax.random.normal(rng, dims, jnp.float32) * scale
    if len(cuts) > 0:
        values = block_levels(rng, dims, cuts, -0.22, 0.18) * values
    return jnp.clip(values, min=-reach, max=reach).astype(held_as)


def setup_inputs(seed: int = 0) -> dict:
    arg_keys = jax.random.split(jax.random.key(seed), 33)
    return {
        "frames": scatter_about(arg_keys[0], (TOKENS, D), 1.0, 6.0, ((0, 32),)),
        "lengths": draw_lengths(jax.random.fold_in(arg_keys[32], 71), 0),
        "first_gain": jnp.clip(1.0 + 0.15 * jax.random.normal(arg_keys[2], (D,), jnp.float32), 0.25, 1.75).astype(jnp.bfloat16),
        "first_shift": scatter_about(arg_keys[3], (D,), 0.2, 1.25),
        "first_up": scatter_about(arg_keys[4], (D, FF), D ** -0.5, 0.5),
        "first_up_bias": scatter_about(arg_keys[5], (FF,), 0.2, 1.25),
        "first_down": scatter_about(arg_keys[6], (FF, D), FF ** -0.5, 0.25),
        "first_down_bias": scatter_about(arg_keys[7], (D,), 0.2, 1.25),
        "mix_gain": jnp.clip(1.0 + 0.15 * jax.random.normal(arg_keys[8], (D,), jnp.float32), 0.25, 1.75).astype(jnp.bfloat16),
        "mix_shift": scatter_about(arg_keys[9], (D,), 0.2, 1.25),
        "mix_inputs": scatter_about(arg_keys[10], (D, 3 * D), D ** -0.5, 0.5),
        "position_bias": scatter_about(arg_keys[11], (HEADS, 2 * REL), 0.5, 3.0),
        "mix_output": scatter_about(arg_keys[12], (D, D), (max(D // 32, 1)) ** -0.5, 3.0),
        "mix_output_bias": scatter_about(arg_keys[13], (D,), 0.2, 1.25),
        "filter_gain": jnp.clip(1.0 + 0.15 * jax.random.normal(arg_keys[14], (D,), jnp.float32), 0.25, 1.75).astype(jnp.bfloat16),
        "filter_shift": scatter_about(arg_keys[15], (D,), 0.2, 1.25),
        "pointwise_in": scatter_about(arg_keys[16], (D, 2 * D), D ** -0.5, 0.5),
        "pointwise_in_bias": scatter_about(arg_keys[17], (2 * D,), 0.2, 1.25),
        "depthwise_taps": scatter_about(arg_keys[18], (KER, D), KER ** -0.5, 1.0),
        "batch_gain": jnp.clip(1.0 + 0.15 * jax.random.normal(arg_keys[19], (D,), jnp.float32), 0.25, 1.75).astype(jnp.bfloat16),
        "batch_shift": scatter_about(arg_keys[20], (D,), 0.2, 1.25),
        "pointwise_out": scatter_about(arg_keys[21], (D, D), D ** -0.5, 0.5),
        "pointwise_out_bias": scatter_about(arg_keys[22], (D,), 0.2, 1.25),
        "second_gain": jnp.clip(1.0 + 0.15 * jax.random.normal(arg_keys[23], (D,), jnp.float32), 0.25, 1.75).astype(jnp.bfloat16),
        "second_shift": scatter_about(arg_keys[24], (D,), 0.2, 1.25),
        "second_up": scatter_about(arg_keys[25], (D, FF), D ** -0.5, 0.5),
        "second_up_bias": scatter_about(arg_keys[26], (FF,), 0.2, 1.25),
        "second_down": scatter_about(arg_keys[27], (FF, D), FF ** -0.5, 0.25),
        "second_down_bias": scatter_about(arg_keys[28], (D,), 0.2, 1.25),
        "final_gain": jnp.clip(1.0 + 0.15 * jax.random.normal(arg_keys[29], (D,), jnp.float32), 0.25, 1.75).astype(jnp.bfloat16),
        "final_shift": scatter_about(arg_keys[30], (D,), 0.2, 1.25),
        "cotangent": scatter_about(arg_keys[31], (TOKENS, D), 1.0, 6.0, ((0, 32),)),
    }


EPSILON = 1e-05
HIGH = lax.Precision.HIGHEST

@jax.custom_vjp
def low(v):
    return lax.optimization_barrier(v.astype(jnp.bfloat16)).astype(jnp.float32)

@jax.custom_vjp
def low_back(v):
    return v

def low_keep(v):
    return (low(v), None)

def low_pass(kept, grad):
    return (grad,)

def back_keep(v):
    return (v, None)

def back_low(kept, grad):
    return (low(grad),)
low.defvjp(low_keep, low_pass)
low_back.defvjp(back_keep, back_low)

def product(left_side, right_side):
    return jnp.dot(left_side, right_side, precision=HIGH)

def layer_norm(values, gain_vec, shift_vec):
    row_mean = lax.optimization_barrier(jnp.mean(values, axis=-1, keepdims=True))
    centered = values - row_mean
    variance = lax.optimization_barrier(jnp.mean(centered * centered, axis=-1, keepdims=True))
    return centered * lax.rsqrt(variance + EPSILON) * gain_vec + shift_vec

def group_segments(length_row, group_len):
    ends_at = jnp.cumsum(length_row, dtype=jnp.int32)
    places = jnp.arange(group_len, dtype=jnp.int32)
    return lax.optimization_barrier(jnp.sum((ends_at[None, :] <= places[:, None]).astype(jnp.int32), axis=1, dtype=jnp.int32))

def feed_forward(values, params):
    gain_vec, shift_vec, up_mat, up_bias, down_mat, down_bias = params
    normed = low(layer_norm(values, gain_vec, shift_vec))
    hidden_pre = low_back(product(normed, up_mat) + up_bias)
    hidden = low(jax.nn.silu(hidden_pre))
    return low_back(product(hidden, down_mat) + down_bias)

def attend_group(packed, segs, bias_table):
    group_len = packed.shape[0]
    head_width = packed.shape[2] // 3
    queries = packed[:, :, :head_width]
    key_rows = packed[:, :, head_width:2 * head_width]
    value_rows = packed[:, :, 2 * head_width:]
    block_rows = min(512, group_len)
    half_span = bias_table.shape[1] // 2
    score_scale = 1.0 / math.sqrt(head_width)

    def one_block(first_row):
        q_block = lax.dynamic_slice_in_dim(queries, first_row, block_rows, 0)
        seg_block = lax.dynamic_slice_in_dim(segs, first_row, block_rows, 0)
        row_ids = first_row + jnp.arange(block_rows, dtype=jnp.int32)
        columns = jnp.arange(group_len, dtype=jnp.int32)
        offsets = jnp.clip(columns[None, :] - row_ids[:, None], -half_span, half_span - 1) + half_span
        scores = jnp.einsum('qhd,khd->hqk', q_block, key_rows, precision=HIGH) * score_scale
        scores = low_back(scores + jnp.take(bias_table, offsets, axis=1))
        same_utt = seg_block[:, None] == segs[None, :]
        masked = jnp.where(same_utt[None], scores, -1000000000.0)
        row_max = lax.optimization_barrier(jnp.max(masked, axis=-1, keepdims=True))
        exp_scores = jnp.exp(masked - row_max)
        softmax_out = low(exp_scores / lax.optimization_barrier(jnp.sum(exp_scores, axis=-1, keepdims=True)))
        return jnp.einsum('hqk,khd->qhd', softmax_out, value_rows, precision=HIGH)
    starts = jnp.arange(group_len // block_rows, dtype=jnp.int32) * block_rows
    block_outputs = lax.map(jax.checkpoint(one_block), starts)
    return block_outputs.reshape(group_len, packed.shape[1], head_width)

def depthwise(mixed_rows, taps_mat, segs):
    kernel = taps_mat.shape[0]
    half_k = kernel // 2
    total_rows = mixed_rows.shape[0]
    padded = jnp.pad(mixed_rows, ((half_k, half_k), (0, 0)))
    seg_pad = jnp.pad(segs, (half_k, half_k), constant_values=-1)
    result = jnp.zeros_like(mixed_rows)
    for tap_index in range(kernel):
        same_utt = (seg_pad[tap_index:tap_index + total_rows] == segs).astype(jnp.float32)
        result = result + taps_mat[tap_index] * padded[tap_index:tap_index + total_rows] * same_utt[:, None]
    return result

def forward(values, params, segs_local, segs_global, live_mask):
    mix_gain, mix_shift, mix_inputs, position_bias, mix_output, mix_output_bias = params[6:12]
    filter_gain, filter_shift, pointwise_in, pointwise_in_bias, depthwise_taps = params[12:17]
    batch_gain, batch_shift, pointwise_out, pointwise_out_bias = params[17:21]
    final_gain, final_shift = params[27:29]
    x_one = values + 0.5 * feed_forward(values, params[0:6])
    normed = low(layer_norm(x_one, mix_gain, mix_shift))
    packed = low_back(low(product(normed, mix_inputs)))
    packed = packed.reshape(GROUPS, GROUP_LEN, HEADS, 3 * HEAD_DIM)
    attended = lax.map(lambda group_pair: attend_group(group_pair[0], group_pair[1], position_bias), (packed, segs_local.reshape(GROUPS, GROUP_LEN)))
    attended = low_back(low(attended.reshape(-1, D)))
    x_two = x_one + low_back(product(attended, mix_output) + mix_output_bias)
    normed = low(layer_norm(x_two, filter_gain, filter_shift))
    gated = low_back(product(normed, pointwise_in) + pointwise_in_bias)
    glu_out = gated[:, :D] * jax.nn.sigmoid(gated[:, D:])
    mixed_rows = low(glu_out * live_mask[:, None])
    conv_out = low_back(depthwise(mixed_rows, depthwise_taps, segs_global))
    live_count = jnp.sum(live_mask)
    batch_mean = lax.optimization_barrier(jnp.sum(live_mask[:, None] * conv_out, axis=0)) / live_count
    centered = conv_out - batch_mean
    spread = lax.optimization_barrier(jnp.sum(live_mask[:, None] * centered * centered, axis=0)) / live_count
    normalized = centered * lax.rsqrt(spread + EPSILON) * batch_gain + batch_shift
    activated = low(jax.nn.silu(normalized))
    x_three = x_two + low_back(product(activated, pointwise_out) + pointwise_out_bias)
    x_four = x_three + 0.5 * feed_forward(x_three, params[21:27])
    return layer_norm(x_four, final_gain, final_shift)

def reference(frames, lengths, first_gain, first_shift, first_up, first_up_bias, first_down, first_down_bias, mix_gain, mix_shift, mix_inputs, position_bias, mix_output, mix_output_bias, filter_gain, filter_shift, pointwise_in, pointwise_in_bias, depthwise_taps, batch_gain, batch_shift, pointwise_out, pointwise_out_bias, second_gain, second_shift, second_up, second_up_bias, second_down, second_down_bias, final_gain, final_shift, cotangent):
    weights = (first_gain, first_shift, first_up, first_up_bias, first_down, first_down_bias, mix_gain, mix_shift, mix_inputs, position_bias, mix_output, mix_output_bias, filter_gain, filter_shift, pointwise_in, pointwise_in_bias, depthwise_taps, batch_gain, batch_shift, pointwise_out, pointwise_out_bias, second_gain, second_shift, second_up, second_up_bias, second_down, second_down_bias, final_gain, final_shift)
    params = tuple((weight_arr.astype(jnp.float32) for weight_arr in weights))
    segs_local = jax.vmap(lambda length_row: group_segments(length_row, GROUP_LEN))(lengths).reshape(-1)
    live_mask = (segs_local < lengths.shape[1]).astype(jnp.float32)
    group_base = jnp.repeat(jnp.arange(GROUPS, dtype=jnp.int32) * (lengths.shape[1] + 1), GROUP_LEN, total_repeat_length=GROUPS * GROUP_LEN)
    segs_global = (segs_local + group_base).astype(jnp.int32)
    output, pullback = jax.vjp(lambda values, params_in: forward(values, params_in, segs_local, segs_global, live_mask), frames.astype(jnp.float32), params)
    grad_frames, grad_params = pullback(cotangent.astype(jnp.float32))
    return (output.astype(jnp.bfloat16), grad_frames, grad_params[0], grad_params[1], grad_params[2], grad_params[3], grad_params[4], grad_params[5], grad_params[6], grad_params[7], grad_params[8], grad_params[9], grad_params[10], grad_params[11], grad_params[12], grad_params[13], grad_params[14], grad_params[15], grad_params[16], grad_params[17], grad_params[18], grad_params[19], grad_params[20], grad_params[21], grad_params[22], grad_params[23], grad_params[24], grad_params[25], grad_params[26], grad_params[27], grad_params[28])
```

```python
import dataclasses
import functools
import math
import types

import jax
import jax.numpy as jnp
from jax import lax
from jax.experimental import pallas as pl
from jax.experimental.pallas import tpu as pltpu
from jax.sharding import PartitionSpec as P

BF = jnp.bfloat16
F32 = jnp.float32
LOG2E = math.log2(math.e)
BLK = 512
UNIT = 128
PER = BLK // UNIT
NEAR = PER + 2
PAD = 8 * UNIT
SLOT = 48
DEPTH = 128
MASKED = -1e30
NN = (((1,), (0,)), ((), ()))
NT = (((1,), (1,)), ((), ()))
TN = (((0,), (0,)), ((), ()))


def dot(a, b, dims=NN):
    return lax.dot_general(a, b, dims, preferred_element_type=F32)


def iota(shape, dim):
    return lax.broadcasted_iota(jnp.int32, shape, dim)


def spread_cols(width, slots, slot_rows, used):
    row, column = iota((slots * slot_rows, width), 0), iota((slots * slot_rows, width), 1)
    hit = jnp.zeros((slots * slot_rows, width), jnp.bool_)
    for s in range(slots):
        f = row - slot_rows * s
        hit = hit | ((f >= 0) & (f < used) & (column == used * s + f))
    return hit.astype(F32).astype(BF)


def split3(v):
    hi = v.astype(BF).astype(F32)
    r1 = v - hi
    mid = r1.astype(BF).astype(F32)
    return hi, mid, r1 - mid


def three_rows(v, rows):
    a, b, e = split3(v)
    row = iota((rows, v.shape[1]), 0)
    return jnp.where(row == 0, a, jnp.where(row == 1, b, jnp.where(row == 2, e, 0.0)))


def pick_row(ref, index):
    values = ref[...].astype(F32)
    return jnp.sum(jnp.where(iota(values.shape, 0) == index, values, 0.0), axis=0, keepdims=True)


def bias_square(table, d):
    span = table.shape[1]
    half = span // 2
    lanes = 2 * UNIT
    u = iota((span, lanes), 1)
    u = jnp.where(u < UNIT, u, u - lanes)
    ids = jnp.clip(-UNIT * d - u, -half, half - 1) + half
    hot = (ids == iota((span, lanes), 0)).astype(F32).astype(BF)
    line = dot(jnp.broadcast_to(table, (UNIT, span)).astype(BF), hot) * LOG2E
    return pltpu.roll(line, 0, 1, stride=1, stride_axis=0)[:, :UNIT]


def bias_near(table, tile, keys_near):
    span = table.shape[1]
    squares = {d: bias_square(table, d) for d in (-1, 0, 1)}
    low = jnp.broadcast_to(table[:, :1] * LOG2E, (UNIT, UNIT))
    high = jnp.broadcast_to(table[:, span - 1 :] * LOG2E, (UNIT, UNIT))
    for r in range(tile.shape[0] // UNIT):
        for c in range(tile.shape[1] // UNIT):
            d = c - (r - 1) if keys_near else (c - 1) - r
            part = squares[d] if abs(d) < 2 else (low if d > 0 else high)
            tile[r * UNIT : (r + 1) * UNIT, c * UNIT : (c + 1) * UNIT] = part


def units_at(u, count):
    return pl.ds(pl.multiple_of(u * UNIT, UNIT), count * UNIT)


def far_windows(low, plain, edge, step, side, up):
    sign = 1 if up else -1

    def run(at, times, size, masked):
        def one(i, carry):
            near = at + sign * i * size
            step(near if up else near - size, size, side, masked)
            return carry

        lax.fori_loop(0, times, one, 0)
        return at + sign * times * size

    at = run(edge, sign * (plain - edge) // 8, 8, False)
    left = sign * (low - at)
    tail = lax.rem(left, 8)
    at = run(at, left // 8 + (tail > 4).astype(jnp.int32), 8, True)
    run(at, ((tail > 0) & (tail <= 4)).astype(jnp.int32), 4, True)


def far_sweep(plan, block, step, before, after):
    low, plain_low, plain_high, high = [plan[block, i] for i in range(4)]
    start, stop = PER * block - 1, PER * block + PER + 1
    far_windows(low, plain_low, start, step, before, False)
    far_windows(high, plain_high, stop, step, after, True)


def has_far(plan, block):
    return (plan[block, 0] < PER * block - 1) | (plan[block, 3] > PER * block + PER + 1)


def segment_rows(ends, lengths, place, total):
    slots = ends.shape[0]
    before = ends <= jnp.broadcast_to(place, (slots, place.shape[1]))
    seg = jnp.sum(before.astype(jnp.int32), axis=0, keepdims=True)
    first = jnp.sum(jnp.where(before, lengths, 0), axis=0, keepdims=True)
    stop = jnp.min(jnp.where(before, total, ends), axis=0, keepdims=True)
    return seg, first, stop


def block_plan(ends, ends_row, total):
    slots = ends.shape[0]
    blocks, units = total // BLK, total // UNIT

    def along(place):
        return jnp.sum((ends <= jnp.broadcast_to(place, (slots, 128))).astype(jnp.int32), axis=0, keepdims=True)

    def down(place):
        return jnp.sum((jnp.broadcast_to(ends_row, (blocks, slots)) <= place).astype(F32), axis=1, keepdims=True).astype(jnp.int32)

    unit = iota((1, 128), 1)
    u_first, u_last = along(unit * UNIT), along(unit * UNIT + UNIT - 1)
    b = iota((blocks, 1), 0)
    first, last = down(b * BLK), down(b * BLK + BLK - 1)
    start, stop = PER * b - 1, PER * b + PER + 1
    inside = unit < units

    def count(hit):
        return jnp.sum((hit & inside).astype(F32), axis=1, keepdims=True).astype(jnp.int32)

    low = jnp.minimum(count(u_last < first), start)
    high = jnp.maximum(units - count(u_first > last), stop)
    plain_low = start - count((unit < start) & (u_first == last))
    plain_high = stop + count((unit >= stop) & (u_last == first))
    lane = iota((blocks, 128), 1)
    out = jnp.zeros((blocks, 128), jnp.int32)
    for i, v in enumerate((low, plain_low, plain_high, high)):
        out = jnp.where(lane == i, v, out)
    return out


def meets(first_key, rows, bounds):
    key = iota((rows, bounds.shape[1]), 0)
    return (key >= bounds[0:1, :] - first_key) & (key < bounds[1:2, :] - first_key)


def fwd_kernel(plan, qkv_ref, table_ref, bound_ref, o_ref, of_ref, lse_ref, qaug, kn, vt, tile, top_ref, acc, *, head_width):
    chunks, packed_rows, rows = qkv_ref.shape
    total = chunks * rows
    blocks = total // BLK
    span = table_ref.shape[1]
    table = pick_row(table_ref, lax.axis_index("head"))
    far = (table[:, :1] * LOG2E, table[:, span - 1 :] * LOG2E)
    pick = spread_cols(packed_rows, 3, SLOT, head_width)
    scale = LOG2E / math.sqrt(head_width)
    o_ref[:, :UNIT] = jnp.zeros((SLOT, UNIT), BF)
    o_ref[:, UNIT + total :] = jnp.zeros((SLOT, UNIT), BF)
    for edge in (slice(0, PAD), slice(PAD + total, 2 * PAD + total)):
        kn[edge, :] = jnp.zeros((PAD, DEPTH), BF)
        vt[:, edge] = jnp.zeros((SLOT, PAD), BF)
    bias_near(table, tile, True)
    rest = DEPTH - 2 * SLOT

    @pl.loop(0, chunks)
    def _(c):
        at = pl.ds(pl.multiple_of(c * rows, rows), rows)
        at_pad = pl.ds(pl.multiple_of(c * rows + PAD, UNIT), rows)
        parts = dot(pick, qkv_ref[c])
        q = parts[:SLOT] * scale
        hi = q.astype(BF)
        lo = (q - hi.astype(F32)).astype(BF)
        for s in range(3):
            qaug[s, :SLOT, at] = hi
            qaug[s, SLOT : 2 * SLOT, at] = lo
            qaug[s, 2 * SLOT :, at] = jnp.zeros((rest, rows), BF)
        k = parts[SLOT : 2 * SLOT]
        one3 = (iota((rest, rows), 0) < 3).astype(F32)
        kn[at_pad, :] = jnp.concatenate([k, k, one3], axis=0).T.astype(BF)
        one = (iota((SLOT, rows), 0) == head_width).astype(F32)
        vt[:, at_pad] = (parts[2 * SLOT :] + one).astype(BF)

    def top(x):
        return jnp.max(x.reshape(x.shape[0] // 8, 8, BLK), axis=0)

    @pl.loop(0, blocks // 2)
    def _(pair):
        for i in range(2):
            b = 2 * pair + i
            at_q = units_at(PER * b, PER)
            near = units_at(PER * b - 1 + PAD // UNIT, NEAR)
            x = dot(kn[near, :], qaug[1, :, at_q]) + tile[...]
            x = jnp.where(meets(PER * b * UNIT - UNIT, NEAR * UNIT, bound_ref[:, units_at(PER * b + PAD // UNIT, PER)]), x, MASKED)
            m = jnp.max(top(x), axis=0, keepdims=True)
            acc[:, at_q] = dot(vt[:, near], jnp.exp2(x - m).astype(BF))
            lse_ref[:, at_q] = m
            qaug[0, 2 * SLOT :, at_q] = three_rows(far[0] - m, rest).astype(BF)
            qaug[2, 2 * SLOT :, at_q] = three_rows(far[1] - m, rest).astype(BF)

    @pl.loop(0, blocks)
    def _(b):
        @pl.when(has_far(plan, b))
        def _():
            at_q = units_at(PER * b, PER)

            def scores(u, count, side, masked):
                x = dot(kn[units_at(u + PAD // UNIT, count), :], qaug[side, :, at_q])
                if masked:
                    x = jnp.where(meets(u * UNIT, count * UNIT, bound_ref[:, units_at(PER * b + PAD // UNIT, PER)]), x, MASKED)
                return x

            near_acc = acc[:, at_q]

            def add(u, count, side, masked):
                p = jnp.exp2(scores(u, count, side, masked)).astype(BF)
                acc[:, at_q] += dot(vt[:, units_at(u + PAD // UNIT, count)], p)

            far_sweep(plan, b, add, 0, 2)
            sums = acc[head_width : head_width + 1, at_q]
            over = jnp.max(jnp.where(sums < 2.0**60, 0.0, 1.0))

            @pl.when(over > 0.5)
            def _():
                top_ref[...] = jnp.zeros_like(top_ref)

                def first(u, count, side, masked):
                    top_ref[...] = jnp.maximum(top_ref[...], top(scores(u, count, side, masked)))

                far_sweep(plan, b, first, 0, 2)
                m = jnp.max(top_ref[...], axis=0, keepdims=True)
                acc[:, at_q] = near_acc * jnp.exp2(-m)
                lse_ref[:, at_q] += m

                def second(u, count, side, masked):
                    p = jnp.exp2(scores(u, count, side, masked) - m).astype(BF)
                    acc[:, at_q] += dot(vt[:, units_at(u + PAD // UNIT, count)], p)

                far_sweep(plan, b, second, 0, 2)

    @pl.loop(0, chunks)
    def _(c):
        at = pl.ds(pl.multiple_of(c * rows, rows), rows)
        total_p = acc[head_width : head_width + 1, at]
        out = acc[:, at] / total_p
        o_ref[:, pl.ds(pl.multiple_of(c * rows + UNIT, UNIT), rows)] = out.astype(BF)
        of_ref[:, at] = out[: of_ref.shape[0]]
        lse_ref[:, at] = lse_ref[:, at] + jnp.log2(total_p)


def attend_forward(qkv, bounds, plan, table, head_width):
    chunks, packed_rows, rows = qkv.shape
    total = chunks * rows
    vm = pltpu.VMEM
    return pl.pallas_call(
        functools.partial(fwd_kernel, head_width=head_width),
        out_shape=(
            jax.ShapeDtypeStruct((SLOT, total + 2 * UNIT), BF),
            jax.ShapeDtypeStruct((40, total), F32),
            jax.ShapeDtypeStruct((1, total), F32),
        ),
        in_specs=[pl.BlockSpec(memory_space=pltpu.SMEM)] + [pl.BlockSpec()] * 3,
        scratch_shapes=[
            vm((3, DEPTH, total), BF),
            vm((total + 2 * PAD, DEPTH), BF),
            vm((SLOT, total + 2 * PAD), BF),
            vm((NEAR * UNIT, BLK), F32),
            vm((8, BLK), F32),
            vm((SLOT, total), F32),
        ],
        compiler_params=pltpu.CompilerParams(vmem_limit_bytes=62 * 2**20),
        name="attend_forward",
    )(plan, qkv, table, bounds)


def bwd_kernel(plan, qkv_ref, do_ref, of_ref, lse_ref, table_ref, bound_ref, dqkv_ref, dtab_ref,
               qaug, kn, kt, vn, dot_t, qn, don, tile, dq, band, ends, dv_acc, dk_acc, dwide, *, head_width):
    chunks, packed_rows, rows = qkv_ref.shape
    total = chunks * rows
    blocks = total // BLK
    span = table_ref.shape[1]
    table = pick_row(table_ref, lax.axis_index("head"))
    pick = spread_cols(packed_rows, 3, SLOT, head_width)
    scale = LOG2E / math.sqrt(head_width)
    back = 1.0 / math.sqrt(head_width)
    rest = DEPTH - 2 * SLOT
    bias_near(table, tile, False)
    for edge in (slice(0, PAD), slice(PAD + total, 2 * PAD + total)):
        for s in range(3):
            qaug[s, :, edge] = jnp.zeros((DEPTH, PAD), BF)
        dot_t[:, edge] = jnp.zeros((DEPTH, PAD), BF)
        qn[edge, :] = jnp.zeros((PAD, DEPTH), BF)
        don[edge, :] = jnp.zeros((PAD, DEPTH), BF)

    @pl.loop(0, chunks)
    def _(c):
        at = pl.ds(pl.multiple_of(c * rows, rows), rows)
        at_pad = pl.ds(pl.multiple_of(c * rows + PAD, UNIT), rows)
        parts = dot(pick, qkv_ref[c])
        q, k, v = parts[:SLOT], parts[SLOT : 2 * SLOT], parts[2 * SLOT :]
        qs = q * scale
        hi = qs.astype(BF)
        lo = (qs - hi.astype(F32)).astype(BF)
        lse = lse_ref[:, at]
        for s, shift in enumerate((table[:, :1] * LOG2E, 0.0, table[:, span - 1 :] * LOG2E)):
            qaug[s, :SLOT, at_pad] = hi
            qaug[s, SLOT : 2 * SLOT, at_pad] = lo
            qaug[s, 2 * SLOT :, at_pad] = three_rows(shift - lse, rest).astype(BF)
        one3 = (iota((rest, rows), 0) < 3).astype(F32)
        row48 = iota((SLOT, rows), 0)
        none = jnp.zeros((rest, rows), F32)
        empty = jnp.zeros((SLOT, rows), F32)
        kn[at, :] = jnp.concatenate([k, k, one3], axis=0).T.astype(BF)
        kt[:, at] = k.astype(BF)
        vn[at, :] = jnp.concatenate([v, empty, one3], axis=0).T.astype(BF)
        do = do_ref[c].astype(F32)
        centre = jnp.sum(do[: of_ref.shape[0]] * of_ref[:, at], axis=0, keepdims=True)
        dot_t[:SLOT, at_pad] = do_ref[c]
        dot_t[SLOT : 2 * SLOT, at_pad] = empty.astype(BF)
        dot_t[2 * SLOT :, at_pad] = three_rows(-centre, rest).astype(BF)
        qn[at_pad, :] = jnp.concatenate([q + (row48 == head_width).astype(F32), empty, none], axis=0).T.astype(BF)
        don[at_pad, :] = jnp.concatenate([do, empty, none], axis=0).T.astype(BF)

    dq[...] = jnp.zeros_like(dq)
    band[...] = jnp.zeros_like(band)
    ends[...] = jnp.zeros_like(ends)

    @pl.loop(0, blocks // 2)
    def _(pair):
        width = NEAR * UNIT
        wide = width + BLK
        whole, lines = [], []
        for i in range(2):
            b = 2 * pair + i
            at_k = units_at(PER * b, PER)
            near = units_at(PER * b - 1 + PAD // UNIT, NEAR)
            p = jnp.exp2(dot(kn[at_k, :], qaug[1, :, near]) + tile[...])
            p = jnp.where(meets(b * BLK, BLK, bound_ref[:, near]), p, 0.0)
            dsb = (p * dot(vn[at_k, :], dot_t[:, near])).astype(BF)
            dv_acc[at_k, :] = dot(p.astype(BF), don[near, :])
            dk_acc[at_k, :] = dot(dsb, qn[near, :])
            part = dot(kt[:, at_k], dsb)
            gap = jnp.zeros((SLOT, BLK), F32)
            whole.append(jnp.concatenate([gap, part] if i else [part, gap], axis=1))
            lines.append(dsb.astype(F32))
        dq[:, units_at(2 * PER * pair - 1 + PAD // UNIT, wide // UNIT)] += whole[0] + whole[1]
        band[...] += lines[0] + lines[1]

    @pl.loop(0, blocks)
    def _(b):
        @pl.when(has_far(plan, b))
        def _():
            at_k = units_at(PER * b, PER)

            def far(u, count, side, masked):
                at_q = units_at(u + PAD // UNIT, count)
                p = jnp.exp2(dot(kn[at_k, :], qaug[side, :, at_q]))
                if masked:
                    p = jnp.where(meets(b * BLK, BLK, bound_ref[:, at_q]), p, 0.0)
                dsb = (p * dot(vn[at_k, :], dot_t[:, at_q])).astype(BF)
                dq[:, at_q] += dot(kt[:, at_k], dsb)
                dv_acc[at_k, :] += dot(p.astype(BF), don[at_q, :])
                dk = dot(dsb, qn[at_q, :])
                dk_acc[at_k, :] += dk
                ends[side // 2] += jnp.sum(dk.reshape(BLK // 8, 8, DEPTH), axis=0)

            far_sweep(plan, b, far, 2, 0)

    @pl.loop(0, chunks)
    def _(c):
        at = pl.ds(pl.multiple_of(c * rows, rows), rows)
        at_pad = pl.ds(pl.multiple_of(c * rows + PAD, UNIT), rows)
        dwide[:SLOT, :] = (dq[:, at_pad] * back).astype(BF)
        dwide[SLOT : 2 * SLOT, :] = (dk_acc[at, :].T[:SLOT] * back).astype(BF)
        dwide[2 * SLOT :, :] = dv_acc[at, :].T[:SLOT].astype(BF)
        dqkv_ref[c] = dot(pick, dwide[...], TN).astype(BF)

    flip = (iota((UNIT, UNIT), 0) + iota((UNIT, UNIT), 1) == UNIT - 1).astype(F32)
    half = span // 2
    lane = iota((8, span), 1)
    column = iota((8, DEPTH), 1) == head_width
    out = jnp.zeros((8, span), F32)
    far_sum = [jnp.where(column, ends[i], 0.0) for i in range(2)]
    for d in range(-PER, PER + 1):
        part = jnp.zeros((UNIT, UNIT), F32)
        for r in range(PER):
            c = r + d + 1
            if 0 <= c < NEAR:
                part = part + band[r * UNIT : (r + 1) * UNIT, c * UNIT : (c + 1) * UNIT]
        if abs(d) > 1:
            far_sum[0 if d > 0 else 1] += jnp.sum(part.reshape(UNIT // 8, 8, UNIT), axis=0)
            continue
        turned = lax.dot_general(flip, part, NN, precision=lax.Precision.HIGHEST, preferred_element_type=F32)
        wide = jnp.concatenate([turned, jnp.zeros_like(turned)], axis=1)
        skewed = pltpu.roll(wide, 0, 1, stride=1, stride_axis=0)
        line = jnp.sum(skewed.reshape(UNIT // 8, 8, 2 * UNIT), axis=0)
        offset = UNIT - 1 - d * UNIT - iota((span, 2 * UNIT), 1)
        hot = (jnp.clip(offset, -half, half - 1) + half == iota((span, 2 * UNIT), 0)).astype(F32)
        out += lax.dot_general(line, hot, NT, precision=lax.Precision.HIGHEST, preferred_element_type=F32)
    out += jnp.where(lane == 0, jnp.sum(far_sum[0], axis=1, keepdims=True), 0.0)
    out += jnp.where(lane == span - 1, jnp.sum(far_sum[1], axis=1, keepdims=True), 0.0)
    out = jnp.sum(out, axis=0, keepdims=True)
    dtab_ref[...] = out


def attend_backward(qkv, do, of, lse, bounds, plan, table, head_width):
    chunks, packed_rows, rows = qkv.shape
    total = chunks * rows
    padded = total + 2 * PAD
    span = table.shape[1]
    vm = pltpu.VMEM
    return pl.pallas_call(
        functools.partial(bwd_kernel, head_width=head_width),
        out_shape=(
            jax.ShapeDtypeStruct((chunks, packed_rows, rows), BF),
            jax.ShapeDtypeStruct((1, span), F32),
        ),
        in_specs=[pl.BlockSpec(memory_space=pltpu.SMEM)] + [pl.BlockSpec()] * 6,
        scratch_shapes=[
            vm((3, DEPTH, padded), BF),
            vm((total, DEPTH), BF),
            vm((SLOT, total), BF),
            vm((total, DEPTH), BF),
            vm((DEPTH, padded), BF),
            vm((padded, DEPTH), BF),
            vm((padded, DEPTH), BF),
            vm((BLK, NEAR * UNIT), F32),
            vm((SLOT, padded), F32),
            vm((BLK, NEAR * UNIT), F32),
            vm((2, 8, DEPTH), F32),
            vm((total, DEPTH), F32),
            vm((total, DEPTH), F32),
            vm((3 * SLOT, rows), BF),
        ],
        compiler_params=pltpu.CompilerParams(vmem_limit_bytes=62 * 2**20),
        name="attend_backward",
    )(plan, qkv, do, of, lse, table, bounds)

VEC = types.SimpleNamespace(
    first_gain=0, first_shift=1, first_up_bias=2, first_down_bias=3, mix_gain=4, mix_shift=5, mix_output_bias=6, filter_gain=7,
    filter_shift=8, pointwise_in_bias=9, batch_gain=10, batch_shift=11, pointwise_out_bias=12, second_gain=13, second_shift=14,
    second_up_bias=15, second_down_bias=16, final_gain=17, final_shift=18,
)
VEC_ROWS = 24
EPSILON = 1e-05
HALO = 64
TILE = 128
STEP = 256


def col(cols_ref, i, size):
    return cols_ref[:size, i : i + 1]


def eye(n):
    return (iota((n, n), 0) == iota((n, n), 1)).astype(F32).astype(BF)


def flipped(mat):
    return dot(eye(mat.shape[1]), mat, NT).astype(BF)


def exact(a, b, dims=NN):
    return lax.dot_general(a, b, dims, precision=lax.Precision.HIGHEST, preferred_element_type=F32)


def row_sums(values):
    part = values[:, :TILE]
    for at in range(TILE, values.shape[1], TILE):
        part = part + values[:, at : at + TILE]
    return exact(jnp.ones((8, TILE), F32), part, NT)


def norm(x):
    m = jnp.mean(x, axis=0, keepdims=True)
    c = x - m
    inv = lax.rsqrt(jnp.mean(c * c, axis=0, keepdims=True) + EPSILON)
    return c * inv, inv


def norm_back(e, n, inv, gain):
    ea = e * gain
    return inv * (ea - jnp.mean(ea, axis=0, keepdims=True) - n * jnp.mean(ea * n, axis=0, keepdims=True))


def sigmoid(v):
    return 1.0 / (1.0 + jnp.exp(-v))


def ones_row(rows, lanes):
    return (iota((rows, lanes), 0) == 0).astype(F32).astype(BF)


def open_kernel(frames_ref, len_ref, up_ref, down_ref, mix_ref, *refs, packed_rows):
    vec_refs, (x1_ref, h2_ref, qkv_ref, cols_ref, bound_ref, plan_ref, ext_ref, line) = refs[:-8], refs[-8:]
    width, rows = frames_ref.shape
    hidden = up_ref.shape[1]
    heads = qkv_ref.shape[0]
    group = bound_ref.shape[1] - 2 * PAD
    vecs = [ref[...].astype(F32).reshape(1, ref.shape[0]) for ref in vec_refs]
    cols_ref[...] = stack_rows(vecs, (VEC_ROWS, hidden)).T
    slots = len_ref.shape[1]
    lengths = jnp.broadcast_to(len_ref[...].astype(F32), (8, slots))
    row, column = iota((slots, slots), 0), iota((slots, slots), 1)
    ends = exact((column <= row).astype(F32), lengths, NT)[:, :1].astype(jnp.int32)
    own_len = exact((column == row).astype(F32), lengths, NT)[:, :1].astype(jnp.int32)
    ends_row = exact(lengths, (row <= column).astype(F32))[:1].astype(jnp.int32)
    plan_ref[...] = block_plan(ends, ends_row, group)
    line[...] = jnp.full_like(line, -1)
    for edge in (slice(0, PAD), slice(PAD + group, 2 * PAD + group)):
        bound_ref[:, edge] = jnp.where(iota((2, PAD), 0) == 0, 1 << 20, -1)

    @pl.loop(0, group // 512)
    def _(c):
        at = pl.multiple_of(c * 512, 512)
        seg, first, stop = segment_rows(ends, own_len, iota((1, 512), 1) + at, group)
        line[:, pl.ds(at + TILE, 512)] = seg
        bound_ref[0:1, pl.ds(at + PAD, 512)] = first
        bound_ref[1:2, pl.ds(at + PAD, 512)] = stop

    first = pl.multiple_of(lax.axis_index("head") * rows, TILE)
    ext_ref[:, :rows] = line[:, pl.ds(first + TILE, rows)]
    left = line[:, pl.ds(first, TILE)]
    right = line[:, pl.ds(first + TILE + rows, TILE)]
    ext_ref[:, rows:] = jnp.where(iota((1, TILE), 1) < HALO, right, left)

    up_t = flipped(up_ref[...])
    mix_t = dot(spread_cols(mix_ref.shape[1], heads, packed_rows, mix_ref.shape[1] // heads), mix_ref[...], NT).astype(BF)

    @pl.loop(0, rows // STEP)
    def _(c):
        at = pl.ds(pl.multiple_of(c * STEP, STEP), STEP)
        x0 = frames_ref[:, at].astype(F32)
        n, _ = norm(x0)
        h1 = (n * col(cols_ref, VEC.first_gain, width) + col(cols_ref, VEC.first_shift, width)).astype(BF)
        a1 = dot(up_t, h1) + col(cols_ref, VEC.first_up_bias, hidden)
        s1 = (a1 * sigmoid(a1)).astype(BF)
        x1 = x0 + 0.5 * (dot(down_ref[...], s1) + col(cols_ref, VEC.first_down_bias, width))
        x1_ref[:, at] = x1
        n, _ = norm(x1)
        h2 = (n * col(cols_ref, VEC.mix_gain, width) + col(cols_ref, VEC.mix_shift, width)).astype(BF)
        h2_ref[:, at] = h2
        qkv = dot(mix_t, h2).astype(BF)
        for h in range(heads):
            qkv_ref[h, :, at] = qkv[h * packed_rows : (h + 1) * packed_rows]


def conv_masks(mask_ref, ext_ref, taps, sign):
    seg = jnp.broadcast_to(ext_ref[...], (8, ext_ref.shape[1]))
    lanes = seg.shape[1]
    for k in range(taps):
        other = pltpu.roll(seg, (sign * (taps // 2 - k)) % lanes, 1)
        mask_ref[k] = (other == seg).astype(F32)


def filter_kernel(x1_ref, x1l_ref, x1r_ref, o_ref, cols_ref, ext_ref, out_ref, pw_ref, taps_ref,
                  x2_ref, oc_ref, u_ref, y_ref, stat_ref, wide, mask, *, head_width, slot_count):
    width, rows = x1_ref.shape
    lanes = rows + TILE
    heads = o_ref.shape[0]
    taps = taps_ref.shape[0]
    out_t = flipped(out_ref[...])
    pw_t = flipped(pw_ref[...])
    gather = spread_cols(width, heads, SLOT, head_width)
    seg = ext_ref[...]
    live = (seg >= 0) & (seg < slot_count)
    mask[0, :1, :] = live.astype(F32)

    def part(x1, o, live_part):
        oc = dot(gather, o, TN).astype(BF)
        x2 = x1 + (dot(out_t, oc) + col(cols_ref, VEC.mix_output_bias, width))
        n, _ = norm(x2)
        h3 = (n * col(cols_ref, VEC.filter_gain, width) + col(cols_ref, VEC.filter_shift, width)).astype(BF)
        g = dot(pw_t, h3) + col(cols_ref, VEC.pointwise_in_bias, 2 * width)
        u = jnp.where(live_part > 0.5, g[:width] * sigmoid(g[width:]), 0.0).astype(BF)
        return oc, x2, u

    @pl.loop(0, rows // STEP)
    def _(c):
        at = pl.ds(pl.multiple_of(c * STEP, STEP), STEP)
        at_o = pl.ds(pl.multiple_of(c * STEP + TILE, TILE), STEP)
        o = jnp.concatenate([o_ref[h, :, at_o] for h in range(heads)], axis=0)
        oc, x2, u = part(x1_ref[:, at], o, mask[0, :1, at])
        oc_ref[:, at] = oc
        x2_ref[:, at] = x2
        u_ref[:, at] = u
        wide[:, at] = u.astype(F32)

    near = iota((1, TILE), 1) < HALO
    x1 = jnp.where(near, x1r_ref[...], x1l_ref[...])
    o = jnp.concatenate([jnp.where(near, o_ref[h, :, TILE + rows :].astype(F32), o_ref[h, :, :TILE].astype(F32)).astype(BF) for h in range(heads)], axis=0)
    _, x2, u = part(x1, o, mask[0, :1, rows:])
    x2_ref[:, rows:] = x2
    u_ref[:, rows:] = u
    wide[:, rows:] = u.astype(F32)

    conv_masks(mask, ext_ref, taps, 1)
    tap_cols = taps_ref[...].astype(F32).T
    wide_taps = tap_cols

    own = (live & (iota((1, lanes), 1) < rows)).astype(F32)
    count = jnp.sum(own, axis=1, keepdims=True)
    safe = jnp.maximum(count, 1.0)
    stats = []
    for r in range(width // 8):
        sl = slice(8 * r, 8 * r + 8)
        u8 = wide[sl, :]
        acc = jnp.zeros((8, lanes), F32)
        for k in range(taps):
            moved = pltpu.roll(u8, (taps // 2 - k) % lanes, 1)
            acc = acc + wide_taps[sl, k : k + 1] * (moved * mask[k])
        y_ref[sl, :] = acc
        mean = jnp.sum(acc * own, axis=1, keepdims=True) / safe
        dev = acc - mean
        spread = jnp.sum(dev * dev * own, axis=1, keepdims=True)
        lane = iota((8, TILE), 1)
        stats.append(jnp.where(lane == 0, mean, jnp.where(lane == 1, spread, jnp.where(lane == 2, count, 0.0))))
    stat_ref[...] = jnp.concatenate(stats, axis=0).T[:8, :]


def total_stats(stats_ref):
    n = stats_ref[:, 2:3, :]
    mean_of = stats_ref[:, 0:1, :]
    count = jnp.sum(n, axis=0)
    mean = jnp.sum(n * mean_of, axis=0) / count
    gap = mean_of - mean[None]
    spread = jnp.sum(stats_ref[:, 1:2, :] + n * gap * gap, axis=0)
    inv = lax.rsqrt(spread / count + EPSILON)
    table = jnp.concatenate([mean, inv, count, jnp.zeros((5, mean.shape[1]), F32)], axis=0).T
    return table[:, 0:1], table[:, 1:2], table[:, 2:3]


def second_kernel(x2_ref, y_ref, stats_ref, cot_ref, cotl_ref, cotr_ref, cols_ref, pwo_ref, up_ref, down_ref,
                  out_ref, dx3_ref, e_ref, sums_ref, pack_ref, small_ref,
                  h4s, das, s4s, dfs, ws, dcs, gains):
    width, rows = out_ref.shape
    hidden = up_ref.shape[1]
    mean, inv_b, _ = total_stats(stats_ref)
    pwo_t = flipped(pwo_ref[...])
    up_t = flipped(up_ref[...])
    down = flipped(down_ref[...])
    gains[...] = jnp.zeros_like(gains)
    bgain = col(cols_ref, VEC.batch_gain, width)

    def part(x2, y, cot, at):
        zh = (y - mean) * inv_b
        z = zh * bgain + col(cols_ref, VEC.batch_shift, width)
        sig_z = sigmoid(z)
        w = (z * sig_z).astype(BF)
        x3 = x2 + (dot(pwo_t, w) + col(cols_ref, VEC.pointwise_out_bias, width))
        n4, inv4 = norm(x3)
        h4 = (n4 * col(cols_ref, VEC.second_gain, width) + col(cols_ref, VEC.second_shift, width)).astype(BF)
        a4 = dot(up_t, h4) + col(cols_ref, VEC.second_up_bias, hidden)
        sig = sigmoid(a4)
        s4 = (a4 * sig).astype(BF)
        x4 = x3 + 0.5 * (dot(down_ref[...], s4) + col(cols_ref, VEC.second_down_bias, width))
        nf, invf = norm(x4)
        fgain = col(cols_ref, VEC.final_gain, width)
        dx4 = norm_back(cot, nf, invf, fgain)
        df = (0.5 * dx4).astype(BF)
        da = (dot(down, df) * (sig * (1.0 + a4 * (1.0 - sig)))).astype(BF)
        dh = dot(up_ref[...], da)
        dx3 = dx4 + norm_back(dh, n4, inv4, col(cols_ref, VEC.second_gain, width))
        dc = dx3.astype(BF)
        dz = dot(pwo_ref[...], dc) * (sig_z * (1.0 + z * (1.0 - sig_z)))
        e = dz * bgain
        if at is not None:
            out = nf * fgain + col(cols_ref, VEC.final_shift, width)
            out_ref[:, at] = out.astype(BF)
            dx3_ref[:, at] = dx3
            h4s[:, at] = h4
            das[:hidden, at] = da
            s4s[:hidden, at] = s4
            dfs[:, at] = df
            ws[:width, at] = w
            dcs[:, at] = dc
            for i, v in enumerate((dh * n4, dh, cot * nf, cot, dz * zh, dz, e, e * zh)):
                gains[i] += v[:, :TILE] + v[:, TILE:]
        return e

    @pl.loop(0, rows // STEP)
    def _(c):
        at = pl.ds(pl.multiple_of(c * STEP, STEP), STEP)
        e_ref[:, at] = part(x2_ref[:, at], y_ref[:, at], cot_ref[:, at].astype(F32), at)

    halo = jnp.where(iota((1, TILE), 1) < HALO, cotr_ref[...].astype(F32), cotl_ref[...].astype(F32))
    e_ref[:, rows:] = part(x2_ref[:, rows:], y_ref[:, rows:], halo, None)

    s4s[hidden:, :] = ones_row(16, rows)
    ws[width:, :] = ones_row(16, rows)
    das[hidden:, :] = jnp.zeros((16, rows), BF)
    up_grad = dot(h4s[...], das[:hidden, :], NT)
    up_bias = dot(ones_row(16, rows), das[:hidden, :], NT)
    down_grad = dot(dfs[...], s4s[...], NT)
    pw_grad = dot(ws[...], dcs[...], NT)
    down_bias = exact(jnp.ones((8, rows), F32), dfs[...].astype(F32), NT)
    put_ff(pack_ref, up_grad, down_grad, 0)
    tall = 9 * width
    pack_ref[tall : tall + width, :] = pw_grad[:width, :TILE].astype(BF)
    pack_ref[tall + width : tall + 2 * width, :] = pad_lanes(pw_grad[:width, TILE:]).astype(BF)
    totals = [row_sums(gains[i])[:1] for i in range(8)]
    small_ref[...] = stack_rows(
        [totals[0], totals[1], up_bias[:1], down_bias[:1], totals[2], totals[3], totals[4], totals[5], pw_grad[width : width + 1]],
        small_ref.shape)
    sums_ref[...] = stack_rows([totals[6], totals[7]], sums_ref.shape)


def pad_lanes(mat, lanes=TILE):
    if mat.shape[1] == lanes:
        return mat
    return jnp.concatenate([mat, jnp.zeros((mat.shape[0], lanes - mat.shape[1]), mat.dtype)], axis=1)


def stack_rows(rows, shape):
    parts = [pad_lanes(r, shape[1]) for r in rows]
    parts.append(jnp.zeros((shape[0] - len(rows), shape[1]), F32))
    return jnp.concatenate(parts, axis=0)


def put_ff(pack_ref, up_grad, down_grad_t, at):
    width, hidden = up_grad.shape
    whole = hidden // TILE
    for i in range(whole):
        pack_ref[at + i * width : at + (i + 1) * width, :] = up_grad[:, i * TILE : (i + 1) * TILE].astype(BF)
        j = whole + i
        pack_ref[at + j * width : at + (j + 1) * width, :] = down_grad_t[:, i * TILE : (i + 1) * TILE].astype(BF)
    rest = jnp.concatenate([up_grad[:, whole * TILE : hidden], down_grad_t[:, whole * TILE : hidden]], axis=1)
    pack_ref[at + 2 * whole * width : at + (2 * whole + 1) * width, :] = rest.astype(BF)


def unfilter_kernel(e_ref, y_ref, stats_ref, sums_ref, u_ref, dx3_ref, x2_ref, oc_ref, cols_ref, ext_ref, pw_ref, taps_ref,
                    out_ref, dx2_ref, do_ref, pack_ref, small_ref, tapg_ref,
                    dyw, du_s, mask, prod, h3s, dgs, dms, ocs, gains, *, head_width, slot_count):
    width, rows = dx3_ref.shape
    lanes = rows + TILE
    heads = do_ref.shape[0]
    taps = taps_ref.shape[0]
    mean, inv_b, count = total_stats(stats_ref)
    sums = jnp.sum(sums_ref[...], axis=0).T
    s1, s2 = sums[:width, 0:1], sums[:width, 1:2]
    seg = ext_ref[...]
    live = ((seg >= 0) & (seg < slot_count)).astype(F32)

    def conv_grad(at, span):
        zh = (y_ref[:, at] - mean) * inv_b
        lv = mask[0, :1, at]
        dy = inv_b * (e_ref[:, at] - lv * ((s1 + zh * s2) / count))
        return dy

    mask[0, :1, :] = live

    @pl.loop(0, rows // STEP)
    def _(c):
        at = pl.ds(pl.multiple_of(c * STEP, STEP), STEP)
        dyw[:, at] = conv_grad(at, STEP).astype(BF).astype(F32)

    last = conv_grad(pl.ds(rows, TILE), TILE)
    dyw[:, rows:] = jnp.where(seg[:, rows:] >= 0, last, 0.0).astype(BF).astype(F32)

    conv_masks(mask, ext_ref, taps, -1)
    tap_cols = taps_ref[...].astype(F32).T
    for r in range(width // 8):
        sl = slice(8 * r, 8 * r + 8)
        dy8 = dyw[sl, :]
        u8 = u_ref[16 * (r // 2) : 16 * (r // 2) + 16, :rows].astype(F32)[8 * (r % 2) : 8 * (r % 2) + 8]
        acc = jnp.zeros((8, rows), F32)
        for k in range(taps):
            moved = pltpu.roll(dy8, (k - taps // 2) % lanes, 1)[:, :rows] * mask[k][:, :rows]
            acc = acc + tap_cols[sl, k : k + 1] * moved
            hit = moved * u8
            part = hit[:, :TILE]
            for at in range(TILE, rows, TILE):
                part = part + hit[:, at : at + TILE]
            prod[k, sl, :] = part
        du_s[sl, :] = acc

    whole = prod[...].reshape(taps * width, TILE)
    hi = whole.astype(BF)
    lo = (whole - hi.astype(F32)).astype(BF)
    ones = jnp.ones((8, TILE), BF)
    lines = dot(ones, hi, NT) + dot(ones, lo, NT)
    for k in range(taps):
        tapg_ref[k : k + 1, :] = lines[:1, k * width : (k + 1) * width]

    pw_t = flipped(pw_ref[...])
    out_w = dot(spread_cols(width, heads, SLOT, head_width), out_ref[...]).astype(BF)
    gains[...] = jnp.zeros_like(gains)
    fgain = col(cols_ref, VEC.filter_gain, width)
    mask[0, :1, :] = live

    @pl.loop(0, rows // STEP)
    def _(c):
        at = pl.ds(pl.multiple_of(c * STEP, STEP), STEP)
        x2 = x2_ref[:, at]
        n, inv = norm(x2)
        h3 = (n * fgain + col(cols_ref, VEC.filter_shift, width)).astype(BF)
        g = dot(pw_t, h3) + col(cols_ref, VEC.pointwise_in_bias, 2 * width)
        sig = sigmoid(g[width:])
        t = mask[0, :1, at] * du_s[:, at] * sig
        dg = jnp.concatenate([t, t * g[:width] * (1.0 - sig)], axis=0).astype(BF)
        dh = dot(pw_ref[...], dg)
        dx2 = dx3_ref[:, at] + norm_back(dh, n, inv, fgain)
        dx2_ref[:, at] = dx2
        dm = dx2.astype(BF)
        do = dot(out_w, dm).astype(BF)
        for h in range(heads):
            do_ref[h, :, at] = do[h * SLOT : (h + 1) * SLOT]
        h3s[:width, at] = h3
        dgs[:, at] = dg
        dms[:, at] = dm
        ocs[:width, at] = oc_ref[:, at]
        for i, v in enumerate((dh * n, dh)):
            gains[i] += v[:, :TILE] + v[:, TILE:]

    h3s[width:, :] = ones_row(16, rows)
    ocs[width:, :] = ones_row(16, rows)
    pw_grad = dot(h3s[...], dgs[...], NT)
    out_grad = dot(ocs[...], dms[...], NT)
    at = 0
    for lo in range(0, 2 * width, TILE):
        pack_ref[at : at + width, :] = pad_lanes(pw_grad[:width, lo : min(lo + TILE, 2 * width)]).astype(BF)
        at += width
    for lo in range(0, width, TILE):
        pack_ref[at : at + width, :] = pad_lanes(out_grad[:width, lo : min(lo + TILE, width)]).astype(BF)
        at += width
    small_ref[...] = stack_rows(
        [row_sums(gains[0])[:1], row_sums(gains[1])[:1], pw_grad[width : width + 1], out_grad[width : width + 1]], small_ref.shape)


def close_kernel(frames_ref, x1_ref, h2_ref, dx2_ref, dqkv_ref, dtab_ref, cols_ref, up_ref, down_ref, mix_ref,
                 packd_ref, packe_ref, smalld_ref, smalle_ref, tapg_ref,
                 grad_ref, pack_ref, h1s, das, s1s, dfs, dqs, gains, *, layout):
    width, rows = frames_ref.shape
    hidden = up_ref.shape[1]
    heads, packed_rows, _ = dqkv_ref.shape
    up_t = flipped(up_ref[...])
    down = flipped(down_ref[...])
    hot = spread_cols(mix_ref.shape[1], heads, packed_rows, mix_ref.shape[1] // heads)
    mix_w = dot(mix_ref[...], hot, NT).astype(BF)
    gains[...] = jnp.zeros_like(gains)
    mgain = col(cols_ref, VEC.mix_gain, width)
    fgain = col(cols_ref, VEC.first_gain, width)

    @pl.loop(0, rows // STEP)
    def _(c):
        at = pl.ds(pl.multiple_of(c * STEP, STEP), STEP)
        dq = jnp.concatenate([dqkv_ref[h, :, at] for h in range(heads)], axis=0)
        dqs[:, at] = dq
        dh2 = dot(mix_w, dq)
        n2, inv2 = norm(x1_ref[:, at])
        dx1 = dx2_ref[:, at] + norm_back(dh2, n2, inv2, mgain)
        x0 = frames_ref[:, at].astype(F32)
        n1, inv1 = norm(x0)
        h1 = (n1 * fgain + col(cols_ref, VEC.first_shift, width)).astype(BF)
        a1 = dot(up_t, h1) + col(cols_ref, VEC.first_up_bias, hidden)
        sig = sigmoid(a1)
        s1s[:, at] = (a1 * sig).astype(BF)
        df = (0.5 * dx1).astype(BF)
        da = (dot(down, df) * (sig * (1.0 + a1 * (1.0 - sig)))).astype(BF)
        dh1 = dot(up_ref[...], da)
        dx0 = dx1 + norm_back(dh1, n1, inv1, fgain)
        grad_ref[:, at] = dx0
        h1s[:, at] = h1
        das[:, at] = da
        dfs[:, at] = df
        for i, v in enumerate((dh1 * n1, dh1, dh2 * n2, dh2)):
            gains[i] += v[:, :TILE] + v[:, TILE:]

    up_grad = dot(h1s[...], das[...], NT)
    up_bias = dot(ones_row(16, rows), das[...], NT)
    down_grad = dot(dfs[...], s1s[...], NT)
    down_bias = exact(jnp.ones((8, rows), F32), dfs[...].astype(F32), NT)
    mix_grad = dot(dot(h2_ref[...], dqs[...], NT).astype(BF), hot)
    put_ff(pack_ref, up_grad, down_grad, layout.first)
    at = layout.mix_inputs
    for lo in range(0, mix_grad.shape[1], TILE):
        pack_ref[at : at + width, :] = pad_lanes(mix_grad[:, lo : min(lo + TILE, mix_grad.shape[1])]).astype(BF)
        at += width
    pack_ref[layout.d : layout.d + packd_ref.shape[0], :] = packd_ref[...]
    pack_ref[layout.e : layout.e + packe_ref.shape[0], :] = packe_ref[...]
    taps = tapg_ref.shape[0]
    pack_ref[layout.taps : layout.taps + taps, :] = tapg_ref[:, :TILE].astype(BF)
    pack_ref[layout.taps + taps : layout.taps + 2 * taps, :] = pad_lanes(tapg_ref[:, TILE:]).astype(BF)
    totals = [row_sums(gains[i])[:1] for i in range(4)]
    mine = stack_rows([totals[0], totals[1], up_bias[:1], down_bias[:1], totals[2], totals[3]], (16, smalld_ref.shape[1]))
    span = dtab_ref.shape[1]
    table = jnp.where(iota((16, span), 0) == lax.axis_index("head"), dtab_ref[...], 0.0)
    small = jnp.concatenate([mine, smalld_ref[...], smalle_ref[...]], axis=0)
    at = layout.small
    for lo in range(0, small.shape[1], TILE):
        pack_ref[at : at + small.shape[0], :] = small[:, lo : lo + TILE].astype(BF)
        at += small.shape[0]
    pack_ref[layout.table : layout.table + 16, :] = table.astype(BF)
    end = layout.table + 16
    if end < pack_ref.shape[0]:
        pack_ref[end:, :] = jnp.zeros((pack_ref.shape[0] - end, TILE), BF)


def unpack_kernel(pack_ref, *out_refs, layout):
    given = Weights(*out_refs)

    def wide(at, rows, lanes):
        parts = [pack_ref[at + i * rows : at + (i + 1) * rows, :].astype(F32) for i in range(-(-lanes // TILE))]
        return jnp.concatenate(parts, axis=1)[:, :lanes]

    for at, up_ref, down_ref in ((layout.first, given.first_up, given.first_down), (layout.second, given.second_up, given.second_down)):
        width, hidden = up_ref.shape
        whole = hidden // TILE
        half = hidden - whole * TILE
        piece = lambda i: pack_ref[at + i * width : at + (i + 1) * width, :].astype(F32)
        rest = piece(2 * whole)
        up_ref[...] = jnp.concatenate([piece(i) for i in range(whole)] + [rest[:, :half]], axis=1)
        down_ref[...] = jnp.concatenate([piece(whole + i) for i in range(whole)] + [rest[:, half:]], axis=1)
    for ref, at in ((given.mix_inputs, layout.mix_inputs), (given.pointwise_in, layout.pointwise_in), (given.mix_output, layout.mix_output),
                    (given.pointwise_out, layout.pointwise_out), (given.depthwise_taps, layout.taps)):
        ref[...] = wide(at, *ref.shape)
    given.position_bias[...] = pack_ref[layout.table : layout.table + 16, :].astype(F32)[: given.position_bias.shape[0]]
    small = wide(layout.small, 48, 5 * TILE)
    rows = (
        (given.first_gain, 0), (given.first_shift, 1), (given.first_up_bias, 2), (given.first_down_bias, 3), (given.mix_gain, 4),
        (given.mix_shift, 5), (given.second_gain, 16), (given.second_shift, 17), (given.second_up_bias, 18),
        (given.second_down_bias, 19), (given.final_gain, 20), (given.final_shift, 21), (given.batch_gain, 22), (given.batch_shift, 23),
        (given.pointwise_out_bias, 24), (given.filter_gain, 32), (given.filter_shift, 33), (given.pointwise_in_bias, 34),
        (given.mix_output_bias, 35),
    )
    for ref, row in rows:
        ref[...] = small[row : row + 1, : ref.shape[0]].reshape(ref.shape)


@dataclasses.dataclass
class Weights:
    first_gain: object
    first_shift: object
    first_up: object
    first_up_bias: object
    first_down: object
    first_down_bias: object
    mix_gain: object
    mix_shift: object
    mix_inputs: object
    position_bias: object
    mix_output: object
    mix_output_bias: object
    filter_gain: object
    filter_shift: object
    pointwise_in: object
    pointwise_in_bias: object
    depthwise_taps: object
    batch_gain: object
    batch_shift: object
    pointwise_out: object
    pointwise_out_bias: object
    second_gain: object
    second_shift: object
    second_up: object
    second_up_bias: object
    second_down: object
    second_down_bias: object
    final_gain: object
    final_shift: object


def pack_layout(width, hidden, mix_width, taps, devices):
    ff = (2 * (hidden // TILE) + 1) * width
    chunks = lambda lanes: -(-lanes // TILE) * width
    at = types.SimpleNamespace(first=0)
    at.mix_inputs = ff
    at.d = at.second = at.mix_inputs + chunks(mix_width)
    at.pointwise_out = at.second + ff
    at.e = at.pointwise_in = at.pointwise_out + chunks(width)
    at.mix_output = at.pointwise_in + chunks(2 * width)
    at.taps = at.mix_output + chunks(width)
    at.small = at.taps + 2 * taps
    at.table = at.small + 48 * 5
    unit = 16 * devices
    at.rows = -(-(at.table + 16) // unit) * unit
    return at


MESH = pl.DeviceIdType.MESH


def meet(peers):
    barrier = pltpu.get_barrier_semaphore()
    for peer in peers:
        pl.semaphore_signal(barrier, inc=1, device_id=peer, device_id_type=MESH)
    pl.semaphore_wait(barrier, len(peers))


def head_peers(n):
    me = lax.axis_index("head")
    return me, [{"head": lax.rem(me + s, n)} for s in range(1, n)], [lax.rem(me + s, n) for s in range(1, n)]


def swap_kernel(src_ref, dst_ref, send, recv, local, *, n, start_of):
    me, peers, ids = head_peers(n)
    meet(peers)
    copies = []
    for s, (peer, p) in enumerate(zip(peers, ids)):
        copies.append(pltpu.make_async_remote_copy(
            src_ref=start_of(src_ref, p), dst_ref=dst_ref.at[me], send_sem=send.at[s], recv_sem=recv.at[s],
            device_id=peer, device_id_type=MESH))
        copies[-1].start()
    own = pltpu.make_async_copy(start_of(src_ref, me), dst_ref.at[me], local)
    own.start()
    own.wait()
    for copy in copies:
        copy.wait()


def swap(src, block_shape, start_of, collective_id, name):
    n = lax.axis_size("head")
    hbm = pl.BlockSpec(memory_space=pl.ANY)
    return pl.pallas_call(
        functools.partial(swap_kernel, n=n, start_of=start_of),
        out_shape=jax.ShapeDtypeStruct((n,) + block_shape, src.dtype),
        in_specs=[hbm], out_specs=hbm,
        scratch_shapes=[pltpu.SemaphoreType.DMA((n - 1,)), pltpu.SemaphoreType.DMA((n - 1,)), pltpu.SemaphoreType.DMA],
        compiler_params=pltpu.CompilerParams(collective_id=collective_id, has_side_effects=True, vmem_limit_bytes=62 * 2**20),
        name=name,
    )(src)


def opening_kernel(qkv_ref, x1_ref, cot_ref, all_ref, x1l_ref, x1r_ref, cotl_ref, cotr_ref, send, recv, local, hsend, hrecv, *, n):
    me, peers, ids = head_peers(n)
    rows = cot_ref.shape[1]
    meet(peers)
    copies = []
    for s, (peer, p) in enumerate(zip(peers, ids)):
        copies.append(pltpu.make_async_remote_copy(
            src_ref=qkv_ref.at[p], dst_ref=all_ref.at[me], send_sem=send.at[s], recv_sem=recv.at[s],
            device_id=peer, device_id_type=MESH))
        copies[-1].start()
    own = pltpu.make_async_copy(qkv_ref.at[me], all_ref.at[me], local)
    own.start()

    def edge(i, src, dst, head):
        return pltpu.make_async_remote_copy(src_ref=src, dst_ref=dst, send_sem=hsend.at[i], recv_sem=hrecv.at[i],
                                            device_id={"head": head}, device_id_type=MESH)

    up = lax.rem(me + 1, n)
    down = lax.rem(me + n - 1, n)
    to_right = [edge(0, x1_ref.at[:, pl.ds(rows - TILE, TILE)], x1l_ref, up), edge(1, cot_ref.at[:, pl.ds(rows - TILE, TILE)], cotl_ref, up)]
    to_left = [edge(2, x1_ref.at[:, pl.ds(0, TILE)], x1r_ref, down), edge(3, cot_ref.at[:, pl.ds(0, TILE)], cotr_ref, down)]

    @pl.when(me < n - 1)
    def _():
        for c in to_right:
            c.start()

    @pl.when(me > 0)
    def _():
        for c in to_left:
            c.start()

    own.wait()
    for copy in copies:
        copy.wait()

    @pl.when(me < n - 1)
    def _():
        for c in to_right:
            c.wait_send()
        for c in to_left:
            c.wait_recv()

    @pl.when(me > 0)
    def _():
        for c in to_left:
            c.wait_send()
        for c in to_right:
            c.wait_recv()


def open_exchange(qkv, x1, cot, collective_id):
    n = lax.axis_size("head")
    width = x1.shape[0]
    hbm = pl.BlockSpec(memory_space=pl.ANY)
    return pl.pallas_call(
        functools.partial(opening_kernel, n=n),
        out_shape=(
            jax.ShapeDtypeStruct(qkv.shape, BF),
            jax.ShapeDtypeStruct((width, TILE), F32), jax.ShapeDtypeStruct((width, TILE), F32),
            jax.ShapeDtypeStruct((width, TILE), BF), jax.ShapeDtypeStruct((width, TILE), BF),
        ),
        in_specs=[hbm] * 3, out_specs=(hbm,) * 5,
        scratch_shapes=[pltpu.SemaphoreType.DMA((n - 1,)), pltpu.SemaphoreType.DMA((n - 1,)), pltpu.SemaphoreType.DMA,
                        pltpu.SemaphoreType.DMA((4,)), pltpu.SemaphoreType.DMA((4,))],
        compiler_params=pltpu.CompilerParams(collective_id=collective_id, has_side_effects=True, vmem_limit_bytes=62 * 2**20),
        name="share_queries_keys_values",
    )(qkv, x1, cot)


def tell_kernel(src_ref, all_ref, send, recv, local, *, n_tm, n_head):
    n = n_tm * n_head
    me = lax.axis_index("tm") * n_head + lax.axis_index("head")
    barrier = pltpu.get_barrier_semaphore()

    def place(s):
        peer = lax.rem(me + s, n)
        return {"tm": peer // n_head, "head": lax.rem(peer, n_head)}

    @pl.loop(1, n)
    def _(s):
        pl.semaphore_signal(barrier, inc=1, device_id=place(s), device_id_type=MESH)

    pl.semaphore_wait(barrier, n - 1)

    def copy(s):
        return pltpu.make_async_remote_copy(src_ref=src_ref, dst_ref=all_ref.at[me], send_sem=send.at[s], recv_sem=recv.at[s],
                                            device_id=place(s), device_id_type=MESH)

    @pl.loop(1, n)
    def _(s):
        copy(s).start()

    own = pltpu.make_async_copy(src_ref, all_ref.at[me], local)
    own.start()
    own.wait()

    @pl.loop(1, n)
    def _(s):
        copy(s).wait()


def tell_all(block, collective_id, name):
    n_tm, n_head = lax.axis_size("tm"), lax.axis_size("head")
    n = n_tm * n_head
    vm = pl.BlockSpec(memory_space=pltpu.VMEM)
    return pl.pallas_call(
        functools.partial(tell_kernel, n_tm=n_tm, n_head=n_head),
        out_shape=jax.ShapeDtypeStruct((n,) + block.shape, block.dtype),
        in_specs=[vm], out_specs=vm,
        scratch_shapes=[pltpu.SemaphoreType.DMA((n,)), pltpu.SemaphoreType.DMA((n,)), pltpu.SemaphoreType.DMA],
        compiler_params=pltpu.CompilerParams(collective_id=collective_id, has_side_effects=True, vmem_limit_bytes=62 * 2**20),
        name=name,
    )(block)


def sum_kernel(src_ref, out_ref, got1, part1, got2, part2, send1, recv1, send2, recv2, send3, recv3, send4, recv4, local, *, n_tm, n_head):
    tm, head = lax.axis_index("tm"), lax.axis_index("head")
    big = src_ref.shape[0] // n_tm
    small = big // n_head
    barrier = pltpu.get_barrier_semaphore()

    def tm_peer(s):
        return lax.rem(tm + s, n_tm)

    def head_peer(s):
        return lax.rem(head + s, n_head)

    @pl.loop(1, n_tm)
    def _(s):
        pl.semaphore_signal(barrier, inc=1, device_id={"tm": tm_peer(s)}, device_id_type=MESH)

    @pl.loop(1, n_head)
    def _(s):
        pl.semaphore_signal(barrier, inc=1, device_id={"head": head_peer(s)}, device_id_type=MESH)

    pl.semaphore_wait(barrier, n_tm + n_head - 2)

    def rows(i, size):
        return pl.ds(pl.multiple_of(i * size, size), size)

    def one(s):
        return pltpu.make_async_remote_copy(src_ref=src_ref.at[rows(tm_peer(s), big)], dst_ref=got1.at[s], send_sem=send1.at[s],
                                            recv_sem=recv1.at[s], device_id={"tm": tm_peer(s)}, device_id_type=MESH)

    def two(s):
        return pltpu.make_async_remote_copy(src_ref=part1.at[rows(head_peer(s), small)], dst_ref=got2.at[s], send_sem=send2.at[s],
                                            recv_sem=recv2.at[s], device_id={"head": head_peer(s)}, device_id_type=MESH)

    def three(s):
        at = part2.at[rows(head, small)]
        return pltpu.make_async_remote_copy(src_ref=at, dst_ref=at, send_sem=send3.at[s],
                                            recv_sem=recv3.at[s], device_id={"head": head_peer(s)}, device_id_type=MESH)

    def four(s):
        return pltpu.make_async_remote_copy(src_ref=part2, dst_ref=out_ref.at[rows(tm, big)], send_sem=send4.at[s],
                                            recv_sem=recv4.at[s], device_id={"tm": tm_peer(s)}, device_id_type=MESH)

    pl.loop(1, n_tm)(lambda s: one(s).start())
    got1[0] = src_ref[rows(tm, big), :]
    pl.loop(1, n_tm)(lambda s: one(s).wait())
    total = got1[0].astype(F32)
    for s in range(1, n_tm):
        total = total + got1[s].astype(F32)
    part1[...] = total.astype(BF)
    pl.loop(1, n_head)(lambda s: two(s).start())
    got2[0] = part1[rows(head, small), :]
    pl.loop(1, n_head)(lambda s: two(s).wait())
    total = got2[0].astype(F32)
    for s in range(1, n_head):
        total = total + got2[s].astype(F32)
    part2[rows(head, small), :] = total.astype(BF)
    pl.loop(1, n_head)(lambda s: three(s).start())
    pl.loop(1, n_head)(lambda s: three(s).wait())
    pl.loop(1, n_tm)(lambda s: four(s).start())
    own = pltpu.make_async_copy(part2, out_ref.at[rows(tm, big)], local)
    own.start()
    own.wait()
    pl.loop(1, n_tm)(lambda s: four(s).wait())


def sum_all(pack, collective_id):
    n_tm, n_head = lax.axis_size("tm"), lax.axis_size("head")
    rows = pack.shape[0]
    big = rows // n_tm
    vm = pl.BlockSpec(memory_space=pltpu.VMEM)
    dma = pltpu.SemaphoreType.DMA
    return pl.pallas_call(
        functools.partial(sum_kernel, n_tm=n_tm, n_head=n_head),
        out_shape=jax.ShapeDtypeStruct(pack.shape, BF),
        in_specs=[vm], out_specs=vm,
        scratch_shapes=[
            pltpu.VMEM((n_tm, big, TILE), BF), pltpu.VMEM((big, TILE), BF),
            pltpu.VMEM((n_head, big // n_head, TILE), BF), pltpu.VMEM((big, TILE), BF),
            dma((n_tm,)), dma((n_tm,)), dma((n_head,)), dma((n_head,)), dma((n_head,)), dma((n_head,)), dma((n_tm,)), dma((n_tm,)), dma,
        ],
        compiler_params=pltpu.CompilerParams(collective_id=collective_id, has_side_effects=True, vmem_limit_bytes=62 * 2**20),
        name="sum_gradients",
    )(pack)


VMEM_MIB = 62


def local_call(kernel, name, ins, outs, scratch, vmem=VMEM_MIB):
    return pl.pallas_call(
        kernel,
        out_shape=tuple(jax.ShapeDtypeStruct(s, t) for s, t in outs),
        scratch_shapes=[pltpu.VMEM(s, t) for s, t in scratch],
        compiler_params=pltpu.CompilerParams(vmem_limit_bytes=vmem * 2**20),
        name=name,
    )(*ins)


def body(
    frames, lengths, first_gain, first_shift, first_up, first_up_bias, first_down, first_down_bias, mix_gain, mix_shift,
    mix_inputs, position_bias, mix_output, mix_output_bias, filter_gain, filter_shift, pointwise_in, pointwise_in_bias,
    depthwise_taps, batch_gain, batch_shift, pointwise_out, pointwise_out_bias, second_gain, second_shift, second_up,
    second_up_bias, second_down, second_down_bias, final_gain, final_shift, cotangent,
):
    weights = Weights(
        first_gain, first_shift, first_up, first_up_bias, first_down, first_down_bias, mix_gain, mix_shift, mix_inputs, position_bias,
        mix_output, mix_output_bias, filter_gain, filter_shift, pointwise_in, pointwise_in_bias, depthwise_taps, batch_gain,
        batch_shift, pointwise_out, pointwise_out_bias, second_gain, second_shift, second_up, second_up_bias, second_down,
        second_down_bias, final_gain, final_shift)
    rows, width = frames.shape
    hidden = first_up.shape[1]
    n_head, n_tm = lax.axis_size("head"), lax.axis_size("tm")
    heads, span = position_bias.shape
    head_width = width // heads
    packed_rows = -(-3 * head_width // 16) * 16
    group = rows * n_head
    lanes = rows + TILE
    slots = lengths.shape[1]
    taps = depthwise_taps.shape[0]
    layout = pack_layout(width, hidden, mix_inputs.shape[1], taps, n_tm * n_head)

    vectors = tuple(getattr(weights, name) for name in VEC.__dict__)
    frames_t, cot_t, first_down_t, second_down_t = frames.T, cotangent.T, first_down.T, second_down.T
    x1, h2, qkv, cols, bounds, plan, ext = local_call(
        functools.partial(open_kernel, packed_rows=packed_rows), "open",
        (frames_t, lengths, first_up, first_down_t, mix_inputs) + vectors,
        [((width, rows), F32), ((width, rows), BF), ((n_head, packed_rows, rows), BF), ((hidden, VEC_ROWS), F32),
         ((2, group + 2 * PAD), jnp.int32), ((group // BLK, 128), jnp.int32), ((1, lanes), jnp.int32)],
        [((1, group + 2 * TILE), jnp.int32)])
    qkv_all, x1l, x1r, cotl, cotr = open_exchange(qkv, x1, cot_t, 1)
    o, of, lse = attend_forward(qkv_all, bounds, plan, position_bias, head_width)
    o_own = swap(o, (SLOT, rows + 2 * TILE),
                 lambda ref, p: ref.at[:, pl.ds(pl.multiple_of(p * rows, TILE), rows + 2 * TILE)], 2, "return_attended")
    x2, oc, u, y, stat = local_call(
        functools.partial(filter_kernel, head_width=head_width, slot_count=slots), "filter",
        (x1, x1l, x1r, o_own, cols, ext, mix_output, pointwise_in, depthwise_taps),
        [((width, lanes), F32), ((width, rows), BF), ((width, lanes), BF), ((width, lanes), F32), ((8, width), F32)],
        [((width, lanes), F32), ((taps, 8, lanes), F32)])
    stats = tell_all(stat, 3, "tell_statistics")
    out, dx3, e, sums, packd, smalld = local_call(
        second_kernel, "second",
        (x2, y, stats, cot_t, cotl, cotr, cols, pointwise_out, second_up, second_down_t),
        [((width, rows), BF), ((width, rows), F32), ((width, lanes), F32), ((8, width), F32),
         ((layout.e - layout.d, TILE), BF), ((16, 5 * TILE), F32)],
        [((width, rows), BF), ((hidden + 16, rows), BF), ((hidden + 16, rows), BF), ((width, rows), BF),
         ((width + 16, rows), BF), ((width, rows), BF), ((8, width, TILE), F32)])
    all_sums = tell_all(sums, 4, "tell_sums")
    dx2, do, packe, smalle, tapg = local_call(
        functools.partial(unfilter_kernel, head_width=head_width, slot_count=slots), "unfilter",
        (e, y, stats, all_sums, u, dx3, x2, oc, cols, ext, pointwise_in, depthwise_taps, mix_output),
        [((width, rows), F32), ((n_head, SLOT, rows), BF), ((layout.taps - layout.e, TILE), BF), ((16, 5 * TILE), F32),
         ((taps, width), F32)],
        [((width, lanes), F32), ((width, rows), F32), ((taps, 8, lanes), F32), ((taps, width, TILE), F32), ((width + 16, rows), BF),
         ((2 * width, rows), BF), ((width, rows), BF), ((width + 16, rows), BF), ((2, width, TILE), F32)])
    do_all = swap(do, (SLOT, rows), lambda ref, p: ref.at[p], 5, "share_attended_gradient")
    dqkv, dtab = attend_backward(qkv_all, do_all, of, lse, bounds, plan, position_bias, head_width)
    dqkv_own = swap(dqkv, (packed_rows, rows), lambda ref, p: ref.at[p], 6, "return_gradients")
    grad, pack = local_call(
        functools.partial(close_kernel, layout=layout), "close",
        (frames_t, x1, h2, dx2, dqkv_own, dtab, cols, first_up, first_down_t, mix_inputs, packd, packe, smalld, smalle, tapg),
        [((width, rows), F32), ((layout.rows, TILE), BF)],
        [((width, rows), BF), ((hidden, rows), BF), ((hidden, rows), BF), ((width, rows), BF),
         ((n_head * packed_rows, rows), BF), ((4, width, TILE), F32)])
    total = sum_all(pack, 7)
    shapes = Weights(**{n: w.shape for n, w in weights.__dict__.items()})
    shapes.first_down = shapes.second_down = first_down_t.shape
    summed = Weights(*local_call(
        functools.partial(unpack_kernel, layout=layout), "unpack", (total,), [(s, F32) for s in shapes.__dict__.values()], []))
    summed.first_down, summed.second_down = summed.first_down.T, summed.second_down.T
    return (out.T, grad.T) + tuple(summed.__dict__.values())


def solution(mesh):
    rows = P(("tm", "head"), None)
    placed = (rows, P("tm", None)) + (P(),) * 29 + (rows,)
    return jax.shard_map(body, mesh=mesh, in_specs=placed, out_specs=(rows, rows) + (P(),) * 29, check_vma=False)
```

```python
import dataclasses
import functools
import math
import types

import jax
import jax.numpy as jnp
from jax import lax
from jax.experimental import pallas as pl
from jax.experimental.pallas import tpu as pltpu
from jax.sharding import PartitionSpec as P

BF = jnp.bfloat16
F32 = jnp.float32
LOG2E = math.log2(math.e)
BLK = 512
UNIT = 128
PER = BLK // UNIT
NEAR = PER + 2
PAD = 8 * UNIT
SLOT = 48
DEPTH = 128
MASKED = -1e30
NN = (((1,), (0,)), ((), ()))
NT = (((1,), (1,)), ((), ()))
TN = (((0,), (0,)), ((), ()))


def dot(a, b, dims=NN):
    return lax.dot_general(a, b, dims, preferred_element_type=F32)


def iota(shape, dim):
    return lax.broadcasted_iota(jnp.int32, shape, dim)


def spread_cols(width, slots, slot_rows, used):
    row, column = iota((slots * slot_rows, width), 0), iota((slots * slot_rows, width), 1)
    hit = jnp.zeros((slots * slot_rows, width), jnp.bool_)
    for s in range(slots):
        f = row - slot_rows * s
        hit = hit | ((f >= 0) & (f < used) & (column == used * s + f))
    return hit.astype(F32).astype(BF)


def split3(v):
    hi = v.astype(BF).astype(F32)
    r1 = v - hi
    mid = r1.astype(BF).astype(F32)
    return hi, mid, r1 - mid


def three_rows(v, rows):
    a, b, e = split3(v)
    row = iota((rows, v.shape[1]), 0)
    return jnp.where(row == 0, a, jnp.where(row == 1, b, jnp.where(row == 2, e, 0.0)))


def pick_row(ref, index):
    values = ref[...].astype(F32)
    return jnp.sum(jnp.where(iota(values.shape, 0) == index, values, 0.0), axis=0, keepdims=True)


def bias_square(table, d):
    span = table.shape[1]
    half = span // 2
    lanes = 2 * UNIT
    u = iota((span, lanes), 1)
    u = jnp.where(u < UNIT, u, u - lanes)
    ids = jnp.clip(-UNIT * d - u, -half, half - 1) + half
    hot = (ids == iota((span, lanes), 0)).astype(F32).astype(BF)
    line = dot(jnp.broadcast_to(table, (UNIT, span)).astype(BF), hot) * LOG2E
    return pltpu.roll(line, 0, 1, stride=1, stride_axis=0)[:, :UNIT]


def bias_near(table, tile, keys_near):
    span = table.shape[1]
    squares = {d: bias_square(table, d) for d in (-1, 0, 1)}
    low = jnp.broadcast_to(table[:, :1] * LOG2E, (UNIT, UNIT))
    high = jnp.broadcast_to(table[:, span - 1 :] * LOG2E, (UNIT, UNIT))
    for r in range(tile.shape[0] // UNIT):
        for c in range(tile.shape[1] // UNIT):
            d = c - (r - 1) if keys_near else (c - 1) - r
            part = squares[d] if abs(d) < 2 else (low if d > 0 else high)
            tile[r * UNIT : (r + 1) * UNIT, c * UNIT : (c + 1) * UNIT] = part


def units_at(u, count):
    return pl.ds(pl.multiple_of(u * UNIT, UNIT), count * UNIT)


def far_windows(low, plain, edge, step, side, up):
    sign = 1 if up else -1

    def run(at, times, size, masked):
        def one(i, carry):
            near = at + sign * i * size
            step(near if up else near - size, size, side, masked)
            return carry

        lax.fori_loop(0, times, one, 0)
        return at + sign * times * size

    at = run(edge, sign * (plain - edge) // 8, 8, False)
    left = sign * (low - at)
    tail = lax.rem(left, 8)
    at = run(at, left // 8 + (tail > 4).astype(jnp.int32), 8, True)
    run(at, ((tail > 0) & (tail <= 4)).astype(jnp.int32), 4, True)


def far_sweep(plan, block, step, before, after):
    low, plain_low, plain_high, high = [plan[block, i] for i in range(4)]
    start, stop = PER * block - 1, PER * block + PER + 1
    far_windows(low, plain_low, start, step, before, False)
    far_windows(high, plain_high, stop, step, after, True)


def has_far(plan, block):
    return (plan[block, 0] < PER * block - 1) | (plan[block, 3] > PER * block + PER + 1)


def segment_rows(ends, lengths, place, total):
    slots = ends.shape[0]
    before = ends <= jnp.broadcast_to(place, (slots, place.shape[1]))
    seg = jnp.sum(before.astype(jnp.int32), axis=0, keepdims=True)
    first = jnp.sum(jnp.where(before, lengths, 0), axis=0, keepdims=True)
    stop = jnp.min(jnp.where(before, total, ends), axis=0, keepdims=True)
    return seg, first, stop


def block_plan(ends, ends_row, total):
    slots = ends.shape[0]
    blocks, units = total // BLK, total // UNIT

    def along(place):
        return jnp.sum((ends <= jnp.broadcast_to(place, (slots, 128))).astype(jnp.int32), axis=0, keepdims=True)

    def down(place):
        return jnp.sum((jnp.broadcast_to(ends_row, (blocks, slots)) <= place).astype(F32), axis=1, keepdims=True).astype(jnp.int32)

    unit = iota((1, 128), 1)
    u_first, u_last = along(unit * UNIT), along(unit * UNIT + UNIT - 1)
    b = iota((blocks, 1), 0)
    first, last = down(b * BLK), down(b * BLK + BLK - 1)
    start, stop = PER * b - 1, PER * b + PER + 1
    inside = unit < units

    def count(hit):
        return jnp.sum((hit & inside).astype(F32), axis=1, keepdims=True).astype(jnp.int32)

    low = jnp.minimum(count(u_last < first), start)
    high = jnp.maximum(units - count(u_first > last), stop)
    plain_low = start - count((unit < start) & (u_first == last))
    plain_high = stop + count((unit >= stop) & (u_last == first))
    lane = iota((blocks, 128), 1)
    out = jnp.zeros((blocks, 128), jnp.int32)
    for i, v in enumerate((low, plain_low, plain_high, high)):
        out = jnp.where(lane == i, v, out)
    return out


def meets(first_key, rows, bounds):
    key = iota((rows, bounds.shape[1]), 0)
    return (key >= bounds[0:1, :] - first_key) & (key < bounds[1:2, :] - first_key)


def fwd_kernel(plan, qkv_ref, table_ref, bound_ref, o_ref, of_ref, lse_ref, qaug, kn, vt, tile, top_ref, acc, *, head_width):
    chunks, packed_rows, rows = qkv_ref.shape
    total = chunks * rows
    blocks = total // BLK
    span = table_ref.shape[1]
    table = pick_row(table_ref, lax.axis_index("head"))
    far = (table[:, :1] * LOG2E, table[:, span - 1 :] * LOG2E)
    pick = spread_cols(packed_rows, 3, SLOT, head_width)
    scale = LOG2E / math.sqrt(head_width)
    o_ref[:, :UNIT] = jnp.zeros((SLOT, UNIT), BF)
    o_ref[:, UNIT + total :] = jnp.zeros((SLOT, UNIT), BF)
    for edge in (slice(0, PAD), slice(PAD + total, 2 * PAD + total)):
        kn[edge, :] = jnp.zeros((PAD, DEPTH), BF)
        vt[:, edge] = jnp.zeros((SLOT, PAD), BF)
    bias_near(table, tile, True)
    rest = DEPTH - 2 * SLOT

    @pl.loop(0, chunks)
    def _(c):
        at = pl.ds(pl.multiple_of(c * rows, rows), rows)
        at_pad = pl.ds(pl.multiple_of(c * rows + PAD, UNIT), rows)
        parts = dot(pick, qkv_ref[c])
        q = parts[:SLOT] * scale
        hi = q.astype(BF)
        lo = (q - hi.astype(F32)).astype(BF)
        for s in range(3):
            qaug[s, :SLOT, at] = hi
            qaug[s, SLOT : 2 * SLOT, at] = lo
            qaug[s, 2 * SLOT :, at] = jnp.zeros((rest, rows), BF)
        k = parts[SLOT : 2 * SLOT]
        one3 = (iota((rest, rows), 0) < 3).astype(F32)
        kn[at_pad, :] = jnp.concatenate([k, k, one3], axis=0).T.astype(BF)
        one = (iota((SLOT, rows), 0) == head_width).astype(F32)
        vt[:, at_pad] = (parts[2 * SLOT :] + one).astype(BF)

    def top(x):
        return jnp.max(x.reshape(x.shape[0] // 8, 8, BLK), axis=0)

    @pl.loop(0, blocks // 2)
    def _(pair):
        for i in range(2):
            b = 2 * pair + i
            at_q = units_at(PER * b, PER)
            near = units_at(PER * b - 1 + PAD // UNIT, NEAR)
            x = dot(kn[near, :], qaug[1, :, at_q]) + tile[...]
            x = jnp.where(meets(PER * b * UNIT - UNIT, NEAR * UNIT, bound_ref[:, units_at(PER * b + PAD // UNIT, PER)]), x, MASKED)
            m = jnp.max(top(x), axis=0, keepdims=True)
            acc[:, at_q] = dot(vt[:, near], jnp.exp2(x - m).astype(BF))
            lse_ref[:, at_q] = m
            qaug[0, 2 * SLOT :, at_q] = three_rows(far[0] - m, rest).astype(BF)
            qaug[2, 2 * SLOT :, at_q] = three_rows(far[1] - m, rest).astype(BF)

    @pl.loop(0, blocks)
    def _(b):
        @pl.when(has_far(plan, b))
        def _():
            at_q = units_at(PER * b, PER)

            def scores(u, count, side, masked):
                x = dot(kn[units_at(u + PAD // UNIT, count), :], qaug[side, :, at_q])
                if masked:
                    x = jnp.where(meets(u * UNIT, count * UNIT, bound_ref[:, units_at(PER * b + PAD // UNIT, PER)]), x, MASKED)
                return x

            near_acc = acc[:, at_q]

            def add(u, count, side, masked):
                p = jnp.exp2(scores(u, count, side, masked)).astype(BF)
                acc[:, at_q] += dot(vt[:, units_at(u + PAD // UNIT, count)], p)

            far_sweep(plan, b, add, 0, 2)
            sums = acc[head_width : head_width + 1, at_q]
            over = jnp.max(jnp.where(sums < 2.0**60, 0.0, 1.0))

            @pl.when(over > 0.5)
            def _():
                top_ref[...] = jnp.zeros_like(top_ref)

                def first(u, count, side, masked):
                    top_ref[...] = jnp.maximum(top_ref[...], top(scores(u, count, side, masked)))

                far_sweep(plan, b, first, 0, 2)
                m = jnp.max(top_ref[...], axis=0, keepdims=True)
                acc[:, at_q] = near_acc * jnp.exp2(-m)
                lse_ref[:, at_q] += m

                def second(u, count, side, masked):
                    p = jnp.exp2(scores(u, count, side, masked) - m).astype(BF)
                    acc[:, at_q] += dot(vt[:, units_at(u + PAD // UNIT, count)], p)

                far_sweep(plan, b, second, 0, 2)

    @pl.loop(0, chunks)
    def _(c):
        at = pl.ds(pl.multiple_of(c * rows, rows), rows)
        total_p = acc[head_width : head_width + 1, at]
        out = acc[:, at] / total_p
        o_ref[:, pl.ds(pl.multiple_of(c * rows + UNIT, UNIT), rows)] = out.astype(BF)
        of_ref[:, at] = out[: of_ref.shape[0]]
        lse_ref[:, at] = lse_ref[:, at] + jnp.log2(total_p)


def attend_forward(qkv, bounds, plan, table, head_width):
    chunks, packed_rows, rows = qkv.shape
    total = chunks * rows
    vm = pltpu.VMEM
    return pl.pallas_call(
        functools.partial(fwd_kernel, head_width=head_width),
        out_shape=(
            jax.ShapeDtypeStruct((SLOT, total + 2 * UNIT), BF),
            jax.ShapeDtypeStruct((40, total), F32),
            jax.ShapeDtypeStruct((1, total), F32),
        ),
        in_specs=[pl.BlockSpec(memory_space=pltpu.SMEM)] + [pl.BlockSpec()] * 3,
        scratch_shapes=[
            vm((3, DEPTH, total), BF),
            vm((total + 2 * PAD, DEPTH), BF),
            vm((SLOT, total + 2 * PAD), BF),
            vm((NEAR * UNIT, BLK), F32),
            vm((8, BLK), F32),
            vm((SLOT, total), F32),
        ],
        compiler_params=pltpu.CompilerParams(vmem_limit_bytes=62 * 2**20),
        name="attend_forward",
    )(plan, qkv, table, bounds)


def bwd_kernel(plan, qkv_ref, do_ref, of_ref, lse_ref, table_ref, bound_ref, dqkv_ref, dtab_ref,
               qaug, kn, kt, vn, dot_t, qn, don, tile, dq, band, ends, dv_acc, dk_acc, dwide, *, head_width):
    chunks, packed_rows, rows = qkv_ref.shape
    total = chunks * rows
    blocks = total // BLK
    span = table_ref.shape[1]
    table = pick_row(table_ref, lax.axis_index("head"))
    pick = spread_cols(packed_rows, 3, SLOT, head_width)
    scale = LOG2E / math.sqrt(head_width)
    back = 1.0 / math.sqrt(head_width)
    rest = DEPTH - 2 * SLOT
    bias_near(table, tile, False)
    for edge in (slice(0, PAD), slice(PAD + total, 2 * PAD + total)):
        for s in range(3):
            qaug[s, :, edge] = jnp.zeros((DEPTH, PAD), BF)
        dot_t[:, edge] = jnp.zeros((DEPTH, PAD), BF)
        qn[edge, :] = jnp.zeros((PAD, DEPTH), BF)
        don[edge, :] = jnp.zeros((PAD, DEPTH), BF)

    @pl.loop(0, chunks)
    def _(c):
        at = pl.ds(pl.multiple_of(c * rows, rows), rows)
        at_pad = pl.ds(pl.multiple_of(c * rows + PAD, UNIT), rows)
        parts = dot(pick, qkv_ref[c])
        q, k, v = parts[:SLOT], parts[SLOT : 2 * SLOT], parts[2 * SLOT :]
        qs = q * scale
        hi = qs.astype(BF)
        lo = (qs - hi.astype(F32)).astype(BF)
        lse = lse_ref[:, at]
        for s, shift in enumerate((table[:, :1] * LOG2E, 0.0, table[:, span - 1 :] * LOG2E)):
            qaug[s, :SLOT, at_pad] = hi
            qaug[s, SLOT : 2 * SLOT, at_pad] = lo
            qaug[s, 2 * SLOT :, at_pad] = three_rows(shift - lse, rest).astype(BF)
        one3 = (iota((rest, rows), 0) < 3).astype(F32)
        row48 = iota((SLOT, rows), 0)
        none = jnp.zeros((rest, rows), F32)
        empty = jnp.zeros((SLOT, rows), F32)
        kn[at, :] = jnp.concatenate([k, k, one3], axis=0).T.astype(BF)
        kt[:, at] = k.astype(BF)
        vn[at, :] = jnp.concatenate([v, empty, one3], axis=0).T.astype(BF)
        do = do_ref[c].astype(F32)
        centre = jnp.sum(do[: of_ref.shape[0]] * of_ref[:, at], axis=0, keepdims=True)
        dot_t[:SLOT, at_pad] = do_ref[c]
        dot_t[SLOT : 2 * SLOT, at_pad] = empty.astype(BF)
        dot_t[2 * SLOT :, at_pad] = three_rows(-centre, rest).astype(BF)
        qn[at_pad, :] = jnp.concatenate([q + (row48 == head_width).astype(F32), empty, none], axis=0).T.astype(BF)
        don[at_pad, :] = jnp.concatenate([do, empty, none], axis=0).T.astype(BF)

    dq[...] = jnp.zeros_like(dq)
    band[...] = jnp.zeros_like(band)
    ends[...] = jnp.zeros_like(ends)

    @pl.loop(0, blocks // 2)
    def _(pair):
        width = NEAR * UNIT
        wide = width + BLK
        whole, lines = [], []
        for i in range(2):
            b = 2 * pair + i
            at_k = units_at(PER * b, PER)
            near = units_at(PER * b - 1 + PAD // UNIT, NEAR)
            p = jnp.exp2(dot(kn[at_k, :], qaug[1, :, near]) + tile[...])
            p = jnp.where(meets(b * BLK, BLK, bound_ref[:, near]), p, 0.0)
            dsb = (p * dot(vn[at_k, :], dot_t[:, near])).astype(BF)
            dv_acc[at_k, :] = dot(p.astype(BF), don[near, :])
            dk_acc[at_k, :] = dot(dsb, qn[near, :])
            part = dot(kt[:, at_k], dsb)
            gap = jnp.zeros((SLOT, BLK), F32)
            whole.append(jnp.concatenate([gap, part] if i else [part, gap], axis=1))
            lines.append(dsb.astype(F32))
        dq[:, units_at(2 * PER * pair - 1 + PAD // UNIT, wide // UNIT)] += whole[0] + whole[1]
        band[...] += lines[0] + lines[1]

    @pl.loop(0, blocks)
    def _(b):
        @pl.when(has_far(plan, b))
        def _():
            at_k = units_at(PER * b, PER)

            def far(u, count, side, masked):
                at_q = units_at(u + PAD // UNIT, count)
                p = jnp.exp2(dot(kn[at_k, :], qaug[side, :, at_q]))
                if masked:
                    p = jnp.where(meets(b * BLK, BLK, bound_ref[:, at_q]), p, 0.0)
                dsb = (p * dot(vn[at_k, :], dot_t[:, at_q])).astype(BF)
                dq[:, at_q] += dot(kt[:, at_k], dsb)
                dv_acc[at_k, :] += dot(p.astype(BF), don[at_q, :])
                dk = dot(dsb, qn[at_q, :])
                dk_acc[at_k, :] += dk
                ends[side // 2] += jnp.sum(dk.reshape(BLK // 8, 8, DEPTH), axis=0)

            far_sweep(plan, b, far, 2, 0)

    @pl.loop(0, chunks)
    def _(c):
        at = pl.ds(pl.multiple_of(c * rows, rows), rows)
        at_pad = pl.ds(pl.multiple_of(c * rows + PAD, UNIT), rows)
        dwide[:SLOT, :] = (dq[:, at_pad] * back).astype(BF)
        dwide[SLOT : 2 * SLOT, :] = (dk_acc[at, :].T[:SLOT] * back).astype(BF)
        dwide[2 * SLOT :, :] = dv_acc[at, :].T[:SLOT].astype(BF)
        dqkv_ref[c] = dot(pick, dwide[...], TN).astype(BF)

    flip = (iota((UNIT, UNIT), 0) + iota((UNIT, UNIT), 1) == UNIT - 1).astype(F32)
    half = span // 2
    lane = iota((8, span), 1)
    column = iota((8, DEPTH), 1) == head_width
    out = jnp.zeros((8, span), F32)
    far_sum = [jnp.where(column, ends[i], 0.0) for i in range(2)]
    for d in range(-PER, PER + 1):
        part = jnp.zeros((UNIT, UNIT), F32)
        for r in range(PER):
            c = r + d + 1
            if 0 <= c < NEAR:
                part = part + band[r * UNIT : (r + 1) * UNIT, c * UNIT : (c + 1) * UNIT]
        if abs(d) > 1:
            far_sum[0 if d > 0 else 1] += jnp.sum(part.reshape(UNIT // 8, 8, UNIT), axis=0)
            continue
        turned = lax.dot_general(flip, part, NN, precision=lax.Precision.HIGHEST, preferred_element_type=F32)
        wide = jnp.concatenate([turned, jnp.zeros_like(turned)], axis=1)
        skewed = pltpu.roll(wide, 0, 1, stride=1, stride_axis=0)
        line = jnp.sum(skewed.reshape(UNIT // 8, 8, 2 * UNIT), axis=0)
        offset = UNIT - 1 - d * UNIT - iota((span, 2 * UNIT), 1)
        hot = (jnp.clip(offset, -half, half - 1) + half == iota((span, 2 * UNIT), 0)).astype(F32)
        out += lax.dot_general(line, hot, NT, precision=lax.Precision.HIGHEST, preferred_element_type=F32)
    out += jnp.where(lane == 0, jnp.sum(far_sum[0], axis=1, keepdims=True), 0.0)
    out += jnp.where(lane == span - 1, jnp.sum(far_sum[1], axis=1, keepdims=True), 0.0)
    out = jnp.sum(out, axis=0, keepdims=True)
    dtab_ref[...] = out


def attend_backward(qkv, do, of, lse, bounds, plan, table, head_width):
    chunks, packed_rows, rows = qkv.shape
    total = chunks * rows
    padded = total + 2 * PAD
    span = table.shape[1]
    vm = pltpu.VMEM
    return pl.pallas_call(
        functools.partial(bwd_kernel, head_width=head_width),
        out_shape=(
            jax.ShapeDtypeStruct((chunks, packed_rows, rows), BF),
            jax.ShapeDtypeStruct((1, span), F32),
        ),
        in_specs=[pl.BlockSpec(memory_space=pltpu.SMEM)] + [pl.BlockSpec()] * 6,
        scratch_shapes=[
            vm((3, DEPTH, padded), BF),
            vm((total, DEPTH), BF),
            vm((SLOT, total), BF),
            vm((total, DEPTH), BF),
            vm((DEPTH, padded), BF),
            vm((padded, DEPTH), BF),
            vm((padded, DEPTH), BF),
            vm((BLK, NEAR * UNIT), F32),
            vm((SLOT, padded), F32),
            vm((BLK, NEAR * UNIT), F32),
            vm((2, 8, DEPTH), F32),
            vm((total, DEPTH), F32),
            vm((total, DEPTH), F32),
            vm((3 * SLOT, rows), BF),
        ],
        compiler_params=pltpu.CompilerParams(vmem_limit_bytes=62 * 2**20),
        name="attend_backward",
    )(plan, qkv, do, of, lse, table, bounds)

VEC = types.SimpleNamespace(
    first_gain=0, first_shift=1, first_up_bias=2, first_down_bias=3, mix_gain=4, mix_shift=5, mix_output_bias=6, filter_gain=7,
    filter_shift=8, pointwise_in_bias=9, batch_gain=10, batch_shift=11, pointwise_out_bias=12, second_gain=13, second_shift=14,
    second_up_bias=15, second_down_bias=16, final_gain=17, final_shift=18,
)
VEC_ROWS = 24
EPSILON = 1e-05
HALO = 64
TILE = 128
STEP = 1024
PIECE = 512


def col(cols_ref, i, size):
    return cols_ref[:size, i : i + 1]


def eye(n):
    return (iota((n, n), 0) == iota((n, n), 1)).astype(F32).astype(BF)


def flipped(mat):
    return dot(eye(mat.shape[1]), mat, NT).astype(BF)


def exact(a, b, dims=NN):
    return lax.dot_general(a, b, dims, precision=lax.Precision.HIGHEST, preferred_element_type=F32)


def folded(values):
    part = values[:, :TILE]
    for at in range(TILE, values.shape[1], TILE):
        part = part + values[:, at : at + TILE]
    return part


def row_sums(values):
    return exact(jnp.ones((8, TILE), F32), values, NT)


def norm(x):
    m = jnp.mean(x, axis=0, keepdims=True)
    c = x - m
    inv = lax.rsqrt(jnp.mean(c * c, axis=0, keepdims=True) + EPSILON)
    return c * inv, inv


def norm_back(e, n, inv, gain):
    ea = e * gain
    return inv * (ea - jnp.mean(ea, axis=0, keepdims=True) - n * jnp.mean(ea * n, axis=0, keepdims=True))


def sigmoid(v):
    return 0.5 + 0.5 * jnp.tanh(0.5 * v)


def ones_row(rows, lanes):
    return (iota((rows, lanes), 0) == 0).astype(F32).astype(BF)


def open_kernel(frames_ref, len_ref, up_ref, down_ref, mix_ref, *refs, packed_rows):
    vec_refs, (x1_ref, h2_ref, qkv_ref, cols_ref, bound_ref, plan_ref, ext_ref, line) = refs[:-8], refs[-8:]
    width, rows = frames_ref.shape
    hidden = up_ref.shape[1]
    heads = qkv_ref.shape[0]
    group = bound_ref.shape[1] - 2 * PAD
    vecs = [ref[...].astype(F32).reshape(1, ref.shape[0]) for ref in vec_refs]
    cols_ref[...] = stack_rows(vecs, (VEC_ROWS, hidden)).T
    slots = len_ref.shape[1]
    lengths = jnp.broadcast_to(len_ref[...].astype(F32), (8, slots))
    row, column = iota((slots, slots), 0), iota((slots, slots), 1)
    ends = exact((column <= row).astype(F32), lengths, NT)[:, :1].astype(jnp.int32)
    own_len = exact((column == row).astype(F32), lengths, NT)[:, :1].astype(jnp.int32)
    ends_row = exact(lengths, (row <= column).astype(F32))[:1].astype(jnp.int32)
    plan_ref[...] = block_plan(ends, ends_row, group)
    line[...] = jnp.full_like(line, -1)
    for edge in (slice(0, PAD), slice(PAD + group, 2 * PAD + group)):
        bound_ref[:, edge] = jnp.where(iota((2, PAD), 0) == 0, 1 << 20, -1)

    @pl.loop(0, group // 512)
    def _(c):
        at = pl.multiple_of(c * 512, 512)
        seg, first, stop = segment_rows(ends, own_len, iota((1, 512), 1) + at, group)
        line[:, pl.ds(at + TILE, 512)] = seg
        bound_ref[0:1, pl.ds(at + PAD, 512)] = first
        bound_ref[1:2, pl.ds(at + PAD, 512)] = stop

    first = pl.multiple_of(lax.axis_index("head") * rows, TILE)
    ext_ref[:, :rows] = line[:, pl.ds(first + TILE, rows)]
    left = line[:, pl.ds(first, TILE)]
    right = line[:, pl.ds(first + TILE + rows, TILE)]
    ext_ref[:, rows:] = jnp.where(iota((1, TILE), 1) < HALO, right, left)

    up_t = flipped(up_ref[...])
    mix_t = dot(spread_cols(mix_ref.shape[1], heads, packed_rows, mix_ref.shape[1] // heads), mix_ref[...], NT).astype(BF)

    @pl.loop(0, rows // STEP)
    def _(c):
        at = pl.ds(pl.multiple_of(c * STEP, STEP), STEP)
        x0 = frames_ref[:, at].astype(F32)
        n, _ = norm(x0)
        h1 = (n * col(cols_ref, VEC.first_gain, width) + col(cols_ref, VEC.first_shift, width)).astype(BF)
        a1 = dot(up_t, h1) + col(cols_ref, VEC.first_up_bias, hidden)
        s1 = (a1 * sigmoid(a1)).astype(BF)
        x1 = x0 + 0.5 * (dot(down_ref[...], s1) + col(cols_ref, VEC.first_down_bias, width))
        x1_ref[:, at] = x1
        n, _ = norm(x1)
        h2 = (n * col(cols_ref, VEC.mix_gain, width) + col(cols_ref, VEC.mix_shift, width)).astype(BF)
        h2_ref[:, at] = h2
        qkv = dot(mix_t, h2).astype(BF)
        for h in range(heads):
            qkv_ref[h, :, at] = qkv[h * packed_rows : (h + 1) * packed_rows]


def conv_masks(mask_ref, ext_ref, taps, sign):
    seg = jnp.broadcast_to(ext_ref[...], (8, ext_ref.shape[1]))
    lanes = seg.shape[1]
    for k in range(taps):
        other = pltpu.roll(seg, (sign * (taps // 2 - k)) % lanes, 1)
        mask_ref[k] = (other == seg).astype(F32)


def filter_kernel(x1_ref, x1l_ref, x1r_ref, o_ref, cols_ref, ext_ref, out_ref, pw_ref, taps_ref,
                  x2_ref, oc_ref, u_ref, y_ref, stat_ref, wide, mask, *, head_width, slot_count):
    width, rows = x1_ref.shape
    lanes = rows + TILE
    heads = o_ref.shape[0]
    taps = taps_ref.shape[0]
    out_t = flipped(out_ref[...])
    pw_t = flipped(pw_ref[...])
    gather = spread_cols(width, heads, SLOT, head_width)
    seg = ext_ref[...]
    live = (seg >= 0) & (seg < slot_count)
    mask[0, :1, :] = live.astype(F32)

    def part(x1, o, live_part):
        oc = dot(gather, o, TN).astype(BF)
        x2 = x1 + (dot(out_t, oc) + col(cols_ref, VEC.mix_output_bias, width))
        n, _ = norm(x2)
        h3 = (n * col(cols_ref, VEC.filter_gain, width) + col(cols_ref, VEC.filter_shift, width)).astype(BF)
        g = dot(pw_t, h3) + col(cols_ref, VEC.pointwise_in_bias, 2 * width)
        u = jnp.where(live_part > 0.5, g[:width] * sigmoid(g[width:]), 0.0).astype(BF)
        return oc, x2, u

    @pl.loop(0, rows // STEP)
    def _(c):
        at = pl.ds(pl.multiple_of(c * STEP, STEP), STEP)
        at_o = pl.ds(pl.multiple_of(c * STEP + TILE, TILE), STEP)
        o = jnp.concatenate([o_ref[h, :, at_o] for h in range(heads)], axis=0)
        oc, x2, u = part(x1_ref[:, at], o, mask[0, :1, at])
        oc_ref[:, at] = oc
        x2_ref[:, at] = x2
        u_ref[:, at] = u
        wide[:, at] = u.astype(F32)

    near = iota((1, TILE), 1) < HALO
    x1 = jnp.where(near, x1r_ref[...], x1l_ref[...])
    o = jnp.concatenate([jnp.where(near, o_ref[h, :, TILE + rows :].astype(F32), o_ref[h, :, :TILE].astype(F32)).astype(BF) for h in range(heads)], axis=0)
    _, x2, u = part(x1, o, mask[0, :1, rows:])
    x2_ref[:, rows:] = x2
    u_ref[:, rows:] = u
    wide[:, rows:] = u.astype(F32)

    conv_masks(mask, ext_ref, taps, 1)
    tap_cols = taps_ref[...].astype(F32).T
    wide_taps = tap_cols

    own = (live & (iota((1, lanes), 1) < rows)).astype(F32)
    count = jnp.sum(own, axis=1, keepdims=True)
    safe = jnp.maximum(count, 1.0)
    stats = []
    for r in range(width // 8):
        sl = slice(8 * r, 8 * r + 8)
        u8 = wide[sl, :]
        acc = jnp.zeros((8, lanes), F32)
        for k in range(taps):
            moved = pltpu.roll(u8, (taps // 2 - k) % lanes, 1)
            acc = acc + wide_taps[sl, k : k + 1] * (moved * mask[k])
        y_ref[sl, :] = acc
        mean = jnp.sum(acc * own, axis=1, keepdims=True) / safe
        dev = acc - mean
        spread = jnp.sum(dev * dev * own, axis=1, keepdims=True)
        lane = iota((8, TILE), 1)
        stats.append(jnp.where(lane == 0, mean, jnp.where(lane == 1, spread, jnp.where(lane == 2, count, 0.0))))
    table = jnp.concatenate(stats, axis=0).T[:8, :]
    stat_ref[...] = two_rows(table[0:1], table[1:2], table[2:3, :1])


def two_rows(a, b, extra):
    rest = a.shape[1] - TILE
    tail = pad_lanes(jnp.concatenate([a[:, TILE:], b[:, TILE:]], axis=0))
    spot = (iota((2, TILE), 0) == 0) & (iota((2, TILE), 1) == rest)
    return jnp.concatenate([a[:, :TILE], b[:, :TILE], jnp.where(spot, extra, tail)], axis=0)


def all_rows(ref, width):
    rest = width - TILE
    values = ref[...]
    a = jnp.concatenate([values[:, 0, :], values[:, 2, :rest]], axis=1)
    b = jnp.concatenate([values[:, 1, :], values[:, 3, :rest]], axis=1)
    return a, b, values[:, 2, rest : rest + 1]


def total_stats(stats_ref, width):
    mean_of, spread_of, n = all_rows(stats_ref, width)
    count = jnp.sum(n, axis=0, keepdims=True)
    mean = jnp.sum(n * mean_of, axis=0, keepdims=True) / count
    gap = mean_of - mean
    spread = jnp.sum(spread_of + n * gap * gap, axis=0, keepdims=True)
    inv = lax.rsqrt(spread / count + EPSILON)
    table = jnp.concatenate([mean, inv, jnp.broadcast_to(count, (1, width)), jnp.zeros((5, width), F32)], axis=0).T
    return table[:, 0:1], table[:, 1:2], table[:, 2:3]


def second_kernel(x2_ref, y_ref, stats_ref, cot_ref, cotl_ref, cotr_ref, cols_ref, pwo_ref, up_ref, down_ref,
                  out_ref, dx3_ref, e_ref, sums_ref, pack_ref, small_ref,
                  h4s, das, s4s, dfs, ws, dcs, gains):
    width, rows = out_ref.shape
    hidden = up_ref.shape[1]
    mean, inv_b, _ = total_stats(stats_ref, width)
    pwo_t = flipped(pwo_ref[...])
    up_t = flipped(up_ref[...])
    down = flipped(down_ref[...])
    gains[...] = jnp.zeros_like(gains)
    bgain = col(cols_ref, VEC.batch_gain, width)

    def part(x2, y, cot, at):
        zh = (y - mean) * inv_b
        z = zh * bgain + col(cols_ref, VEC.batch_shift, width)
        sig_z = sigmoid(z)
        w = (z * sig_z).astype(BF)
        x3 = x2 + (dot(pwo_t, w) + col(cols_ref, VEC.pointwise_out_bias, width))
        n4, inv4 = norm(x3)
        h4 = (n4 * col(cols_ref, VEC.second_gain, width) + col(cols_ref, VEC.second_shift, width)).astype(BF)
        a4 = dot(up_t, h4) + col(cols_ref, VEC.second_up_bias, hidden)
        sig = sigmoid(a4)
        s4 = (a4 * sig).astype(BF)
        x4 = x3 + 0.5 * (dot(down_ref[...], s4) + col(cols_ref, VEC.second_down_bias, width))
        nf, invf = norm(x4)
        fgain = col(cols_ref, VEC.final_gain, width)
        dx4 = norm_back(cot, nf, invf, fgain)
        df = (0.5 * dx4).astype(BF)
        da = (dot(down, df) * (sig * (1.0 + a4 * (1.0 - sig)))).astype(BF)
        dh = dot(up_ref[...], da)
        dx3 = dx4 + norm_back(dh, n4, inv4, col(cols_ref, VEC.second_gain, width))
        dc = dx3.astype(BF)
        dz = dot(pwo_ref[...], dc) * (sig_z * (1.0 + z * (1.0 - sig_z)))
        e = dz * bgain
        if at is not None:
            out = nf * fgain + col(cols_ref, VEC.final_shift, width)
            out_ref[:, at] = out.astype(BF)
            dx3_ref[:, at] = dx3
            h4s[:, at] = h4
            das[:hidden, at] = da
            s4s[:hidden, at] = s4
            dfs[:, at] = df
            ws[:width, at] = w
            dcs[:, at] = dc
            for i, v in enumerate((dh * n4, dh, cot * nf, cot, dz * zh, dz, e, e * zh)):
                gains[i] += folded(v)
        return e

    @pl.loop(0, rows // STEP)
    def _(c):
        at = pl.ds(pl.multiple_of(c * STEP, STEP), STEP)
        e_ref[:, at] = part(x2_ref[:, at], y_ref[:, at], cot_ref[:, at].astype(F32), at)

    halo = jnp.where(iota((1, TILE), 1) < HALO, cotr_ref[...].astype(F32), cotl_ref[...].astype(F32))
    e_ref[:, rows:] = part(x2_ref[:, rows:], y_ref[:, rows:], halo, None)

    s4s[hidden:, :] = ones_row(16, rows)
    ws[width:, :] = ones_row(16, rows)
    das[hidden:, :] = jnp.zeros((16, rows), BF)
    up_grad = dot(h4s[...], das[:hidden, :], NT)
    up_bias = dot(ones_row(16, rows), das[:hidden, :], NT)
    down_grad = dot(dfs[...], s4s[...], NT)
    pw_grad = dot(ws[...], dcs[...], NT)
    down_bias = exact(jnp.ones((8, rows), F32), dfs[...].astype(F32), NT)
    put_ff(pack_ref, up_grad, down_grad, 0)
    tall = 9 * width
    pack_ref[tall : tall + width, :] = pw_grad[:width, :TILE].astype(BF)
    pack_ref[tall + width : tall + 2 * width, :] = pad_lanes(pw_grad[:width, TILE:]).astype(BF)
    totals = [row_sums(gains[i])[:1] for i in range(8)]
    small_ref[...] = stack_rows(
        [totals[0], totals[1], up_bias[:1], down_bias[:1], totals[2], totals[3], totals[4], totals[5], pw_grad[width : width + 1]],
        small_ref.shape)
    sums_ref[...] = two_rows(totals[6], totals[7], 0.0)


def pad_lanes(mat, lanes=TILE):
    if mat.shape[1] == lanes:
        return mat
    return jnp.concatenate([mat, jnp.zeros((mat.shape[0], lanes - mat.shape[1]), mat.dtype)], axis=1)


def stack_rows(rows, shape):
    parts = [pad_lanes(r, shape[1]) for r in rows]
    parts.append(jnp.zeros((shape[0] - len(rows), shape[1]), F32))
    return jnp.concatenate(parts, axis=0)


def put_ff(pack_ref, up_grad, down_grad_t, at):
    width, hidden = up_grad.shape
    whole = hidden // TILE
    for i in range(whole):
        pack_ref[at + i * width : at + (i + 1) * width, :] = up_grad[:, i * TILE : (i + 1) * TILE].astype(BF)
        j = whole + i
        pack_ref[at + j * width : at + (j + 1) * width, :] = down_grad_t[:, i * TILE : (i + 1) * TILE].astype(BF)
    rest = jnp.concatenate([up_grad[:, whole * TILE : hidden], down_grad_t[:, whole * TILE : hidden]], axis=1)
    pack_ref[at + 2 * whole * width : at + (2 * whole + 1) * width, :] = rest.astype(BF)


def unfilter_kernel(e_ref, y_ref, stats_ref, sums_ref, u_ref, dx3_ref, x2_ref, oc_ref, cols_ref, ext_ref, pw_ref, taps_ref,
                    out_ref, dx2_ref, do_ref, pack_ref, small_ref, tapg_ref,
                    dyw, du_s, mask, prod, h3s, dgs, dms, ocs, gains, *, head_width, slot_count, ship):
    width, rows = dx3_ref.shape
    lanes = rows + TILE
    heads = do_ref.shape[0]
    taps = taps_ref.shape[0]
    mean, inv_b, count = total_stats(stats_ref, width)
    one_of, two_of, _ = all_rows(sums_ref, width)
    sums = jnp.concatenate([jnp.sum(one_of, axis=0, keepdims=True), jnp.sum(two_of, axis=0, keepdims=True), jnp.zeros((6, width), F32)], axis=0).T
    s1, s2 = sums[:, 0:1], sums[:, 1:2]
    seg = ext_ref[...]
    live = ((seg >= 0) & (seg < slot_count)).astype(F32)

    def conv_grad(at, span):
        zh = (y_ref[:, at] - mean) * inv_b
        lv = mask[0, :1, at]
        dy = inv_b * (e_ref[:, at] - lv * ((s1 + zh * s2) / count))
        return dy

    mask[0, :1, :] = live

    @pl.loop(0, rows // STEP)
    def _(c):
        at = pl.ds(pl.multiple_of(c * STEP, STEP), STEP)
        dyw[:, at] = conv_grad(at, STEP).astype(BF).astype(F32)

    last = conv_grad(pl.ds(rows, TILE), TILE)
    dyw[:, rows:] = jnp.where(seg[:, rows:] >= 0, last, 0.0).astype(BF).astype(F32)

    conv_masks(mask, ext_ref, taps, -1)
    tap_cols = taps_ref[...].astype(F32).T
    for r in range(width // 8):
        sl = slice(8 * r, 8 * r + 8)
        dy8 = dyw[sl, :]
        u8 = u_ref[16 * (r // 2) : 16 * (r // 2) + 16, :rows].astype(F32)[8 * (r % 2) : 8 * (r % 2) + 8]
        acc = jnp.zeros((8, rows), F32)
        for k in range(taps):
            moved = pltpu.roll(dy8, (k - taps // 2) % lanes, 1)[:, :rows] * mask[k][:, :rows]
            acc = acc + tap_cols[sl, k : k + 1] * moved
            hit = moved * u8
            prod[k, sl, :] = folded(hit)
        du_s[sl, :] = acc

    whole = prod[...].reshape(taps * width, TILE)
    hi = whole.astype(BF)
    lo = (whole - hi.astype(F32)).astype(BF)
    ones = jnp.ones((8, TILE), BF)
    lines = dot(ones, hi, NT) + dot(ones, lo, NT)
    for k in range(taps):
        tapg_ref[k : k + 1, :] = lines[:1, k * width : (k + 1) * width]

    pw_t = flipped(pw_ref[...])
    out_w = dot(spread_cols(width, heads, SLOT, head_width), out_ref[...]).astype(BF)
    gains[...] = jnp.zeros_like(gains)
    fgain = col(cols_ref, VEC.filter_gain, width)
    mask[0, :1, :] = live

    @pl.loop(0, rows // PIECE)
    def _(c):
        at = pl.ds(pl.multiple_of(c * PIECE, PIECE), PIECE)
        x2 = x2_ref[:, at]
        n, inv = norm(x2)
        h3 = (n * fgain + col(cols_ref, VEC.filter_shift, width)).astype(BF)
        g = dot(pw_t, h3) + col(cols_ref, VEC.pointwise_in_bias, 2 * width)
        sig = sigmoid(g[width:])
        t = mask[0, :1, at] * du_s[:, at] * sig
        dg = jnp.concatenate([t, t * g[:width] * (1.0 - sig)], axis=0).astype(BF)
        dh = dot(pw_ref[...], dg)
        dx2 = dx3_ref[:, at] + norm_back(dh, n, inv, fgain)
        dx2_ref[:, at] = dx2
        dm = dx2.astype(BF)
        do = dot(out_w, dm).astype(BF)
        for h in range(heads):
            do_ref[h, :, at] = do[h * SLOT : (h + 1) * SLOT]
        ship(c)
        h3s[:width, at] = h3
        dgs[:, at] = dg
        dms[:, at] = dm
        ocs[:width, at] = oc_ref[:, at]
        for i, v in enumerate((dh * n, dh)):
            gains[i] += folded(v)

    h3s[width:, :] = ones_row(16, rows)
    ocs[width:, :] = ones_row(16, rows)
    pw_grad = dot(h3s[...], dgs[...], NT)
    out_grad = dot(ocs[...], dms[...], NT)
    at = 0
    for lo in range(0, 2 * width, TILE):
        pack_ref[at : at + width, :] = pad_lanes(pw_grad[:width, lo : min(lo + TILE, 2 * width)]).astype(BF)
        at += width
    for lo in range(0, width, TILE):
        pack_ref[at : at + width, :] = pad_lanes(out_grad[:width, lo : min(lo + TILE, width)]).astype(BF)
        at += width
    small_ref[...] = stack_rows(
        [row_sums(gains[0])[:1], row_sums(gains[1])[:1], pw_grad[width : width + 1], out_grad[width : width + 1]], small_ref.shape)


def close_kernel(frames_ref, x1_ref, h2_ref, dx2_ref, dqkv_ref, dtab_ref, cols_ref, up_ref, down_ref, mix_ref,
                 grad_ref, pack_ref, h1s, das, s1s, dfs, dqs, gains, *, arrive, between):
    width, rows = frames_ref.shape
    hidden = up_ref.shape[1]
    heads, packed_rows, _ = dqkv_ref.shape
    up_t = flipped(up_ref[...])
    down = flipped(down_ref[...])
    hot = spread_cols(mix_ref.shape[1], heads, packed_rows, mix_ref.shape[1] // heads)
    mix_w = dot(mix_ref[...], hot, NT).astype(BF)
    gains[...] = jnp.zeros_like(gains)
    mgain = col(cols_ref, VEC.mix_gain, width)
    fgain = col(cols_ref, VEC.first_gain, width)

    @pl.loop(0, rows // PIECE)
    def _(c):
        arrive(c)
        at = pl.ds(pl.multiple_of(c * PIECE, PIECE), PIECE)
        dq = jnp.concatenate([dqkv_ref[h, :, at] for h in range(heads)], axis=0)
        dqs[:, at] = dq
        dh2 = dot(mix_w, dq)
        n2, inv2 = norm(x1_ref[:, at])
        dx1 = dx2_ref[:, at] + norm_back(dh2, n2, inv2, mgain)
        x0 = frames_ref[:, at].astype(F32)
        n1, inv1 = norm(x0)
        h1 = (n1 * fgain + col(cols_ref, VEC.first_shift, width)).astype(BF)
        a1 = dot(up_t, h1) + col(cols_ref, VEC.first_up_bias, hidden)
        sig = sigmoid(a1)
        s1s[:, at] = (a1 * sig).astype(BF)
        df = (0.5 * dx1).astype(BF)
        da = (dot(down, df) * (sig * (1.0 + a1 * (1.0 - sig)))).astype(BF)
        dh1 = dot(up_ref[...], da)
        grad_ref[:, at] = dx1 + norm_back(dh1, n1, inv1, fgain)
        h1s[:, at] = h1
        das[:, at] = da
        dfs[:, at] = df
        for i, v in enumerate((dh1 * n1, dh1, dh2 * n2, dh2)):
            gains[i] += folded(v)
        between(c)

    up_grad = dot(h1s[...], das[...], NT)
    up_bias = dot(ones_row(16, rows), das[...], NT)
    down_grad = dot(dfs[...], s1s[...], NT)
    down_bias = exact(jnp.ones((8, rows), F32), dfs[...].astype(F32), NT)
    mix_grad = dot(dot(h2_ref[...], dqs[...], NT).astype(BF), hot)
    put_ff(pack_ref, up_grad, down_grad, 0)
    at = (2 * (hidden // TILE) + 1) * width
    for lo in range(0, mix_grad.shape[1], TILE):
        pack_ref[at : at + width, :] = pad_lanes(mix_grad[:, lo : min(lo + TILE, mix_grad.shape[1])]).astype(BF)
        at += width
    totals = [row_sums(gains[i])[:1] for i in range(4)]
    small = stack_rows([totals[0], totals[1], up_bias[:1], down_bias[:1], totals[2], totals[3]], (16, 5 * TILE))
    at = put_small(pack_ref, small, at)
    span = dtab_ref.shape[1]
    table = jnp.where(iota((16, span), 0) == lax.axis_index("head"), dtab_ref[...], 0.0)
    pack_ref[at : at + 16, :] = table.astype(BF)
    if at + 16 < pack_ref.shape[0]:
        pack_ref[at + 16 :, :] = jnp.zeros((pack_ref.shape[0] - at - 16, TILE), BF)


def put_small(pack_ref, small, at):
    for lo in range(0, small.shape[1], TILE):
        pack_ref[at : at + small.shape[0], :] = small[:, lo : lo + TILE].astype(BF)
        at += small.shape[0]
    return at


def put_taps(pack_ref, tapg, at):
    taps = tapg.shape[0]
    pack_ref[at : at + taps, :] = tapg[:, :TILE].astype(BF)
    pack_ref[at + taps : at + 2 * taps, :] = pad_lanes(tapg[:, TILE:]).astype(BF)
    return at + 2 * taps


def unpack_kernel(pack_ref, *out_refs, layout):
    given = Weights(*out_refs)

    def wide(at, rows, lanes):
        parts = [pack_ref[at + i * rows : at + (i + 1) * rows, :].astype(F32) for i in range(-(-lanes // TILE))]
        return jnp.concatenate(parts, axis=1)[:, :lanes]

    for at, up_ref, down_ref in ((layout.first, given.first_up, given.first_down), (layout.second, given.second_up, given.second_down)):
        width, hidden = up_ref.shape
        whole = hidden // TILE
        half = hidden - whole * TILE
        piece = lambda i: pack_ref[at + i * width : at + (i + 1) * width, :].astype(F32)
        rest = piece(2 * whole)
        up_ref[...] = jnp.concatenate([piece(i) for i in range(whole)] + [rest[:, :half]], axis=1)
        down_ref[...] = jnp.concatenate([piece(whole + i) for i in range(whole)] + [rest[:, half:]], axis=1)
    for ref, at in ((given.mix_inputs, layout.mix_inputs), (given.pointwise_in, layout.pointwise_in), (given.mix_output, layout.mix_output),
                    (given.pointwise_out, layout.pointwise_out), (given.depthwise_taps, layout.taps)):
        ref[...] = wide(at, *ref.shape)
    given.position_bias[...] = pack_ref[layout.table : layout.table + 16, :].astype(F32)[: given.position_bias.shape[0]]
    late = wide(layout.small_late, 16, 5 * TILE)
    early = wide(layout.small, 32, 5 * TILE)
    late_rows = (
        given.first_gain, given.first_shift, given.first_up_bias, given.first_down_bias, given.mix_gain, given.mix_shift,
    )
    second_rows = (
        given.second_gain, given.second_shift, given.second_up_bias, given.second_down_bias, given.final_gain, given.final_shift,
        given.batch_gain, given.batch_shift, given.pointwise_out_bias,
    )
    filter_rows = (given.filter_gain, given.filter_shift, given.pointwise_in_bias, given.mix_output_bias)
    for small, first, refs in ((late, 0, late_rows), (early, 0, second_rows), (early, 16, filter_rows)):
        for row, ref in enumerate(refs, first):
            ref[...] = small[row : row + 1, : ref.shape[0]].reshape(ref.shape)


@dataclasses.dataclass
class Weights:
    first_gain: object
    first_shift: object
    first_up: object
    first_up_bias: object
    first_down: object
    first_down_bias: object
    mix_gain: object
    mix_shift: object
    mix_inputs: object
    position_bias: object
    mix_output: object
    mix_output_bias: object
    filter_gain: object
    filter_shift: object
    pointwise_in: object
    pointwise_in_bias: object
    depthwise_taps: object
    batch_gain: object
    batch_shift: object
    pointwise_out: object
    pointwise_out_bias: object
    second_gain: object
    second_shift: object
    second_up: object
    second_up_bias: object
    second_down: object
    second_down_bias: object
    final_gain: object
    final_shift: object


def pack_layout(width, hidden, mix_width, taps, devices):
    ff = (2 * (hidden // TILE) + 1) * width
    chunks = lambda lanes: -(-lanes // TILE) * width
    unit = 16 * devices
    at = types.SimpleNamespace(second=0)
    at.pointwise_out = ff
    at.pointwise_in = at.pointwise_out + chunks(width)
    at.mix_output = at.pointwise_in + chunks(2 * width)
    at.taps = at.mix_output + chunks(width)
    at.small = at.taps + 2 * taps
    at.early_end = at.small + 32 * 5
    at.first = -(-at.early_end // unit) * unit
    at.mix_inputs = at.first + ff
    at.small_late = at.mix_inputs + chunks(mix_width)
    at.table = at.small_late + 16 * 5
    at.rows = -(-(at.table + 16) // unit) * unit
    return at


MESH = pl.DeviceIdType.MESH


def meet(peers):
    barrier = pltpu.get_barrier_semaphore()
    for peer in peers:
        pl.semaphore_signal(barrier, inc=1, device_id=peer, device_id_type=MESH)
    pl.semaphore_wait(barrier, len(peers))


def head_peers(n):
    me = lax.axis_index("head")
    return me, [{"head": lax.rem(me + s, n)} for s in range(1, n)], [lax.rem(me + s, n) for s in range(1, n)]


def opening_kernel(qkv_ref, x1_ref, cot_ref, all_ref, x1l_ref, x1r_ref, cotl_ref, cotr_ref, send, recv, local, hsend, hrecv, *, n):
    me, peers, ids = head_peers(n)
    rows = cot_ref.shape[1]
    meet(peers)
    copies = []
    for s, (peer, p) in enumerate(zip(peers, ids)):
        copies.append(pltpu.make_async_remote_copy(
            src_ref=qkv_ref.at[p], dst_ref=all_ref.at[me], send_sem=send.at[s], recv_sem=recv.at[s],
            device_id=peer, device_id_type=MESH))
        copies[-1].start()
    own = pltpu.make_async_copy(qkv_ref.at[me], all_ref.at[me], local)
    own.start()

    def edge(i, src, dst, head):
        return pltpu.make_async_remote_copy(src_ref=src, dst_ref=dst, send_sem=hsend.at[i], recv_sem=hrecv.at[i],
                                            device_id={"head": head}, device_id_type=MESH)

    up = lax.rem(me + 1, n)
    down = lax.rem(me + n - 1, n)
    to_right = [edge(0, x1_ref.at[:, pl.ds(rows - TILE, TILE)], x1l_ref, up), edge(1, cot_ref.at[:, pl.ds(rows - TILE, TILE)], cotl_ref, up)]
    to_left = [edge(2, x1_ref.at[:, pl.ds(0, TILE)], x1r_ref, down), edge(3, cot_ref.at[:, pl.ds(0, TILE)], cotr_ref, down)]

    @pl.when(me < n - 1)
    def _():
        for c in to_right:
            c.start()

    @pl.when(me > 0)
    def _():
        for c in to_left:
            c.start()

    own.wait()
    for copy in copies:
        copy.wait()

    @pl.when(me < n - 1)
    def _():
        for c in to_right:
            c.wait_send()
        for c in to_left:
            c.wait_recv()

    @pl.when(me > 0)
    def _():
        for c in to_left:
            c.wait_send()
        for c in to_right:
            c.wait_recv()


def open_exchange(qkv, x1, cot, collective_id):
    n = lax.axis_size("head")
    width = x1.shape[0]
    hbm = pl.BlockSpec(memory_space=pl.ANY)
    return pl.pallas_call(
        functools.partial(opening_kernel, n=n),
        out_shape=(
            jax.ShapeDtypeStruct(qkv.shape, BF),
            jax.ShapeDtypeStruct((width, TILE), F32), jax.ShapeDtypeStruct((width, TILE), F32),
            jax.ShapeDtypeStruct((width, TILE), BF), jax.ShapeDtypeStruct((width, TILE), BF),
        ),
        in_specs=[hbm] * 3, out_specs=(hbm,) * 5,
        scratch_shapes=[pltpu.SemaphoreType.DMA((n - 1,)), pltpu.SemaphoreType.DMA((n - 1,)), pltpu.SemaphoreType.DMA,
                        pltpu.SemaphoreType.DMA((4,)), pltpu.SemaphoreType.DMA((4,))],
        compiler_params=pltpu.CompilerParams(collective_id=collective_id, has_side_effects=True, vmem_limit_bytes=62 * 2**20),
        name="share_queries_keys_values",
    )(qkv, x1, cot)


def everyone(n_tm, n_head):
    n = n_tm * n_head
    me = lax.axis_index("tm") * n_head + lax.axis_index("head")

    def place(s):
        peer = lax.rem(me + s, n)
        return {"tm": peer // n_head, "head": lax.rem(peer, n_head)}

    return me, n, place


def tell(src_ref, all_ref, send, recv, n_tm, n_head):
    me, n, place = everyone(n_tm, n_head)

    def copy(s):
        return pltpu.make_async_remote_copy(src_ref=src_ref, dst_ref=all_ref.at[me], send_sem=send.at[s], recv_sem=recv.at[s],
                                            device_id=place(s), device_id_type=MESH)

    pl.loop(1, n)(lambda s: copy(s).start())
    all_ref[me] = src_ref[...]
    pl.loop(1, n)(lambda s: copy(s).wait())


def middle_kernel(o_ref, x1_ref, x1l_ref, x1r_ref, cot_ref, cotl_ref, cotr_ref, cols_ref, ext_ref, mixo_ref, pwi_ref, taps_ref,
                  pwo_ref, up_ref, down_ref,
                  out_ref, dx2_ref, do_all, early_ref,
                  o_own, x2, oc, u, y, stat, stats, dx3, e, sums, all_sums, do, wide, mask,
                  h4s, das, s4s, dfs, ws, dcs, gains8, dyw, du, prod, h3s, dgs, dms, ocs, gains2,
                  smalld, smalle, tapg, send_o, recv_o, local_o, send_a, recv_a, send_b, recv_b, send_d, recv_d, local_d,
                  *, n_tm, n_head, head_width, slot_count, layout):
    me, peers, ids = head_peers(n_head)
    _, n, place = everyone(n_tm, n_head)
    barrier = pltpu.get_barrier_semaphore()
    rows = x1_ref.shape[1]

    @pl.loop(1, n)
    def _(s):
        pl.semaphore_signal(barrier, inc=1, device_id=place(s), device_id_type=MESH)

    pl.semaphore_wait(barrier, n - 1)

    def part(p):
        return o_ref.at[:, pl.ds(pl.multiple_of(p * rows, TILE), rows + 2 * TILE)]

    copies = [
        pltpu.make_async_remote_copy(src_ref=part(p), dst_ref=o_own.at[me], send_sem=send_o.at[s], recv_sem=recv_o.at[s],
                                     device_id=peer, device_id_type=MESH)
        for s, (peer, p) in enumerate(zip(peers, ids))
    ]
    for copy in copies:
        copy.start()
    own = pltpu.make_async_copy(part(me), o_own.at[me], local_o)
    own.start()
    own.wait()
    for copy in copies:
        copy.wait()
    filter_kernel(x1_ref, x1l_ref, x1r_ref, o_own, cols_ref, ext_ref, mixo_ref, pwi_ref, taps_ref, x2, oc, u, y, stat, wide, mask,
                  head_width=head_width, slot_count=slot_count)
    tell(stat, stats, send_a, recv_a, n_tm, n_head)
    second_kernel(x2, y, stats, cot_ref, cotl_ref, cotr_ref, cols_ref, pwo_ref, up_ref, down_ref,
                  out_ref, dx3, e, sums, early_ref, smalld, h4s, das, s4s, dfs, ws, dcs, gains8)
    tell(sums, all_sums, send_b, recv_b, n_tm, n_head)

    def piece(c, s):
        at = pl.ds(pl.multiple_of(c * PIECE, PIECE), PIECE)
        return pltpu.make_async_remote_copy(src_ref=do.at[ids[s], :, at], dst_ref=do_all.at[me, :, at], send_sem=send_d.at[c, s],
                                            recv_sem=recv_d.at[c, s], device_id=peers[s], device_id_type=MESH)

    def ship(c):
        for s in range(n_head - 1):
            piece(c, s).start()

    unfilter_kernel(e, y, stats, all_sums, u, dx3, x2, oc, cols_ref, ext_ref, pwi_ref, taps_ref, mixo_ref,
                    dx2_ref, do, early_ref.at[pl.ds(layout.pointwise_in, layout.taps - layout.pointwise_in)], smalle, tapg, dyw, du, mask, prod, h3s, dgs, dms, ocs, gains2,
                    head_width=head_width, slot_count=slot_count, ship=ship)
    own = pltpu.make_async_copy(do.at[me], do_all.at[me], local_d)
    own.start()
    end = put_taps(early_ref, tapg[...], layout.taps)
    end = put_small(early_ref, jnp.concatenate([smalld[...], smalle[...]], axis=0), end)
    if end < early_ref.shape[0]:
        early_ref[end:, :] = jnp.zeros((early_ref.shape[0] - end, TILE), BF)
    own.wait()

    @pl.loop(0, rows // PIECE)
    def _(c):
        for s in range(n_head - 1):
            piece(c, s).wait()


def gradient_sum(src_ref, out_ref, first, got1, part1, got2, part2, sems, local, n_tm, n_head):
    tm, head = lax.axis_index("tm"), lax.axis_index("head")
    big = src_ref.shape[0] // n_tm
    small = big // n_head

    def rows(i, size, base=0):
        return pl.ds(pl.multiple_of(base + i * size, 16), size)

    def send(src, dst, phase, s, peer):
        return pltpu.make_async_remote_copy(src_ref=src, dst_ref=dst, send_sem=sems.at[2 * phase, s], recv_sem=sems.at[2 * phase + 1, s],
                                            device_id=peer, device_id_type=MESH)

    def tm_peer(s):
        return lax.rem(tm + s, n_tm)

    def head_peer(s):
        return lax.rem(head + s, n_head)

    def one(s):
        return send(src_ref.at[rows(tm_peer(s), big)], got1.at[s], 0, s, {"tm": tm_peer(s)})

    def two(s):
        return send(part1.at[rows(head_peer(s), small)], got2.at[s], 1, s, {"head": head_peer(s)})

    def three(s):
        at = part2.at[rows(head, small)]
        return send(at, at, 2, s, {"head": head_peer(s)})

    def four(s):
        return send(part2, out_ref.at[rows(tm, big, first)], 3, s, {"tm": tm_peer(s)})

    def added(got, n):
        total = got[0].astype(F32)
        for s in range(1, n):
            total = total + got[s].astype(F32)
        return total.astype(BF)

    def step0():
        pl.loop(1, n_tm)(lambda s: one(s).start())
        got1[0] = src_ref[rows(tm, big), :]

    def step1():
        pl.loop(1, n_tm)(lambda s: one(s).wait())
        part1[...] = added(got1, n_tm)
        pl.loop(1, n_head)(lambda s: two(s).start())
        got2[0] = part1[rows(head, small), :]

    def step2():
        pl.loop(1, n_head)(lambda s: two(s).wait())
        part2[rows(head, small), :] = added(got2, n_head)
        pl.loop(1, n_head)(lambda s: three(s).start())

    def step3():
        pl.loop(1, n_head)(lambda s: three(s).wait())
        pl.loop(1, n_tm)(lambda s: four(s).start())
        pltpu.make_async_copy(part2, out_ref.at[rows(tm, big, first)], local).start()

    def step4():
        pltpu.make_async_copy(part2, out_ref.at[rows(tm, big, first)], local).wait()
        pl.loop(1, n_tm)(lambda s: four(s).wait())

    return step0, step1, step2, step3, step4


def final_kernel(dqkv_ref, early_ref, frames_ref, x1_ref, h2_ref, dx2_ref, dtab_ref, cols_ref, up_ref, down_ref, mix_ref,
                 grad_ref, total_ref,
                 dqkv, late, h1s, das, s1s, dfs, dqs, gains, a1, a2, a3, a4, b1, b2, b3, b4,
                 send_q, recv_q, local_q, sems_a, local_a, sems_b, local_b, *, n_tm, n_head):
    me, peers, ids = head_peers(n_head)
    tm = lax.axis_index("tm")
    rows = x1_ref.shape[1]
    barrier = pltpu.get_barrier_semaphore()
    for peer in peers + [{"tm": lax.rem(tm + s, n_tm)} for s in range(1, n_tm)]:
        pl.semaphore_signal(barrier, inc=1, device_id=peer, device_id_type=MESH)
    pl.semaphore_wait(barrier, n_head + n_tm - 2)

    def piece(c, s):
        at = pl.ds(pl.multiple_of(c * PIECE, PIECE), PIECE)
        return pltpu.make_async_remote_copy(src_ref=dqkv_ref.at[ids[s], :, at], dst_ref=dqkv.at[me, :, at], send_sem=send_q.at[c, s],
                                            recv_sem=recv_q.at[c, s], device_id=peers[s], device_id_type=MESH)

    @pl.loop(0, rows // PIECE)
    def _(c):
        for s in range(n_head - 1):
            piece(c, s).start()

    own = pltpu.make_async_copy(dqkv_ref.at[me], dqkv.at[me], local_q)
    own.start()
    early = gradient_sum(early_ref, total_ref, 0, a1, a2, a3, a4, sems_a, local_a, n_tm, n_head)
    after = gradient_sum(late, total_ref, early_ref.shape[0], b1, b2, b3, b4, sems_b, local_b, n_tm, n_head)
    early[0]()
    own.wait()

    def arrive(c):
        for s in range(n_head - 1):
            piece(c, s).wait()

    inside = min(3, rows // PIECE)

    def between(c):
        for i in range(inside):
            pl.when(c == i)(early[i + 1])

    close_kernel(frames_ref, x1_ref, h2_ref, dx2_ref, dqkv, dtab_ref, cols_ref, up_ref, down_ref, mix_ref,
                 grad_ref, late, h1s, das, s1s, dfs, dqs, gains, arrive=arrive, between=between)
    for step in early[inside + 1 : 4]:
        step()
    after[0]()
    early[4]()
    for step in after[1:]:
        step()


VMEM_MIB = 62


def local_call(kernel, name, ins, outs, scratch, vmem=VMEM_MIB):
    return pl.pallas_call(
        kernel,
        out_shape=tuple(jax.ShapeDtypeStruct(s, t) for s, t in outs),
        scratch_shapes=[pltpu.VMEM(s, t) for s, t in scratch],
        compiler_params=pltpu.CompilerParams(vmem_limit_bytes=vmem * 2**20),
        name=name,
    )(*ins)


def body(
    frames, lengths, first_gain, first_shift, first_up, first_up_bias, first_down, first_down_bias, mix_gain, mix_shift,
    mix_inputs, position_bias, mix_output, mix_output_bias, filter_gain, filter_shift, pointwise_in, pointwise_in_bias,
    depthwise_taps, batch_gain, batch_shift, pointwise_out, pointwise_out_bias, second_gain, second_shift, second_up,
    second_up_bias, second_down, second_down_bias, final_gain, final_shift, cotangent,
):
    weights = Weights(
        first_gain, first_shift, first_up, first_up_bias, first_down, first_down_bias, mix_gain, mix_shift, mix_inputs, position_bias,
        mix_output, mix_output_bias, filter_gain, filter_shift, pointwise_in, pointwise_in_bias, depthwise_taps, batch_gain,
        batch_shift, pointwise_out, pointwise_out_bias, second_gain, second_shift, second_up, second_up_bias, second_down,
        second_down_bias, final_gain, final_shift)
    rows, width = frames.shape
    hidden = first_up.shape[1]
    n_head, n_tm = lax.axis_size("head"), lax.axis_size("tm")
    heads, span = position_bias.shape
    head_width = width // heads
    packed_rows = -(-3 * head_width // 16) * 16
    group = rows * n_head
    lanes = rows + TILE
    slots = lengths.shape[1]
    taps = depthwise_taps.shape[0]
    layout = pack_layout(width, hidden, mix_inputs.shape[1], taps, n_tm * n_head)

    vectors = tuple(getattr(weights, name) for name in VEC.__dict__)
    frames_t, cot_t, first_down_t, second_down_t = frames.T, cotangent.T, first_down.T, second_down.T
    x1, h2, qkv, cols, bounds, plan, ext = local_call(
        functools.partial(open_kernel, packed_rows=packed_rows), "open",
        (frames_t, lengths, first_up, first_down_t, mix_inputs) + vectors,
        [((width, rows), F32), ((width, rows), BF), ((n_head, packed_rows, rows), BF), ((hidden, VEC_ROWS), F32),
         ((2, group + 2 * PAD), jnp.int32), ((group // BLK, 128), jnp.int32), ((1, lanes), jnp.int32)],
        [((1, group + 2 * TILE), jnp.int32)])
    qkv_all, x1l, x1r, cotl, cotr = open_exchange(qkv, x1, cot_t, 1)
    o, of, lse = attend_forward(qkv_all, bounds, plan, position_bias, head_width)
    vm, dma, hbm = pltpu.VMEM, pltpu.SemaphoreType.DMA, pl.BlockSpec(memory_space=pl.ANY)
    steps = rows // PIECE
    everyone_sems = dma((n_tm * n_head,))
    piece_sems = dma((steps, n_head - 1))
    outs = [((width, rows), BF), ((width, rows), F32), ((n_head, SLOT, rows), BF), ((layout.first, TILE), BF)]
    out, dx2, do_all, early = pl.pallas_call(
        functools.partial(middle_kernel, n_tm=n_tm, n_head=n_head, head_width=head_width, slot_count=slots, layout=layout),
        out_shape=tuple(jax.ShapeDtypeStruct(s, t) for s, t in outs),
        in_specs=[hbm] + [pl.BlockSpec()] * 14,
        out_specs=tuple(hbm if i == 2 else pl.BlockSpec() for i in range(len(outs))),
        scratch_shapes=[
            vm((n_head, SLOT, rows + 2 * TILE), BF), vm((width, lanes), F32), vm((width, rows), BF), vm((width, lanes), BF),
            vm((width, lanes), F32), vm((4, TILE), F32), vm((n_tm * n_head, 4, TILE), F32), vm((width, rows), F32),
            vm((width, lanes), F32), vm((4, TILE), F32), vm((n_tm * n_head, 4, TILE), F32), vm((n_head, SLOT, rows), BF),
            vm((width, lanes), F32), vm((taps, 8, lanes), F32),
            vm((width, rows), BF), vm((hidden + 16, rows), BF), vm((hidden + 16, rows), BF), vm((width, rows), BF),
            vm((width + 16, rows), BF), vm((width, rows), BF), vm((8, width, TILE), F32),
            vm((width, lanes), F32), vm((width, rows), F32), vm((taps, width, TILE), F32), vm((width + 16, rows), BF),
            vm((2 * width, rows), BF), vm((width, rows), BF), vm((width + 16, rows), BF), vm((2, width, TILE), F32),
            vm((16, 5 * TILE), F32), vm((16, 5 * TILE), F32), vm((taps, width), F32),
            dma((n_head - 1,)), dma((n_head - 1,)), dma, everyone_sems, everyone_sems, everyone_sems, everyone_sems,
            piece_sems, piece_sems, dma,
        ],
        compiler_params=pltpu.CompilerParams(collective_id=2, has_side_effects=True, vmem_limit_bytes=VMEM_MIB * 2**20),
        name="middle",
    )(o, x1, x1l, x1r, cot_t, cotl, cotr, cols, ext, mix_output, pointwise_in, depthwise_taps, pointwise_out, second_up, second_down_t)
    dqkv, dtab = attend_backward(qkv_all, do_all, of, lse, bounds, plan, position_bias, head_width)
    late_rows = layout.rows - layout.first

    def sum_scratch(count):
        big = count // n_tm
        return [vm((n_tm, big, TILE), BF), vm((big, TILE), BF), vm((n_head, big // n_head, TILE), BF), vm((big, TILE), BF)]

    sum_sems = dma((8, max(n_tm, n_head)))
    grad, total = pl.pallas_call(
        functools.partial(final_kernel, n_tm=n_tm, n_head=n_head),
        out_shape=(jax.ShapeDtypeStruct((width, rows), F32), jax.ShapeDtypeStruct((layout.rows, TILE), BF)),
        in_specs=[hbm] + [pl.BlockSpec()] * 10,
        out_specs=(pl.BlockSpec(), hbm),
        scratch_shapes=[
            vm((n_head, packed_rows, rows), BF), vm((late_rows, TILE), BF),
            vm((width, rows), BF), vm((hidden, rows), BF), vm((hidden, rows), BF), vm((width, rows), BF),
            vm((n_head * packed_rows, rows), BF), vm((4, width, TILE), F32),
            *sum_scratch(layout.first), *sum_scratch(late_rows),
            piece_sems, piece_sems, dma, sum_sems, dma, sum_sems, dma,
        ],
        compiler_params=pltpu.CompilerParams(collective_id=3, has_side_effects=True, vmem_limit_bytes=VMEM_MIB * 2**20),
        name="final",
    )(dqkv, early, frames_t, x1, h2, dx2, dtab, cols, first_up, first_down_t, mix_inputs)
    shapes = Weights(**{n: w.shape for n, w in weights.__dict__.items()})
    shapes.first_down = shapes.second_down = first_down_t.shape
    summed = Weights(*local_call(
        functools.partial(unpack_kernel, layout=layout), "unpack", (total,), [(s, F32) for s in shapes.__dict__.values()], []))
    summed.first_down, summed.second_down = summed.first_down.T, summed.second_down.T
    return (out.T, grad.T) + tuple(summed.__dict__.values())


def solution(mesh):
    rows = P(("tm", "head"), None)
    placed = (rows, P("tm", None)) + (P(),) * 29 + (rows,)
    return jax.shard_map(body, mesh=mesh, in_specs=placed, out_specs=(rows, rows) + (P(),) * 29, check_vma=False)
```

```python
import dataclasses
import functools
import math
import types

import jax
import jax.numpy as jnp
from jax import lax
from jax.experimental import pallas as pl
from jax.experimental.pallas import tpu as pltpu
from jax.sharding import PartitionSpec as P

BF = jnp.bfloat16
F32 = jnp.float32
LOG2E = math.log2(math.e)
BLK = 512
UNIT = 128
PER = BLK // UNIT
NEAR = PER + 2
PAD = 8 * UNIT
SLOT = 48
DEPTH = 128
MASKED = -1e30
NN = (((1,), (0,)), ((), ()))
NT = (((1,), (1,)), ((), ()))
TN = (((0,), (0,)), ((), ()))


def dot(a, b, dims=NN):
    return lax.dot_general(a, b, dims, preferred_element_type=F32)


def iota(shape, dim):
    return lax.broadcasted_iota(jnp.int32, shape, dim)


def spread_cols(width, slots, slot_rows, used):
    row, column = iota((slots * slot_rows, width), 0), iota((slots * slot_rows, width), 1)
    hit = jnp.zeros((slots * slot_rows, width), jnp.bool_)
    for s in range(slots):
        f = row - slot_rows * s
        hit = hit | ((f >= 0) & (f < used) & (column == used * s + f))
    return hit.astype(F32).astype(BF)


def split3(v):
    hi = v.astype(BF).astype(F32)
    r1 = v - hi
    mid = r1.astype(BF).astype(F32)
    return hi, mid, r1 - mid


def three_rows(v, rows):
    a, b, e = split3(v)
    row = iota((rows, v.shape[1]), 0)
    return jnp.where(row == 0, a, jnp.where(row == 1, b, jnp.where(row == 2, e, 0.0)))


def pick_row(ref, index):
    values = ref[...].astype(F32)
    return jnp.sum(jnp.where(iota(values.shape, 0) == index, values, 0.0), axis=0, keepdims=True)


def bias_square(table, d):
    span = table.shape[1]
    half = span // 2
    lanes = 2 * UNIT
    u = iota((span, lanes), 1)
    u = jnp.where(u < UNIT, u, u - lanes)
    ids = jnp.clip(-UNIT * d - u, -half, half - 1) + half
    hot = (ids == iota((span, lanes), 0)).astype(F32).astype(BF)
    line = dot(jnp.broadcast_to(table, (UNIT, span)).astype(BF), hot) * LOG2E
    return pltpu.roll(line, 0, 1, stride=1, stride_axis=0)[:, :UNIT]


def bias_near(table, tile, keys_near):
    span = table.shape[1]
    squares = {d: bias_square(table, d) for d in (-1, 0, 1)}
    low = jnp.broadcast_to(table[:, :1] * LOG2E, (UNIT, UNIT))
    high = jnp.broadcast_to(table[:, span - 1 :] * LOG2E, (UNIT, UNIT))
    for r in range(tile.shape[0] // UNIT):
        for c in range(tile.shape[1] // UNIT):
            d = c - (r - 1) if keys_near else (c - 1) - r
            part = squares[d] if abs(d) < 2 else (low if d > 0 else high)
            tile[r * UNIT : (r + 1) * UNIT, c * UNIT : (c + 1) * UNIT] = part


def units_at(u, count):
    return pl.ds(pl.multiple_of(u * UNIT, UNIT), count * UNIT)


def far_windows(low, plain, edge, step, side, up, fine):
    sign = 1 if up else -1

    def run(at, times, size, masked):
        def one(i, carry):
            near = at + sign * i * size
            step(near if up else near - size, size, side, masked)
            return carry

        lax.fori_loop(0, times, one, 0)
        return at + sign * times * size

    at = run(edge, sign * (plain - edge) // 8, 8, False)
    left = sign * (low - at)
    tail = lax.rem(left, 8)
    more = tail > (6 if fine else 4)
    at = run(at, left // 8 + more.astype(jnp.int32), 8, True)
    tail = jnp.where(more, 0, tail)
    four = tail > (2 if fine else 0)
    at = run(at, four.astype(jnp.int32), 4, True)
    if fine:
        run(at, (tail - jnp.where(four, 4, 0) > 0).astype(jnp.int32), 2, True)


def far_sweep(plan, block, step, before, after, fine):
    low, plain_low, plain_high, high = [plan[block, i] for i in range(4)]
    start, stop = PER * block - 1, PER * block + PER + 1
    far_windows(low, plain_low, start, step, before, False, fine)
    far_windows(high, plain_high, stop, step, after, True, fine)


def has_far(plan, block):
    return (plan[block, 0] < PER * block - 1) | (plan[block, 3] > PER * block + PER + 1)


def segment_rows(ends, lengths, place, total):
    slots = ends.shape[0]
    before = ends <= jnp.broadcast_to(place, (slots, place.shape[1]))
    seg = jnp.sum(before.astype(jnp.int32), axis=0, keepdims=True)
    first = jnp.sum(jnp.where(before, lengths, 0), axis=0, keepdims=True)
    stop = jnp.min(jnp.where(before, total, ends), axis=0, keepdims=True)
    return seg, first, stop


def block_plan(ends, ends_row, total):
    slots = ends.shape[0]
    blocks, units = total // BLK, total // UNIT

    def along(place):
        return jnp.sum((ends <= jnp.broadcast_to(place, (slots, 128))).astype(jnp.int32), axis=0, keepdims=True)

    def down(place):
        return jnp.sum((jnp.broadcast_to(ends_row, (blocks, slots)) <= place).astype(F32), axis=1, keepdims=True).astype(jnp.int32)

    unit = iota((1, 128), 1)
    u_first, u_last = along(unit * UNIT), along(unit * UNIT + UNIT - 1)
    b = iota((blocks, 1), 0)
    first, last = down(b * BLK), down(b * BLK + BLK - 1)
    start, stop = PER * b - 1, PER * b + PER + 1
    inside = unit < units

    def count(hit):
        return jnp.sum((hit & inside).astype(F32), axis=1, keepdims=True).astype(jnp.int32)

    low = jnp.minimum(count(u_last < first), start)
    high = jnp.maximum(units - count(u_first > last), stop)
    plain_low = start - count((unit < start) & (u_first == last))
    plain_high = stop + count((unit >= stop) & (u_last == first))
    lane = iota((blocks, 128), 1)
    out = jnp.zeros((blocks, 128), jnp.int32)
    for i, v in enumerate((low, plain_low, plain_high, high)):
        out = jnp.where(lane == i, v, out)
    return out


def meets(first_key, rows, bounds):
    key = iota((rows, bounds.shape[1]), 0)
    return (key >= bounds[0:1, :] - first_key) & (key < bounds[1:2, :] - first_key)


def fwd_kernel(plan, qkv_ref, table_ref, bound_ref, o_ref, of_ref, lse_ref, qaug, kn, vt, tile, top_ref, acc, *, head_width):
    chunks, packed_rows, rows = qkv_ref.shape
    total = chunks * rows
    blocks = total // BLK
    span = table_ref.shape[1]
    table = pick_row(table_ref, lax.axis_index("head"))
    far = (table[:, :1] * LOG2E, table[:, span - 1 :] * LOG2E)
    pick = spread_cols(packed_rows, 3, SLOT, head_width)
    scale = LOG2E / math.sqrt(head_width)
    o_ref[:, :UNIT] = jnp.zeros((SLOT, UNIT), BF)
    o_ref[:, UNIT + total :] = jnp.zeros((SLOT, UNIT), BF)
    for edge in (slice(0, PAD), slice(PAD + total, 2 * PAD + total)):
        kn[edge, :] = jnp.zeros((PAD, DEPTH), BF)
        vt[:, edge] = jnp.zeros((SLOT, PAD), BF)
    bias_near(table, tile, True)
    rest = DEPTH - 2 * SLOT

    @pl.loop(0, chunks)
    def _(c):
        at = pl.ds(pl.multiple_of(c * rows, rows), rows)
        at_pad = pl.ds(pl.multiple_of(c * rows + PAD, UNIT), rows)
        parts = dot(pick, qkv_ref[c])
        q = parts[:SLOT] * scale
        hi = q.astype(BF)
        lo = (q - hi.astype(F32)).astype(BF)
        for s in range(3):
            qaug[s, :SLOT, at] = hi
            qaug[s, SLOT : 2 * SLOT, at] = lo
            qaug[s, 2 * SLOT :, at] = jnp.zeros((rest, rows), BF)
        k = parts[SLOT : 2 * SLOT]
        one3 = (iota((rest, rows), 0) < 3).astype(F32)
        kn[at_pad, :] = jnp.concatenate([k, k, one3], axis=0).T.astype(BF)
        one = (iota((SLOT, rows), 0) == head_width).astype(F32)
        vt[:, at_pad] = (parts[2 * SLOT :] + one).astype(BF)

    def top(x):
        return jnp.max(x.reshape(x.shape[0] // 8, 8, BLK), axis=0)

    @pl.loop(0, blocks // 2)
    def _(pair):
        for i in range(2):
            b = 2 * pair + i
            at_q = units_at(PER * b, PER)
            near = units_at(PER * b - 1 + PAD // UNIT, NEAR)
            x = dot(kn[near, :], qaug[1, :, at_q]) + tile[...]
            x = jnp.where(meets(PER * b * UNIT - UNIT, NEAR * UNIT, bound_ref[:, units_at(PER * b + PAD // UNIT, PER)]), x, MASKED)
            m = jnp.max(top(x), axis=0, keepdims=True)
            acc[:, at_q] = dot(vt[:, near], jnp.exp2(x - m).astype(BF))
            lse_ref[:, at_q] = m
            qaug[0, 2 * SLOT :, at_q] = three_rows(far[0] - m, rest).astype(BF)
            qaug[2, 2 * SLOT :, at_q] = three_rows(far[1] - m, rest).astype(BF)

    @pl.loop(0, blocks)
    def _(b):
        @pl.when(has_far(plan, b))
        def _():
            at_q = units_at(PER * b, PER)

            def scores(u, count, side, masked):
                x = dot(kn[units_at(u + PAD // UNIT, count), :], qaug[side, :, at_q])
                if masked:
                    x = jnp.where(meets(u * UNIT, count * UNIT, bound_ref[:, units_at(PER * b + PAD // UNIT, PER)]), x, MASKED)
                return x

            near_acc = acc[:, at_q]

            def add(u, count, side, masked):
                p = jnp.exp2(scores(u, count, side, masked)).astype(BF)
                acc[:, at_q] += dot(vt[:, units_at(u + PAD // UNIT, count)], p)

            far_sweep(plan, b, add, 0, 2, False)
            sums = acc[head_width : head_width + 1, at_q]
            over = jnp.max(jnp.where(sums < 2.0**60, 0.0, 1.0))

            @pl.when(over > 0.5)
            def _():
                top_ref[...] = jnp.zeros_like(top_ref)

                def first(u, count, side, masked):
                    top_ref[...] = jnp.maximum(top_ref[...], top(scores(u, count, side, masked)))

                far_sweep(plan, b, first, 0, 2, False)
                m = jnp.max(top_ref[...], axis=0, keepdims=True)
                acc[:, at_q] = near_acc * jnp.exp2(-m)
                lse_ref[:, at_q] += m

                def second(u, count, side, masked):
                    p = jnp.exp2(scores(u, count, side, masked) - m).astype(BF)
                    acc[:, at_q] += dot(vt[:, units_at(u + PAD // UNIT, count)], p)

                far_sweep(plan, b, second, 0, 2, False)

    @pl.loop(0, chunks)
    def _(c):
        at = pl.ds(pl.multiple_of(c * rows, rows), rows)
        total_p = acc[head_width : head_width + 1, at]
        out = acc[:, at] / total_p
        o_ref[:, pl.ds(pl.multiple_of(c * rows + UNIT, UNIT), rows)] = out.astype(BF)
        of_ref[:, at] = out[: of_ref.shape[0]]
        lse_ref[:, at] = lse_ref[:, at] + jnp.log2(total_p)


def attend_forward(qkv, bounds, plan, table, head_width):
    chunks, packed_rows, rows = qkv.shape
    total = chunks * rows
    vm = pltpu.VMEM
    return pl.pallas_call(
        functools.partial(fwd_kernel, head_width=head_width),
        out_shape=(
            jax.ShapeDtypeStruct((SLOT, total + 2 * UNIT), BF),
            jax.ShapeDtypeStruct((40, total), F32),
            jax.ShapeDtypeStruct((1, total), F32),
        ),
        in_specs=[pl.BlockSpec(memory_space=pltpu.SMEM)] + [pl.BlockSpec()] * 3,
        scratch_shapes=[
            vm((3, DEPTH, total), BF),
            vm((total + 2 * PAD, DEPTH), BF),
            vm((SLOT, total + 2 * PAD), BF),
            vm((NEAR * UNIT, BLK), F32),
            vm((8, BLK), F32),
            vm((SLOT, total), F32),
        ],
        compiler_params=pltpu.CompilerParams(vmem_limit_bytes=62 * 2**20),
        name="attend_forward",
    )(plan, qkv, table, bounds)


def bwd_kernel(plan, qkv_ref, do_ref, of_ref, lse_ref, table_ref, bound_ref, dqkv_ref, dtab_ref,
               qaug, kn, kt, vn, dot_t, qn, don, tile, dq, band, ends, dv_acc, dk_acc, dwide, *, head_width):
    chunks, packed_rows, rows = qkv_ref.shape
    total = chunks * rows
    blocks = total // BLK
    span = table_ref.shape[1]
    table = pick_row(table_ref, lax.axis_index("head"))
    pick = spread_cols(packed_rows, 3, SLOT, head_width)
    scale = LOG2E / math.sqrt(head_width)
    back = 1.0 / math.sqrt(head_width)
    rest = DEPTH - 2 * SLOT
    bias_near(table, tile, False)
    for edge in (slice(0, PAD), slice(PAD + total, 2 * PAD + total)):
        for s in range(3):
            qaug[s, :, edge] = jnp.zeros((DEPTH, PAD), BF)
        dot_t[:, edge] = jnp.zeros((DEPTH, PAD), BF)
        qn[edge, :] = jnp.zeros((PAD, DEPTH), BF)
        don[edge, :] = jnp.zeros((PAD, DEPTH), BF)

    @pl.loop(0, chunks)
    def _(c):
        at = pl.ds(pl.multiple_of(c * rows, rows), rows)
        at_pad = pl.ds(pl.multiple_of(c * rows + PAD, UNIT), rows)
        parts = dot(pick, qkv_ref[c])
        q, k, v = parts[:SLOT], parts[SLOT : 2 * SLOT], parts[2 * SLOT :]
        qs = q * scale
        hi = qs.astype(BF)
        lo = (qs - hi.astype(F32)).astype(BF)
        lse = lse_ref[:, at]
        for s, shift in enumerate((table[:, :1] * LOG2E, 0.0, table[:, span - 1 :] * LOG2E)):
            qaug[s, :SLOT, at_pad] = hi
            qaug[s, SLOT : 2 * SLOT, at_pad] = lo
            qaug[s, 2 * SLOT :, at_pad] = three_rows(shift - lse, rest).astype(BF)
        one3 = (iota((rest, rows), 0) < 3).astype(F32)
        row48 = iota((SLOT, rows), 0)
        none = jnp.zeros((rest, rows), F32)
        empty = jnp.zeros((SLOT, rows), F32)
        kn[at, :] = jnp.concatenate([k, k, one3], axis=0).T.astype(BF)
        kt[:, at] = k.astype(BF)
        vn[at, :] = jnp.concatenate([v, empty, one3], axis=0).T.astype(BF)
        do = do_ref[c].astype(F32)
        centre = jnp.sum(do[: of_ref.shape[0]] * of_ref[:, at], axis=0, keepdims=True)
        dot_t[:SLOT, at_pad] = do_ref[c]
        dot_t[SLOT : 2 * SLOT, at_pad] = empty.astype(BF)
        dot_t[2 * SLOT :, at_pad] = three_rows(-centre, rest).astype(BF)
        qn[at_pad, :] = jnp.concatenate([q + (row48 == head_width).astype(F32), empty, none], axis=0).T.astype(BF)
        don[at_pad, :] = jnp.concatenate([do, empty, none], axis=0).T.astype(BF)

    dq[...] = jnp.zeros_like(dq)
    band[...] = jnp.zeros_like(band)
    ends[...] = jnp.zeros_like(ends)

    @pl.loop(0, blocks // 2)
    def _(pair):
        width = NEAR * UNIT
        wide = width + BLK
        whole, lines = [], []
        for i in range(2):
            b = 2 * pair + i
            at_k = units_at(PER * b, PER)
            near = units_at(PER * b - 1 + PAD // UNIT, NEAR)
            p = jnp.exp2(dot(kn[at_k, :], qaug[1, :, near]) + tile[...])
            p = jnp.where(meets(b * BLK, BLK, bound_ref[:, near]), p, 0.0)
            dsb = (p * dot(vn[at_k, :], dot_t[:, near])).astype(BF)
            dv_acc[at_k, :] = dot(p.astype(BF), don[near, :])
            dk_acc[at_k, :] = dot(dsb, qn[near, :])
            part = dot(kt[:, at_k], dsb)
            gap = jnp.zeros((SLOT, BLK), F32)
            whole.append(jnp.concatenate([gap, part] if i else [part, gap], axis=1))
            lines.append(dsb.astype(F32))
        dq[:, units_at(2 * PER * pair - 1 + PAD // UNIT, wide // UNIT)] += whole[0] + whole[1]
        band[...] += lines[0] + lines[1]

    @pl.loop(0, blocks)
    def _(b):
        @pl.when(has_far(plan, b))
        def _():
            at_k = units_at(PER * b, PER)

            def far(u, count, side, masked):
                at_q = units_at(u + PAD // UNIT, count)
                p = jnp.exp2(dot(kn[at_k, :], qaug[side, :, at_q]))
                if masked:
                    p = jnp.where(meets(b * BLK, BLK, bound_ref[:, at_q]), p, 0.0)
                dsb = (p * dot(vn[at_k, :], dot_t[:, at_q])).astype(BF)
                dq[:, at_q] += dot(kt[:, at_k], dsb)
                dv_acc[at_k, :] += dot(p.astype(BF), don[at_q, :])
                dk = dot(dsb, qn[at_q, :])
                dk_acc[at_k, :] += dk
                ends[side // 2] += jnp.sum(dk.reshape(BLK // 8, 8, DEPTH), axis=0)

            far_sweep(plan, b, far, 2, 0, True)

    @pl.loop(0, chunks)
    def _(c):
        at = pl.ds(pl.multiple_of(c * rows, rows), rows)
        at_pad = pl.ds(pl.multiple_of(c * rows + PAD, UNIT), rows)
        dwide[:SLOT, :] = (dq[:, at_pad] * back).astype(BF)
        dwide[SLOT : 2 * SLOT, :] = (dk_acc[at, :].T[:SLOT] * back).astype(BF)
        dwide[2 * SLOT :, :] = dv_acc[at, :].T[:SLOT].astype(BF)
        dqkv_ref[c] = dot(pick, dwide[...], TN).astype(BF)

    flip = (iota((UNIT, UNIT), 0) + iota((UNIT, UNIT), 1) == UNIT - 1).astype(F32)
    half = span // 2
    lane = iota((8, span), 1)
    column = iota((8, DEPTH), 1) == head_width
    out = jnp.zeros((8, span), F32)
    far_sum = [jnp.where(column, ends[i], 0.0) for i in range(2)]
    for d in range(-PER, PER + 1):
        part = jnp.zeros((UNIT, UNIT), F32)
        for r in range(PER):
            c = r + d + 1
            if 0 <= c < NEAR:
                part = part + band[r * UNIT : (r + 1) * UNIT, c * UNIT : (c + 1) * UNIT]
        if abs(d) > 1:
            far_sum[0 if d > 0 else 1] += jnp.sum(part.reshape(UNIT // 8, 8, UNIT), axis=0)
            continue
        turned = lax.dot_general(flip, part, NN, precision=lax.Precision.HIGHEST, preferred_element_type=F32)
        wide = jnp.concatenate([turned, jnp.zeros_like(turned)], axis=1)
        skewed = pltpu.roll(wide, 0, 1, stride=1, stride_axis=0)
        line = jnp.sum(skewed.reshape(UNIT // 8, 8, 2 * UNIT), axis=0)
        offset = UNIT - 1 - d * UNIT - iota((span, 2 * UNIT), 1)
        hot = (jnp.clip(offset, -half, half - 1) + half == iota((span, 2 * UNIT), 0)).astype(F32)
        out += lax.dot_general(line, hot, NT, precision=lax.Precision.HIGHEST, preferred_element_type=F32)
    out += jnp.where(lane == 0, jnp.sum(far_sum[0], axis=1, keepdims=True), 0.0)
    out += jnp.where(lane == span - 1, jnp.sum(far_sum[1], axis=1, keepdims=True), 0.0)
    out = jnp.sum(out, axis=0, keepdims=True)
    dtab_ref[...] = out


def attend_backward(qkv, do, of, lse, bounds, plan, table, head_width):
    chunks, packed_rows, rows = qkv.shape
    total = chunks * rows
    padded = total + 2 * PAD
    span = table.shape[1]
    vm = pltpu.VMEM
    return pl.pallas_call(
        functools.partial(bwd_kernel, head_width=head_width),
        out_shape=(
            jax.ShapeDtypeStruct((chunks, packed_rows, rows), BF),
            jax.ShapeDtypeStruct((1, span), F32),
        ),
        in_specs=[pl.BlockSpec(memory_space=pltpu.SMEM)] + [pl.BlockSpec()] * 6,
        scratch_shapes=[
            vm((3, DEPTH, padded), BF),
            vm((total, DEPTH), BF),
            vm((SLOT, total), BF),
            vm((total, DEPTH), BF),
            vm((DEPTH, padded), BF),
            vm((padded, DEPTH), BF),
            vm((padded, DEPTH), BF),
            vm((BLK, NEAR * UNIT), F32),
            vm((SLOT, padded), F32),
            vm((BLK, NEAR * UNIT), F32),
            vm((2, 8, DEPTH), F32),
            vm((total, DEPTH), F32),
            vm((total, DEPTH), F32),
            vm((3 * SLOT, rows), BF),
        ],
        compiler_params=pltpu.CompilerParams(vmem_limit_bytes=62 * 2**20),
        name="attend_backward",
    )(plan, qkv, do, of, lse, table, bounds)

VEC = types.SimpleNamespace(
    first_gain=0, first_shift=1, first_up_bias=2, first_down_bias=3, mix_gain=4, mix_shift=5, mix_output_bias=6, filter_gain=7,
    filter_shift=8, pointwise_in_bias=9, batch_gain=10, batch_shift=11, pointwise_out_bias=12, second_gain=13, second_shift=14,
    second_up_bias=15, second_down_bias=16, final_gain=17, final_shift=18,
)
VEC_ROWS = 24
EPSILON = 1e-05
HALO = 64
TILE = 128
PIECE = 256


def col(cols_ref, i, size):
    return cols_ref[:size, i : i + 1]


def eye(n):
    return (iota((n, n), 0) == iota((n, n), 1)).astype(F32).astype(BF)


def flipped(mat):
    return dot(eye(mat.shape[1]), mat, NT).astype(BF)


def exact(a, b, dims=NN):
    return lax.dot_general(a, b, dims, precision=lax.Precision.HIGHEST, preferred_element_type=F32)


def folded(values):
    part = values[:, :TILE]
    for at in range(TILE, values.shape[1], TILE):
        part = part + values[:, at : at + TILE]
    return part


def row_sums(values):
    return exact(jnp.ones((8, TILE), F32), values, NT)


def norm(x):
    m = jnp.mean(x, axis=0, keepdims=True)
    c = x - m
    inv = lax.rsqrt(jnp.mean(c * c, axis=0, keepdims=True) + EPSILON)
    return c * inv, inv


def norm_back(e, n, inv, gain):
    ea = e * gain
    return inv * (ea - jnp.mean(ea, axis=0, keepdims=True) - n * jnp.mean(ea * n, axis=0, keepdims=True))


def sigmoid(v):
    return 0.5 + 0.5 * jnp.tanh(0.5 * v)


def ones_row(rows, lanes):
    return (iota((rows, lanes), 0) == 0).astype(F32).astype(BF)


def open_rows(frames_ref, up_ref, down_ref, mix_ref, x1_ref, h2_ref, qkv_ref, cols_ref, packed_rows, ship):
    width, rows = frames_ref.shape
    hidden = up_ref.shape[1]
    heads = qkv_ref.shape[0]
    up_t = flipped(up_ref[...])
    mix_t = dot(spread_cols(mix_ref.shape[1], heads, packed_rows, mix_ref.shape[1] // heads), mix_ref[...], NT).astype(BF)

    @pl.loop(0, rows // PIECE)
    def _(c):
        at = pl.ds(pl.multiple_of(c * PIECE, PIECE), PIECE)
        x0 = frames_ref[:, at].astype(F32)
        n, _ = norm(x0)
        h1 = (n * col(cols_ref, VEC.first_gain, width) + col(cols_ref, VEC.first_shift, width)).astype(BF)
        a1 = dot(up_t, h1) + col(cols_ref, VEC.first_up_bias, hidden)
        s1 = (a1 * sigmoid(a1)).astype(BF)
        x1 = x0 + 0.5 * (dot(down_ref[...], s1) + col(cols_ref, VEC.first_down_bias, width))
        x1_ref[:, at] = x1
        n, _ = norm(x1)
        h2 = (n * col(cols_ref, VEC.mix_gain, width) + col(cols_ref, VEC.mix_shift, width)).astype(BF)
        h2_ref[:, at] = h2
        qkv = dot(mix_t, h2).astype(BF)
        for h in range(heads):
            qkv_ref[h, :, at] = qkv[h * packed_rows : (h + 1) * packed_rows]
        ship(c)


def open_segments(len_ref, bound_ref, plan_ref, ext_ref, line):
    rows = ext_ref.shape[1] - TILE
    group = bound_ref.shape[1] - 2 * PAD
    slots = len_ref.shape[1]
    lengths = jnp.broadcast_to(len_ref[...].astype(F32), (8, slots))
    row, column = iota((slots, slots), 0), iota((slots, slots), 1)
    ends = exact((column <= row).astype(F32), lengths, NT)[:, :1].astype(jnp.int32)
    own_len = exact((column == row).astype(F32), lengths, NT)[:, :1].astype(jnp.int32)
    ends_row = exact(lengths, (row <= column).astype(F32))[:1].astype(jnp.int32)
    plan_ref[...] = block_plan(ends, ends_row, group)
    line[...] = jnp.full_like(line, -1)
    for edge in (slice(0, PAD), slice(PAD + group, 2 * PAD + group)):
        bound_ref[:, edge] = jnp.where(iota((2, PAD), 0) == 0, 1 << 20, -1)

    @pl.loop(0, group // 512)
    def _(c):
        at = pl.multiple_of(c * 512, 512)
        seg, first, stop = segment_rows(ends, own_len, iota((1, 512), 1) + at, group)
        line[:, pl.ds(at + TILE, 512)] = seg
        bound_ref[0:1, pl.ds(at + PAD, 512)] = first
        bound_ref[1:2, pl.ds(at + PAD, 512)] = stop

    first = pl.multiple_of(lax.axis_index("head") * rows, TILE)
    ext_ref[:, :rows] = line[:, pl.ds(first + TILE, rows)]
    left = line[:, pl.ds(first, TILE)]
    right = line[:, pl.ds(first + TILE + rows, TILE)]
    ext_ref[:, rows:] = jnp.where(iota((1, TILE), 1) < HALO, right, left)


def conv_masks(mask_ref, ext_ref, taps, sign):
    seg = jnp.broadcast_to(ext_ref[...], (8, ext_ref.shape[1]))
    lanes = seg.shape[1]
    for k in range(taps):
        other = pltpu.roll(seg, (sign * (taps // 2 - k)) % lanes, 1)
        mask_ref[k] = (other == seg).astype(F32)


def filter_kernel(x1_ref, x1l_ref, x1r_ref, o_ref, cols_ref, ext_ref, out_ref, pw_ref, taps_ref,
                  x2_ref, oc_ref, u_ref, y_ref, stat_ref, wide, mask, live_ref, *, head_width, slot_count, arrive):
    width, rows = x1_ref.shape
    lanes = rows + TILE
    heads = o_ref.shape[0]
    taps = taps_ref.shape[0]
    out_t = flipped(out_ref[...])
    pw_t = flipped(pw_ref[...])
    gather = spread_cols(width, heads, SLOT, head_width)
    seg = ext_ref[...]
    live = (seg >= 0) & (seg < slot_count)
    live_ref[...] = live.astype(F32)
    conv_masks(mask, ext_ref, taps, 1)
    wide_taps = taps_ref[...].astype(F32).T
    arrive()

    near = iota((1, TILE), 1) < HALO

    def extended(own, left, right):
        edge = jnp.where(near, right.astype(F32), left.astype(F32)).astype(own.dtype)
        return jnp.concatenate([own, edge], axis=1)

    x1 = extended(x1_ref[...], x1l_ref[...], x1r_ref[...])
    o = jnp.concatenate(
        [extended(o_ref[h, :, TILE : TILE + rows], o_ref[h, :, :TILE], o_ref[h, :, TILE + rows :]) for h in range(heads)], axis=0)
    oc = dot(gather, o, TN).astype(BF)
    x2 = x1 + (dot(out_t, oc) + col(cols_ref, VEC.mix_output_bias, width))
    n, _ = norm(x2)
    h3 = (n * col(cols_ref, VEC.filter_gain, width) + col(cols_ref, VEC.filter_shift, width)).astype(BF)
    g = dot(pw_t, h3) + col(cols_ref, VEC.pointwise_in_bias, 2 * width)
    u = jnp.where(live_ref[...] > 0.5, g[:width] * sigmoid(g[width:]), 0.0).astype(BF)
    oc_ref[...] = oc[:, :rows]
    x2_ref[...] = x2
    u_ref[...] = u
    wide[...] = u.astype(F32)

    own = (live & (iota((1, lanes), 1) < rows)).astype(F32)
    count = jnp.sum(own, axis=1, keepdims=True)
    safe = jnp.maximum(count, 1.0)
    for r in range(width // 8):
        sl = slice(8 * r, 8 * r + 8)
        u8 = wide[sl, :]
        acc = jnp.zeros((8, lanes), F32)
        for k in range(taps):
            moved = pltpu.roll(u8, (taps // 2 - k) % lanes, 1)
            acc = acc + wide_taps[sl, k : k + 1] * (moved * mask[k])
        y_ref[sl, :] = acc
    y = y_ref[...]
    part = folded(y * own)
    mean = exact(part, jnp.ones((TILE, TILE), F32)) / safe
    dev = (y - jnp.concatenate([mean] * (lanes // TILE), axis=1)) * own
    stat_ref[...] = two_rows(row_sums(part)[:1] / safe, row_sums(folded(dev * dev))[:1], count)


def two_rows(a, b, extra):
    rest = a.shape[1] - TILE
    tail = pad_lanes(jnp.concatenate([a[:, TILE:], b[:, TILE:]], axis=0))
    spot = (iota((2, TILE), 0) == 0) & (iota((2, TILE), 1) == rest)
    return jnp.concatenate([a[:, :TILE], b[:, :TILE], jnp.where(spot, extra, tail)], axis=0)


def all_rows(ref, width):
    rest = width - TILE
    values = ref[...]
    a = jnp.concatenate([values[:, 0, :], values[:, 2, :rest]], axis=1)
    b = jnp.concatenate([values[:, 1, :], values[:, 3, :rest]], axis=1)
    return a, b, values[:, 2, rest : rest + 1]


def total_stats(stats_ref, width):
    mean_of, spread_of, n = all_rows(stats_ref, width)
    count = jnp.sum(n, axis=0, keepdims=True)
    mean = jnp.sum(n * mean_of, axis=0, keepdims=True) / count
    gap = mean_of - mean
    spread = jnp.sum(spread_of + n * gap * gap, axis=0, keepdims=True)
    inv = lax.rsqrt(spread / count + EPSILON)
    table = jnp.concatenate([mean, inv, jnp.broadcast_to(count, (1, width)), jnp.zeros((5, width), F32)], axis=0).T
    return table[:, 0:1], table[:, 1:2], table[:, 2:3]


def second_kernel(x2_ref, y_ref, stats_ref, cot_ref, cotl_ref, cotr_ref, cols_ref, pwo_ref, up_ref, down_ref,
                  out_ref, dx3_ref, e_ref, sums_ref, pack_ref, small_ref,
                  h4s, das, s4s, dfs, ws, dcs, *, arrive, leave):
    width, rows = out_ref.shape
    hidden = up_ref.shape[1]
    pwo_t = flipped(pwo_ref[...])
    up_t = flipped(up_ref[...])
    down = flipped(down_ref[...])
    arrive()
    mean, inv_b, _ = total_stats(stats_ref, width)
    bgain = col(cols_ref, VEC.batch_gain, width)

    near = iota((1, TILE), 1) < HALO
    edge = jnp.where(near, cotr_ref[...].astype(F32), cotl_ref[...].astype(F32))
    cot = jnp.concatenate([cot_ref[...].astype(F32), edge], axis=1)
    zh = (y_ref[...] - mean) * inv_b
    z = zh * bgain + col(cols_ref, VEC.batch_shift, width)
    sig_z = sigmoid(z)
    w = (z * sig_z).astype(BF)
    x3 = x2_ref[...] + (dot(pwo_t, w) + col(cols_ref, VEC.pointwise_out_bias, width))
    n4, inv4 = norm(x3)
    h4 = (n4 * col(cols_ref, VEC.second_gain, width) + col(cols_ref, VEC.second_shift, width)).astype(BF)
    a4 = dot(up_t, h4) + col(cols_ref, VEC.second_up_bias, hidden)
    sig = sigmoid(a4)
    s4 = (a4 * sig).astype(BF)
    x4 = x3 + 0.5 * (dot(down_ref[...], s4) + col(cols_ref, VEC.second_down_bias, width))
    nf, invf = norm(x4)
    fgain = col(cols_ref, VEC.final_gain, width)
    dx4 = norm_back(cot, nf, invf, fgain)
    df = (0.5 * dx4).astype(BF)
    da = (dot(down, df) * (sig * (1.0 + a4 * (1.0 - sig)))).astype(BF)
    dh = dot(up_ref[...], da)
    dx3 = dx4 + norm_back(dh, n4, inv4, col(cols_ref, VEC.second_gain, width))
    dc = dx3.astype(BF)
    dz = dot(pwo_ref[...], dc) * (sig_z * (1.0 + z * (1.0 - sig_z)))
    e = dz * bgain
    e_ref[...] = e
    sums_ref[...] = two_rows(row_sums(folded(e[:, :rows]))[:1], row_sums(folded((e * zh)[:, :rows]))[:1], 0.0)
    leave()

    out_ref[...] = (nf * fgain + col(cols_ref, VEC.final_shift, width))[:, :rows].astype(BF)
    dx3_ref[...] = dx3[:, :rows]
    h4s[...] = h4[:, :rows]
    das[...] = da[:, :rows]
    s4s[:hidden, :] = s4[:, :rows]
    dfs[...] = df[:, :rows]
    ws[:width, :] = w[:, :rows]
    dcs[...] = dc[:, :rows]
    totals = [row_sums(folded(v[:, :rows]))[:1] for v in (dh * n4, dh, cot * nf, cot, dz * zh, dz)]
    s4s[hidden:, :] = ones_row(16, rows)
    ws[width:, :] = ones_row(16, rows)
    up_grad = dot(h4s[...], das[...], NT)
    up_bias = dot(ones_row(16, rows), das[...], NT)
    down_grad = dot(dfs[...], s4s[...], NT)
    pw_grad = dot(ws[...], dcs[...], NT)
    down_bias = exact(jnp.ones((8, rows), F32), dfs[...].astype(F32), NT)
    put_ff(pack_ref, up_grad, down_grad, 0)
    tall = 9 * width
    pack_ref[tall : tall + width, :] = pw_grad[:width, :TILE].astype(BF)
    pack_ref[tall + width : tall + 2 * width, :] = pad_lanes(pw_grad[:width, TILE:]).astype(BF)
    small_ref[...] = stack_rows(
        [totals[0], totals[1], up_bias[:1], down_bias[:1], totals[2], totals[3], totals[4], totals[5], pw_grad[width : width + 1]],
        small_ref.shape)


def pad_lanes(mat, lanes=TILE):
    if mat.shape[1] == lanes:
        return mat
    return jnp.concatenate([mat, jnp.zeros((mat.shape[0], lanes - mat.shape[1]), mat.dtype)], axis=1)


def stack_rows(rows, shape):
    parts = [pad_lanes(r, shape[1]) for r in rows]
    parts.append(jnp.zeros((shape[0] - len(rows), shape[1]), F32))
    return jnp.concatenate(parts, axis=0)


def put_ff(pack_ref, up_grad, down_grad_t, at):
    width, hidden = up_grad.shape
    whole = hidden // TILE
    for i in range(whole):
        pack_ref[at + i * width : at + (i + 1) * width, :] = up_grad[:, i * TILE : (i + 1) * TILE].astype(BF)
        j = whole + i
        pack_ref[at + j * width : at + (j + 1) * width, :] = down_grad_t[:, i * TILE : (i + 1) * TILE].astype(BF)
    rest = jnp.concatenate([up_grad[:, whole * TILE : hidden], down_grad_t[:, whole * TILE : hidden]], axis=1)
    pack_ref[at + 2 * whole * width : at + (2 * whole + 1) * width, :] = rest.astype(BF)


def unfilter_kernel(e_ref, y_ref, stats_ref, sums_ref, u_ref, dx3_ref, x2_ref, oc_ref, cols_ref, ext_ref, pw_ref, taps_ref,
                    out_ref, dx2_ref, do_ref, pack_ref, small_ref, tapg_ref,
                    dyw, du_s, mask, prod, h3s, dgs, dms, ocs, gains, live_ref, *, head_width, slot_count, ship, arrive):
    width, rows = dx3_ref.shape
    lanes = rows + TILE
    heads = do_ref.shape[0]
    taps = taps_ref.shape[0]
    conv_masks(mask, ext_ref, taps, -1)
    tap_cols = taps_ref[...].astype(F32).T
    pw_t = flipped(pw_ref[...])
    out_w = dot(spread_cols(width, heads, SLOT, head_width), out_ref[...]).astype(BF)
    gains[...] = jnp.zeros_like(gains)
    fgain = col(cols_ref, VEC.filter_gain, width)
    mean, inv_b, count = total_stats(stats_ref, width)
    arrive()
    one_of, two_of, _ = all_rows(sums_ref, width)
    sums = jnp.concatenate([jnp.sum(one_of, axis=0, keepdims=True), jnp.sum(two_of, axis=0, keepdims=True), jnp.zeros((6, width), F32)], axis=0).T
    s1, s2 = sums[:, 0:1], sums[:, 1:2]
    seg = ext_ref[...]
    live = ((seg >= 0) & (seg < slot_count)).astype(F32)

    live_ref[...] = live

    zh = (y_ref[...] - mean) * inv_b
    dy = inv_b * (e_ref[...] - live * ((s1 + zh * s2) / count))
    dyw[...] = jnp.where(seg >= 0, dy, 0.0).astype(BF).astype(F32)

    for r in range(width // 8):
        sl = slice(8 * r, 8 * r + 8)
        dy8 = dyw[sl, :]
        u8 = u_ref[16 * (r // 2) : 16 * (r // 2) + 16, :rows].astype(F32)[8 * (r % 2) : 8 * (r % 2) + 8]
        acc = jnp.zeros((8, rows), F32)
        for k in range(taps):
            moved = pltpu.roll(dy8, (k - taps // 2) % lanes, 1)[:, :rows] * mask[k][:, :rows]
            acc = acc + tap_cols[sl, k : k + 1] * moved
            hit = moved * u8
            prod[k, sl, :] = folded(hit)
        du_s[sl, :] = acc

    whole = prod[...].reshape(taps * width, TILE)
    hi = whole.astype(BF)
    lo = (whole - hi.astype(F32)).astype(BF)
    ones = jnp.ones((8, TILE), BF)
    lines = dot(ones, hi, NT) + dot(ones, lo, NT)
    for k in range(taps):
        tapg_ref[k : k + 1, :] = lines[:1, k * width : (k + 1) * width]

    @pl.loop(0, rows // PIECE)
    def _(c):
        at = pl.ds(pl.multiple_of(c * PIECE, PIECE), PIECE)
        x2 = x2_ref[:, at]
        n, inv = norm(x2)
        h3 = (n * fgain + col(cols_ref, VEC.filter_shift, width)).astype(BF)
        g = dot(pw_t, h3) + col(cols_ref, VEC.pointwise_in_bias, 2 * width)
        sig = sigmoid(g[width:])
        t = live_ref[:, at] * du_s[:, at] * sig
        dg = jnp.concatenate([t, t * g[:width] * (1.0 - sig)], axis=0).astype(BF)
        dh = dot(pw_ref[...], dg)
        dx2 = dx3_ref[:, at] + norm_back(dh, n, inv, fgain)
        dx2_ref[:, at] = dx2
        dm = dx2.astype(BF)
        do = dot(out_w, dm).astype(BF)
        for h in range(heads):
            do_ref[h, :, at] = do[h * SLOT : (h + 1) * SLOT]
        ship(c)
        h3s[:width, at] = h3
        dgs[:, at] = dg
        dms[:, at] = dm
        ocs[:width, at] = oc_ref[:, at]
        for i, v in enumerate((dh * n, dh)):
            gains[i] += folded(v)

    h3s[width:, :] = ones_row(16, rows)
    ocs[width:, :] = ones_row(16, rows)
    pw_grad = dot(h3s[...], dgs[...], NT)
    out_grad = dot(ocs[...], dms[...], NT)
    at = 0
    for lo in range(0, 2 * width, TILE):
        pack_ref[at : at + width, :] = pad_lanes(pw_grad[:width, lo : min(lo + TILE, 2 * width)]).astype(BF)
        at += width
    for lo in range(0, width, TILE):
        pack_ref[at : at + width, :] = pad_lanes(out_grad[:width, lo : min(lo + TILE, width)]).astype(BF)
        at += width
    small_ref[...] = stack_rows(
        [row_sums(gains[0])[:1], row_sums(gains[1])[:1], pw_grad[width : width + 1], out_grad[width : width + 1]], small_ref.shape)


def close_kernel(frames_ref, x1_ref, h2_ref, dx2_ref, dqkv_ref, dtab_ref, cols_ref, up_ref, down_ref, mix_ref,
                 grad_ref, pack_ref, h1s, das, s1s, dfs, dqs, gains, *, arrive, between, mixed):
    width, rows = frames_ref.shape
    hidden = up_ref.shape[1]
    heads, packed_rows, _ = dqkv_ref.shape
    up_t = flipped(up_ref[...])
    down = flipped(down_ref[...])
    hot = spread_cols(mix_ref.shape[1], heads, packed_rows, mix_ref.shape[1] // heads)
    mix_w = dot(mix_ref[...], hot, NT).astype(BF)
    gains[...] = jnp.zeros_like(gains)
    mgain = col(cols_ref, VEC.mix_gain, width)
    fgain = col(cols_ref, VEC.first_gain, width)

    @pl.loop(0, rows // PIECE)
    def _(c):
        arrive(c)
        at = pl.ds(pl.multiple_of(c * PIECE, PIECE), PIECE)
        dq = jnp.concatenate([dqkv_ref[h, :, at] for h in range(heads)], axis=0)
        dqs[:, at] = dq
        dh2 = dot(mix_w, dq)
        n2, inv2 = norm(x1_ref[:, at])
        dx1 = dx2_ref[:, at] + norm_back(dh2, n2, inv2, mgain)
        x0 = frames_ref[:, at].astype(F32)
        n1, inv1 = norm(x0)
        h1 = (n1 * fgain + col(cols_ref, VEC.first_shift, width)).astype(BF)
        a1 = dot(up_t, h1) + col(cols_ref, VEC.first_up_bias, hidden)
        sig = sigmoid(a1)
        s1s[:, at] = (a1 * sig).astype(BF)
        df = (0.5 * dx1).astype(BF)
        da = (dot(down, df) * (sig * (1.0 + a1 * (1.0 - sig)))).astype(BF)
        dh1 = dot(up_ref[...], da)
        grad_ref[:, at] = dx1 + norm_back(dh1, n1, inv1, fgain)
        h1s[:, at] = h1
        das[:, at] = da
        dfs[:, at] = df
        for i, v in enumerate((dh1 * n1, dh1, dh2 * n2, dh2)):
            gains[i] += folded(v)
        between(c)

    mix_grad = dot(dot(h2_ref[...], dqs[...], NT).astype(BF), hot)
    at = 0
    for lo in range(0, mix_grad.shape[1], TILE):
        pack_ref[at : at + width, :] = pad_lanes(mix_grad[:, lo : min(lo + TILE, mix_grad.shape[1])]).astype(BF)
        at += width
    mixed()
    up_grad = dot(h1s[...], das[...], NT)
    up_bias = dot(ones_row(16, rows), das[...], NT)
    down_grad = dot(dfs[...], s1s[...], NT)
    down_bias = exact(jnp.ones((8, rows), F32), dfs[...].astype(F32), NT)
    put_ff(pack_ref, up_grad, down_grad, at)
    at += (2 * (hidden // TILE) + 1) * width
    totals = [row_sums(gains[i])[:1] for i in range(4)]
    small = stack_rows([totals[0], totals[1], up_bias[:1], down_bias[:1], totals[2], totals[3]], (16, 5 * TILE))
    at = put_small(pack_ref, small, at)
    span = dtab_ref.shape[1]
    table = jnp.where(iota((16, span), 0) == lax.axis_index("head"), dtab_ref[...], 0.0)
    pack_ref[at : at + 16, :] = table.astype(BF)
    if at + 16 < pack_ref.shape[0]:
        pack_ref[at + 16 :, :] = jnp.zeros((pack_ref.shape[0] - at - 16, TILE), BF)


def put_small(pack_ref, small, at):
    for lo in range(0, small.shape[1], TILE):
        pack_ref[at : at + small.shape[0], :] = small[:, lo : lo + TILE].astype(BF)
        at += small.shape[0]
    return at


def put_taps(pack_ref, tapg, at):
    taps = tapg.shape[0]
    pack_ref[at : at + taps, :] = tapg[:, :TILE].astype(BF)
    pack_ref[at + taps : at + 2 * taps, :] = pad_lanes(tapg[:, TILE:]).astype(BF)
    return at + 2 * taps


def unpack_kernel(pack_ref, out_ref, grad_ref, *refs, layout):
    refs[0][...] = out_ref[...]
    refs[1][...] = grad_ref[...]
    out_refs = refs[2:]
    given = Weights(*out_refs)

    def wide(at, rows, lanes):
        parts = [pack_ref[at + i * rows : at + (i + 1) * rows, :].astype(F32) for i in range(-(-lanes // TILE))]
        return jnp.concatenate(parts, axis=1)[:, :lanes]

    for at, up_ref, down_ref in ((layout.first, given.first_up, given.first_down), (layout.second, given.second_up, given.second_down)):
        width, hidden = up_ref.shape
        whole = hidden // TILE
        half = hidden - whole * TILE
        piece = lambda i: pack_ref[at + i * width : at + (i + 1) * width, :].astype(F32)
        rest = piece(2 * whole)
        up_ref[...] = jnp.concatenate([piece(i) for i in range(whole)] + [rest[:, :half]], axis=1)
        down_ref[...] = jnp.concatenate([piece(whole + i) for i in range(whole)] + [rest[:, half:]], axis=1)
    for ref, at in ((given.mix_inputs, layout.mix_inputs), (given.pointwise_in, layout.pointwise_in), (given.mix_output, layout.mix_output),
                    (given.pointwise_out, layout.pointwise_out), (given.depthwise_taps, layout.taps)):
        ref[...] = wide(at, *ref.shape)
    given.position_bias[...] = pack_ref[layout.table : layout.table + 16, :].astype(F32)[: given.position_bias.shape[0]]
    late = wide(layout.small_late, 16, 5 * TILE)
    early = wide(layout.small, 32, 5 * TILE)
    late_rows = (
        given.first_gain, given.first_shift, given.first_up_bias, given.first_down_bias, given.mix_gain, given.mix_shift,
    )
    second_rows = (
        given.second_gain, given.second_shift, given.second_up_bias, given.second_down_bias, given.final_gain, given.final_shift,
        given.batch_gain, given.batch_shift, given.pointwise_out_bias,
    )
    filter_rows = (given.filter_gain, given.filter_shift, given.pointwise_in_bias, given.mix_output_bias)
    for small, first, refs in ((late, 0, late_rows), (early, 0, second_rows), (early, 16, filter_rows)):
        for row, ref in enumerate(refs, first):
            ref[...] = small[row : row + 1, : ref.shape[0]].reshape(ref.shape)


@dataclasses.dataclass
class Weights:
    first_gain: object
    first_shift: object
    first_up: object
    first_up_bias: object
    first_down: object
    first_down_bias: object
    mix_gain: object
    mix_shift: object
    mix_inputs: object
    position_bias: object
    mix_output: object
    mix_output_bias: object
    filter_gain: object
    filter_shift: object
    pointwise_in: object
    pointwise_in_bias: object
    depthwise_taps: object
    batch_gain: object
    batch_shift: object
    pointwise_out: object
    pointwise_out_bias: object
    second_gain: object
    second_shift: object
    second_up: object
    second_up_bias: object
    second_down: object
    second_down_bias: object
    final_gain: object
    final_shift: object


def pack_layout(width, hidden, mix_width, taps, devices):
    ff = (2 * (hidden // TILE) + 1) * width
    chunks = lambda lanes: -(-lanes // TILE) * width
    unit = 16 * devices
    whole = lambda rows: -(-rows // unit) * unit
    at = types.SimpleNamespace(second=0, pointwise_out=ff)
    at.pointwise_in = ff + chunks(width)
    at.mix_output = at.pointwise_in + chunks(2 * width)
    at.taps = at.mix_output + chunks(width)
    at.small = at.taps + 2 * taps
    at.late = at.mix_inputs = whole(at.small + 32 * 5)
    at.last = at.late + chunks(mix_width) // unit * unit
    at.first = at.mix_inputs + chunks(mix_width)
    at.small_late = at.first + ff
    at.table = at.small_late + 16 * 5
    at.rows = at.late + whole(at.table + 16 - at.late)
    return at


MESH = pl.DeviceIdType.MESH


def meet(peers):
    barrier = pltpu.get_barrier_semaphore()
    for peer in peers:
        pl.semaphore_signal(barrier, inc=1, device_id=peer, device_id_type=MESH)
    pl.semaphore_wait(barrier, len(peers))


def head_peers(n):
    me = lax.axis_index("head")
    return me, [{"head": lax.rem(me + s, n)} for s in range(1, n)], [lax.rem(me + s, n) for s in range(1, n)]


def opening_kernel(frames_ref, len_ref, up_ref, down_ref, mix_ref, *refs, packed_rows, n):
    count = len(VEC.__dict__)
    vec_refs, refs = refs[:count], refs[count:]
    (cot_ref, x1_ref, h2_ref, cols_ref, bound_ref, plan_ref, ext_ref, all_ref, x1l_ref, x1r_ref, cotl_ref, cotr_ref,
     qkv, line, send, recv, local, hsend, hrecv) = refs
    me, peers, ids = head_peers(n)
    rows = cot_ref.shape[1]
    barrier = pltpu.get_barrier_semaphore()
    for peer in peers:
        pl.semaphore_signal(barrier, inc=1, device_id=peer, device_id_type=MESH)
    vecs = [ref[...].astype(F32).reshape(1, ref.shape[0]) for ref in vec_refs]
    cols_ref[...] = stack_rows(vecs, (VEC_ROWS, up_ref.shape[1])).T
    pl.semaphore_wait(barrier, len(peers))

    def piece(c, s):
        at = pl.ds(pl.multiple_of(c * PIECE, PIECE), PIECE)
        return pltpu.make_async_remote_copy(src_ref=qkv.at[ids[s], :, at], dst_ref=all_ref.at[me, :, at], send_sem=send.at[c, s],
                                            recv_sem=recv.at[c, s], device_id=peers[s], device_id_type=MESH)

    def ship(c):
        for s in range(n - 1):
            piece(c, s).start()

    open_rows(frames_ref, up_ref, down_ref, mix_ref, x1_ref, h2_ref, qkv, cols_ref, packed_rows, ship)
    own = pltpu.make_async_copy(qkv.at[me], all_ref.at[me], local)
    own.start()

    def edge(i, src, dst, head):
        return pltpu.make_async_remote_copy(src_ref=src, dst_ref=dst, send_sem=hsend.at[i], recv_sem=hrecv.at[i],
                                            device_id={"head": head}, device_id_type=MESH)

    up = lax.rem(me + 1, n)
    down = lax.rem(me + n - 1, n)
    last, start = pl.ds(rows - TILE, TILE), pl.ds(0, TILE)
    to_right = [edge(0, x1_ref.at[:, last], x1l_ref, up), edge(1, cot_ref.at[:, last], cotl_ref, up)]
    to_left = [edge(2, x1_ref.at[:, start], x1r_ref, down), edge(3, cot_ref.at[:, start], cotr_ref, down)]

    @pl.when(me < n - 1)
    def _():
        for c in to_right:
            c.start()

    @pl.when(me > 0)
    def _():
        for c in to_left:
            c.start()

    open_segments(len_ref, bound_ref, plan_ref, ext_ref, line)
    own.wait()

    @pl.loop(0, rows // PIECE)
    def _(c):
        for s in range(n - 1):
            piece(c, s).wait()

    @pl.when(me < n - 1)
    def _():
        for c in to_right:
            c.wait_send()
        for c in to_left:
            c.wait_recv()

    @pl.when(me > 0)
    def _():
        for c in to_left:
            c.wait_send()
        for c in to_right:
            c.wait_recv()


def everyone(n_tm, n_head):
    n = n_tm * n_head
    me = lax.axis_index("tm") * n_head + lax.axis_index("head")

    def place(s):
        peer = lax.rem(me + s, n)
        return {"tm": peer // n_head, "head": lax.rem(peer, n_head)}

    return me, n, place


def tell(src_ref, all_ref, send, recv, n_tm, n_head):
    me, n, place = everyone(n_tm, n_head)

    def copy(s):
        return pltpu.make_async_remote_copy(src_ref=src_ref, dst_ref=all_ref.at[me], send_sem=send.at[s], recv_sem=recv.at[s],
                                            device_id=place(s), device_id_type=MESH)

    def start():
        pl.loop(1, n)(lambda s: copy(s).start())
        all_ref[me] = src_ref[...]

    def end():
        pl.loop(1, n)(lambda s: copy(s).wait())

    return start, end


def load_all(sources, targets, sems):
    copies = [pltpu.make_async_copy(src, dst, sems.at[i]) for i, (src, dst) in enumerate(zip(sources, targets))]
    for copy in copies:
        copy.start()
    return copies


def middle_kernel(*refs, n_tm, n_head, head_width, slot_count, layout):
    o_ref, sources, refs = refs[0], refs[1:15], refs[15:]
    (out_ref, dx2_ref, do_all, pack_ref), refs = refs[:4], refs[4:]
    loaded, refs = refs[:14], refs[14:]
    (x1_ref, x1l_ref, x1r_ref, cot_ref, cotl_ref, cotr_ref, cols_ref, ext_ref, mixo_ref, pwi_ref, taps_ref, pwo_ref, up_ref,
     down_ref) = loaded
    (o_own, x2, oc, u, y, stat, stats, dx3, e, sums, all_sums, do, wide, mask, live,
     h4s, das, s4s, dfs, ws, dcs, dyw, du, prod, h3s, dgs, dms, ocs, gains2, smalld, smalle, tapg), refs = refs[:32], refs[32:]
    (load_sems, send_o, recv_o, local_o, send_a, recv_a, send_b, recv_b, send_d, recv_d, local_d) = refs
    me, peers, ids = head_peers(n_head)
    _, n, place = everyone(n_tm, n_head)
    barrier = pltpu.get_barrier_semaphore()
    rows = x1_ref.shape[1]

    @pl.loop(1, n)
    def _(s):
        pl.semaphore_signal(barrier, inc=1, device_id=place(s), device_id_type=MESH)

    loads = load_all(sources, loaded, load_sems)
    pl.semaphore_wait(barrier, n - 1)

    def part(p):
        return o_ref.at[:, pl.ds(pl.multiple_of(p * rows, TILE), rows + 2 * TILE)]

    copies = [
        pltpu.make_async_remote_copy(src_ref=part(p), dst_ref=o_own.at[me], send_sem=send_o.at[s], recv_sem=recv_o.at[s],
                                     device_id=peer, device_id_type=MESH)
        for s, (peer, p) in enumerate(zip(peers, ids))
    ]
    for copy in copies:
        copy.start()
    own = pltpu.make_async_copy(part(me), o_own.at[me], local_o)
    own.start()
    for load in loads:
        load.wait()

    def arrive():
        own.wait()
        for copy in copies:
            copy.wait()

    filter_kernel(x1_ref, x1l_ref, x1r_ref, o_own, cols_ref, ext_ref, mixo_ref, pwi_ref, taps_ref, x2, oc, u, y, stat, wide, mask, live,
                  head_width=head_width, slot_count=slot_count, arrive=arrive)
    stats_out, stats_in = tell(stat, stats, send_a, recv_a, n_tm, n_head)
    sums_out, sums_in = tell(sums, all_sums, send_b, recv_b, n_tm, n_head)
    stats_out()
    second_kernel(x2, y, stats, cot_ref, cotl_ref, cotr_ref, cols_ref, pwo_ref, up_ref, down_ref,
                  out_ref, dx3, e, sums, pack_ref, smalld, h4s, das, s4s, dfs, ws, dcs, arrive=stats_in, leave=sums_out)

    def piece(c, s):
        at = pl.ds(pl.multiple_of(c * PIECE, PIECE), PIECE)
        return pltpu.make_async_remote_copy(src_ref=do.at[ids[s], :, at], dst_ref=do_all.at[me, :, at], send_sem=send_d.at[c, s],
                                            recv_sem=recv_d.at[c, s], device_id=peers[s], device_id_type=MESH)

    def ship(c):
        for s in range(n_head - 1):
            piece(c, s).start()

    unfilter_kernel(e, y, stats, all_sums, u, dx3, x2, oc, cols_ref, ext_ref, pwi_ref, taps_ref, mixo_ref,
                    dx2_ref, do, pack_ref.at[pl.ds(layout.pointwise_in, layout.taps - layout.pointwise_in)], smalle, tapg, dyw, du, mask, prod, h3s, dgs, dms, ocs, gains2, live,
                    head_width=head_width, slot_count=slot_count, ship=ship, arrive=sums_in)
    own = pltpu.make_async_copy(do.at[me], do_all.at[me], local_d)
    own.start()
    end = put_taps(pack_ref, tapg[...], layout.taps)
    end = put_small(pack_ref, jnp.concatenate([smalld[...], smalle[...]], axis=0), end)
    if end < pack_ref.shape[0]:
        pack_ref[end:, :] = jnp.zeros((pack_ref.shape[0] - end, TILE), BF)
    own.wait()

    @pl.loop(0, rows // PIECE)
    def _(c):
        for s in range(n_head - 1):
            piece(c, s).wait()


def sum_scratch(count, n_tm, n_head):
    half = count // 2
    big = half // (n_tm // 2)
    shapes = [(half, TILE), (half, TILE), (n_tm // 2, big, TILE), (big, TILE), (n_head, big // n_head, TILE), (big, TILE), (half, TILE)]
    return [pltpu.VMEM(shape, BF) for shape in shapes]


def gradient_sum(src_ref, out_ref, first, scratch, sems, local, n_tm, n_head):
    got0, half, got1, part1, got2, part2, whole = scratch
    tm, head = lax.axis_index("tm"), lax.axis_index("head")
    n_chip = n_tm // 2
    chip, core = tm // 2, lax.rem(tm, 2)
    size = src_ref.shape[0] // 2
    big = size // n_chip
    small = big // n_head
    sibling = {"tm": chip * 2 + 1 - core}

    def rows(i, count, base=0):
        return pl.ds(pl.multiple_of(base + i * count, 16), count)

    def send(src, dst, phase, s, peer):
        return pltpu.make_async_remote_copy(src_ref=src, dst_ref=dst, send_sem=sems.at[2 * phase, s], recv_sem=sems.at[2 * phase + 1, s],
                                            device_id=peer, device_id_type=MESH)

    def chip_peer(s):
        return lax.rem(chip + s, n_chip)

    def head_peer(s):
        return lax.rem(head + s, n_head)

    def zero():
        return send(src_ref.at[rows(1 - core, size)], got0, 0, 0, sibling)

    def one(s):
        return send(half.at[rows(chip_peer(s), big)], got1.at[s], 1, s, {"tm": chip_peer(s) * 2 + core})

    def two(s):
        return send(part1.at[rows(head_peer(s), small)], got2.at[s], 2, s, {"head": head_peer(s)})

    def three(s):
        at = part2.at[rows(head, small)]
        return send(at, at, 3, s, {"head": head_peer(s)})

    def four(s):
        return send(part2, whole.at[rows(chip, big)], 4, s, {"tm": chip_peer(s) * 2 + core})

    def five():
        return send(whole, out_ref.at[rows(core, size, first)], 5, 0, sibling)

    def keep():
        return pltpu.make_async_copy(whole, out_ref.at[rows(core, size, first)], local)

    def added(got, n):
        total = got[0].astype(F32)
        for s in range(1, n):
            total = total + got[s].astype(F32)
        return total.astype(BF)

    def step0():
        zero().start()

    def step1():
        zero().wait()
        half[...] = (src_ref[rows(core, size), :].astype(F32) + got0[...].astype(F32)).astype(BF)
        pl.loop(1, n_chip)(lambda s: one(s).start())
        got1[0] = half[rows(chip, big), :]

    def step2():
        pl.loop(1, n_chip)(lambda s: one(s).wait())
        part1[...] = added(got1, n_chip)
        pl.loop(1, n_head)(lambda s: two(s).start())
        got2[0] = part1[rows(head, small), :]

    def step3():
        pl.loop(1, n_head)(lambda s: two(s).wait())
        part2[rows(head, small), :] = added(got2, n_head)
        pl.loop(1, n_head)(lambda s: three(s).start())

    def step4():
        pl.loop(1, n_head)(lambda s: three(s).wait())
        pl.loop(1, n_chip)(lambda s: four(s).start())
        whole[rows(chip, big), :] = part2[...]

    def step5():
        pl.loop(1, n_chip)(lambda s: four(s).wait())
        five().start()
        keep().start()

    def step6():
        keep().wait()
        five().wait()

    return step0, step1, step2, step3, step4, step5, step6


def final_kernel(*refs, n_tm, n_head, parts):
    dqkv_ref, sources, refs = refs[0], refs[1:11], refs[11:]
    (grad_ref, total_ref), loaded, refs = refs[:2], refs[2:12], refs[12:]
    early_ref, frames_ref, x1_ref, h2_ref, dx2_ref, dtab_ref, cols_ref, up_ref, down_ref, mix_ref = loaded
    (dqkv, late, h1s, das, s1s, dfs, dqs, gains), refs = refs[:8], refs[8:]
    sum_refs = [refs[7 * i : 7 * i + 7] for i in range(3)]
    load_sems, send_q, recv_q, local_q, sum_sems, sum_local = refs[21:]
    me, peers, ids = head_peers(n_head)
    tm = lax.axis_index("tm")
    rows = x1_ref.shape[1]
    barrier = pltpu.get_barrier_semaphore()
    for peer in peers:
        pl.semaphore_signal(barrier, inc=1, device_id=peer, device_id_type=MESH)

    @pl.loop(1, n_tm)
    def _(s):
        pl.semaphore_signal(barrier, inc=1, device_id={"tm": lax.rem(tm + s, n_tm)}, device_id_type=MESH)

    loads = load_all(sources, loaded, load_sems)
    pl.semaphore_wait(barrier, n_head + n_tm - 2)

    def piece(c, s):
        at = pl.ds(pl.multiple_of(c * PIECE, PIECE), PIECE)
        return pltpu.make_async_remote_copy(src_ref=dqkv_ref.at[ids[s], :, at], dst_ref=dqkv.at[me, :, at], send_sem=send_q.at[c, s],
                                            recv_sem=recv_q.at[c, s], device_id=peers[s], device_id_type=MESH)

    @pl.loop(0, rows // PIECE)
    def _(c):
        for s in range(n_head - 1):
            piece(c, s).start()

    own = pltpu.make_async_copy(dqkv_ref.at[me], dqkv.at[me], local_q)
    own.start()
    for load in loads:
        load.wait()
    late_at, last_at, end = parts

    def summed(i, src, first):
        return gradient_sum(src, total_ref, first, sum_refs[i], sum_sems.at[i], sum_local.at[i], n_tm, n_head)

    early = summed(0, early_ref, 0)
    last = summed(2, late.at[pl.ds(last_at - late_at, end - last_at)], last_at)
    late_sum = summed(1, late.at[pl.ds(0, last_at - late_at)], late_at) if last_at > late_at else [lambda: None] * 7
    early[0]()
    early[1]()
    own.wait()

    def arrive(c):
        for s in range(n_head - 1):
            piece(c, s).wait()

    def between(c):
        pl.when(c == 0)(early[2])

    def mixed():
        early[3]()
        late_sum[0]()

    close_kernel(frames_ref, x1_ref, h2_ref, dx2_ref, dqkv, dtab_ref, cols_ref, up_ref, down_ref, mix_ref,
                 grad_ref, late, h1s, das, s1s, dfs, dqs, gains, arrive=arrive, between=between, mixed=mixed)
    for step in (last[0], late_sum[1], last[1], late_sum[2], last[2], early[4], late_sum[3], last[3], late_sum[4], early[5], last[4],
                 late_sum[5], early[6], last[5], late_sum[6], last[6]):
        step()


VMEM_MIB = 62


def body(
    frames, lengths, first_gain, first_shift, first_up, first_up_bias, first_down, first_down_bias, mix_gain, mix_shift,
    mix_inputs, position_bias, mix_output, mix_output_bias, filter_gain, filter_shift, pointwise_in, pointwise_in_bias,
    depthwise_taps, batch_gain, batch_shift, pointwise_out, pointwise_out_bias, second_gain, second_shift, second_up,
    second_up_bias, second_down, second_down_bias, final_gain, final_shift, cotangent,
):
    weights = Weights(
        first_gain, first_shift, first_up, first_up_bias, first_down, first_down_bias, mix_gain, mix_shift, mix_inputs, position_bias,
        mix_output, mix_output_bias, filter_gain, filter_shift, pointwise_in, pointwise_in_bias, depthwise_taps, batch_gain,
        batch_shift, pointwise_out, pointwise_out_bias, second_gain, second_shift, second_up, second_up_bias, second_down,
        second_down_bias, final_gain, final_shift)
    rows, width = frames.shape
    hidden = first_up.shape[1]
    n_head, n_tm = lax.axis_size("head"), lax.axis_size("tm")
    heads, span = position_bias.shape
    head_width = width // heads
    packed_rows = -(-3 * head_width // 16) * 16
    group = rows * n_head
    lanes = rows + TILE
    slots = lengths.shape[1]
    taps = depthwise_taps.shape[0]
    layout = pack_layout(width, hidden, mix_inputs.shape[1], taps, n_tm * n_head)

    vectors = tuple(getattr(weights, name) for name in VEC.__dict__)
    frames_t, cot_t, first_down_t, second_down_t = frames.T, cotangent.T, first_down.T, second_down.T
    vm, dma, hbm = pltpu.VMEM, pltpu.SemaphoreType.DMA, pl.BlockSpec(memory_space=pl.ANY)
    steps = rows // PIECE
    piece_sems = dma((steps, n_head - 1))

    def comm_call(kernel, name, collective_id, ins, in_hbm, outs, out_hbm, scratch):
        return pl.pallas_call(
            kernel,
            out_shape=tuple(jax.ShapeDtypeStruct(s, t) for s, t in outs),
            in_specs=[hbm if i in in_hbm else pl.BlockSpec() for i in range(len(ins))],
            out_specs=tuple(hbm if i in out_hbm else pl.BlockSpec() for i in range(len(outs))),
            scratch_shapes=scratch,
            compiler_params=pltpu.CompilerParams(collective_id=collective_id, has_side_effects=True, vmem_limit_bytes=VMEM_MIB * 2**20),
            name=name,
        )(*ins)

    ins = (frames_t, lengths, first_up, first_down_t, mix_inputs) + vectors + (cot_t,)
    x1, h2, cols, bounds, plan, ext, qkv_all, x1l, x1r, cotl, cotr = comm_call(
        functools.partial(opening_kernel, packed_rows=packed_rows, n=n_head), "opening", 1, ins, (len(ins) - 1,),
        [((width, rows), F32), ((width, rows), BF), ((hidden, VEC_ROWS), F32), ((2, group + 2 * PAD), jnp.int32),
         ((group // BLK, 128), jnp.int32), ((1, lanes), jnp.int32), ((n_head, packed_rows, rows), BF),
         ((width, TILE), F32), ((width, TILE), F32), ((width, TILE), BF), ((width, TILE), BF)], range(6, 11),
        [vm((n_head, packed_rows, rows), BF), vm((1, group + 2 * TILE), jnp.int32), piece_sems, piece_sems, dma, dma((4,)), dma((4,))])
    o, of, lse = attend_forward(qkv_all, bounds, plan, position_bias, head_width)
    everyone_sems = dma((n_tm * n_head,))
    ins = (x1, x1l, x1r, cot_t, cotl, cotr, cols, ext, mix_output, pointwise_in, depthwise_taps, pointwise_out, second_up, second_down_t)
    out, dx2, do_all, pack = comm_call(
        functools.partial(middle_kernel, n_tm=n_tm, n_head=n_head, head_width=head_width, slot_count=slots, layout=layout),
        "middle", 2, (o,) + ins, range(len(ins) + 1),
        [((width, rows), BF), ((width, rows), F32), ((n_head, SLOT, rows), BF), ((layout.late, TILE), BF)],
        (2,),
        [vm(a.shape, a.dtype) for a in ins] + [
            vm((n_head, SLOT, rows + 2 * TILE), BF), vm((width, lanes), F32), vm((width, rows), BF), vm((width, lanes), BF),
            vm((width, lanes), F32), vm((4, TILE), F32), vm((n_tm * n_head, 4, TILE), F32), vm((width, rows), F32),
            vm((width, lanes), F32), vm((4, TILE), F32), vm((n_tm * n_head, 4, TILE), F32), vm((n_head, SLOT, rows), BF),
            vm((width, lanes), F32), vm((taps, 8, lanes), F32), vm((1, lanes), F32),
            vm((width, rows), BF), vm((hidden, rows), BF), vm((hidden + 16, rows), BF), vm((width, rows), BF),
            vm((width + 16, rows), BF), vm((width, rows), BF),
            vm((width, lanes), F32), vm((width, rows), F32), vm((taps, width, TILE), F32), vm((width + 16, rows), BF),
            vm((2 * width, rows), BF), vm((width, rows), BF), vm((width + 16, rows), BF), vm((2, width, TILE), F32),
            vm((16, 5 * TILE), F32), vm((16, 5 * TILE), F32), vm((taps, width), F32),
            dma((len(ins),)), dma((n_head - 1,)), dma((n_head - 1,)), dma, everyone_sems, everyone_sems, everyone_sems, everyone_sems,
            piece_sems, piece_sems, dma,
        ])
    dqkv, dtab = attend_backward(qkv_all, do_all, of, lse, bounds, plan, position_bias, head_width)
    parts = (layout.late, layout.last, layout.rows)
    sizes = (layout.late, max(layout.last - layout.late, 16 * n_tm * n_head), layout.rows - layout.last)
    ins = (pack, frames_t, x1, h2, dx2, dtab, cols, first_up, first_down_t, mix_inputs)
    grad, total = comm_call(
        functools.partial(final_kernel, n_tm=n_tm, n_head=n_head, parts=parts), "final", 3, (dqkv,) + ins, range(len(ins) + 1),
        [((width, rows), F32), ((layout.rows, TILE), BF)], (1,),
        [vm(a.shape, a.dtype) for a in ins] + [
            vm((n_head, packed_rows, rows), BF), vm((layout.rows - layout.late, TILE), BF),
            vm((width, rows), BF), vm((hidden, rows), BF), vm((hidden, rows), BF), vm((width, rows), BF),
            vm((n_head * packed_rows, rows), BF), vm((4, width, TILE), F32),
            *[s for size in sizes for s in sum_scratch(size, n_tm, n_head)],
            dma((len(ins),)), piece_sems, piece_sems, dma, dma((3, 12, max(n_tm // 2, n_head))), dma((3,)),
        ])
    shapes = Weights(**{n: w.shape for n, w in weights.__dict__.items()})
    shapes.first_down = shapes.second_down = first_down_t.shape
    results = [((width, rows), BF), ((width, rows), F32)] + [(s, F32) for s in shapes.__dict__.values()]
    out, grad, *summed = pl.pallas_call(
        functools.partial(unpack_kernel, layout=layout),
        out_shape=tuple(jax.ShapeDtypeStruct(s, t) for s, t in results),
        compiler_params=pltpu.CompilerParams(vmem_limit_bytes=VMEM_MIB * 2**20),
        name="unpack",
    )(total, out, grad)
    summed = Weights(*summed)
    summed.first_down, summed.second_down = summed.first_down.T, summed.second_down.T
    return (out.T, grad.T) + tuple(summed.__dict__.values())


def solution(mesh):
    rows = P(("tm", "head"), None)
    placed = (rows, P("tm", None)) + (P(),) * 29 + (rows,)
    return jax.shard_map(body, mesh=mesh, in_specs=placed, out_specs=(rows, rows) + (P(),) * 29, check_vma=False)
```

```python
import dataclasses
import functools
import math
import types

import jax
import jax.numpy as jnp
from jax import lax
from jax.experimental import pallas as pl
from jax.experimental.pallas import tpu as pltpu
from jax.sharding import PartitionSpec as P

BF = jnp.bfloat16
F32 = jnp.float32
LOG2E = math.log2(math.e)
BLK = 512
UNIT = 128
PER = BLK // UNIT
NEAR = PER + 2
PAD = 8 * UNIT
SLOT = 48
DEPTH = 128
MASKED = -1e30
GANG = 4
NN = (((1,), (0,)), ((), ()))
NT = (((1,), (1,)), ((), ()))
TN = (((0,), (0,)), ((), ()))


def dot(a, b, dims=NN):
    return lax.dot_general(a, b, dims, preferred_element_type=F32)


def iota(shape, dim):
    return lax.broadcasted_iota(jnp.int32, shape, dim)


def spread_cols(width, slots, slot_rows, used):
    row, column = iota((slots * slot_rows, width), 0), iota((slots * slot_rows, width), 1)
    hit = jnp.zeros((slots * slot_rows, width), jnp.bool_)
    for s in range(slots):
        f = row - slot_rows * s
        hit = hit | ((f >= 0) & (f < used) & (column == used * s + f))
    return hit.astype(F32).astype(BF)


def split3(v):
    hi = v.astype(BF).astype(F32)
    r1 = v - hi
    mid = r1.astype(BF).astype(F32)
    return hi, mid, r1 - mid


def three_rows(v, rows):
    a, b, e = split3(v)
    row = iota((rows, v.shape[1]), 0)
    return jnp.where(row == 0, a, jnp.where(row == 1, b, jnp.where(row == 2, e, 0.0)))


def pick_row(ref, index):
    values = ref[...].astype(F32)
    return jnp.sum(jnp.where(iota(values.shape, 0) == index, values, 0.0), axis=0, keepdims=True)


def bias_square(table, d):
    span = table.shape[1]
    half = span // 2
    lanes = 2 * UNIT
    u = iota((span, lanes), 1)
    u = jnp.where(u < UNIT, u, u - lanes)
    ids = jnp.clip(-UNIT * d - u, -half, half - 1) + half
    hot = (ids == iota((span, lanes), 0)).astype(F32).astype(BF)
    line = dot(jnp.broadcast_to(table, (UNIT, span)).astype(BF), hot) * LOG2E
    return pltpu.roll(line, 0, 1, stride=1, stride_axis=0)[:, :UNIT]


def bias_near(table, tile, keys_near):
    span = table.shape[1]
    squares = {d: bias_square(table, d) for d in (-1, 0, 1)}
    low = jnp.broadcast_to(table[:, :1] * LOG2E, (UNIT, UNIT))
    high = jnp.broadcast_to(table[:, span - 1 :] * LOG2E, (UNIT, UNIT))
    for r in range(tile.shape[0] // UNIT):
        for c in range(tile.shape[1] // UNIT):
            d = c - (r - 1) if keys_near else (c - 1) - r
            part = squares[d] if abs(d) < 2 else (low if d > 0 else high)
            tile[r * UNIT : (r + 1) * UNIT, c * UNIT : (c + 1) * UNIT] = part


def units_at(u, count):
    return pl.ds(pl.multiple_of(u * UNIT, UNIT), count * UNIT)


def far_windows(low, plain, edge, step, side, up, fine):
    sign = 1 if up else -1

    def run(at, times, size, masked):
        def one(i, carry):
            near = at + sign * i * size
            step(near if up else near - size, size, side, masked)
            return carry

        lax.fori_loop(0, times, one, 0)
        return at + sign * times * size

    at = edge if plain is None else run(edge, sign * (plain - edge) // 8, 8, False)
    left = sign * (low - at)
    tail = lax.rem(left, 8)
    more = tail > (6 if fine else 4)
    at = run(at, left // 8 + more.astype(jnp.int32), 8, True)
    tail = jnp.where(more, 0, tail)
    four = tail > (2 if fine else 0)
    at = run(at, four.astype(jnp.int32), 4, True)
    if fine:
        run(at, (tail - jnp.where(four, 4, 0) > 0).astype(jnp.int32), 2, True)


def far_sweep(plan, block, step, before, after, fine):
    low, plain_low, plain_high, high, low_half, high_half = [plan[block, i] for i in range(6)]
    start, stop = PER * block - 1, PER * block + PER + 1
    for whole, part in ((True, None), (False, 0)):
        @pl.when((low_half == 0) if whole else (low_half != 0))
        def _():
            far_windows(low, plain_low if whole else None, start, functools.partial(step, part=part), before, False, fine)

    for whole, part in ((True, None), (False, 1)):
        @pl.when((high_half == 0) if whole else (high_half != 0))
        def _():
            far_windows(high, plain_high if whole else None, stop, functools.partial(step, part=part), after, True, fine)


def part_at(block, part):
    if part is None:
        return units_at(PER * block, PER)
    return units_at(PER * block + part * (PER // 2), PER // 2)


def has_far(plan, block):
    return (plan[block, 0] < PER * block - 1) | (plan[block, 3] > PER * block + PER + 1)


def segment_rows(ends, lengths, place, total):
    slots = ends.shape[0]
    before = ends <= jnp.broadcast_to(place, (slots, place.shape[1]))
    seg = jnp.sum(before.astype(jnp.int32), axis=0, keepdims=True)
    first = jnp.sum(jnp.where(before, lengths, 0), axis=0, keepdims=True)
    stop = jnp.min(jnp.where(before, total, ends), axis=0, keepdims=True)
    return seg, first, stop


def block_plan(ends, ends_row, total):
    slots = ends.shape[0]
    blocks, units = total // BLK, total // UNIT

    def along(place):
        return jnp.sum((ends <= jnp.broadcast_to(place, (slots, 128))).astype(jnp.int32), axis=0, keepdims=True)

    def down(place):
        return jnp.sum((jnp.broadcast_to(ends_row, (blocks, slots)) <= place).astype(F32), axis=1, keepdims=True).astype(jnp.int32)

    unit = iota((1, 128), 1)
    u_first, u_last = along(unit * UNIT), along(unit * UNIT + UNIT - 1)
    b = iota((blocks, 1), 0)
    first, last = down(b * BLK), down(b * BLK + BLK - 1)
    low_half = (down(b * BLK + BLK // 2) != first).astype(jnp.int32)
    high_half = (down(b * BLK + BLK // 2 - 1) != last).astype(jnp.int32)
    start, stop = PER * b - 1, PER * b + PER + 1
    inside = unit < units

    def count(hit):
        return jnp.sum((hit & inside).astype(F32), axis=1, keepdims=True).astype(jnp.int32)

    low = jnp.minimum(count(u_last < first), start)
    high = jnp.maximum(units - count(u_first > last), stop)
    plain_low = start - count((unit < start) & (u_first == last))
    plain_high = stop + count((unit >= stop) & (u_last == first))
    lane = iota((blocks, 128), 1)
    out = jnp.zeros((blocks, 128), jnp.int32)
    for i, v in enumerate((low, plain_low, plain_high, high, low_half, high_half)):
        out = jnp.where(lane == i, v, out)
    return out


def meets(first_key, rows, bounds):
    key = iota((rows, bounds.shape[1]), 0)
    return (key >= bounds[0:1, :] - first_key) & (key < bounds[1:2, :] - first_key)


def fwd_kernel(plan, qkv_ref, table_ref, bound_ref, o_ref, of_ref, lse_ref, qaug, kn, vt, tile, top_ref, acc, *, head_width):
    chunks, packed_rows, rows = qkv_ref.shape
    total = chunks * rows
    blocks = total // BLK
    span = table_ref.shape[1]
    table = pick_row(table_ref, lax.axis_index("head"))
    far = (table[:, :1] * LOG2E, table[:, span - 1 :] * LOG2E)
    pick = spread_cols(packed_rows, 3, SLOT, head_width)
    scale = LOG2E / math.sqrt(head_width)
    o_ref[:, :UNIT] = jnp.zeros((SLOT, UNIT), BF)
    o_ref[:, UNIT + total :] = jnp.zeros((SLOT, UNIT), BF)
    for edge in (slice(0, PAD), slice(PAD + total, 2 * PAD + total)):
        kn[edge, :] = jnp.zeros((PAD, DEPTH), BF)
        vt[:, edge] = jnp.zeros((SLOT, PAD), BF)
    bias_near(table, tile, True)
    rest = DEPTH - 2 * SLOT

    @pl.loop(0, chunks)
    def _(c):
        at = pl.ds(pl.multiple_of(c * rows, rows), rows)
        at_pad = pl.ds(pl.multiple_of(c * rows + PAD, UNIT), rows)
        parts = dot(pick, qkv_ref[c])
        q = parts[:SLOT] * scale
        hi = q.astype(BF)
        lo = (q - hi.astype(F32)).astype(BF)
        for s in range(3):
            qaug[s, :SLOT, at] = hi
            qaug[s, SLOT : 2 * SLOT, at] = lo
            qaug[s, 2 * SLOT :, at] = jnp.zeros((rest, rows), BF)
        k = parts[SLOT : 2 * SLOT]
        one3 = (iota((rest, rows), 0) < 3).astype(F32)
        kn[at_pad, :] = jnp.concatenate([k, k, one3], axis=0).T.astype(BF)
        one = (iota((SLOT, rows), 0) == head_width).astype(F32)
        vt[:, at_pad] = (parts[2 * SLOT :] + one).astype(BF)

    def top(x):
        return jnp.max(x.reshape(x.shape[0] // 8, 8, BLK), axis=0)

    @pl.loop(0, blocks // GANG)
    def _(pair):
        blocks_now = [GANG * pair + i for i in range(GANG)]
        at_q = [units_at(PER * b, PER) for b in blocks_now]
        near = [units_at(PER * b - 1 + PAD // UNIT, NEAR) for b in blocks_now]
        x = [dot(kn[n, :], qaug[1, :, q]) + tile[...] for n, q in zip(near, at_q)]
        x = [
            jnp.where(meets(PER * b * UNIT - UNIT, NEAR * UNIT, bound_ref[:, units_at(PER * b + PAD // UNIT, PER)]), v, MASKED)
            for b, v in zip(blocks_now, x)
        ]
        m = [jnp.max(top(v), axis=0, keepdims=True) for v in x]
        p = [jnp.exp2(v - w).astype(BF) for v, w in zip(x, m)]
        out = [dot(vt[:, n], v) for n, v in zip(near, p)]
        for q, w, v in zip(at_q, m, out):
            acc[:, q] = v
            lse_ref[:, q] = w
            qaug[0, 2 * SLOT :, q] = three_rows(far[0] - w, rest).astype(BF)
            qaug[2, 2 * SLOT :, q] = three_rows(far[1] - w, rest).astype(BF)

    @pl.loop(0, blocks)
    def _(b):
        @pl.when(has_far(plan, b))
        def _():
            at_q = units_at(PER * b, PER)

            def scores(u, count, side, masked, part):
                x = dot(kn[units_at(u + PAD // UNIT, count), :], qaug[side, :, part_at(b, part)])
                if masked:
                    x = jnp.where(meets(u * UNIT, count * UNIT, bound_ref[:, part_at(b + PAD // BLK, part)]), x, MASKED)
                return x

            near_acc = acc[:, at_q]

            def add(u, count, side, masked, part):
                p = jnp.exp2(scores(u, count, side, masked, part)).astype(BF)
                acc[:, part_at(b, part)] += dot(vt[:, units_at(u + PAD // UNIT, count)], p)

            far_sweep(plan, b, add, 0, 2, False)
            sums = acc[head_width : head_width + 1, at_q]
            over = jnp.max(jnp.where(sums < 2.0**60, 0.0, 1.0))

            @pl.when(over > 0.5)
            def _():
                top_ref[...] = jnp.zeros_like(top_ref)

                def half_of(part):
                    return slice(None) if part is None else slice(part * BLK // 2, (part + 1) * BLK // 2)

                def first(u, count, side, masked, part):
                    x = scores(u, count, side, masked, part)
                    best = jnp.max(x.reshape(x.shape[0] // 8, 8, x.shape[1]), axis=0)
                    top_ref[:, half_of(part)] = jnp.maximum(top_ref[:, half_of(part)], best)

                far_sweep(plan, b, first, 0, 2, False)
                m = jnp.max(top_ref[...], axis=0, keepdims=True)
                acc[:, at_q] = near_acc * jnp.exp2(-m)
                lse_ref[:, at_q] += m

                def second(u, count, side, masked, part):
                    p = jnp.exp2(scores(u, count, side, masked, part) - m[:, half_of(part)]).astype(BF)
                    acc[:, part_at(b, part)] += dot(vt[:, units_at(u + PAD // UNIT, count)], p)

                far_sweep(plan, b, second, 0, 2, False)

    @pl.loop(0, chunks)
    def _(c):
        at = pl.ds(pl.multiple_of(c * rows, rows), rows)
        total_p = acc[head_width : head_width + 1, at]
        out = acc[:, at] / total_p
        o_ref[:, pl.ds(pl.multiple_of(c * rows + UNIT, UNIT), rows)] = out.astype(BF)
        of_ref[:, at] = out[: of_ref.shape[0]]
        lse_ref[:, at] = lse_ref[:, at] + jnp.log2(total_p)


def attend_forward(qkv, bounds, plan, table, head_width):
    chunks, packed_rows, rows = qkv.shape
    total = chunks * rows
    vm = pltpu.VMEM
    return pl.pallas_call(
        functools.partial(fwd_kernel, head_width=head_width),
        out_shape=(
            jax.ShapeDtypeStruct((SLOT, total + 2 * UNIT), BF),
            jax.ShapeDtypeStruct((40, total), F32),
            jax.ShapeDtypeStruct((1, total), F32),
        ),
        in_specs=[pl.BlockSpec(memory_space=pltpu.SMEM)] + [pl.BlockSpec()] * 3,
        scratch_shapes=[
            vm((3, DEPTH, total), BF),
            vm((total + 2 * PAD, DEPTH), BF),
            vm((SLOT, total + 2 * PAD), BF),
            vm((NEAR * UNIT, BLK), F32),
            vm((8, BLK), F32),
            vm((SLOT, total), F32),
        ],
        compiler_params=pltpu.CompilerParams(vmem_limit_bytes=62 * 2**20),
        name="attend_forward",
    )(plan, qkv, table, bounds)


def bwd_kernel(plan, qkv_ref, do_ref, of_ref, lse_ref, table_ref, bound_ref, dqkv_ref, dtab_ref,
               qaug, kn, kt, vn, dot_t, qn, don, tile, dq, band, ends, dv_acc, dk_acc, *, head_width):
    chunks, packed_rows, rows = qkv_ref.shape
    total = chunks * rows
    blocks = total // BLK
    span = table_ref.shape[1]
    table = pick_row(table_ref, lax.axis_index("head"))
    pick = spread_cols(packed_rows, 3, SLOT, head_width)
    scale = LOG2E / math.sqrt(head_width)
    back = 1.0 / math.sqrt(head_width)
    rest = DEPTH - 2 * SLOT
    bias_near(table, tile, False)
    for edge in (slice(0, PAD), slice(PAD + total, 2 * PAD + total)):
        for s in range(3):
            qaug[s, :, edge] = jnp.zeros((DEPTH, PAD), BF)
        dot_t[:, edge] = jnp.zeros((DEPTH, PAD), BF)
        qn[edge, :] = jnp.zeros((PAD, DEPTH), BF)
        don[edge, :] = jnp.zeros((PAD, DEPTH), BF)

    @pl.loop(0, chunks)
    def _(c):
        at = pl.ds(pl.multiple_of(c * rows, rows), rows)
        at_pad = pl.ds(pl.multiple_of(c * rows + PAD, UNIT), rows)
        parts = dot(pick, qkv_ref[c])
        q, k, v = parts[:SLOT], parts[SLOT : 2 * SLOT], parts[2 * SLOT :]
        qs = q * scale
        hi = qs.astype(BF)
        lo = (qs - hi.astype(F32)).astype(BF)
        lse = lse_ref[:, at]
        for s, shift in enumerate((table[:, :1] * LOG2E, 0.0, table[:, span - 1 :] * LOG2E)):
            qaug[s, :SLOT, at_pad] = hi
            qaug[s, SLOT : 2 * SLOT, at_pad] = lo
            qaug[s, 2 * SLOT :, at_pad] = three_rows(shift - lse, rest).astype(BF)
        one3 = (iota((rest, rows), 0) < 3).astype(F32)
        row48 = iota((SLOT, rows), 0)
        none = jnp.zeros((rest, rows), F32)
        empty = jnp.zeros((SLOT, rows), F32)
        kn[at, :] = jnp.concatenate([k, k, one3], axis=0).T.astype(BF)
        kt[:, at] = k.astype(BF)
        vn[at, :] = jnp.concatenate([v, empty, one3], axis=0).T.astype(BF)
        do = do_ref[c].astype(F32)
        centre = jnp.sum(do[: of_ref.shape[0]] * of_ref[:, at], axis=0, keepdims=True)
        dot_t[:SLOT, at_pad] = do_ref[c]
        dot_t[SLOT : 2 * SLOT, at_pad] = empty.astype(BF)
        dot_t[2 * SLOT :, at_pad] = three_rows(-centre, rest).astype(BF)
        qn[at_pad, :] = jnp.concatenate([q + (row48 == head_width).astype(F32), empty, none], axis=0).T.astype(BF)
        don[at_pad, :] = jnp.concatenate([do, empty, none], axis=0).T.astype(BF)

    dq[...] = jnp.zeros_like(dq)
    band[...] = jnp.zeros_like(band)
    ends[...] = jnp.zeros_like(ends)

    @pl.loop(0, blocks // GANG)
    def _(pair):
        width = NEAR * UNIT
        wide = width + (GANG - 1) * BLK
        blocks_now = [GANG * pair + i for i in range(GANG)]
        at_k = [units_at(PER * b, PER) for b in blocks_now]
        near = [units_at(PER * b - 1 + PAD // UNIT, NEAR) for b in blocks_now]
        x = [dot(kn[k, :], qaug[1, :, n]) + tile[...] for k, n in zip(at_k, near)]
        dp = [dot(vn[k, :], dot_t[:, n]) for k, n in zip(at_k, near)]
        p = [jnp.where(meets(b * BLK, BLK, bound_ref[:, n]), jnp.exp2(v), 0.0) for b, n, v in zip(blocks_now, near, x)]
        dsb = [(v * w).astype(BF) for v, w in zip(p, dp)]
        dv = [dot(v.astype(BF), don[n, :]) for n, v in zip(near, p)]
        dk = [dot(v, qn[n, :]) for n, v in zip(near, dsb)]
        part = [dot(kt[:, k], v) for k, v in zip(at_k, dsb)]
        for k, v, w in zip(at_k, dv, dk):
            dv_acc[k, :] = v
            dk_acc[k, :] = w
        gap = [jnp.zeros((SLOT, BLK), F32)]
        whole = [jnp.concatenate(gap * i + [v] + gap * (GANG - 1 - i), axis=1) for i, v in enumerate(part)]
        lines = [v.astype(F32) for v in dsb]
        dq[:, units_at(GANG * PER * pair - 1 + PAD // UNIT, wide // UNIT)] += functools.reduce(jnp.add, whole)
        band[...] += functools.reduce(jnp.add, lines)

    @pl.loop(0, blocks)
    def _(b):
        @pl.when(has_far(plan, b))
        def _():
            def far(u, count, side, masked, part):
                at_k = part_at(b, part)
                at_q = units_at(u + PAD // UNIT, count)
                p = jnp.exp2(dot(kn[at_k, :], qaug[side, :, at_q]))
                if masked:
                    first_key = b * BLK + (0 if part is None else part * BLK // 2)
                    p = jnp.where(meets(first_key, at_k.size, bound_ref[:, at_q]), p, 0.0)
                dsb = (p * dot(vn[at_k, :], dot_t[:, at_q])).astype(BF)
                dq[:, at_q] += dot(kt[:, at_k], dsb)
                dv_acc[at_k, :] += dot(p.astype(BF), don[at_q, :])
                dk = dot(dsb, qn[at_q, :])
                dk_acc[at_k, :] += dk
                ends[side // 2] += jnp.sum(dk.reshape(dk.shape[0] // 8, 8, DEPTH), axis=0)

            far_sweep(plan, b, far, 2, 0, True)

    def take(part, lanes):
        row, lane = iota((packed_rows, lanes), 0), iota((packed_rows, lanes), 1)
        return ((row - head_width * part == lane) & (lane < head_width)).astype(F32).astype(BF)

    @pl.loop(0, chunks)
    def _(c):
        at = pl.ds(pl.multiple_of(c * rows, rows), rows)
        at_pad = pl.ds(pl.multiple_of(c * rows + PAD, UNIT), rows)
        packed = dot(take(0, SLOT), (dq[:, at_pad] * back).astype(BF))
        packed += dot(take(1, DEPTH), (dk_acc[at, :] * back).astype(BF), NT)
        packed += dot(take(2, DEPTH), dv_acc[at, :].astype(BF), NT)
        dqkv_ref[c] = packed.astype(BF)

    flip = (iota((UNIT, UNIT), 0) + iota((UNIT, UNIT), 1) == UNIT - 1).astype(F32)
    half = span // 2
    lane = iota((8, span), 1)
    column = iota((8, DEPTH), 1) == head_width
    out = jnp.zeros((8, span), F32)
    far_sum = [jnp.where(column, ends[i], 0.0) for i in range(2)]
    for d in range(-PER, PER + 1):
        part = jnp.zeros((UNIT, UNIT), F32)
        for r in range(PER):
            c = r + d + 1
            if 0 <= c < NEAR:
                part = part + band[r * UNIT : (r + 1) * UNIT, c * UNIT : (c + 1) * UNIT]
        if abs(d) > 1:
            far_sum[0 if d > 0 else 1] += jnp.sum(part.reshape(UNIT // 8, 8, UNIT), axis=0)
            continue
        turned = lax.dot_general(flip, part, NN, precision=lax.Precision.HIGHEST, preferred_element_type=F32)
        wide = jnp.concatenate([turned, jnp.zeros_like(turned)], axis=1)
        skewed = pltpu.roll(wide, 0, 1, stride=1, stride_axis=0)
        line = jnp.sum(skewed.reshape(UNIT // 8, 8, 2 * UNIT), axis=0)
        offset = UNIT - 1 - d * UNIT - iota((span, 2 * UNIT), 1)
        hot = (jnp.clip(offset, -half, half - 1) + half == iota((span, 2 * UNIT), 0)).astype(F32)
        out += lax.dot_general(line, hot, NT, precision=lax.Precision.HIGHEST, preferred_element_type=F32)
    out += jnp.where(lane == 0, jnp.sum(far_sum[0], axis=1, keepdims=True), 0.0)
    out += jnp.where(lane == span - 1, jnp.sum(far_sum[1], axis=1, keepdims=True), 0.0)
    out = jnp.sum(out, axis=0, keepdims=True)
    dtab_ref[...] = out


def attend_backward(qkv, do, of, lse, bounds, plan, table, head_width):
    chunks, packed_rows, rows = qkv.shape
    total = chunks * rows
    padded = total + 2 * PAD
    span = table.shape[1]
    vm = pltpu.VMEM
    return pl.pallas_call(
        functools.partial(bwd_kernel, head_width=head_width),
        out_shape=(
            jax.ShapeDtypeStruct((chunks, packed_rows, rows), BF),
            jax.ShapeDtypeStruct((1, span), F32),
        ),
        in_specs=[pl.BlockSpec(memory_space=pltpu.SMEM)] + [pl.BlockSpec()] * 6,
        scratch_shapes=[
            vm((3, DEPTH, padded), BF),
            vm((total, DEPTH), BF),
            vm((SLOT, total), BF),
            vm((total, DEPTH), BF),
            vm((DEPTH, padded), BF),
            vm((padded, DEPTH), BF),
            vm((padded, DEPTH), BF),
            vm((BLK, NEAR * UNIT), F32),
            vm((SLOT, padded), F32),
            vm((BLK, NEAR * UNIT), F32),
            vm((2, 8, DEPTH), F32),
            vm((total, DEPTH), F32),
            vm((total, DEPTH), F32),
        ],
        compiler_params=pltpu.CompilerParams(vmem_limit_bytes=62 * 2**20),
        name="attend_backward",
    )(plan, qkv, do, of, lse, table, bounds)

VEC = types.SimpleNamespace(
    first_gain=0, first_shift=1, first_up_bias=2, first_down_bias=3, mix_gain=4, mix_shift=5, mix_output_bias=6, filter_gain=7,
    filter_shift=8, pointwise_in_bias=9, batch_gain=10, batch_shift=11, pointwise_out_bias=12, second_gain=13, second_shift=14,
    second_up_bias=15, second_down_bias=16, final_gain=17, final_shift=18,
)
VEC_ROWS = 24
EPSILON = 1e-05
HALO = 64
TILE = 128
PIECE = 256


def col(cols_ref, i, size):
    return cols_ref[:size, i : i + 1]


def eye(n):
    return (iota((n, n), 0) == iota((n, n), 1)).astype(F32).astype(BF)


def flipped(mat):
    return dot(eye(mat.shape[1]), mat, NT).astype(BF)


def exact(a, b, dims=NN):
    return lax.dot_general(a, b, dims, precision=lax.Precision.HIGHEST, preferred_element_type=F32)


def folded(values):
    part = values[:, :TILE]
    for at in range(TILE, values.shape[1], TILE):
        part = part + values[:, at : at + TILE]
    return part


def row_sums(values):
    return exact(jnp.ones((8, TILE), F32), values, NT)


def norm(x):
    m = jnp.mean(x, axis=0, keepdims=True)
    c = x - m
    inv = lax.rsqrt(jnp.mean(c * c, axis=0, keepdims=True) + EPSILON)
    return c * inv, inv


def norm_back(e, n, inv, gain):
    ea = e * gain
    return inv * (ea - jnp.mean(ea, axis=0, keepdims=True) - n * jnp.mean(ea * n, axis=0, keepdims=True))


def sigmoid(v):
    return 0.5 + 0.5 * jnp.tanh(0.5 * v)


def ones_row(rows, lanes):
    return (iota((rows, lanes), 0) == 0).astype(F32).astype(BF)


def open_rows(frames_ref, up_ref, down_ref, mix_ref, x1_ref, h2_ref, qkv_ref, cols_ref, packed_rows, ship):
    width, rows = frames_ref.shape
    hidden = up_ref.shape[1]
    heads = qkv_ref.shape[0]
    up_t = flipped(up_ref[...])
    mix_t = dot(spread_cols(mix_ref.shape[1], heads, packed_rows, mix_ref.shape[1] // heads), mix_ref[...], NT).astype(BF)

    @pl.loop(0, rows // PIECE)
    def _(c):
        at = pl.ds(pl.multiple_of(c * PIECE, PIECE), PIECE)
        x0 = frames_ref[:, at].astype(F32)
        n, _ = norm(x0)
        h1 = (n * col(cols_ref, VEC.first_gain, width) + col(cols_ref, VEC.first_shift, width)).astype(BF)
        a1 = dot(up_t, h1) + col(cols_ref, VEC.first_up_bias, hidden)
        s1 = (a1 * sigmoid(a1)).astype(BF)
        x1 = x0 + 0.5 * (dot(down_ref[...], s1) + col(cols_ref, VEC.first_down_bias, width))
        x1_ref[:, at] = x1
        n, _ = norm(x1)
        h2 = (n * col(cols_ref, VEC.mix_gain, width) + col(cols_ref, VEC.mix_shift, width)).astype(BF)
        h2_ref[:, at] = h2
        qkv = dot(mix_t, h2).astype(BF)
        for h in range(heads):
            qkv_ref[h, :, at] = qkv[h * packed_rows : (h + 1) * packed_rows]
        ship(c)


def open_segments(len_ref, bound_ref, plan_ref, ext_ref, line):
    rows = ext_ref.shape[1] - TILE
    group = bound_ref.shape[1] - 2 * PAD
    slots = len_ref.shape[1]
    lengths = jnp.broadcast_to(len_ref[...].astype(F32), (8, slots))
    row, column = iota((slots, slots), 0), iota((slots, slots), 1)
    ends = exact((column <= row).astype(F32), lengths, NT)[:, :1].astype(jnp.int32)
    own_len = exact((column == row).astype(F32), lengths, NT)[:, :1].astype(jnp.int32)
    ends_row = exact(lengths, (row <= column).astype(F32))[:1].astype(jnp.int32)
    plan_ref[...] = block_plan(ends, ends_row, group)
    line[...] = jnp.full_like(line, -1)
    for edge in (slice(0, PAD), slice(PAD + group, 2 * PAD + group)):
        bound_ref[:, edge] = jnp.where(iota((2, PAD), 0) == 0, 1 << 20, -1)

    @pl.loop(0, group // 512)
    def _(c):
        at = pl.multiple_of(c * 512, 512)
        seg, first, stop = segment_rows(ends, own_len, iota((1, 512), 1) + at, group)
        line[:, pl.ds(at + TILE, 512)] = seg
        bound_ref[0:1, pl.ds(at + PAD, 512)] = first
        bound_ref[1:2, pl.ds(at + PAD, 512)] = stop

    first = pl.multiple_of(lax.axis_index("head") * rows, TILE)
    ext_ref[:, :rows] = line[:, pl.ds(first + TILE, rows)]
    left = line[:, pl.ds(first, TILE)]
    right = line[:, pl.ds(first + TILE + rows, TILE)]
    ext_ref[:, rows:] = jnp.where(iota((1, TILE), 1) < HALO, right, left)


def conv_masks(mask_ref, ext_ref):
    seg = jnp.broadcast_to(ext_ref[...], (8, ext_ref.shape[1]))
    lanes = seg.shape[1]
    reach = mask_ref.shape[0] // 2
    for i in range(mask_ref.shape[0]):
        mask_ref[i] = (pltpu.roll(seg, (reach - i) % lanes, 1) == seg).astype(F32)


def filter_kernel(x1_ref, x1l_ref, x1r_ref, o_ref, cols_ref, ext_ref, out_ref, pw_ref, taps_ref,
                  x2_ref, oc_ref, u_ref, y_ref, stat_ref, wide, mask, live_ref, h3s, n_ref, inv_ref, value_ref, gate_ref, *, head_width, slot_count, arrive):
    width, rows = x1_ref.shape
    lanes = rows + TILE
    heads = o_ref.shape[0]
    taps = taps_ref.shape[0]
    out_t = flipped(out_ref[...])
    pw_t = flipped(pw_ref[...])
    gather = spread_cols(width, heads, SLOT, head_width)
    seg = ext_ref[...]
    live = (seg >= 0) & (seg < slot_count)
    live_ref[...] = live.astype(F32)
    conv_masks(mask, ext_ref)
    wide_taps = taps_ref[...].astype(F32).T
    arrive()

    near = iota((1, TILE), 1) < HALO

    def extended(own, left, right):
        edge = jnp.where(near, right.astype(F32), left.astype(F32)).astype(own.dtype)
        return jnp.concatenate([own, edge], axis=1)

    x1 = extended(x1_ref[...], x1l_ref[...], x1r_ref[...])
    o = jnp.concatenate(
        [extended(o_ref[h, :, TILE : TILE + rows], o_ref[h, :, :TILE], o_ref[h, :, TILE + rows :]) for h in range(heads)], axis=0)
    oc = dot(gather, o, TN).astype(BF)
    x2 = x1 + (dot(out_t, oc) + col(cols_ref, VEC.mix_output_bias, width))
    n, inv = norm(x2)
    h3 = (n * col(cols_ref, VEC.filter_gain, width) + col(cols_ref, VEC.filter_shift, width)).astype(BF)
    g = dot(pw_t, h3) + col(cols_ref, VEC.pointwise_in_bias, 2 * width)
    gate = sigmoid(g[width:])
    u = jnp.where(live_ref[...] > 0.5, g[:width] * gate, 0.0).astype(BF)
    n_ref[...] = n[:, :rows]
    inv_ref[...] = inv[:, :rows]
    h3s[:width, :] = h3[:, :rows]
    value_ref[...] = g[:width, :rows]
    gate_ref[...] = gate[:, :rows]
    oc_ref[:width, :] = oc[:, :rows]
    x2_ref[...] = x2
    u_ref[...] = u
    wide[...] = u.astype(F32)

    own = (live & (iota((1, lanes), 1) < rows)).astype(F32)
    count = jnp.sum(own, axis=1, keepdims=True)
    safe = jnp.maximum(count, 1.0)
    for r in range(width // 8):
        sl = slice(8 * r, 8 * r + 8)
        u8 = wide[sl, :]
        acc = jnp.zeros((8, lanes), F32)
        for k in range(taps):
            moved = pltpu.roll(u8, (taps // 2 - k) % lanes, 1)
            acc = acc + wide_taps[sl, k : k + 1] * (moved * mask[k])
        y_ref[sl, :] = acc
    y = y_ref[...]
    part = folded(y * own)
    mean = exact(part, jnp.ones((TILE, TILE), F32)) / safe
    dev = (y - jnp.concatenate([mean] * (lanes // TILE), axis=1)) * own
    stat_ref[...] = two_rows(row_sums(part)[:1] / safe, row_sums(folded(dev * dev))[:1], count)


def two_rows(a, b, extra):
    rest = a.shape[1] - TILE
    tail = pad_lanes(jnp.concatenate([a[:, TILE:], b[:, TILE:]], axis=0))
    spot = (iota((2, TILE), 0) == 0) & (iota((2, TILE), 1) == rest)
    return jnp.concatenate([a[:, :TILE], b[:, :TILE], jnp.where(spot, extra, tail)], axis=0)


def all_rows(ref, width):
    rest = width - TILE
    values = ref[...]
    a = jnp.concatenate([values[:, 0, :], values[:, 2, :rest]], axis=1)
    b = jnp.concatenate([values[:, 1, :], values[:, 3, :rest]], axis=1)
    return a, b, values[:, 2, rest : rest + 1]


def total_stats(stats_ref, width):
    mean_of, spread_of, n = all_rows(stats_ref, width)
    count = jnp.sum(n, axis=0, keepdims=True)
    mean = jnp.sum(n * mean_of, axis=0, keepdims=True) / count
    gap = mean_of - mean
    spread = jnp.sum(spread_of + n * gap * gap, axis=0, keepdims=True)
    inv = lax.rsqrt(spread / count + EPSILON)
    table = jnp.concatenate([mean, inv, jnp.broadcast_to(count, (1, width)), jnp.zeros((5, width), F32)], axis=0).T
    return table[:, 0:1], table[:, 1:2], table[:, 2:3]


def second_kernel(x2_ref, y_ref, stats_ref, cot_ref, cotl_ref, cotr_ref, cols_ref, pwo_ref, up_ref, down_ref,
                  out_ref, dx3_ref, e_ref, sums_ref, pack_ref, small_ref,
                  h4s, das, s4s, dfs, ws, dcs, *, arrive, leave):
    width, rows = out_ref.shape
    hidden = up_ref.shape[1]
    pwo_t = flipped(pwo_ref[...])
    up_t = flipped(up_ref[...])
    down = flipped(down_ref[...])
    arrive()
    mean, inv_b, _ = total_stats(stats_ref, width)
    bgain = col(cols_ref, VEC.batch_gain, width)

    near = iota((1, TILE), 1) < HALO
    edge = jnp.where(near, cotr_ref[...].astype(F32), cotl_ref[...].astype(F32))
    cot = jnp.concatenate([cot_ref[...].astype(F32), edge], axis=1)
    zh = (y_ref[...] - mean) * inv_b
    z = zh * bgain + col(cols_ref, VEC.batch_shift, width)
    sig_z = sigmoid(z)
    w = (z * sig_z).astype(BF)
    x3 = x2_ref[...] + (dot(pwo_t, w) + col(cols_ref, VEC.pointwise_out_bias, width))
    n4, inv4 = norm(x3)
    h4 = (n4 * col(cols_ref, VEC.second_gain, width) + col(cols_ref, VEC.second_shift, width)).astype(BF)
    a4 = dot(up_t, h4) + col(cols_ref, VEC.second_up_bias, hidden)
    sig = sigmoid(a4)
    s4 = (a4 * sig).astype(BF)
    x4 = x3 + 0.5 * (dot(down_ref[...], s4) + col(cols_ref, VEC.second_down_bias, width))
    nf, invf = norm(x4)
    fgain = col(cols_ref, VEC.final_gain, width)
    dx4 = norm_back(cot, nf, invf, fgain)
    df = (0.5 * dx4).astype(BF)
    da = (dot(down, df) * (sig * (1.0 + a4 * (1.0 - sig)))).astype(BF)
    dh = dot(up_ref[...], da)
    dx3 = dx4 + norm_back(dh, n4, inv4, col(cols_ref, VEC.second_gain, width))
    dc = dx3.astype(BF)
    dz = dot(pwo_ref[...], dc) * (sig_z * (1.0 + z * (1.0 - sig_z)))
    e = dz * bgain
    e_ref[...] = e
    sums_ref[...] = two_rows(row_sums(folded(e[:, :rows]))[:1], row_sums(folded((e * zh)[:, :rows]))[:1], 0.0)
    leave()

    out_ref[...] = (nf * fgain + col(cols_ref, VEC.final_shift, width))[:, :rows].astype(BF)
    dx3_ref[...] = dx3[:, :rows]
    h4s[...] = h4[:, :rows]
    das[...] = da[:, :rows]
    s4s[:hidden, :] = s4[:, :rows]
    dfs[...] = df[:, :rows]
    ws[:width, :] = w[:, :rows]
    dcs[...] = dc[:, :rows]
    totals = [row_sums(folded(v[:, :rows]))[:1] for v in (dh * n4, dh, cot * nf, cot, dz * zh, dz)]
    s4s[hidden:, :] = ones_row(16, rows)
    ws[width:, :] = ones_row(16, rows)
    up_grad = dot(h4s[...], das[...], NT)
    up_bias = dot(ones_row(16, rows), das[...], NT)
    down_grad = dot(dfs[...], s4s[...], NT)
    pw_grad = dot(ws[...], dcs[...], NT)
    down_bias = exact(jnp.ones((8, rows), F32), dfs[...].astype(F32), NT)
    put_ff(pack_ref, up_grad, down_grad, 0)
    tall = 9 * width
    pack_ref[tall : tall + width, :] = pw_grad[:width, :TILE].astype(BF)
    pack_ref[tall + width : tall + 2 * width, :] = pad_lanes(pw_grad[:width, TILE:]).astype(BF)
    small_ref[...] = stack_rows(
        [totals[0], totals[1], up_bias[:1], down_bias[:1], totals[2], totals[3], totals[4], totals[5], pw_grad[width : width + 1]],
        small_ref.shape)


def pad_lanes(mat, lanes=TILE):
    if mat.shape[1] == lanes:
        return mat
    return jnp.concatenate([mat, jnp.zeros((mat.shape[0], lanes - mat.shape[1]), mat.dtype)], axis=1)


def stack_rows(rows, shape):
    parts = [pad_lanes(r, shape[1]) for r in rows]
    parts.append(jnp.zeros((shape[0] - len(rows), shape[1]), F32))
    return jnp.concatenate(parts, axis=0)


def put_ff(pack_ref, up_grad, down_grad_t, at):
    width, hidden = up_grad.shape
    whole = hidden // TILE
    for i in range(whole):
        pack_ref[at + i * width : at + (i + 1) * width, :] = up_grad[:, i * TILE : (i + 1) * TILE].astype(BF)
        j = whole + i
        pack_ref[at + j * width : at + (j + 1) * width, :] = down_grad_t[:, i * TILE : (i + 1) * TILE].astype(BF)
    rest = jnp.concatenate([up_grad[:, whole * TILE : hidden], down_grad_t[:, whole * TILE : hidden]], axis=1)
    pack_ref[at + 2 * whole * width : at + (2 * whole + 1) * width, :] = rest.astype(BF)


def unfilter_kernel(e_ref, y_ref, stats_ref, sums_ref, u_ref, dx3_ref, ocs, cols_ref, ext_ref, pw_ref, taps_ref,
                    out_ref, dx2_ref, do_ref, pack_ref, small_ref, tapg_ref,
                    dyw, du_s, mask, prod, h3s, dgs, dms, gains, live_ref, n_ref, inv_ref, value_ref, gate_ref, *, head_width, ship, arrive):
    width, rows = dx3_ref.shape
    lanes = rows + TILE
    heads = do_ref.shape[0]
    taps = taps_ref.shape[0]
    tap_cols = taps_ref[...].astype(F32).T
    out_w = dot(spread_cols(width, heads, SLOT, head_width), out_ref[...]).astype(BF)
    gains[...] = jnp.zeros_like(gains)
    fgain = col(cols_ref, VEC.filter_gain, width)
    mean, inv_b, count = total_stats(stats_ref, width)
    arrive()
    one_of, two_of, _ = all_rows(sums_ref, width)
    sums = jnp.concatenate([jnp.sum(one_of, axis=0, keepdims=True), jnp.sum(two_of, axis=0, keepdims=True), jnp.zeros((6, width), F32)], axis=0).T
    s1, s2 = sums[:, 0:1], sums[:, 1:2]
    seg = ext_ref[...]
    live = live_ref[...]
    zh = (y_ref[...] - mean) * inv_b
    dy = inv_b * (e_ref[...] - live * ((s1 + zh * s2) / count))
    dyw[...] = jnp.where(seg >= 0, dy, 0.0).astype(BF).astype(F32)

    for r in range(width // 8):
        sl = slice(8 * r, 8 * r + 8)
        dy8 = dyw[sl, :]
        u8 = u_ref[16 * (r // 2) : 16 * (r // 2) + 16, :rows].astype(F32)[8 * (r % 2) : 8 * (r % 2) + 8]
        acc = jnp.zeros((8, rows), F32)
        for k in range(taps):
            moved = pltpu.roll(dy8, (k - taps // 2) % lanes, 1)[:, :rows] * mask[taps - k][:, :rows]
            acc = acc + tap_cols[sl, k : k + 1] * moved
            hit = moved * u8
            prod[k, sl, :] = folded(hit)
        du_s[sl, :] = acc

    @pl.loop(0, rows // PIECE)
    def _(c):
        at = pl.ds(pl.multiple_of(c * PIECE, PIECE), PIECE)
        n, inv = n_ref[:, at], inv_ref[:, at]
        gate = gate_ref[:, at]
        t = live_ref[:, at] * du_s[:, at] * gate
        dg = jnp.concatenate([t, t * value_ref[:, at] * (1.0 - gate)], axis=0).astype(BF)
        dh = dot(pw_ref[...], dg)
        dx2 = dx3_ref[:, at] + norm_back(dh, n, inv, fgain)
        dx2_ref[:, at] = dx2
        dm = dx2.astype(BF)
        do = dot(out_w, dm).astype(BF)
        for h in range(heads):
            do_ref[h, :, at] = do[h * SLOT : (h + 1) * SLOT]
        ship(c)
        dgs[:, at] = dg
        dms[:, at] = dm
        for i, v in enumerate((dh * n, dh)):
            gains[i] += folded(v)

    whole = prod[...].reshape(taps * width, TILE)
    hi = whole.astype(BF)
    lo = (whole - hi.astype(F32)).astype(BF)
    ones = jnp.ones((8, TILE), BF)
    lines = dot(ones, hi, NT) + dot(ones, lo, NT)
    for k in range(taps):
        tapg_ref[k : k + 1, :] = lines[:1, k * width : (k + 1) * width]

    h3s[width:, :] = ones_row(16, rows)
    ocs[width:, :] = ones_row(16, rows)
    pw_grad = dot(h3s[...], dgs[...], NT)
    out_grad = dot(ocs[...], dms[...], NT)
    at = 0
    for lo in range(0, 2 * width, TILE):
        pack_ref[at : at + width, :] = pad_lanes(pw_grad[:width, lo : min(lo + TILE, 2 * width)]).astype(BF)
        at += width
    for lo in range(0, width, TILE):
        pack_ref[at : at + width, :] = pad_lanes(out_grad[:width, lo : min(lo + TILE, width)]).astype(BF)
        at += width
    small_ref[...] = stack_rows(
        [row_sums(gains[0])[:1], row_sums(gains[1])[:1], pw_grad[width : width + 1], out_grad[width : width + 1]], small_ref.shape)


def close_kernel(frames_ref, x1_ref, h2_ref, dx2_ref, dqkv_ref, dtab_ref, cols_ref, up_ref, down_ref, mix_ref,
                 grad_ref, pack_ref, h1s, das, s1s, dfs, dqs, gains, up_part, down_part, mix_part, *, arrive, between, mixed):
    width, rows = frames_ref.shape
    most = slice(0, rows - PIECE)
    hidden = up_ref.shape[1]
    heads, packed_rows, _ = dqkv_ref.shape
    up_t = flipped(up_ref[...])
    down = flipped(down_ref[...])
    hot = spread_cols(mix_ref.shape[1], heads, packed_rows, mix_ref.shape[1] // heads)
    mix_w = dot(mix_ref[...], hot, NT).astype(BF)
    gains[...] = jnp.zeros_like(gains)
    mgain = col(cols_ref, VEC.mix_gain, width)
    fgain = col(cols_ref, VEC.first_gain, width)

    @pl.loop(0, rows // PIECE)
    def _(c):
        arrive(c)
        at = pl.ds(pl.multiple_of(c * PIECE, PIECE), PIECE)
        dq = jnp.concatenate([dqkv_ref[h, :, at] for h in range(heads)], axis=0)
        dqs[:, at] = dq
        dh2 = dot(mix_w, dq)
        n2, inv2 = norm(x1_ref[:, at])
        dx1 = dx2_ref[:, at] + norm_back(dh2, n2, inv2, mgain)
        x0 = frames_ref[:, at].astype(F32)
        n1, inv1 = norm(x0)
        h1 = (n1 * fgain + col(cols_ref, VEC.first_shift, width)).astype(BF)
        a1 = dot(up_t, h1) + col(cols_ref, VEC.first_up_bias, hidden)
        sig = sigmoid(a1)
        s1s[:, at] = (a1 * sig).astype(BF)
        df = (0.5 * dx1).astype(BF)
        da = (dot(down, df) * (sig * (1.0 + a1 * (1.0 - sig)))).astype(BF)
        dh1 = dot(up_ref[...], da)
        grad_ref[:, at] = dx1 + norm_back(dh1, n1, inv1, fgain)
        h1s[:, at] = h1
        das[:, at] = da
        dfs[:, at] = df
        for i, v in enumerate((dh1 * n1, dh1, dh2 * n2, dh2)):
            gains[i] += folded(v)
        between(c)

        @pl.when(c == rows // PIECE - 2)
        def _():
            up_part[...] = dot(h1s[:, most], das[:, most], NT)
            down_part[...] = dot(dfs[:, most], s1s[:, most], NT)
            mix_part[...] = dot(h2_ref[:, most], dqs[:, most], NT)

    rest = slice(rows - PIECE, rows)
    mix_grad = dot((mix_part[...] + dot(h2_ref[:, rest], dqs[:, rest], NT)).astype(BF), hot)
    at = 0
    for lo in range(0, mix_grad.shape[1], TILE):
        pack_ref[at : at + width, :] = pad_lanes(mix_grad[:, lo : min(lo + TILE, mix_grad.shape[1])]).astype(BF)
        at += width
    mixed()
    up_grad = up_part[...] + dot(h1s[:, rest], das[:, rest], NT)
    up_bias = dot(ones_row(16, rows), das[...], NT)
    down_grad = down_part[...] + dot(dfs[:, rest], s1s[:, rest], NT)
    down_bias = exact(jnp.ones((8, rows), F32), dfs[...].astype(F32), NT)
    put_ff(pack_ref, up_grad, down_grad, at)
    at += (2 * (hidden // TILE) + 1) * width
    totals = [row_sums(gains[i])[:1] for i in range(4)]
    small = stack_rows([totals[0], totals[1], up_bias[:1], down_bias[:1], totals[2], totals[3]], (16, 5 * TILE))
    at = put_small(pack_ref, small, at)
    span = dtab_ref.shape[1]
    table = jnp.where(iota((16, span), 0) == lax.axis_index("head"), dtab_ref[...], 0.0)
    pack_ref[at : at + 16, :] = table.astype(BF)
    if at + 16 < pack_ref.shape[0]:
        pack_ref[at + 16 :, :] = jnp.zeros((pack_ref.shape[0] - at - 16, TILE), BF)


def put_small(pack_ref, small, at):
    for lo in range(0, small.shape[1], TILE):
        pack_ref[at : at + small.shape[0], :] = small[:, lo : lo + TILE].astype(BF)
        at += small.shape[0]
    return at


def put_taps(pack_ref, tapg, at):
    taps = tapg.shape[0]
    pack_ref[at : at + taps, :] = tapg[:, :TILE].astype(BF)
    pack_ref[at + taps : at + 2 * taps, :] = pad_lanes(tapg[:, TILE:]).astype(BF)
    return at + 2 * taps


def unpack_kernel(pack_ref, out_ref, grad_ref, *refs, layout):
    refs[0][...] = out_ref[...]
    refs[1][...] = grad_ref[...]
    out_refs = refs[2:]
    given = Weights(*out_refs)

    def wide(at, rows, lanes):
        parts = [pack_ref[at + i * rows : at + (i + 1) * rows, :].astype(F32) for i in range(-(-lanes // TILE))]
        return jnp.concatenate(parts, axis=1)[:, :lanes]

    for at, up_ref, down_ref in ((layout.first, given.first_up, given.first_down), (layout.second, given.second_up, given.second_down)):
        width, hidden = up_ref.shape
        whole = hidden // TILE
        half = hidden - whole * TILE
        piece = lambda i: pack_ref[at + i * width : at + (i + 1) * width, :].astype(F32)
        rest = piece(2 * whole)
        up_ref[...] = jnp.concatenate([piece(i) for i in range(whole)] + [rest[:, :half]], axis=1)
        down_ref[...] = jnp.concatenate([piece(whole + i) for i in range(whole)] + [rest[:, half:]], axis=1)
    for ref, at in ((given.mix_inputs, layout.mix_inputs), (given.pointwise_in, layout.pointwise_in), (given.mix_output, layout.mix_output),
                    (given.pointwise_out, layout.pointwise_out), (given.depthwise_taps, layout.taps)):
        ref[...] = wide(at, *ref.shape)
    given.position_bias[...] = pack_ref[layout.table : layout.table + 16, :].astype(F32)[: given.position_bias.shape[0]]
    late = wide(layout.small_late, 16, 5 * TILE)
    early = wide(layout.small, 32, 5 * TILE)
    late_rows = (
        given.first_gain, given.first_shift, given.first_up_bias, given.first_down_bias, given.mix_gain, given.mix_shift,
    )
    second_rows = (
        given.second_gain, given.second_shift, given.second_up_bias, given.second_down_bias, given.final_gain, given.final_shift,
        given.batch_gain, given.batch_shift, given.pointwise_out_bias,
    )
    filter_rows = (given.filter_gain, given.filter_shift, given.pointwise_in_bias, given.mix_output_bias)
    for small, first, refs in ((late, 0, late_rows), (early, 0, second_rows), (early, 16, filter_rows)):
        for row, ref in enumerate(refs, first):
            ref[...] = small[row : row + 1, : ref.shape[0]].reshape(ref.shape)


@dataclasses.dataclass
class Weights:
    first_gain: object
    first_shift: object
    first_up: object
    first_up_bias: object
    first_down: object
    first_down_bias: object
    mix_gain: object
    mix_shift: object
    mix_inputs: object
    position_bias: object
    mix_output: object
    mix_output_bias: object
    filter_gain: object
    filter_shift: object
    pointwise_in: object
    pointwise_in_bias: object
    depthwise_taps: object
    batch_gain: object
    batch_shift: object
    pointwise_out: object
    pointwise_out_bias: object
    second_gain: object
    second_shift: object
    second_up: object
    second_up_bias: object
    second_down: object
    second_down_bias: object
    final_gain: object
    final_shift: object


def pack_layout(width, hidden, mix_width, taps, devices):
    ff = (2 * (hidden // TILE) + 1) * width
    chunks = lambda lanes: -(-lanes // TILE) * width
    unit = 16 * devices
    whole = lambda rows: -(-rows // unit) * unit
    at = types.SimpleNamespace(second=0, pointwise_out=ff)
    at.pointwise_in = ff + chunks(width)
    at.mix_output = at.pointwise_in + chunks(2 * width)
    at.taps = at.mix_output + chunks(width)
    at.small = at.taps + 2 * taps
    at.late = at.mix_inputs = whole(at.small + 32 * 5)
    at.last = at.late + chunks(mix_width) // unit * unit
    at.first = at.mix_inputs + chunks(mix_width)
    at.small_late = at.first + ff
    at.table = at.small_late + 16 * 5
    at.rows = at.late + whole(at.table + 16 - at.late)
    return at


MESH = pl.DeviceIdType.MESH


def meet(peers):
    barrier = pltpu.get_barrier_semaphore()
    for peer in peers:
        pl.semaphore_signal(barrier, inc=1, device_id=peer, device_id_type=MESH)
    pl.semaphore_wait(barrier, len(peers))


def head_peers(n):
    me = lax.axis_index("head")
    return me, [{"head": lax.rem(me + s, n)} for s in range(1, n)], [lax.rem(me + s, n) for s in range(1, n)]


def opening_kernel(frames_ref, len_ref, up_ref, down_ref, mix_ref, *refs, packed_rows, n):
    count = len(VEC.__dict__)
    vec_refs, refs = refs[:count], refs[count:]
    (cot_ref, x1_ref, h2_ref, cols_ref, bound_ref, plan_ref, ext_ref, all_ref, x1l_ref, x1r_ref, cotl_ref, cotr_ref,
     qkv, line, send, recv, local, hsend, hrecv) = refs
    me, peers, ids = head_peers(n)
    rows = cot_ref.shape[1]
    barrier = pltpu.get_barrier_semaphore()
    for peer in peers:
        pl.semaphore_signal(barrier, inc=1, device_id=peer, device_id_type=MESH)
    vecs = [ref[...].astype(F32).reshape(1, ref.shape[0]) for ref in vec_refs]
    cols_ref[...] = stack_rows(vecs, (VEC_ROWS, up_ref.shape[1])).T
    pl.semaphore_wait(barrier, len(peers))

    def piece(c, s):
        at = pl.ds(pl.multiple_of(c * PIECE, PIECE), PIECE)
        return pltpu.make_async_remote_copy(src_ref=qkv.at[ids[s], :, at], dst_ref=all_ref.at[me, :, at], send_sem=send.at[c, s],
                                            recv_sem=recv.at[c, s], device_id=peers[s], device_id_type=MESH)

    def ship(c):
        for s in range(n - 1):
            piece(c, s).start()

    open_rows(frames_ref, up_ref, down_ref, mix_ref, x1_ref, h2_ref, qkv, cols_ref, packed_rows, ship)
    own = pltpu.make_async_copy(qkv.at[me], all_ref.at[me], local)
    own.start()

    def edge(i, src, dst, head):
        return pltpu.make_async_remote_copy(src_ref=src, dst_ref=dst, send_sem=hsend.at[i], recv_sem=hrecv.at[i],
                                            device_id={"head": head}, device_id_type=MESH)

    up = lax.rem(me + 1, n)
    down = lax.rem(me + n - 1, n)
    last, start = pl.ds(rows - TILE, TILE), pl.ds(0, TILE)
    to_right = [edge(0, x1_ref.at[:, last], x1l_ref, up), edge(1, cot_ref.at[:, last], cotl_ref, up)]
    to_left = [edge(2, x1_ref.at[:, start], x1r_ref, down), edge(3, cot_ref.at[:, start], cotr_ref, down)]

    @pl.when(me < n - 1)
    def _():
        for c in to_right:
            c.start()

    @pl.when(me > 0)
    def _():
        for c in to_left:
            c.start()

    open_segments(len_ref, bound_ref, plan_ref, ext_ref, line)
    own.wait()

    @pl.loop(0, rows // PIECE)
    def _(c):
        for s in range(n - 1):
            piece(c, s).wait()

    @pl.when(me < n - 1)
    def _():
        for c in to_right:
            c.wait_send()
        for c in to_left:
            c.wait_recv()

    @pl.when(me > 0)
    def _():
        for c in to_left:
            c.wait_send()
        for c in to_right:
            c.wait_recv()


def everyone(n_tm, n_head):
    n = n_tm * n_head
    me = lax.axis_index("tm") * n_head + lax.axis_index("head")

    def place(s):
        peer = lax.rem(me + s, n)
        return {"tm": peer // n_head, "head": lax.rem(peer, n_head)}

    return me, n, place


def tell(src_ref, all_ref, send, recv, n_tm, n_head):
    me, n, place = everyone(n_tm, n_head)

    def copy(s):
        return pltpu.make_async_remote_copy(src_ref=src_ref, dst_ref=all_ref.at[me], send_sem=send.at[s], recv_sem=recv.at[s],
                                            device_id=place(s), device_id_type=MESH)

    def start():
        pl.loop(1, n)(lambda s: copy(s).start())
        all_ref[me] = src_ref[...]

    def end():
        pl.loop(1, n)(lambda s: copy(s).wait())

    return start, end


def load_all(sources, targets, sems):
    copies = [pltpu.make_async_copy(src, dst, sems.at[i]) for i, (src, dst) in enumerate(zip(sources, targets))]
    for copy in copies:
        copy.start()
    return copies


def middle_kernel(*refs, n_tm, n_head, head_width, slot_count, layout):
    o_ref, sources, refs = refs[0], refs[1:15], refs[15:]
    (out_ref, dx2_ref, do_all, pack_ref), refs = refs[:4], refs[4:]
    loaded, refs = refs[:14], refs[14:]
    (x1_ref, x1l_ref, x1r_ref, cot_ref, cotl_ref, cotr_ref, cols_ref, ext_ref, mixo_ref, pwi_ref, taps_ref, pwo_ref, up_ref,
     down_ref) = loaded
    (o_own, x2, oc, u, y, stat, stats, dx3, e, sums, all_sums, do, wide, mask, live,
     h4s, das, s4s, dfs, ws, dcs, dyw, du, prod, h3s, dgs, dms, gains2, smalld, smalle, tapg,
     n3, inv3, value3, gate3), refs = refs[:35], refs[35:]
    (load_sems, send_o, recv_o, local_o, send_a, recv_a, send_b, recv_b, send_d, recv_d, local_d) = refs
    me, peers, ids = head_peers(n_head)
    _, n, place = everyone(n_tm, n_head)
    barrier = pltpu.get_barrier_semaphore()
    rows = x1_ref.shape[1]

    @pl.loop(1, n)
    def _(s):
        pl.semaphore_signal(barrier, inc=1, device_id=place(s), device_id_type=MESH)

    loads = load_all(sources, loaded, load_sems)
    pl.semaphore_wait(barrier, n - 1)

    def part(p):
        return o_ref.at[:, pl.ds(pl.multiple_of(p * rows, TILE), rows + 2 * TILE)]

    copies = [
        pltpu.make_async_remote_copy(src_ref=part(p), dst_ref=o_own.at[me], send_sem=send_o.at[s], recv_sem=recv_o.at[s],
                                     device_id=peer, device_id_type=MESH)
        for s, (peer, p) in enumerate(zip(peers, ids))
    ]
    for copy in copies:
        copy.start()
    own = pltpu.make_async_copy(part(me), o_own.at[me], local_o)
    own.start()
    for load in loads:
        load.wait()

    def arrive():
        own.wait()
        for copy in copies:
            copy.wait()

    filter_kernel(x1_ref, x1l_ref, x1r_ref, o_own, cols_ref, ext_ref, mixo_ref, pwi_ref, taps_ref, x2, oc, u, y, stat, wide, mask, live,
                  h3s, n3, inv3, value3, gate3, head_width=head_width, slot_count=slot_count, arrive=arrive)
    stats_out, stats_in = tell(stat, stats, send_a, recv_a, n_tm, n_head)
    sums_out, sums_in = tell(sums, all_sums, send_b, recv_b, n_tm, n_head)
    stats_out()
    second_kernel(x2, y, stats, cot_ref, cotl_ref, cotr_ref, cols_ref, pwo_ref, up_ref, down_ref,
                  out_ref, dx3, e, sums, pack_ref, smalld, h4s, das, s4s, dfs, ws, dcs, arrive=stats_in, leave=sums_out)

    def piece(c, s):
        at = pl.ds(pl.multiple_of(c * PIECE, PIECE), PIECE)
        return pltpu.make_async_remote_copy(src_ref=do.at[ids[s], :, at], dst_ref=do_all.at[me, :, at], send_sem=send_d.at[c, s],
                                            recv_sem=recv_d.at[c, s], device_id=peers[s], device_id_type=MESH)

    def ship(c):
        for s in range(n_head - 1):
            piece(c, s).start()

    unfilter_kernel(e, y, stats, all_sums, u, dx3, oc, cols_ref, ext_ref, pwi_ref, taps_ref, mixo_ref,
                    dx2_ref, do, pack_ref.at[pl.ds(layout.pointwise_in, layout.taps - layout.pointwise_in)], smalle, tapg, dyw, du, mask, prod, h3s, dgs, dms, gains2, live, n3, inv3, value3, gate3,
                    head_width=head_width, ship=ship, arrive=sums_in)
    own = pltpu.make_async_copy(do.at[me], do_all.at[me], local_d)
    own.start()
    end = put_taps(pack_ref, tapg[...], layout.taps)
    end = put_small(pack_ref, jnp.concatenate([smalld[...], smalle[...]], axis=0), end)
    if end < pack_ref.shape[0]:
        pack_ref[end:, :] = jnp.zeros((pack_ref.shape[0] - end, TILE), BF)
    own.wait()

    @pl.loop(0, rows // PIECE)
    def _(c):
        for s in range(n_head - 1):
            piece(c, s).wait()


def sum_scratch(count, n_tm, n_head):
    half = count // 2
    big = half // (n_tm // 2)
    shapes = [(half, TILE), (half, TILE), (n_tm // 2, big, TILE), (big, TILE), (n_head, big // n_head, TILE), (big, TILE), (half, TILE)]
    return [pltpu.VMEM(shape, BF) for shape in shapes]


def gradient_sum(src_ref, out_ref, first, scratch, sems, local, n_tm, n_head):
    got0, half, got1, part1, got2, part2, whole = scratch
    tm, head = lax.axis_index("tm"), lax.axis_index("head")
    n_chip = n_tm // 2
    chip, core = tm // 2, lax.rem(tm, 2)
    size = src_ref.shape[0] // 2
    big = size // n_chip
    small = big // n_head
    sibling = {"tm": chip * 2 + 1 - core}

    def rows(i, count, base=0):
        return pl.ds(pl.multiple_of(base + i * count, 16), count)

    def send(src, dst, phase, s, peer):
        return pltpu.make_async_remote_copy(src_ref=src, dst_ref=dst, send_sem=sems.at[2 * phase, s], recv_sem=sems.at[2 * phase + 1, s],
                                            device_id=peer, device_id_type=MESH)

    def chip_peer(s):
        return lax.rem(chip + s, n_chip)

    def head_peer(s):
        return lax.rem(head + s, n_head)

    def zero():
        return send(src_ref.at[rows(1 - core, size)], got0, 0, 0, sibling)

    def one(s):
        return send(half.at[rows(chip_peer(s), big)], got1.at[s], 1, s, {"tm": chip_peer(s) * 2 + core})

    def two(s):
        return send(part1.at[rows(head_peer(s), small)], got2.at[s], 2, s, {"head": head_peer(s)})

    def three(s):
        at = part2.at[rows(head, small)]
        return send(at, at, 3, s, {"head": head_peer(s)})

    def four(s):
        return send(part2, whole.at[rows(chip, big)], 4, s, {"tm": chip_peer(s) * 2 + core})

    def five():
        return send(whole, out_ref.at[rows(core, size, first)], 5, 0, sibling)

    def keep():
        return pltpu.make_async_copy(whole, out_ref.at[rows(core, size, first)], local)

    def added(got, n):
        total = got[0].astype(F32)
        for s in range(1, n):
            total = total + got[s].astype(F32)
        return total.astype(BF)

    def step0():
        zero().start()

    def step1():
        zero().wait()
        half[...] = (src_ref[rows(core, size), :].astype(F32) + got0[...].astype(F32)).astype(BF)
        pl.loop(1, n_chip)(lambda s: one(s).start())
        got1[0] = half[rows(chip, big), :]

    def step2():
        pl.loop(1, n_chip)(lambda s: one(s).wait())
        part1[...] = added(got1, n_chip)
        pl.loop(1, n_head)(lambda s: two(s).start())
        got2[0] = part1[rows(head, small), :]

    def step3():
        pl.loop(1, n_head)(lambda s: two(s).wait())
        part2[rows(head, small), :] = added(got2, n_head)
        pl.loop(1, n_head)(lambda s: three(s).start())

    def step4():
        pl.loop(1, n_head)(lambda s: three(s).wait())
        pl.loop(1, n_chip)(lambda s: four(s).start())
        whole[rows(chip, big), :] = part2[...]

    def step5():
        pl.loop(1, n_chip)(lambda s: four(s).wait())
        five().start()
        keep().start()

    def step6():
        keep().wait()
        five().wait()

    return step0, step1, step2, step3, step4, step5, step6


def final_kernel(*refs, n_tm, n_head, parts):
    dqkv_ref, sources, refs = refs[0], refs[1:11], refs[11:]
    (grad_ref, total_ref), loaded, refs = refs[:2], refs[2:12], refs[12:]
    early_ref, frames_ref, x1_ref, h2_ref, dx2_ref, dtab_ref, cols_ref, up_ref, down_ref, mix_ref = loaded
    (dqkv, late, h1s, das, s1s, dfs, dqs, gains, up_part, down_part, mix_part), refs = refs[:11], refs[11:]
    sum_refs = [refs[7 * i : 7 * i + 7] for i in range(3)]
    load_sems, send_q, recv_q, local_q, sum_sems, sum_local = refs[21:]
    me, peers, ids = head_peers(n_head)
    tm = lax.axis_index("tm")
    rows = x1_ref.shape[1]
    barrier = pltpu.get_barrier_semaphore()
    for peer in peers:
        pl.semaphore_signal(barrier, inc=1, device_id=peer, device_id_type=MESH)

    @pl.loop(1, n_tm)
    def _(s):
        pl.semaphore_signal(barrier, inc=1, device_id={"tm": lax.rem(tm + s, n_tm)}, device_id_type=MESH)

    loads = load_all(sources, loaded, load_sems)
    pl.semaphore_wait(barrier, n_head + n_tm - 2)

    def piece(c, s):
        at = pl.ds(pl.multiple_of(c * PIECE, PIECE), PIECE)
        return pltpu.make_async_remote_copy(src_ref=dqkv_ref.at[ids[s], :, at], dst_ref=dqkv.at[me, :, at], send_sem=send_q.at[c, s],
                                            recv_sem=recv_q.at[c, s], device_id=peers[s], device_id_type=MESH)

    @pl.loop(0, rows // PIECE)
    def _(c):
        for s in range(n_head - 1):
            piece(c, s).start()

    own = pltpu.make_async_copy(dqkv_ref.at[me], dqkv.at[me], local_q)
    own.start()
    for load in loads:
        load.wait()
    late_at, last_at, end = parts

    def summed(i, src, first):
        return gradient_sum(src, total_ref, first, sum_refs[i], sum_sems.at[i], sum_local.at[i], n_tm, n_head)

    early = summed(0, early_ref, 0)
    last = summed(2, late.at[pl.ds(last_at - late_at, end - last_at)], last_at)
    late_sum = summed(1, late.at[pl.ds(0, last_at - late_at)], late_at) if last_at > late_at else [lambda: None] * 7
    early[0]()
    early[1]()
    own.wait()

    def arrive(c):
        for s in range(n_head - 1):
            piece(c, s).wait()

    def between(c):
        pl.when(c == 0)(early[2])

    def mixed():
        early[3]()
        late_sum[0]()

    close_kernel(frames_ref, x1_ref, h2_ref, dx2_ref, dqkv, dtab_ref, cols_ref, up_ref, down_ref, mix_ref,
                 grad_ref, late, h1s, das, s1s, dfs, dqs, gains, up_part, down_part, mix_part, arrive=arrive, between=between, mixed=mixed)
    for step in (last[0], late_sum[1], last[1], late_sum[2], last[2], early[4], late_sum[3], last[3], late_sum[4], early[5], last[4],
                 late_sum[5], early[6], last[5], late_sum[6], last[6]):
        step()


VMEM_MIB = 62


def body(
    frames, lengths, first_gain, first_shift, first_up, first_up_bias, first_down, first_down_bias, mix_gain, mix_shift,
    mix_inputs, position_bias, mix_output, mix_output_bias, filter_gain, filter_shift, pointwise_in, pointwise_in_bias,
    depthwise_taps, batch_gain, batch_shift, pointwise_out, pointwise_out_bias, second_gain, second_shift, second_up,
    second_up_bias, second_down, second_down_bias, final_gain, final_shift, cotangent,
):
    weights = Weights(
        first_gain, first_shift, first_up, first_up_bias, first_down, first_down_bias, mix_gain, mix_shift, mix_inputs, position_bias,
        mix_output, mix_output_bias, filter_gain, filter_shift, pointwise_in, pointwise_in_bias, depthwise_taps, batch_gain,
        batch_shift, pointwise_out, pointwise_out_bias, second_gain, second_shift, second_up, second_up_bias, second_down,
        second_down_bias, final_gain, final_shift)
    rows, width = frames.shape
    hidden = first_up.shape[1]
    n_head, n_tm = lax.axis_size("head"), lax.axis_size("tm")
    heads, span = position_bias.shape
    head_width = width // heads
    packed_rows = -(-3 * head_width // 16) * 16
    group = rows * n_head
    lanes = rows + TILE
    slots = lengths.shape[1]
    taps = depthwise_taps.shape[0]
    layout = pack_layout(width, hidden, mix_inputs.shape[1], taps, n_tm * n_head)

    vectors = tuple(getattr(weights, name) for name in VEC.__dict__)
    frames_t, cot_t, first_down_t, second_down_t = frames.T, cotangent.T, first_down.T, second_down.T
    vm, dma, hbm = pltpu.VMEM, pltpu.SemaphoreType.DMA, pl.BlockSpec(memory_space=pl.ANY)
    steps = rows // PIECE
    piece_sems = dma((steps, n_head - 1))

    def comm_call(kernel, name, collective_id, ins, in_hbm, outs, out_hbm, scratch):
        return pl.pallas_call(
            kernel,
            out_shape=tuple(jax.ShapeDtypeStruct(s, t) for s, t in outs),
            in_specs=[hbm if i in in_hbm else pl.BlockSpec() for i in range(len(ins))],
            out_specs=tuple(hbm if i in out_hbm else pl.BlockSpec() for i in range(len(outs))),
            scratch_shapes=scratch,
            compiler_params=pltpu.CompilerParams(collective_id=collective_id, has_side_effects=True, vmem_limit_bytes=VMEM_MIB * 2**20),
            name=name,
        )(*ins)

    ins = (frames_t, lengths, first_up, first_down_t, mix_inputs) + vectors + (cot_t,)
    x1, h2, cols, bounds, plan, ext, qkv_all, x1l, x1r, cotl, cotr = comm_call(
        functools.partial(opening_kernel, packed_rows=packed_rows, n=n_head), "opening", 1, ins, (len(ins) - 1,),
        [((width, rows), F32), ((width, rows), BF), ((hidden, VEC_ROWS), F32), ((2, group + 2 * PAD), jnp.int32),
         ((group // BLK, 128), jnp.int32), ((1, lanes), jnp.int32), ((n_head, packed_rows, rows), BF),
         ((width, TILE), F32), ((width, TILE), F32), ((width, TILE), BF), ((width, TILE), BF)], range(6, 11),
        [vm((n_head, packed_rows, rows), BF), vm((1, group + 2 * TILE), jnp.int32), piece_sems, piece_sems, dma, dma((4,)), dma((4,))])
    o, of, lse = attend_forward(qkv_all, bounds, plan, position_bias, head_width)
    everyone_sems = dma((n_tm * n_head,))
    ins = (x1, x1l, x1r, cot_t, cotl, cotr, cols, ext, mix_output, pointwise_in, depthwise_taps, pointwise_out, second_up, second_down_t)
    out, dx2, do_all, pack = comm_call(
        functools.partial(middle_kernel, n_tm=n_tm, n_head=n_head, head_width=head_width, slot_count=slots, layout=layout),
        "middle", 2, (o,) + ins, range(len(ins) + 1),
        [((width, rows), BF), ((width, rows), F32), ((n_head, SLOT, rows), BF), ((layout.late, TILE), BF)],
        (2,),
        [vm(a.shape, a.dtype) for a in ins] + [
            vm((n_head, SLOT, rows + 2 * TILE), BF), vm((width, lanes), F32), vm((width + 16, rows), BF), vm((width, lanes), BF),
            vm((width, lanes), F32), vm((4, TILE), F32), vm((n_tm * n_head, 4, TILE), F32), vm((width, rows), F32),
            vm((width, lanes), F32), vm((4, TILE), F32), vm((n_tm * n_head, 4, TILE), F32), vm((n_head, SLOT, rows), BF),
            vm((width, lanes), F32), vm((taps + 1, 8, lanes), F32), vm((1, lanes), F32),
            vm((width, rows), BF), vm((hidden, rows), BF), vm((hidden + 16, rows), BF), vm((width, rows), BF),
            vm((width + 16, rows), BF), vm((width, rows), BF),
            vm((width, lanes), F32), vm((width, rows), F32), vm((taps, width, TILE), F32), vm((width + 16, rows), BF),
            vm((2 * width, rows), BF), vm((width, rows), BF), vm((2, width, TILE), F32),
            vm((16, 5 * TILE), F32), vm((16, 5 * TILE), F32), vm((taps, width), F32),
            vm((width, rows), F32), vm((1, rows), F32), vm((width, rows), F32), vm((width, rows), F32),
            dma((len(ins),)), dma((n_head - 1,)), dma((n_head - 1,)), dma, everyone_sems, everyone_sems, everyone_sems, everyone_sems,
            piece_sems, piece_sems, dma,
        ])
    dqkv, dtab = attend_backward(qkv_all, do_all, of, lse, bounds, plan, position_bias, head_width)
    parts = (layout.late, layout.last, layout.rows)
    sizes = (layout.late, max(layout.last - layout.late, 16 * n_tm * n_head), layout.rows - layout.last)
    ins = (pack, frames_t, x1, h2, dx2, dtab, cols, first_up, first_down_t, mix_inputs)
    grad, total = comm_call(
        functools.partial(final_kernel, n_tm=n_tm, n_head=n_head, parts=parts), "final", 3, (dqkv,) + ins, range(len(ins) + 1),
        [((width, rows), F32), ((layout.rows, TILE), BF)], (1,),
        [vm(a.shape, a.dtype) for a in ins] + [
            vm((n_head, packed_rows, rows), BF), vm((layout.rows - layout.late, TILE), BF),
            vm((width, rows), BF), vm((hidden, rows), BF), vm((hidden, rows), BF), vm((width, rows), BF),
            vm((n_head * packed_rows, rows), BF), vm((4, width, TILE), F32), vm((width, hidden), F32), vm((width, hidden), F32),
            vm((width, n_head * packed_rows), F32),
            *[s for size in sizes for s in sum_scratch(size, n_tm, n_head)],
            dma((len(ins),)), piece_sems, piece_sems, dma, dma((3, 12, max(n_tm // 2, n_head))), dma((3,)),
        ])
    shapes = Weights(**{n: w.shape for n, w in weights.__dict__.items()})
    shapes.first_down = shapes.second_down = first_down_t.shape
    results = [((width, rows), BF), ((width, rows), F32)] + [(s, F32) for s in shapes.__dict__.values()]
    out, grad, *summed = pl.pallas_call(
        functools.partial(unpack_kernel, layout=layout),
        out_shape=tuple(jax.ShapeDtypeStruct(s, t) for s, t in results),
        compiler_params=pltpu.CompilerParams(vmem_limit_bytes=VMEM_MIB * 2**20),
        name="unpack",
    )(total, out, grad)
    summed = Weights(*summed)
    summed.first_down, summed.second_down = summed.first_down.T, summed.second_down.T
    return (out.T, grad.T) + tuple(summed.__dict__.values())


def solution(mesh):
    rows = P(("tm", "head"), None)
    placed = (rows, P("tm", None)) + (P(),) * 29 + (rows,)
    return jax.shard_map(body, mesh=mesh, in_specs=placed, out_specs=(rows, rows) + (P(),) * 29, check_vma=False)
```

```python
import dataclasses
import functools
import math
import types

import jax
import jax.numpy as jnp
from jax import lax
from jax.experimental import pallas as pl
from jax.experimental.pallas import tpu as pltpu
from jax.sharding import PartitionSpec as P

BF = jnp.bfloat16
F32 = jnp.float32
LOG2E = math.log2(math.e)
BLK = 512
UNIT = 128
PER = BLK // UNIT
NEAR = PER + 2
PAD = 8 * UNIT
SLOT = 48
MAIN = 32
DEPTH = 128
MASKED = -1e30
GANG = 4
NN = (((1,), (0,)), ((), ()))
NT = (((1,), (1,)), ((), ()))
TN = (((0,), (0,)), ((), ()))


def dot(a, b, dims=NN):
    return lax.dot_general(a, b, dims, preferred_element_type=F32)


def iota(shape, dim):
    return lax.broadcasted_iota(jnp.int32, shape, dim)


def spread_cols(width, slots, slot_rows, used):
    row, column = iota((slots * slot_rows, width), 0), iota((slots * slot_rows, width), 1)
    hit = jnp.zeros((slots * slot_rows, width), jnp.bool_)
    for s in range(slots):
        f = row - slot_rows * s
        hit = hit | ((f >= 0) & (f < used) & (column == used * s + f))
    return hit.astype(F32).astype(BF)


def split3(v):
    hi = v.astype(BF).astype(F32)
    r1 = v - hi
    mid = r1.astype(BF).astype(F32)
    return hi, mid, r1 - mid


def three_rows(v, rows):
    a, b, e = split3(v)
    row = iota((rows, v.shape[1]), 0)
    return jnp.where(row == 0, a, jnp.where(row == 1, b, jnp.where(row == 2, e, 0.0)))


def pick_row(ref, index):
    values = ref[...].astype(F32)
    return jnp.sum(jnp.where(iota(values.shape, 0) == index, values, 0.0), axis=0, keepdims=True)


def bias_square(table, d):
    span = table.shape[1]
    half = span // 2
    lanes = 2 * UNIT
    u = iota((span, lanes), 1)
    u = jnp.where(u < UNIT, u, u - lanes)
    ids = jnp.clip(-UNIT * d - u, -half, half - 1) + half
    hot = (ids == iota((span, lanes), 0)).astype(F32).astype(BF)
    line = dot(jnp.broadcast_to(table, (UNIT, span)).astype(BF), hot) * LOG2E
    return pltpu.roll(line, 0, 1, stride=1, stride_axis=0)[:, :UNIT]


def bias_near(table, tile, keys_near):
    span = table.shape[1]
    squares = {d: bias_square(table, d) for d in (-1, 0, 1)}
    low = jnp.broadcast_to(table[:, :1] * LOG2E, (UNIT, UNIT))
    high = jnp.broadcast_to(table[:, span - 1 :] * LOG2E, (UNIT, UNIT))
    for r in range(tile.shape[0] // UNIT):
        for c in range(tile.shape[1] // UNIT):
            d = c - (r - 1) if keys_near else (c - 1) - r
            part = squares[d] if abs(d) < 2 else (low if d > 0 else high)
            tile[r * UNIT : (r + 1) * UNIT, c * UNIT : (c + 1) * UNIT] = part


def units_at(u, count):
    return pl.ds(pl.multiple_of(u * UNIT, UNIT), count * UNIT)


def far_windows(low, plain, edge, step, side, up, fine):
    sign = 1 if up else -1

    def run(at, times, size, masked):
        def one(i, carry):
            near = at + sign * i * size
            step(near if up else near - size, size, side, masked)
            return carry

        lax.fori_loop(0, times, one, 0)
        return at + sign * times * size

    at = edge if plain is None else run(edge, sign * (plain - edge) // 8, 8, False)
    left = sign * (low - at)
    tail = lax.rem(left, 8)
    more = tail > (6 if fine else 4)
    at = run(at, left // 8 + more.astype(jnp.int32), 8, True)
    tail = jnp.where(more, 0, tail)
    four = tail > (2 if fine else 0)
    at = run(at, four.astype(jnp.int32), 4, True)
    if fine:
        run(at, (tail - jnp.where(four, 4, 0) > 0).astype(jnp.int32), 2, True)


def far_sweep(plan, block, step, before, after, fine):
    low, plain_low, plain_high, high, low_half, high_half = [plan[block, i] for i in range(6)]
    start, stop = PER * block - 1, PER * block + PER + 1
    for whole, part in ((True, None), (False, 0)):
        @pl.when((low_half == 0) if whole else (low_half != 0))
        def _():
            far_windows(low, plain_low if whole else None, start, functools.partial(step, part=part), before, False, fine)

    for whole, part in ((True, None), (False, 1)):
        @pl.when((high_half == 0) if whole else (high_half != 0))
        def _():
            far_windows(high, plain_high if whole else None, stop, functools.partial(step, part=part), after, True, fine)


def fold_rows(four, pieces):
    size = four.shape[1] // pieces
    return jnp.concatenate([four[:, i * size : (i + 1) * size] for i in range(pieces)], axis=0)


def unfold_rows(folded):
    return jnp.concatenate([folded[i : i + 4, :] for i in range(0, folded.shape[0], 4)], axis=1)


def part_at(block, part):
    if part is None:
        return units_at(PER * block, PER)
    return units_at(PER * block + part * (PER // 2), PER // 2)


def has_far(plan, block):
    return (plan[block, 0] < PER * block - 1) | (plan[block, 3] > PER * block + PER + 1)


def segment_rows(ends, lengths, place, total):
    slots = ends.shape[0]
    before = ends <= jnp.broadcast_to(place, (slots, place.shape[1]))
    seg = jnp.sum(before.astype(jnp.int32), axis=0, keepdims=True)
    first = jnp.sum(jnp.where(before, lengths, 0), axis=0, keepdims=True)
    stop = jnp.min(jnp.where(before, total, ends), axis=0, keepdims=True)
    return seg, first, stop


def block_plan(ends, ends_row, total):
    slots = ends.shape[0]
    blocks, units = total // BLK, total // UNIT

    def along(place):
        return jnp.sum((ends <= jnp.broadcast_to(place, (slots, 128))).astype(jnp.int32), axis=0, keepdims=True)

    def down(place):
        return jnp.sum((jnp.broadcast_to(ends_row, (blocks, slots)) <= place).astype(F32), axis=1, keepdims=True).astype(jnp.int32)

    unit = iota((1, 128), 1)
    u_first, u_last = along(unit * UNIT), along(unit * UNIT + UNIT - 1)
    b = iota((blocks, 1), 0)
    first, last = down(b * BLK), down(b * BLK + BLK - 1)
    low_half = (down(b * BLK + BLK // 2) != first).astype(jnp.int32)
    high_half = (down(b * BLK + BLK // 2 - 1) != last).astype(jnp.int32)
    start, stop = PER * b - 1, PER * b + PER + 1
    inside = unit < units

    def count(hit):
        return jnp.sum((hit & inside).astype(F32), axis=1, keepdims=True).astype(jnp.int32)

    low = jnp.minimum(count(u_last < first), start)
    high = jnp.maximum(units - count(u_first > last), stop)
    plain_low = start - count((unit < start) & (u_first == last))
    plain_high = stop + count((unit >= stop) & (u_last == first))
    lane = iota((blocks, 128), 1)
    out = jnp.zeros((blocks, 128), jnp.int32)
    for i, v in enumerate((low, plain_low, plain_high, high, low_half, high_half)):
        out = jnp.where(lane == i, v, out)
    return out


def meets(first_key, rows, bounds):
    key = iota((rows, bounds.shape[1]), 0)
    return (key >= bounds[0:1, :] - first_key) & (key < bounds[1:2, :] - first_key)


def fwd_kernel(plan, qkv_ref, table_ref, bound_ref, o_ref, tail_ref, of_ref, lse_ref, qaug, kn, vt, tile, top_ref, acc, *, head_width):
    chunks, packed_rows, rows = qkv_ref.shape
    total = chunks * rows
    blocks = total // BLK
    span = table_ref.shape[1]
    table = pick_row(table_ref, lax.axis_index("head"))
    far = (table[:, :1] * LOG2E, table[:, span - 1 :] * LOG2E)
    pick = spread_cols(packed_rows, 3, SLOT, head_width)
    scale = LOG2E / math.sqrt(head_width)
    o_ref[:, :UNIT] = jnp.zeros((SLOT, UNIT), BF)
    o_ref[:, UNIT + total :] = jnp.zeros((SLOT, UNIT), BF)
    for edge in (slice(0, PAD), slice(PAD + total, 2 * PAD + total)):
        kn[edge, :] = jnp.zeros((PAD, DEPTH), BF)
        vt[:, edge] = jnp.zeros((SLOT, PAD), BF)
    bias_near(table, tile, True)
    rest = DEPTH - 2 * SLOT

    @pl.loop(0, chunks)
    def _(c):
        at = pl.ds(pl.multiple_of(c * rows, rows), rows)
        at_pad = pl.ds(pl.multiple_of(c * rows + PAD, UNIT), rows)
        parts = dot(pick, qkv_ref[c])
        q = parts[:SLOT] * scale
        hi = q.astype(BF)
        lo = (q - hi.astype(F32)).astype(BF)
        for s in range(3):
            qaug[s, :SLOT, at] = hi
            qaug[s, SLOT : 2 * SLOT, at] = lo
            qaug[s, 2 * SLOT :, at] = jnp.zeros((rest, rows), BF)
        k = parts[SLOT : 2 * SLOT]
        one3 = (iota((rest, rows), 0) < 3).astype(F32)
        kn[at_pad, :] = jnp.concatenate([k, k, one3], axis=0).T.astype(BF)
        one = (iota((SLOT, rows), 0) == head_width).astype(F32)
        vt[:, at_pad] = (parts[2 * SLOT :] + one).astype(BF)

    def top(x):
        return jnp.max(x.reshape(x.shape[0] // 8, 8, BLK), axis=0)

    @pl.loop(0, blocks // GANG)
    def _(pair):
        blocks_now = [GANG * pair + i for i in range(GANG)]
        at_q = [units_at(PER * b, PER) for b in blocks_now]
        near = [units_at(PER * b - 1 + PAD // UNIT, NEAR) for b in blocks_now]
        x = [dot(kn[n, :], qaug[1, :, q]) + tile[...] for n, q in zip(near, at_q)]
        x = [
            jnp.where(meets(PER * b * UNIT - UNIT, NEAR * UNIT, bound_ref[:, units_at(PER * b + PAD // UNIT, PER)]), v, MASKED)
            for b, v in zip(blocks_now, x)
        ]
        m = [jnp.max(top(v), axis=0, keepdims=True) for v in x]
        p = [jnp.exp2(v - w).astype(BF) for v, w in zip(x, m)]
        out = [dot(vt[:, n], v) for n, v in zip(near, p)]
        for q, w, v in zip(at_q, m, out):
            acc[:, q] = v
            lse_ref[:, q] = w
            qaug[0, 2 * SLOT :, q] = three_rows(far[0] - w, rest).astype(BF)
            qaug[2, 2 * SLOT :, q] = three_rows(far[1] - w, rest).astype(BF)

    @pl.loop(0, blocks)
    def _(b):
        @pl.when(has_far(plan, b))
        def _():
            at_q = units_at(PER * b, PER)

            def scores(u, count, side, masked, part):
                x = dot(kn[units_at(u + PAD // UNIT, count), :], qaug[side, :, part_at(b, part)])
                if masked:
                    x = jnp.where(meets(u * UNIT, count * UNIT, bound_ref[:, part_at(b + PAD // BLK, part)]), x, MASKED)
                return x

            near_acc = acc[:, at_q]

            def add(u, count, side, masked, part):
                p = jnp.exp2(scores(u, count, side, masked, part)).astype(BF)
                acc[:, part_at(b, part)] += dot(vt[:, units_at(u + PAD // UNIT, count)], p)

            far_sweep(plan, b, add, 0, 2, False)
            sums = acc[head_width : head_width + 1, at_q]
            over = jnp.max(jnp.where(sums < 2.0**60, 0.0, 1.0))

            @pl.when(over > 0.5)
            def _():
                top_ref[...] = jnp.zeros_like(top_ref)

                def half_of(part):
                    return slice(None) if part is None else slice(part * BLK // 2, (part + 1) * BLK // 2)

                def first(u, count, side, masked, part):
                    x = scores(u, count, side, masked, part)
                    best = jnp.max(x.reshape(x.shape[0] // 8, 8, x.shape[1]), axis=0)
                    top_ref[:, half_of(part)] = jnp.maximum(top_ref[:, half_of(part)], best)

                far_sweep(plan, b, first, 0, 2, False)
                m = jnp.max(top_ref[...], axis=0, keepdims=True)
                acc[:, at_q] = near_acc * jnp.exp2(-m)
                lse_ref[:, at_q] += m

                def second(u, count, side, masked, part):
                    p = jnp.exp2(scores(u, count, side, masked, part) - m[:, half_of(part)]).astype(BF)
                    acc[:, part_at(b, part)] += dot(vt[:, units_at(u + PAD // UNIT, count)], p)

                far_sweep(plan, b, second, 0, 2, False)

    @pl.loop(0, chunks)
    def _(c):
        at = pl.ds(pl.multiple_of(c * rows, rows), rows)
        total_p = acc[head_width : head_width + 1, at]
        out = acc[:, at] / total_p
        o_ref[:, pl.ds(pl.multiple_of(c * rows + UNIT, UNIT), rows)] = out.astype(BF)
        tail_ref[c] = fold_rows(out[MAIN : MAIN + 4], 4).astype(BF)
        of_ref[:, at] = out[: of_ref.shape[0]]
        lse_ref[:, at] = lse_ref[:, at] + jnp.log2(total_p)


def attend_forward(qkv, bounds, plan, table, head_width):
    chunks, packed_rows, rows = qkv.shape
    total = chunks * rows
    vm = pltpu.VMEM
    return pl.pallas_call(
        functools.partial(fwd_kernel, head_width=head_width),
        out_shape=(
            jax.ShapeDtypeStruct((SLOT, total + 2 * UNIT), BF),
            jax.ShapeDtypeStruct((chunks, 16, rows // 4), BF),
            jax.ShapeDtypeStruct((40, total), F32),
            jax.ShapeDtypeStruct((1, total), F32),
        ),
        in_specs=[pl.BlockSpec(memory_space=pltpu.SMEM)] + [pl.BlockSpec()] * 3,
        scratch_shapes=[
            vm((3, DEPTH, total), BF),
            vm((total + 2 * PAD, DEPTH), BF),
            vm((SLOT, total + 2 * PAD), BF),
            vm((NEAR * UNIT, BLK), F32),
            vm((8, BLK), F32),
            vm((SLOT, total), F32),
        ],
        compiler_params=pltpu.CompilerParams(vmem_limit_bytes=62 * 2**20),
        name="attend_forward",
    )(plan, qkv, table, bounds)


def bwd_kernel(plan, qkv_ref, do_ref, tail_ref, of_ref, lse_ref, table_ref, bound_ref, dqkv_ref, dtab_ref,
               qaug, kn, kt, vn, dot_t, qn, don, tile, dq, band, ends, dv_acc, dk_acc, *, head_width):
    chunks, packed_rows, rows = qkv_ref.shape
    total = chunks * rows
    blocks = total // BLK
    span = table_ref.shape[1]
    table = pick_row(table_ref, lax.axis_index("head"))
    pick = spread_cols(packed_rows, 3, SLOT, head_width)
    scale = LOG2E / math.sqrt(head_width)
    back = 1.0 / math.sqrt(head_width)
    rest = DEPTH - 2 * SLOT
    bias_near(table, tile, False)
    for edge in (slice(0, PAD), slice(PAD + total, 2 * PAD + total)):
        for s in range(3):
            qaug[s, :, edge] = jnp.zeros((DEPTH, PAD), BF)
        dot_t[:, edge] = jnp.zeros((DEPTH, PAD), BF)
        qn[edge, :] = jnp.zeros((PAD, DEPTH), BF)
        don[edge, :] = jnp.zeros((PAD, DEPTH), BF)

    @pl.loop(0, chunks)
    def _(c):
        at = pl.ds(pl.multiple_of(c * rows, rows), rows)
        at_pad = pl.ds(pl.multiple_of(c * rows + PAD, UNIT), rows)
        parts = dot(pick, qkv_ref[c])
        q, k, v = parts[:SLOT], parts[SLOT : 2 * SLOT], parts[2 * SLOT :]
        qs = q * scale
        hi = qs.astype(BF)
        lo = (qs - hi.astype(F32)).astype(BF)
        lse = lse_ref[:, at]
        for s, shift in enumerate((table[:, :1] * LOG2E, 0.0, table[:, span - 1 :] * LOG2E)):
            qaug[s, :SLOT, at_pad] = hi
            qaug[s, SLOT : 2 * SLOT, at_pad] = lo
            qaug[s, 2 * SLOT :, at_pad] = three_rows(shift - lse, rest).astype(BF)
        one3 = (iota((rest, rows), 0) < 3).astype(F32)
        row48 = iota((SLOT, rows), 0)
        none = jnp.zeros((rest, rows), F32)
        empty = jnp.zeros((SLOT, rows), F32)
        kn[at, :] = jnp.concatenate([k, k, one3], axis=0).T.astype(BF)
        kt[:, at] = k.astype(BF)
        vn[at, :] = jnp.concatenate([v, empty, one3], axis=0).T.astype(BF)
        tail = unfold_rows(tail_ref[c].astype(F32))
        do = jnp.concatenate([do_ref[c].astype(F32), tail, jnp.zeros((SLOT - MAIN - 4, rows), F32)], axis=0)
        centre = jnp.sum(do[: of_ref.shape[0]] * of_ref[:, at], axis=0, keepdims=True)
        dot_t[:SLOT, at_pad] = do.astype(BF)
        dot_t[SLOT : 2 * SLOT, at_pad] = empty.astype(BF)
        dot_t[2 * SLOT :, at_pad] = three_rows(-centre, rest).astype(BF)
        qn[at_pad, :] = jnp.concatenate([q + (row48 == head_width).astype(F32), empty, none], axis=0).T.astype(BF)
        don[at_pad, :] = jnp.concatenate([do, empty, none], axis=0).T.astype(BF)

    dq[...] = jnp.zeros_like(dq)
    band[...] = jnp.zeros_like(band)
    ends[...] = jnp.zeros_like(ends)

    @pl.loop(0, blocks // GANG)
    def _(pair):
        width = NEAR * UNIT
        wide = width + (GANG - 1) * BLK
        blocks_now = [GANG * pair + i for i in range(GANG)]
        at_k = [units_at(PER * b, PER) for b in blocks_now]
        near = [units_at(PER * b - 1 + PAD // UNIT, NEAR) for b in blocks_now]
        x = [dot(kn[k, :], qaug[1, :, n]) + tile[...] for k, n in zip(at_k, near)]
        dp = [dot(vn[k, :], dot_t[:, n]) for k, n in zip(at_k, near)]
        p = [jnp.where(meets(b * BLK, BLK, bound_ref[:, n]), jnp.exp2(v), 0.0) for b, n, v in zip(blocks_now, near, x)]
        dsb = [(v * w).astype(BF) for v, w in zip(p, dp)]
        dv = [dot(v.astype(BF), don[n, :]) for n, v in zip(near, p)]
        dk = [dot(v, qn[n, :]) for n, v in zip(near, dsb)]
        part = [dot(kt[:, k], v) for k, v in zip(at_k, dsb)]
        for k, v, w in zip(at_k, dv, dk):
            dv_acc[k, :] = v
            dk_acc[k, :] = w
        gap = [jnp.zeros((SLOT, BLK), F32)]
        whole = [jnp.concatenate(gap * i + [v] + gap * (GANG - 1 - i), axis=1) for i, v in enumerate(part)]
        lines = [v.astype(F32) for v in dsb]
        dq[:, units_at(GANG * PER * pair - 1 + PAD // UNIT, wide // UNIT)] += functools.reduce(jnp.add, whole)
        band[...] += functools.reduce(jnp.add, lines)

    @pl.loop(0, blocks)
    def _(b):
        @pl.when(has_far(plan, b))
        def _():
            def far(u, count, side, masked, part):
                at_k = part_at(b, part)
                at_q = units_at(u + PAD // UNIT, count)
                p = jnp.exp2(dot(kn[at_k, :], qaug[side, :, at_q]))
                if masked:
                    first_key = b * BLK + (0 if part is None else part * BLK // 2)
                    p = jnp.where(meets(first_key, at_k.size, bound_ref[:, at_q]), p, 0.0)
                dsb = (p * dot(vn[at_k, :], dot_t[:, at_q])).astype(BF)
                dq[:, at_q] += dot(kt[:, at_k], dsb)
                dv_acc[at_k, :] += dot(p.astype(BF), don[at_q, :])
                dk = dot(dsb, qn[at_q, :])
                dk_acc[at_k, :] += dk
                ends[side // 2] += jnp.sum(dk.reshape(dk.shape[0] // 8, 8, DEPTH), axis=0)

            far_sweep(plan, b, far, 2, 0, True)

    def take(part, lanes):
        row, lane = iota((packed_rows, lanes), 0), iota((packed_rows, lanes), 1)
        return ((row - head_width * part == lane) & (lane < head_width)).astype(F32).astype(BF)

    @pl.loop(0, chunks)
    def _(c):
        at = pl.ds(pl.multiple_of(c * rows, rows), rows)
        at_pad = pl.ds(pl.multiple_of(c * rows + PAD, UNIT), rows)
        packed = dot(take(0, SLOT), (dq[:, at_pad] * back).astype(BF))
        packed += dot(take(1, DEPTH), (dk_acc[at, :] * back).astype(BF), NT)
        packed += dot(take(2, DEPTH), dv_acc[at, :].astype(BF), NT)
        dqkv_ref[c] = packed.astype(BF)

    flip = (iota((UNIT, UNIT), 0) + iota((UNIT, UNIT), 1) == UNIT - 1).astype(F32)
    half = span // 2
    lane = iota((8, span), 1)
    column = iota((8, DEPTH), 1) == head_width
    out = jnp.zeros((8, span), F32)
    far_sum = [jnp.where(column, ends[i], 0.0) for i in range(2)]
    for d in range(-PER, PER + 1):
        part = jnp.zeros((UNIT, UNIT), F32)
        for r in range(PER):
            c = r + d + 1
            if 0 <= c < NEAR:
                part = part + band[r * UNIT : (r + 1) * UNIT, c * UNIT : (c + 1) * UNIT]
        if abs(d) > 1:
            far_sum[0 if d > 0 else 1] += jnp.sum(part.reshape(UNIT // 8, 8, UNIT), axis=0)
            continue
        turned = lax.dot_general(flip, part, NN, precision=lax.Precision.HIGHEST, preferred_element_type=F32)
        wide = jnp.concatenate([turned, jnp.zeros_like(turned)], axis=1)
        skewed = pltpu.roll(wide, 0, 1, stride=1, stride_axis=0)
        line = jnp.sum(skewed.reshape(UNIT // 8, 8, 2 * UNIT), axis=0)
        offset = UNIT - 1 - d * UNIT - iota((span, 2 * UNIT), 1)
        hot = (jnp.clip(offset, -half, half - 1) + half == iota((span, 2 * UNIT), 0)).astype(F32)
        out += lax.dot_general(line, hot, NT, precision=lax.Precision.HIGHEST, preferred_element_type=F32)
    out += jnp.where(lane == 0, jnp.sum(far_sum[0], axis=1, keepdims=True), 0.0)
    out += jnp.where(lane == span - 1, jnp.sum(far_sum[1], axis=1, keepdims=True), 0.0)
    out = jnp.sum(out, axis=0, keepdims=True)
    dtab_ref[...] = out


def attend_backward(qkv, do, tail, of, lse, bounds, plan, table, head_width):
    chunks, packed_rows, rows = qkv.shape
    total = chunks * rows
    padded = total + 2 * PAD
    span = table.shape[1]
    vm = pltpu.VMEM
    return pl.pallas_call(
        functools.partial(bwd_kernel, head_width=head_width),
        out_shape=(
            jax.ShapeDtypeStruct((chunks, packed_rows, rows), BF),
            jax.ShapeDtypeStruct((1, span), F32),
        ),
        in_specs=[pl.BlockSpec(memory_space=pltpu.SMEM)] + [pl.BlockSpec()] * 7,
        scratch_shapes=[
            vm((3, DEPTH, padded), BF),
            vm((total, DEPTH), BF),
            vm((SLOT, total), BF),
            vm((total, DEPTH), BF),
            vm((DEPTH, padded), BF),
            vm((padded, DEPTH), BF),
            vm((padded, DEPTH), BF),
            vm((BLK, NEAR * UNIT), F32),
            vm((SLOT, padded), F32),
            vm((BLK, NEAR * UNIT), F32),
            vm((2, 8, DEPTH), F32),
            vm((total, DEPTH), F32),
            vm((total, DEPTH), F32),
        ],
        compiler_params=pltpu.CompilerParams(vmem_limit_bytes=62 * 2**20),
        name="attend_backward",
    )(plan, qkv, do, tail, of, lse, table, bounds)

VEC = types.SimpleNamespace(
    first_gain=0, first_shift=1, first_up_bias=2, first_down_bias=3, mix_gain=4, mix_shift=5, mix_output_bias=6, filter_gain=7,
    filter_shift=8, pointwise_in_bias=9, batch_gain=10, batch_shift=11, pointwise_out_bias=12, second_gain=13, second_shift=14,
    second_up_bias=15, second_down_bias=16, final_gain=17, final_shift=18,
)
VEC_ROWS = 24
EPSILON = 1e-05
HALO = 64
TILE = 128
PIECE = 256


def col(cols_ref, i, size):
    return cols_ref[:size, i : i + 1]


def eye(n):
    return (iota((n, n), 0) == iota((n, n), 1)).astype(F32).astype(BF)


def flipped(mat):
    return dot(eye(mat.shape[1]), mat, NT).astype(BF)


def exact(a, b, dims=NN):
    return lax.dot_general(a, b, dims, precision=lax.Precision.HIGHEST, preferred_element_type=F32)


def folded(values):
    part = values[:, :TILE]
    for at in range(TILE, values.shape[1], TILE):
        part = part + values[:, at : at + TILE]
    return part


def row_sums(values):
    return exact(jnp.ones((8, TILE), F32), values, NT)


def norm(x):
    m = jnp.mean(x, axis=0, keepdims=True)
    c = x - m
    inv = lax.rsqrt(jnp.mean(c * c, axis=0, keepdims=True) + EPSILON)
    return c * inv, inv


def norm_back(e, n, inv, gain):
    ea = e * gain
    return inv * (ea - jnp.mean(ea, axis=0, keepdims=True) - n * jnp.mean(ea * n, axis=0, keepdims=True))


def sigmoid(v):
    return 0.5 + 0.5 * jnp.tanh(0.5 * v)


def ones_row(rows, lanes):
    return (iota((rows, lanes), 0) == 0).astype(F32).astype(BF)


def open_rows(frames_ref, up_ref, down_ref, mix_ref, x1_ref, h2_ref, qkv_ref, cols_ref, packed_rows, ship):
    width, rows = frames_ref.shape
    hidden = up_ref.shape[1]
    heads = qkv_ref.shape[0]
    up_t = flipped(up_ref[...])
    mix_t = dot(spread_cols(mix_ref.shape[1], heads, packed_rows, mix_ref.shape[1] // heads), mix_ref[...], NT).astype(BF)

    @pl.loop(0, rows // PIECE)
    def _(c):
        at = pl.ds(pl.multiple_of(c * PIECE, PIECE), PIECE)
        x0 = frames_ref[:, at].astype(F32)
        n, _ = norm(x0)
        h1 = (n * col(cols_ref, VEC.first_gain, width) + col(cols_ref, VEC.first_shift, width)).astype(BF)
        a1 = dot(up_t, h1) + col(cols_ref, VEC.first_up_bias, hidden)
        s1 = (a1 * sigmoid(a1)).astype(BF)
        x1 = x0 + 0.5 * (dot(down_ref[...], s1) + col(cols_ref, VEC.first_down_bias, width))
        x1_ref[:, at] = x1
        n, _ = norm(x1)
        h2 = (n * col(cols_ref, VEC.mix_gain, width) + col(cols_ref, VEC.mix_shift, width)).astype(BF)
        h2_ref[:, at] = h2
        qkv = dot(mix_t, h2).astype(BF)
        for h in range(heads):
            qkv_ref[h, :, at] = qkv[h * packed_rows : (h + 1) * packed_rows]
        ship(c)


def open_segments(len_ref, bound_ref, plan_ref, ext_ref, line):
    rows = ext_ref.shape[1] - TILE
    group = bound_ref.shape[1] - 2 * PAD
    slots = len_ref.shape[1]
    lengths = jnp.broadcast_to(len_ref[...].astype(F32), (8, slots))
    row, column = iota((slots, slots), 0), iota((slots, slots), 1)
    ends = exact((column <= row).astype(F32), lengths, NT)[:, :1].astype(jnp.int32)
    own_len = exact((column == row).astype(F32), lengths, NT)[:, :1].astype(jnp.int32)
    ends_row = exact(lengths, (row <= column).astype(F32))[:1].astype(jnp.int32)
    plan_ref[...] = block_plan(ends, ends_row, group)
    line[...] = jnp.full_like(line, -1)
    for edge in (slice(0, PAD), slice(PAD + group, 2 * PAD + group)):
        bound_ref[:, edge] = jnp.where(iota((2, PAD), 0) == 0, 1 << 20, -1)

    @pl.loop(0, group // 512)
    def _(c):
        at = pl.multiple_of(c * 512, 512)
        seg, first, stop = segment_rows(ends, own_len, iota((1, 512), 1) + at, group)
        line[:, pl.ds(at + TILE, 512)] = seg
        bound_ref[0:1, pl.ds(at + PAD, 512)] = first
        bound_ref[1:2, pl.ds(at + PAD, 512)] = stop

    first = pl.multiple_of(lax.axis_index("head") * rows, TILE)
    ext_ref[:, :rows] = line[:, pl.ds(first + TILE, rows)]
    left = line[:, pl.ds(first, TILE)]
    right = line[:, pl.ds(first + TILE + rows, TILE)]
    ext_ref[:, rows:] = jnp.where(iota((1, TILE), 1) < HALO, right, left)


def split_heads(heads, head_width):
    size = heads * head_width
    row, column = iota((size, size), 0), iota((size, size), 1)
    hit = jnp.zeros((size, size), jnp.bool_)
    for h in range(heads):
        f = column - head_width * h
        mine = (f >= 0) & (f < head_width)
        hit = hit | (mine & (f < MAIN) & (row == MAIN * h + f)) | (mine & (f >= MAIN) & (row == MAIN * heads + 4 * h + f - MAIN))
    return hit.astype(F32).astype(BF)


def conv_masks(mask_ref, ext_ref):
    seg = jnp.broadcast_to(ext_ref[...], (8, ext_ref.shape[1]))
    lanes = seg.shape[1]
    reach = mask_ref.shape[0] // 2
    for i in range(mask_ref.shape[0]):
        mask_ref[i] = (pltpu.roll(seg, (reach - i) % lanes, 1) == seg).astype(F32)


def filter_kernel(x1_ref, x1l_ref, x1r_ref, o_ref, tail_ref, cols_ref, ext_ref, out_ref, pw_ref, taps_ref,
                  x2_ref, oc_ref, u_ref, y_ref, stat_ref, wide, mask, live_ref, h3s, n_ref, inv_ref, value_ref, gate_ref, *, head_width, slot_count, arrive):
    width, rows = x1_ref.shape
    lanes = rows + TILE
    heads = o_ref.shape[0]
    taps = taps_ref.shape[0]
    out_t = flipped(out_ref[...])
    pw_t = flipped(pw_ref[...])
    gather = split_heads(heads, head_width)
    seg = ext_ref[...]
    live = (seg >= 0) & (seg < slot_count)
    live_ref[...] = live.astype(F32)
    conv_masks(mask, ext_ref)
    wide_taps = taps_ref[...].astype(F32).T
    arrive()

    near = iota((1, TILE), 1) < HALO

    def extended(own, left, right):
        edge = jnp.where(near, right.astype(F32), left.astype(F32)).astype(own.dtype)
        return jnp.concatenate([own, edge], axis=1)

    x1 = extended(x1_ref[...], x1l_ref[...], x1r_ref[...])
    main = [extended(o_ref[h, :MAIN, TILE : TILE + rows], o_ref[h, :MAIN, :TILE], o_ref[h, :MAIN, TILE + rows :]) for h in range(heads)]
    tails = []
    for h in range(heads):
        left, right = (o_ref[h, MAIN:, at].astype(F32)[:4] for at in (slice(0, TILE), slice(TILE + rows, rows + 2 * TILE)))
        tails.append(extended(unfold_rows(tail_ref[h].astype(F32)), left, right))
    o = jnp.concatenate(main + [jnp.concatenate(tails, axis=0).astype(BF)], axis=0)
    oc = dot(gather, o, TN).astype(BF)
    x2 = x1 + (dot(out_t, oc) + col(cols_ref, VEC.mix_output_bias, width))
    n, inv = norm(x2)
    h3 = (n * col(cols_ref, VEC.filter_gain, width) + col(cols_ref, VEC.filter_shift, width)).astype(BF)
    g = dot(pw_t, h3) + col(cols_ref, VEC.pointwise_in_bias, 2 * width)
    gate = sigmoid(g[width:])
    u = jnp.where(live_ref[...] > 0.5, g[:width] * gate, 0.0).astype(BF)
    n_ref[...] = n[:, :rows]
    inv_ref[...] = inv[:, :rows]
    h3s[:width, :] = h3[:, :rows]
    value_ref[...] = g[:width, :rows]
    gate_ref[...] = gate[:, :rows]
    oc_ref[:width, :] = oc[:, :rows]
    x2_ref[...] = x2
    u_ref[...] = u
    wide[...] = u.astype(F32)

    own = (live & (iota((1, lanes), 1) < rows)).astype(F32)
    count = jnp.sum(own, axis=1, keepdims=True)
    safe = jnp.maximum(count, 1.0)
    for r in range(width // 8):
        sl = slice(8 * r, 8 * r + 8)
        u8 = wide[sl, :]
        acc = jnp.zeros((8, lanes), F32)
        for k in range(taps):
            moved = pltpu.roll(u8, (taps // 2 - k) % lanes, 1)
            acc = acc + wide_taps[sl, k : k + 1] * (moved * mask[k])
        y_ref[sl, :] = acc
    y = y_ref[...]
    part = folded(y * own)
    mean = exact(part, jnp.ones((TILE, TILE), F32)) / safe
    dev = (y - jnp.concatenate([mean] * (lanes // TILE), axis=1)) * own
    stat_ref[...] = two_rows(row_sums(part)[:1] / safe, row_sums(folded(dev * dev))[:1], count)


def two_rows(a, b, extra):
    rest = a.shape[1] - TILE
    tail = pad_lanes(jnp.concatenate([a[:, TILE:], b[:, TILE:]], axis=0))
    spot = (iota((2, TILE), 0) == 0) & (iota((2, TILE), 1) == rest)
    return jnp.concatenate([a[:, :TILE], b[:, :TILE], jnp.where(spot, extra, tail)], axis=0)


def all_rows(ref, width):
    rest = width - TILE
    values = ref[...]
    a = jnp.concatenate([values[:, 0, :], values[:, 2, :rest]], axis=1)
    b = jnp.concatenate([values[:, 1, :], values[:, 3, :rest]], axis=1)
    return a, b, values[:, 2, rest : rest + 1]


def total_stats(stats_ref, width):
    mean_of, spread_of, n = all_rows(stats_ref, width)
    count = jnp.sum(n, axis=0, keepdims=True)
    mean = jnp.sum(n * mean_of, axis=0, keepdims=True) / count
    gap = mean_of - mean
    spread = jnp.sum(spread_of + n * gap * gap, axis=0, keepdims=True)
    inv = lax.rsqrt(spread / count + EPSILON)
    table = jnp.concatenate([mean, inv, jnp.broadcast_to(count, (1, width)), jnp.zeros((5, width), F32)], axis=0).T
    return table[:, 0:1], table[:, 1:2], table[:, 2:3]


def second_kernel(x2_ref, y_ref, stats_ref, cot_ref, cotl_ref, cotr_ref, cols_ref, pwo_ref, up_ref, down_ref,
                  out_ref, dx3_ref, e_ref, sums_ref, pack_ref, small_ref,
                  h4s, das, s4s, dfs, ws, dcs, *, arrive, leave):
    width, rows = out_ref.shape
    hidden = up_ref.shape[1]
    pwo_t = flipped(pwo_ref[...])
    up_t = flipped(up_ref[...])
    down = flipped(down_ref[...])
    arrive()
    mean, inv_b, _ = total_stats(stats_ref, width)
    bgain = col(cols_ref, VEC.batch_gain, width)

    near = iota((1, TILE), 1) < HALO
    edge = jnp.where(near, cotr_ref[...].astype(F32), cotl_ref[...].astype(F32))
    cot = jnp.concatenate([cot_ref[...].astype(F32), edge], axis=1)
    zh = (y_ref[...] - mean) * inv_b
    z = zh * bgain + col(cols_ref, VEC.batch_shift, width)
    sig_z = sigmoid(z)
    w = (z * sig_z).astype(BF)
    x3 = x2_ref[...] + (dot(pwo_t, w) + col(cols_ref, VEC.pointwise_out_bias, width))
    n4, inv4 = norm(x3)
    h4 = (n4 * col(cols_ref, VEC.second_gain, width) + col(cols_ref, VEC.second_shift, width)).astype(BF)
    a4 = dot(up_t, h4) + col(cols_ref, VEC.second_up_bias, hidden)
    sig = sigmoid(a4)
    s4 = (a4 * sig).astype(BF)
    x4 = x3 + 0.5 * (dot(down_ref[...], s4) + col(cols_ref, VEC.second_down_bias, width))
    nf, invf = norm(x4)
    fgain = col(cols_ref, VEC.final_gain, width)
    dx4 = norm_back(cot, nf, invf, fgain)
    df = (0.5 * dx4).astype(BF)
    da = (dot(down, df) * (sig * (1.0 + a4 * (1.0 - sig)))).astype(BF)
    dh = dot(up_ref[...], da)
    dx3 = dx4 + norm_back(dh, n4, inv4, col(cols_ref, VEC.second_gain, width))
    dc = dx3.astype(BF)
    dz = dot(pwo_ref[...], dc) * (sig_z * (1.0 + z * (1.0 - sig_z)))
    e = dz * bgain
    e_ref[...] = e
    sums_ref[...] = two_rows(row_sums(folded(e[:, :rows]))[:1], row_sums(folded((e * zh)[:, :rows]))[:1], 0.0)
    leave()

    out_ref[...] = (nf * fgain + col(cols_ref, VEC.final_shift, width))[:, :rows].astype(BF)
    dx3_ref[...] = dx3[:, :rows]
    h4s[...] = h4[:, :rows]
    das[...] = da[:, :rows]
    s4s[:hidden, :] = s4[:, :rows]
    dfs[...] = df[:, :rows]
    ws[:width, :] = w[:, :rows]
    dcs[...] = dc[:, :rows]
    totals = [row_sums(folded(v[:, :rows]))[:1] for v in (dh * n4, dh, cot * nf, cot, dz * zh, dz)]
    s4s[hidden:, :] = ones_row(16, rows)
    ws[width:, :] = ones_row(16, rows)
    up_grad = dot(h4s[...], das[...], NT)
    up_bias = dot(ones_row(16, rows), das[...], NT)
    down_grad = dot(dfs[...], s4s[...], NT)
    pw_grad = dot(ws[...], dcs[...], NT)
    down_bias = exact(jnp.ones((8, rows), F32), dfs[...].astype(F32), NT)
    put_ff(pack_ref, up_grad, down_grad, 0)
    tall = 9 * width
    pack_ref[tall : tall + width, :] = pw_grad[:width, :TILE].astype(BF)
    pack_ref[tall + width : tall + 2 * width, :] = pad_lanes(pw_grad[:width, TILE:]).astype(BF)
    small_ref[...] = stack_rows(
        [totals[0], totals[1], up_bias[:1], down_bias[:1], totals[2], totals[3], totals[4], totals[5], pw_grad[width : width + 1]],
        small_ref.shape)


def pad_lanes(mat, lanes=TILE):
    if mat.shape[1] == lanes:
        return mat
    return jnp.concatenate([mat, jnp.zeros((mat.shape[0], lanes - mat.shape[1]), mat.dtype)], axis=1)


def stack_rows(rows, shape):
    parts = [pad_lanes(r, shape[1]) for r in rows]
    parts.append(jnp.zeros((shape[0] - len(rows), shape[1]), F32))
    return jnp.concatenate(parts, axis=0)


def put_ff(pack_ref, up_grad, down_grad_t, at):
    width, hidden = up_grad.shape
    whole = hidden // TILE
    for i in range(whole):
        pack_ref[at + i * width : at + (i + 1) * width, :] = up_grad[:, i * TILE : (i + 1) * TILE].astype(BF)
        j = whole + i
        pack_ref[at + j * width : at + (j + 1) * width, :] = down_grad_t[:, i * TILE : (i + 1) * TILE].astype(BF)
    rest = jnp.concatenate([up_grad[:, whole * TILE : hidden], down_grad_t[:, whole * TILE : hidden]], axis=1)
    pack_ref[at + 2 * whole * width : at + (2 * whole + 1) * width, :] = rest.astype(BF)


def unfilter_kernel(e_ref, y_ref, stats_ref, sums_ref, u_ref, dx3_ref, ocs, cols_ref, ext_ref, pw_ref, taps_ref,
                    out_ref, dx2_ref, do_ref, pack_ref, small_ref, tapg_ref,
                    dyw, du_s, mask, prod, h3s, dgs, dms, gains, live_ref, n_ref, inv_ref, value_ref, gate_ref, tail_ref, *, head_width, ship, arrive):
    width, rows = dx3_ref.shape
    lanes = rows + TILE
    heads = do_ref.shape[0]
    taps = taps_ref.shape[0]
    tap_cols = taps_ref[...].astype(F32).T
    out_w = dot(split_heads(heads, head_width), out_ref[...]).astype(BF)
    gains[...] = jnp.zeros_like(gains)
    fgain = col(cols_ref, VEC.filter_gain, width)
    mean, inv_b, count = total_stats(stats_ref, width)
    arrive()
    one_of, two_of, _ = all_rows(sums_ref, width)
    sums = jnp.concatenate([jnp.sum(one_of, axis=0, keepdims=True), jnp.sum(two_of, axis=0, keepdims=True), jnp.zeros((6, width), F32)], axis=0).T
    s1, s2 = sums[:, 0:1], sums[:, 1:2]
    seg = ext_ref[...]
    live = live_ref[...]
    zh = (y_ref[...] - mean) * inv_b
    dy = inv_b * (e_ref[...] - live * ((s1 + zh * s2) / count))
    dyw[...] = jnp.where(seg >= 0, dy, 0.0).astype(BF).astype(F32)

    for r in range(width // 8):
        sl = slice(8 * r, 8 * r + 8)
        dy8 = dyw[sl, :]
        u8 = u_ref[16 * (r // 2) : 16 * (r // 2) + 16, :rows].astype(F32)[8 * (r % 2) : 8 * (r % 2) + 8]
        acc = jnp.zeros((8, rows), F32)
        for k in range(taps):
            moved = pltpu.roll(dy8, (k - taps // 2) % lanes, 1)[:, :rows] * mask[taps - k][:, :rows]
            acc = acc + tap_cols[sl, k : k + 1] * moved
            hit = moved * u8
            prod[k, sl, :] = folded(hit)
        du_s[sl, :] = acc

    @pl.loop(0, rows // PIECE)
    def _(c):
        at = pl.ds(pl.multiple_of(c * PIECE, PIECE), PIECE)
        n, inv = n_ref[:, at], inv_ref[:, at]
        gate = gate_ref[:, at]
        t = live_ref[:, at] * du_s[:, at] * gate
        dg = jnp.concatenate([t, t * value_ref[:, at] * (1.0 - gate)], axis=0).astype(BF)
        dh = dot(pw_ref[...], dg)
        dx2 = dx3_ref[:, at] + norm_back(dh, n, inv, fgain)
        dx2_ref[:, at] = dx2
        dm = dx2.astype(BF)
        do = dot(out_w, dm)
        for h in range(heads):
            do_ref[h, :, at] = do[h * MAIN : (h + 1) * MAIN].astype(BF)
        tail_ref[:, at] = do[heads * MAIN :]
        ship(c)
        dgs[:, at] = dg
        dms[:, at] = dm
        for i, v in enumerate((dh * n, dh)):
            gains[i] += folded(v)

    ship(rows // PIECE)
    whole = prod[...].reshape(taps * width, TILE)
    hi = whole.astype(BF)
    lo = (whole - hi.astype(F32)).astype(BF)
    ones = jnp.ones((8, TILE), BF)
    lines = dot(ones, hi, NT) + dot(ones, lo, NT)
    for k in range(taps):
        tapg_ref[k : k + 1, :] = lines[:1, k * width : (k + 1) * width]

    h3s[width:, :] = ones_row(16, rows)
    ocs[width:, :] = ones_row(16, rows)
    pw_grad = dot(h3s[...], dgs[...], NT)
    out_grad = dot(ocs[...], dms[...], NT)
    at = 0
    for lo in range(0, 2 * width, TILE):
        pack_ref[at : at + width, :] = pad_lanes(pw_grad[:width, lo : min(lo + TILE, 2 * width)]).astype(BF)
        at += width
    for lo in range(0, width, TILE):
        pack_ref[at : at + width, :] = pad_lanes(out_grad[:width, lo : min(lo + TILE, width)]).astype(BF)
        at += width
    small_ref[...] = stack_rows(
        [row_sums(gains[0])[:1], row_sums(gains[1])[:1], pw_grad[width : width + 1], out_grad[width : width + 1]], small_ref.shape)


def close_kernel(frames_ref, x1_ref, h2_ref, dx2_ref, dqkv_ref, dtab_ref, cols_ref, up_ref, down_ref, mix_ref,
                 grad_ref, pack_ref, h1s, das, s1s, dfs, dqs, gains, up_part, down_part, mix_part, *, arrive, between, mixed):
    width, rows = frames_ref.shape
    most = slice(0, rows - PIECE)
    hidden = up_ref.shape[1]
    heads, packed_rows, _ = dqkv_ref.shape
    up_t = flipped(up_ref[...])
    down = flipped(down_ref[...])
    hot = spread_cols(mix_ref.shape[1], heads, packed_rows, mix_ref.shape[1] // heads)
    mix_w = dot(mix_ref[...], hot, NT).astype(BF)
    gains[...] = jnp.zeros_like(gains)
    mgain = col(cols_ref, VEC.mix_gain, width)
    fgain = col(cols_ref, VEC.first_gain, width)

    @pl.loop(0, rows // PIECE)
    def _(c):
        arrive(c)
        at = pl.ds(pl.multiple_of(c * PIECE, PIECE), PIECE)
        dq = jnp.concatenate([dqkv_ref[h, :, at] for h in range(heads)], axis=0)
        dqs[:, at] = dq
        dh2 = dot(mix_w, dq)
        n2, inv2 = norm(x1_ref[:, at])
        dx1 = dx2_ref[:, at] + norm_back(dh2, n2, inv2, mgain)
        x0 = frames_ref[:, at].astype(F32)
        n1, inv1 = norm(x0)
        h1 = (n1 * fgain + col(cols_ref, VEC.first_shift, width)).astype(BF)
        a1 = dot(up_t, h1) + col(cols_ref, VEC.first_up_bias, hidden)
        sig = sigmoid(a1)
        s1s[:, at] = (a1 * sig).astype(BF)
        df = (0.5 * dx1).astype(BF)
        da = (dot(down, df) * (sig * (1.0 + a1 * (1.0 - sig)))).astype(BF)
        dh1 = dot(up_ref[...], da)
        grad_ref[:, at] = dx1 + norm_back(dh1, n1, inv1, fgain)
        h1s[:, at] = h1
        das[:, at] = da
        dfs[:, at] = df
        for i, v in enumerate((dh1 * n1, dh1, dh2 * n2, dh2)):
            gains[i] += folded(v)
        between(c)

        @pl.when(c == rows // PIECE - 2)
        def _():
            up_part[...] = dot(h1s[:, most], das[:, most], NT)
            down_part[...] = dot(dfs[:, most], s1s[:, most], NT)
            mix_part[...] = dot(h2_ref[:, most], dqs[:, most], NT)

    rest = slice(rows - PIECE, rows)
    mix_grad = dot((mix_part[...] + dot(h2_ref[:, rest], dqs[:, rest], NT)).astype(BF), hot)
    at = 0
    for lo in range(0, mix_grad.shape[1], TILE):
        pack_ref[at : at + width, :] = pad_lanes(mix_grad[:, lo : min(lo + TILE, mix_grad.shape[1])]).astype(BF)
        at += width
    mixed()
    up_grad = up_part[...] + dot(h1s[:, rest], das[:, rest], NT)
    up_bias = dot(ones_row(16, rows), das[...], NT)
    down_grad = down_part[...] + dot(dfs[:, rest], s1s[:, rest], NT)
    down_bias = exact(jnp.ones((8, rows), F32), dfs[...].astype(F32), NT)
    put_ff(pack_ref, up_grad, down_grad, at)
    at += (2 * (hidden // TILE) + 1) * width
    totals = [row_sums(gains[i])[:1] for i in range(4)]
    small = stack_rows([totals[0], totals[1], up_bias[:1], down_bias[:1], totals[2], totals[3]], (16, 5 * TILE))
    at = put_small(pack_ref, small, at)
    span = dtab_ref.shape[1]
    table = jnp.where(iota((16, span), 0) == lax.axis_index("head"), dtab_ref[...], 0.0)
    pack_ref[at : at + 16, :] = table.astype(BF)
    if at + 16 < pack_ref.shape[0]:
        pack_ref[at + 16 :, :] = jnp.zeros((pack_ref.shape[0] - at - 16, TILE), BF)


def put_small(pack_ref, small, at):
    for lo in range(0, small.shape[1], TILE):
        pack_ref[at : at + small.shape[0], :] = small[:, lo : lo + TILE].astype(BF)
        at += small.shape[0]
    return at


def put_taps(pack_ref, tapg, at):
    taps = tapg.shape[0]
    pack_ref[at : at + taps, :] = tapg[:, :TILE].astype(BF)
    pack_ref[at + taps : at + 2 * taps, :] = pad_lanes(tapg[:, TILE:]).astype(BF)
    return at + 2 * taps


def unpack_kernel(pack_ref, out_ref, grad_ref, *refs, layout):
    refs[0][...] = out_ref[...]
    refs[1][...] = grad_ref[...]
    out_refs = refs[2:]
    given = Weights(*out_refs)

    def wide(at, rows, lanes):
        parts = [pack_ref[at + i * rows : at + (i + 1) * rows, :].astype(F32) for i in range(-(-lanes // TILE))]
        return jnp.concatenate(parts, axis=1)[:, :lanes]

    for at, up_ref, down_ref in ((layout.first, given.first_up, given.first_down), (layout.second, given.second_up, given.second_down)):
        width, hidden = up_ref.shape
        whole = hidden // TILE
        half = hidden - whole * TILE
        piece = lambda i: pack_ref[at + i * width : at + (i + 1) * width, :].astype(F32)
        rest = piece(2 * whole)
        up_ref[...] = jnp.concatenate([piece(i) for i in range(whole)] + [rest[:, :half]], axis=1)
        down_ref[...] = jnp.concatenate([piece(whole + i) for i in range(whole)] + [rest[:, half:]], axis=1)
    for ref, at in ((given.mix_inputs, layout.mix_inputs), (given.pointwise_in, layout.pointwise_in), (given.mix_output, layout.mix_output),
                    (given.pointwise_out, layout.pointwise_out), (given.depthwise_taps, layout.taps)):
        ref[...] = wide(at, *ref.shape)
    given.position_bias[...] = pack_ref[layout.table : layout.table + 16, :].astype(F32)[: given.position_bias.shape[0]]
    late = wide(layout.small_late, 16, 5 * TILE)
    early = wide(layout.small, 32, 5 * TILE)
    late_rows = (
        given.first_gain, given.first_shift, given.first_up_bias, given.first_down_bias, given.mix_gain, given.mix_shift,
    )
    second_rows = (
        given.second_gain, given.second_shift, given.second_up_bias, given.second_down_bias, given.final_gain, given.final_shift,
        given.batch_gain, given.batch_shift, given.pointwise_out_bias,
    )
    filter_rows = (given.filter_gain, given.filter_shift, given.pointwise_in_bias, given.mix_output_bias)
    for small, first, refs in ((late, 0, late_rows), (early, 0, second_rows), (early, 16, filter_rows)):
        for row, ref in enumerate(refs, first):
            ref[...] = small[row : row + 1, : ref.shape[0]].reshape(ref.shape)


@dataclasses.dataclass
class Weights:
    first_gain: object
    first_shift: object
    first_up: object
    first_up_bias: object
    first_down: object
    first_down_bias: object
    mix_gain: object
    mix_shift: object
    mix_inputs: object
    position_bias: object
    mix_output: object
    mix_output_bias: object
    filter_gain: object
    filter_shift: object
    pointwise_in: object
    pointwise_in_bias: object
    depthwise_taps: object
    batch_gain: object
    batch_shift: object
    pointwise_out: object
    pointwise_out_bias: object
    second_gain: object
    second_shift: object
    second_up: object
    second_up_bias: object
    second_down: object
    second_down_bias: object
    final_gain: object
    final_shift: object


def pack_layout(width, hidden, mix_width, taps, devices):
    ff = (2 * (hidden // TILE) + 1) * width
    chunks = lambda lanes: -(-lanes // TILE) * width
    unit = 16 * devices
    whole = lambda rows: -(-rows // unit) * unit
    at = types.SimpleNamespace(second=0, pointwise_out=ff)
    at.pointwise_in = ff + chunks(width)
    at.mix_output = at.pointwise_in + chunks(2 * width)
    at.taps = at.mix_output + chunks(width)
    at.small = at.taps + 2 * taps
    at.late = at.mix_inputs = whole(at.small + 32 * 5)
    at.last = at.late + chunks(mix_width) // unit * unit
    at.first = at.mix_inputs + chunks(mix_width)
    at.small_late = at.first + ff
    at.table = at.small_late + 16 * 5
    at.rows = at.late + whole(at.table + 16 - at.late)
    return at


MESH = pl.DeviceIdType.MESH


def meet(peers):
    barrier = pltpu.get_barrier_semaphore()
    for peer in peers:
        pl.semaphore_signal(barrier, inc=1, device_id=peer, device_id_type=MESH)
    pl.semaphore_wait(barrier, len(peers))


def head_peers(n):
    me = lax.axis_index("head")
    return me, [{"head": lax.rem(me + s, n)} for s in range(1, n)], [lax.rem(me + s, n) for s in range(1, n)]


def opening_kernel(frames_ref, len_ref, up_ref, down_ref, mix_ref, *refs, packed_rows, n):
    count = len(VEC.__dict__)
    vec_refs, refs = refs[:count], refs[count:]
    (cot_ref, x1_ref, h2_ref, cols_ref, bound_ref, plan_ref, ext_ref, all_ref, x1l_ref, x1r_ref, cotl_ref, cotr_ref,
     qkv, line, send, recv, local, hsend, hrecv) = refs
    me, peers, ids = head_peers(n)
    rows = cot_ref.shape[1]
    barrier = pltpu.get_barrier_semaphore()
    for peer in peers:
        pl.semaphore_signal(barrier, inc=1, device_id=peer, device_id_type=MESH)
    vecs = [ref[...].astype(F32).reshape(1, ref.shape[0]) for ref in vec_refs]
    cols_ref[...] = stack_rows(vecs, (VEC_ROWS, up_ref.shape[1])).T
    pl.semaphore_wait(barrier, len(peers))

    def piece(c, s):
        at = pl.ds(pl.multiple_of(c * PIECE, PIECE), PIECE)
        return pltpu.make_async_remote_copy(src_ref=qkv.at[ids[s], :, at], dst_ref=all_ref.at[me, :, at], send_sem=send.at[c, s],
                                            recv_sem=recv.at[c, s], device_id=peers[s], device_id_type=MESH)

    def ship(c):
        for s in range(n - 1):
            piece(c, s).start()

    open_rows(frames_ref, up_ref, down_ref, mix_ref, x1_ref, h2_ref, qkv, cols_ref, packed_rows, ship)
    own = pltpu.make_async_copy(qkv.at[me], all_ref.at[me], local)
    own.start()

    def edge(i, src, dst, head):
        return pltpu.make_async_remote_copy(src_ref=src, dst_ref=dst, send_sem=hsend.at[i], recv_sem=hrecv.at[i],
                                            device_id={"head": head}, device_id_type=MESH)

    up = lax.rem(me + 1, n)
    down = lax.rem(me + n - 1, n)
    last, start = pl.ds(rows - TILE, TILE), pl.ds(0, TILE)
    to_right = [edge(0, x1_ref.at[:, last], x1l_ref, up), edge(1, cot_ref.at[:, last], cotl_ref, up)]
    to_left = [edge(2, x1_ref.at[:, start], x1r_ref, down), edge(3, cot_ref.at[:, start], cotr_ref, down)]

    @pl.when(me < n - 1)
    def _():
        for c in to_right:
            c.start()

    @pl.when(me > 0)
    def _():
        for c in to_left:
            c.start()

    open_segments(len_ref, bound_ref, plan_ref, ext_ref, line)
    own.wait()

    @pl.loop(0, rows // PIECE)
    def _(c):
        for s in range(n - 1):
            piece(c, s).wait()

    @pl.when(me < n - 1)
    def _():
        for c in to_right:
            c.wait_send()
        for c in to_left:
            c.wait_recv()

    @pl.when(me > 0)
    def _():
        for c in to_left:
            c.wait_send()
        for c in to_right:
            c.wait_recv()


def everyone(n_tm, n_head):
    n = n_tm * n_head
    me = lax.axis_index("tm") * n_head + lax.axis_index("head")

    def place(s):
        peer = lax.rem(me + s, n)
        return {"tm": peer // n_head, "head": lax.rem(peer, n_head)}

    return me, n, place


def tell(src_ref, all_ref, send, recv, n_tm, n_head):
    me, n, place = everyone(n_tm, n_head)

    def copy(s):
        return pltpu.make_async_remote_copy(src_ref=src_ref, dst_ref=all_ref.at[me], send_sem=send.at[s], recv_sem=recv.at[s],
                                            device_id=place(s), device_id_type=MESH)

    def start():
        pl.loop(1, n)(lambda s: copy(s).start())
        all_ref[me] = src_ref[...]

    def end():
        pl.loop(1, n)(lambda s: copy(s).wait())

    return start, end


def load_all(sources, targets, sems):
    copies = [pltpu.make_async_copy(src, dst, sems.at[i]) for i, (src, dst) in enumerate(zip(sources, targets))]
    for copy in copies:
        copy.start()
    return copies


def middle_kernel(*refs, n_tm, n_head, head_width, slot_count, layout):
    o_ref, o_tail, sources, refs = refs[0], refs[1], refs[2:16], refs[16:]
    (out_ref, dx2_ref, do_all, do_tails, pack_ref), refs = refs[:5], refs[5:]
    loaded, refs = refs[:14], refs[14:]
    (x1_ref, x1l_ref, x1r_ref, cot_ref, cotl_ref, cotr_ref, cols_ref, ext_ref, mixo_ref, pwi_ref, taps_ref, pwo_ref, up_ref,
     down_ref) = loaded
    (o_own, x2, oc, u, y, stat, stats, dx3, e, sums, all_sums, do, wide, mask, live,
     h4s, das, s4s, dfs, ws, dcs, dyw, du, prod, h3s, dgs, dms, gains2, smalld, smalle, tapg,
     n3, inv3, value3, gate3, tail_own, tail_wide, tail), refs = refs[:38], refs[38:]
    (load_sems, send_o, recv_o, local_o, send_a, recv_a, send_b, recv_b, send_d, recv_d, local_d) = refs
    me, peers, ids = head_peers(n_head)
    _, n, place = everyone(n_tm, n_head)
    barrier = pltpu.get_barrier_semaphore()
    rows = x1_ref.shape[1]

    @pl.loop(1, n)
    def _(s):
        pl.semaphore_signal(barrier, inc=1, device_id=place(s), device_id_type=MESH)

    loads = load_all(sources, loaded, load_sems)
    pl.semaphore_wait(barrier, n - 1)

    def parts(p):
        first = pl.multiple_of(p * rows, TILE)
        mine = o_own.at[me]
        low, high = pl.ds(0, MAIN), pl.ds(MAIN, SLOT - MAIN)
        left, right = pl.ds(0, TILE), pl.ds(rows + TILE, TILE)
        return (
            (o_ref.at[low, pl.ds(first, rows + 2 * TILE)], mine.at[low]),
            (o_tail.at[p], tail_own.at[me]),
            (o_ref.at[high, pl.ds(first, TILE)], mine.at[high, left]),
            (o_ref.at[high, pl.ds(pl.multiple_of(first + rows + TILE, TILE), TILE)], mine.at[high, right]),
        )

    copies = [
        pltpu.make_async_remote_copy(src_ref=src, dst_ref=dst, send_sem=send_o.at[s, i], recv_sem=recv_o.at[s, i],
                                     device_id=peer, device_id_type=MESH)
        for s, (peer, p) in enumerate(zip(peers, ids)) for i, (src, dst) in enumerate(parts(p))
    ]
    for copy in copies:
        copy.start()
    own = [pltpu.make_async_copy(src, dst, local_o.at[i]) for i, (src, dst) in enumerate(parts(me))]
    for copy in own:
        copy.start()
    for load in loads:
        load.wait()

    def arrive():
        for copy in own + copies:
            copy.wait()

    filter_kernel(x1_ref, x1l_ref, x1r_ref, o_own, tail_own, cols_ref, ext_ref, mixo_ref, pwi_ref, taps_ref, x2, oc, u, y, stat, wide, mask, live,
                  h3s, n3, inv3, value3, gate3, head_width=head_width, slot_count=slot_count, arrive=arrive)
    stats_out, stats_in = tell(stat, stats, send_a, recv_a, n_tm, n_head)
    sums_out, sums_in = tell(sums, all_sums, send_b, recv_b, n_tm, n_head)
    stats_out()
    second_kernel(x2, y, stats, cot_ref, cotl_ref, cotr_ref, cols_ref, pwo_ref, up_ref, down_ref,
                  out_ref, dx3, e, sums, pack_ref, smalld, h4s, das, s4s, dfs, ws, dcs, arrive=stats_in, leave=sums_out)

    def piece(c, s):
        at = pl.ds(pl.multiple_of(c * PIECE, PIECE), PIECE)
        return pltpu.make_async_remote_copy(src_ref=do.at[ids[s], :, at], dst_ref=do_all.at[me, :, at], send_sem=send_d.at[c, s],
                                            recv_sem=recv_d.at[c, s], device_id=peers[s], device_id_type=MESH)

    def ending(s):
        return pltpu.make_async_remote_copy(src_ref=tail.at[ids[s]], dst_ref=do_tails.at[me], send_sem=send_d.at[rows // PIECE, s],
                                            recv_sem=recv_d.at[rows // PIECE, s], device_id=peers[s], device_id_type=MESH)

    def ship(c):
        if isinstance(c, int):
            for h in range(n_head):
                tail[h] = fold_rows(tail_wide[4 * h : 4 * h + 4, :], 4).astype(BF)
        for s in range(n_head - 1):
            (ending(s) if isinstance(c, int) else piece(c, s)).start()

    unfilter_kernel(e, y, stats, all_sums, u, dx3, oc, cols_ref, ext_ref, pwi_ref, taps_ref, mixo_ref,
                    dx2_ref, do, pack_ref.at[pl.ds(layout.pointwise_in, layout.taps - layout.pointwise_in)], smalle, tapg, dyw, du, mask, prod, h3s, dgs, dms, gains2, live, n3, inv3, value3, gate3, tail_wide,
                    head_width=head_width, ship=ship, arrive=sums_in)
    own = [pltpu.make_async_copy(do.at[me], do_all.at[me], local_d.at[0]), pltpu.make_async_copy(tail.at[me], do_tails.at[me], local_d.at[1])]
    for copy in own:
        copy.start()
    end = put_taps(pack_ref, tapg[...], layout.taps)
    end = put_small(pack_ref, jnp.concatenate([smalld[...], smalle[...]], axis=0), end)
    if end < pack_ref.shape[0]:
        pack_ref[end:, :] = jnp.zeros((pack_ref.shape[0] - end, TILE), BF)
    for copy in own:
        copy.wait()
    for s in range(n_head - 1):
        ending(s).wait()

    @pl.loop(0, rows // PIECE)
    def _(c):
        for s in range(n_head - 1):
            piece(c, s).wait()


def sum_scratch(count, n_tm, n_head):
    half = count // 2
    big = half // (n_tm // 2)
    shapes = [(half, TILE), (half, TILE), (n_tm // 2, big, TILE), (big, TILE), (n_head, big // n_head, TILE), (big, TILE), (half, TILE)]
    return [pltpu.VMEM(shape, BF) for shape in shapes]


def gradient_sum(src_ref, out_ref, first, scratch, sems, local, n_tm, n_head):
    got0, half, got1, part1, got2, part2, whole = scratch
    tm, head = lax.axis_index("tm"), lax.axis_index("head")
    n_chip = n_tm // 2
    chip, core = tm // 2, lax.rem(tm, 2)
    size = src_ref.shape[0] // 2
    big = size // n_chip
    small = big // n_head
    sibling = {"tm": chip * 2 + 1 - core}

    def rows(i, count, base=0):
        return pl.ds(pl.multiple_of(base + i * count, 16), count)

    def send(src, dst, phase, s, peer):
        return pltpu.make_async_remote_copy(src_ref=src, dst_ref=dst, send_sem=sems.at[2 * phase, s], recv_sem=sems.at[2 * phase + 1, s],
                                            device_id=peer, device_id_type=MESH)

    def chip_peer(s):
        return lax.rem(chip + s, n_chip)

    def head_peer(s):
        return lax.rem(head + s, n_head)

    def zero():
        return send(src_ref.at[rows(1 - core, size)], got0, 0, 0, sibling)

    def one(s):
        return send(half.at[rows(chip_peer(s), big)], got1.at[s], 1, s, {"tm": chip_peer(s) * 2 + core})

    def two(s):
        return send(part1.at[rows(head_peer(s), small)], got2.at[s], 2, s, {"head": head_peer(s)})

    def three(s):
        at = part2.at[rows(head, small)]
        return send(at, at, 3, s, {"head": head_peer(s)})

    def four(s):
        return send(part2, whole.at[rows(chip, big)], 4, s, {"tm": chip_peer(s) * 2 + core})

    def five():
        return send(whole, out_ref.at[rows(core, size, first)], 5, 0, sibling)

    def keep():
        return pltpu.make_async_copy(whole, out_ref.at[rows(core, size, first)], local)

    def added(got, n):
        total = got[0].astype(F32)
        for s in range(1, n):
            total = total + got[s].astype(F32)
        return total.astype(BF)

    def step0():
        zero().start()

    def step1():
        zero().wait()
        half[...] = (src_ref[rows(core, size), :].astype(F32) + got0[...].astype(F32)).astype(BF)
        pl.loop(1, n_chip)(lambda s: one(s).start())
        got1[0] = half[rows(chip, big), :]

    def step2():
        pl.loop(1, n_chip)(lambda s: one(s).wait())
        part1[...] = added(got1, n_chip)
        pl.loop(1, n_head)(lambda s: two(s).start())
        got2[0] = part1[rows(head, small), :]

    def step3():
        pl.loop(1, n_head)(lambda s: two(s).wait())
        part2[rows(head, small), :] = added(got2, n_head)
        pl.loop(1, n_head)(lambda s: three(s).start())

    def step4():
        pl.loop(1, n_head)(lambda s: three(s).wait())
        pl.loop(1, n_chip)(lambda s: four(s).start())
        whole[rows(chip, big), :] = part2[...]

    def step5():
        pl.loop(1, n_chip)(lambda s: four(s).wait())
        five().start()
        keep().start()

    def step6():
        keep().wait()
        five().wait()

    return step0, step1, step2, step3, step4, step5, step6


def final_kernel(*refs, n_tm, n_head, parts):
    dqkv_ref, sources, refs = refs[0], refs[1:11], refs[11:]
    (grad_ref, total_ref), loaded, refs = refs[:2], refs[2:12], refs[12:]
    early_ref, frames_ref, x1_ref, h2_ref, dx2_ref, dtab_ref, cols_ref, up_ref, down_ref, mix_ref = loaded
    (dqkv, late, h1s, das, s1s, dfs, dqs, gains, up_part, down_part, mix_part), refs = refs[:11], refs[11:]
    sum_refs = [refs[7 * i : 7 * i + 7] for i in range(3)]
    load_sems, send_q, recv_q, local_q, sum_sems, sum_local = refs[21:]
    me, peers, ids = head_peers(n_head)
    tm = lax.axis_index("tm")
    rows = x1_ref.shape[1]
    barrier = pltpu.get_barrier_semaphore()
    for peer in peers:
        pl.semaphore_signal(barrier, inc=1, device_id=peer, device_id_type=MESH)

    @pl.loop(1, n_tm)
    def _(s):
        pl.semaphore_signal(barrier, inc=1, device_id={"tm": lax.rem(tm + s, n_tm)}, device_id_type=MESH)

    loads = load_all(sources, loaded, load_sems)
    pl.semaphore_wait(barrier, n_head + n_tm - 2)

    def piece(c, s):
        at = pl.ds(pl.multiple_of(c * PIECE, PIECE), PIECE)
        return pltpu.make_async_remote_copy(src_ref=dqkv_ref.at[ids[s], :, at], dst_ref=dqkv.at[me, :, at], send_sem=send_q.at[c, s],
                                            recv_sem=recv_q.at[c, s], device_id=peers[s], device_id_type=MESH)

    @pl.loop(0, rows // PIECE)
    def _(c):
        for s in range(n_head - 1):
            piece(c, s).start()

    own = pltpu.make_async_copy(dqkv_ref.at[me], dqkv.at[me], local_q)
    own.start()
    for load in loads:
        load.wait()
    late_at, last_at, end = parts

    def summed(i, src, first):
        return gradient_sum(src, total_ref, first, sum_refs[i], sum_sems.at[i], sum_local.at[i], n_tm, n_head)

    early = summed(0, early_ref, 0)
    last = summed(2, late.at[pl.ds(last_at - late_at, end - last_at)], last_at)
    late_sum = summed(1, late.at[pl.ds(0, last_at - late_at)], late_at) if last_at > late_at else [lambda: None] * 7
    early[0]()
    early[1]()
    own.wait()

    def arrive(c):
        for s in range(n_head - 1):
            piece(c, s).wait()

    def between(c):
        pl.when(c == 0)(early[2])

    def mixed():
        early[3]()
        late_sum[0]()

    close_kernel(frames_ref, x1_ref, h2_ref, dx2_ref, dqkv, dtab_ref, cols_ref, up_ref, down_ref, mix_ref,
                 grad_ref, late, h1s, das, s1s, dfs, dqs, gains, up_part, down_part, mix_part, arrive=arrive, between=between, mixed=mixed)
    for step in (last[0], late_sum[1], last[1], late_sum[2], last[2], early[4], late_sum[3], last[3], late_sum[4], early[5], last[4],
                 late_sum[5], early[6], last[5], late_sum[6], last[6]):
        step()


VMEM_MIB = 62


def body(
    frames, lengths, first_gain, first_shift, first_up, first_up_bias, first_down, first_down_bias, mix_gain, mix_shift,
    mix_inputs, position_bias, mix_output, mix_output_bias, filter_gain, filter_shift, pointwise_in, pointwise_in_bias,
    depthwise_taps, batch_gain, batch_shift, pointwise_out, pointwise_out_bias, second_gain, second_shift, second_up,
    second_up_bias, second_down, second_down_bias, final_gain, final_shift, cotangent,
):
    weights = Weights(
        first_gain, first_shift, first_up, first_up_bias, first_down, first_down_bias, mix_gain, mix_shift, mix_inputs, position_bias,
        mix_output, mix_output_bias, filter_gain, filter_shift, pointwise_in, pointwise_in_bias, depthwise_taps, batch_gain,
        batch_shift, pointwise_out, pointwise_out_bias, second_gain, second_shift, second_up, second_up_bias, second_down,
        second_down_bias, final_gain, final_shift)
    rows, width = frames.shape
    hidden = first_up.shape[1]
    n_head, n_tm = lax.axis_size("head"), lax.axis_size("tm")
    heads, span = position_bias.shape
    head_width = width // heads
    packed_rows = -(-3 * head_width // 16) * 16
    group = rows * n_head
    lanes = rows + TILE
    slots = lengths.shape[1]
    taps = depthwise_taps.shape[0]
    layout = pack_layout(width, hidden, mix_inputs.shape[1], taps, n_tm * n_head)

    vectors = tuple(getattr(weights, name) for name in VEC.__dict__)
    frames_t, cot_t, first_down_t, second_down_t = frames.T, cotangent.T, first_down.T, second_down.T
    vm, dma, hbm = pltpu.VMEM, pltpu.SemaphoreType.DMA, pl.BlockSpec(memory_space=pl.ANY)
    steps = rows // PIECE
    piece_sems = dma((steps, n_head - 1))

    def comm_call(kernel, name, collective_id, ins, in_hbm, outs, out_hbm, scratch):
        return pl.pallas_call(
            kernel,
            out_shape=tuple(jax.ShapeDtypeStruct(s, t) for s, t in outs),
            in_specs=[hbm if i in in_hbm else pl.BlockSpec() for i in range(len(ins))],
            out_specs=tuple(hbm if i in out_hbm else pl.BlockSpec() for i in range(len(outs))),
            scratch_shapes=scratch,
            compiler_params=pltpu.CompilerParams(collective_id=collective_id, has_side_effects=True, vmem_limit_bytes=VMEM_MIB * 2**20),
            name=name,
        )(*ins)

    ins = (frames_t, lengths, first_up, first_down_t, mix_inputs) + vectors + (cot_t,)
    x1, h2, cols, bounds, plan, ext, qkv_all, x1l, x1r, cotl, cotr = comm_call(
        functools.partial(opening_kernel, packed_rows=packed_rows, n=n_head), "opening", 1, ins, (len(ins) - 1,),
        [((width, rows), F32), ((width, rows), BF), ((hidden, VEC_ROWS), F32), ((2, group + 2 * PAD), jnp.int32),
         ((group // BLK, 128), jnp.int32), ((1, lanes), jnp.int32), ((n_head, packed_rows, rows), BF),
         ((width, TILE), F32), ((width, TILE), F32), ((width, TILE), BF), ((width, TILE), BF)], range(6, 11),
        [vm((n_head, packed_rows, rows), BF), vm((1, group + 2 * TILE), jnp.int32), piece_sems, piece_sems, dma, dma((4,)), dma((4,))])
    o, o_tail, of, lse = attend_forward(qkv_all, bounds, plan, position_bias, head_width)
    everyone_sems = dma((n_tm * n_head,))
    ins = (x1, x1l, x1r, cot_t, cotl, cotr, cols, ext, mix_output, pointwise_in, depthwise_taps, pointwise_out, second_up, second_down_t)
    out, dx2, do_all, do_tails, pack = comm_call(
        functools.partial(middle_kernel, n_tm=n_tm, n_head=n_head, head_width=head_width, slot_count=slots, layout=layout),
        "middle", 2, (o, o_tail) + ins, range(len(ins) + 2),
        [((width, rows), BF), ((width, rows), F32), ((n_head, MAIN, rows), BF), ((n_head, 16, rows // 4), BF), ((layout.late, TILE), BF)],
        (2, 3),
        [vm(a.shape, a.dtype) for a in ins] + [
            vm((n_head, SLOT, rows + 2 * TILE), BF), vm((width, lanes), F32), vm((width + 16, rows), BF), vm((width, lanes), BF),
            vm((width, lanes), F32), vm((4, TILE), F32), vm((n_tm * n_head, 4, TILE), F32), vm((width, rows), F32),
            vm((width, lanes), F32), vm((4, TILE), F32), vm((n_tm * n_head, 4, TILE), F32), vm((n_head, MAIN, rows), BF),
            vm((width, lanes), F32), vm((taps + 1, 8, lanes), F32), vm((1, lanes), F32),
            vm((width, rows), BF), vm((hidden, rows), BF), vm((hidden + 16, rows), BF), vm((width, rows), BF),
            vm((width + 16, rows), BF), vm((width, rows), BF),
            vm((width, lanes), F32), vm((width, rows), F32), vm((taps, width, TILE), F32), vm((width + 16, rows), BF),
            vm((2 * width, rows), BF), vm((width, rows), BF), vm((2, width, TILE), F32),
            vm((16, 5 * TILE), F32), vm((16, 5 * TILE), F32), vm((taps, width), F32),
            vm((width, rows), F32), vm((1, rows), F32), vm((width, rows), F32), vm((width, rows), F32),
            vm((n_head, 16, rows // 4), BF), vm((4 * n_head, rows), F32), vm((n_head, 16, rows // 4), BF),
            dma((len(ins),)), dma((n_head - 1, 4)), dma((n_head - 1, 4)), dma((4,)), everyone_sems, everyone_sems, everyone_sems, everyone_sems,
            dma((steps + 1, n_head - 1)), dma((steps + 1, n_head - 1)), dma((2,)),
        ])
    dqkv, dtab = attend_backward(qkv_all, do_all, do_tails, of, lse, bounds, plan, position_bias, head_width)
    parts = (layout.late, layout.last, layout.rows)
    sizes = (layout.late, max(layout.last - layout.late, 16 * n_tm * n_head), layout.rows - layout.last)
    ins = (pack, frames_t, x1, h2, dx2, dtab, cols, first_up, first_down_t, mix_inputs)
    grad, total = comm_call(
        functools.partial(final_kernel, n_tm=n_tm, n_head=n_head, parts=parts), "final", 3, (dqkv,) + ins, range(len(ins) + 1),
        [((width, rows), F32), ((layout.rows, TILE), BF)], (1,),
        [vm(a.shape, a.dtype) for a in ins] + [
            vm((n_head, packed_rows, rows), BF), vm((layout.rows - layout.late, TILE), BF),
            vm((width, rows), BF), vm((hidden, rows), BF), vm((hidden, rows), BF), vm((width, rows), BF),
            vm((n_head * packed_rows, rows), BF), vm((4, width, TILE), F32), vm((width, hidden), F32), vm((width, hidden), F32),
            vm((width, n_head * packed_rows), F32),
            *[s for size in sizes for s in sum_scratch(size, n_tm, n_head)],
            dma((len(ins),)), piece_sems, piece_sems, dma, dma((3, 12, max(n_tm // 2, n_head))), dma((3,)),
        ])
    shapes = Weights(**{n: w.shape for n, w in weights.__dict__.items()})
    shapes.first_down = shapes.second_down = first_down_t.shape
    results = [((width, rows), BF), ((width, rows), F32)] + [(s, F32) for s in shapes.__dict__.values()]
    out, grad, *summed = pl.pallas_call(
        functools.partial(unpack_kernel, layout=layout),
        out_shape=tuple(jax.ShapeDtypeStruct(s, t) for s, t in results),
        compiler_params=pltpu.CompilerParams(vmem_limit_bytes=VMEM_MIB * 2**20),
        name="unpack",
    )(total, out, grad)
    summed = Weights(*summed)
    summed.first_down, summed.second_down = summed.first_down.T, summed.second_down.T
    return (out.T, grad.T) + tuple(summed.__dict__.values())


def solution(mesh):
    rows = P(("tm", "head"), None)
    placed = (rows, P("tm", None)) + (P(),) * 29 + (rows,)
    return jax.shard_map(body, mesh=mesh, in_specs=placed, out_specs=(rows, rows) + (P(),) * 29, check_vma=False)
```

```python
import dataclasses
import functools
import math
import types

import jax
import jax.numpy as jnp
from jax import lax
from jax.experimental import pallas as pl
from jax.experimental.pallas import tpu as pltpu
from jax.sharding import PartitionSpec as P

BF = jnp.bfloat16
F32 = jnp.float32
LOG2E = math.log2(math.e)
BLK = 512
UNIT = 128
PER = BLK // UNIT
NEAR = PER + 2
PAD = 8 * UNIT
SLOT = 48
MAIN = 32
DEPTH = 128
MASKED = -1e30
GANG = 4
NN = (((1,), (0,)), ((), ()))
NT = (((1,), (1,)), ((), ()))
TN = (((0,), (0,)), ((), ()))


def dot(a, b, dims=NN):
    return lax.dot_general(a, b, dims, preferred_element_type=F32)


def iota(shape, dim):
    return lax.broadcasted_iota(jnp.int32, shape, dim)


def spread_cols(width, slots, slot_rows, used):
    row, column = iota((slots * slot_rows, width), 0), iota((slots * slot_rows, width), 1)
    hit = jnp.zeros((slots * slot_rows, width), jnp.bool_)
    for s in range(slots):
        f = row - slot_rows * s
        hit = hit | ((f >= 0) & (f < used) & (column == used * s + f))
    return hit.astype(F32).astype(BF)


def split3(v):
    hi = v.astype(BF).astype(F32)
    r1 = v - hi
    mid = r1.astype(BF).astype(F32)
    return hi, mid, r1 - mid


def three_rows(v, rows):
    a, b, e = split3(v)
    row = iota((rows, v.shape[1]), 0)
    return jnp.where(row == 0, a, jnp.where(row == 1, b, jnp.where(row == 2, e, 0.0)))


def pick_row(ref, index):
    values = ref[...].astype(F32)
    return jnp.sum(jnp.where(iota(values.shape, 0) == index, values, 0.0), axis=0, keepdims=True)


def bias_square(table, d):
    span = table.shape[1]
    half = span // 2
    lanes = 2 * UNIT
    u = iota((span, lanes), 1)
    u = jnp.where(u < UNIT, u, u - lanes)
    ids = jnp.clip(-UNIT * d - u, -half, half - 1) + half
    hot = (ids == iota((span, lanes), 0)).astype(F32).astype(BF)
    line = dot(jnp.broadcast_to(table, (UNIT, span)).astype(BF), hot) * LOG2E
    return pltpu.roll(line, 0, 1, stride=1, stride_axis=0)[:, :UNIT]


def bias_near(table, tile, keys_near):
    span = table.shape[1]
    squares = {d: bias_square(table, d) for d in (-1, 0, 1)}
    low = jnp.broadcast_to(table[:, :1] * LOG2E, (UNIT, UNIT))
    high = jnp.broadcast_to(table[:, span - 1 :] * LOG2E, (UNIT, UNIT))
    for r in range(tile.shape[0] // UNIT):
        for c in range(tile.shape[1] // UNIT):
            d = c - (r - 1) if keys_near else (c - 1) - r
            part = squares[d] if abs(d) < 2 else (low if d > 0 else high)
            tile[r * UNIT : (r + 1) * UNIT, c * UNIT : (c + 1) * UNIT] = part


def units_at(u, count):
    return pl.ds(pl.multiple_of(u * UNIT, UNIT), count * UNIT)


def far_windows(low, plain, edge, step, side, up, fine):
    sign = 1 if up else -1

    def run(at, times, size, masked):
        def one(i, carry):
            near = at + sign * i * size
            step(near if up else near - size, size, side, masked)
            return carry

        lax.fori_loop(0, times, one, 0)
        return at + sign * times * size

    at = edge if plain is None else run(edge, sign * (plain - edge) // 8, 8, False)
    left = sign * (low - at)
    tail = lax.rem(left, 8)
    more = tail > (6 if fine else 4)
    at = run(at, left // 8 + more.astype(jnp.int32), 8, True)
    tail = jnp.where(more, 0, tail)
    four = tail > (2 if fine else 0)
    at = run(at, four.astype(jnp.int32), 4, True)
    if fine:
        run(at, (tail - jnp.where(four, 4, 0) > 0).astype(jnp.int32), 2, True)


def far_sweep(plan, block, step, before, after, fine):
    low, plain_low, plain_high, high, low_half, high_half = [plan[block, i] for i in range(6)]
    start, stop = PER * block - 1, PER * block + PER + 1
    for whole, part in ((True, None), (False, 0)):
        @pl.when((low_half == 0) if whole else (low_half != 0))
        def _():
            far_windows(low, plain_low if whole else None, start, functools.partial(step, part=part), before, False, fine)

    for whole, part in ((True, None), (False, 1)):
        @pl.when((high_half == 0) if whole else (high_half != 0))
        def _():
            far_windows(high, plain_high if whole else None, stop, functools.partial(step, part=part), after, True, fine)


def fold_rows(four, pieces):
    size = four.shape[1] // pieces
    return jnp.concatenate([four[:, i * size : (i + 1) * size] for i in range(pieces)], axis=0)


def unfold_rows(folded):
    return jnp.concatenate([folded[i : i + 4, :] for i in range(0, folded.shape[0], 4)], axis=1)


def part_at(block, part):
    if part is None:
        return units_at(PER * block, PER)
    return units_at(PER * block + part * (PER // 2), PER // 2)


def has_far(plan, block):
    return (plan[block, 0] < PER * block - 1) | (plan[block, 3] > PER * block + PER + 1)


def segment_rows(ends, lengths, place, total):
    slots = ends.shape[0]
    before = ends <= jnp.broadcast_to(place, (slots, place.shape[1]))
    seg = jnp.sum(before.astype(jnp.int32), axis=0, keepdims=True)
    first = jnp.sum(jnp.where(before, lengths, 0), axis=0, keepdims=True)
    stop = jnp.min(jnp.where(before, total, ends), axis=0, keepdims=True)
    return seg, first, stop


def block_plan(ends, ends_row, total):
    slots = ends.shape[0]
    blocks, units = total // BLK, total // UNIT

    def along(place):
        return jnp.sum((ends <= jnp.broadcast_to(place, (slots, 128))).astype(jnp.int32), axis=0, keepdims=True)

    def down(place):
        return jnp.sum((jnp.broadcast_to(ends_row, (blocks, slots)) <= place).astype(F32), axis=1, keepdims=True).astype(jnp.int32)

    unit = iota((1, 128), 1)
    u_first, u_last = along(unit * UNIT), along(unit * UNIT + UNIT - 1)
    b = iota((blocks, 1), 0)
    first, last = down(b * BLK), down(b * BLK + BLK - 1)
    low_half = (down(b * BLK + BLK // 2) != first).astype(jnp.int32)
    high_half = (down(b * BLK + BLK // 2 - 1) != last).astype(jnp.int32)
    start, stop = PER * b - 1, PER * b + PER + 1
    inside = unit < units

    def count(hit):
        return jnp.sum((hit & inside).astype(F32), axis=1, keepdims=True).astype(jnp.int32)

    low = jnp.minimum(count(u_last < first), start)
    high = jnp.maximum(units - count(u_first > last), stop)
    plain_low = start - count((unit < start) & (u_first == last))
    plain_high = stop + count((unit >= stop) & (u_last == first))
    lane = iota((blocks, 128), 1)
    out = jnp.zeros((blocks, 128), jnp.int32)
    for i, v in enumerate((low, plain_low, plain_high, high, low_half, high_half)):
        out = jnp.where(lane == i, v, out)
    return out


def meets(first_key, rows, bounds):
    key = iota((rows, bounds.shape[1]), 0)
    return (key >= bounds[0:1, :] - first_key) & (key < bounds[1:2, :] - first_key)


def fwd_kernel(plan, qkv_ref, table_ref, bound_ref, o_ref, tail_ref, of_ref, lse_ref, qaug, kn, vt, tile, top_ref, acc, *, head_width):
    chunks, packed_rows, rows = qkv_ref.shape
    total = chunks * rows
    blocks = total // BLK
    span = table_ref.shape[1]
    table = pick_row(table_ref, lax.axis_index("head"))
    far = (table[:, :1] * LOG2E, table[:, span - 1 :] * LOG2E)
    pick = spread_cols(packed_rows, 3, SLOT, head_width)
    scale = LOG2E / math.sqrt(head_width)
    o_ref[:, :UNIT] = jnp.zeros((SLOT, UNIT), BF)
    o_ref[:, UNIT + total :] = jnp.zeros((SLOT, UNIT), BF)
    for edge in (slice(0, PAD), slice(PAD + total, 2 * PAD + total)):
        kn[edge, :] = jnp.zeros((PAD, DEPTH), BF)
        vt[:, edge] = jnp.zeros((SLOT, PAD), BF)
    bias_near(table, tile, True)
    rest = DEPTH - 2 * SLOT

    @pl.loop(0, chunks)
    def _(c):
        at = pl.ds(pl.multiple_of(c * rows, rows), rows)
        at_pad = pl.ds(pl.multiple_of(c * rows + PAD, UNIT), rows)
        parts = dot(pick, qkv_ref[c])
        q = parts[:SLOT] * scale
        hi = q.astype(BF)
        lo = (q - hi.astype(F32)).astype(BF)
        for s in range(3):
            qaug[s, :SLOT, at] = hi
            qaug[s, SLOT : 2 * SLOT, at] = lo
            qaug[s, 2 * SLOT :, at] = jnp.zeros((rest, rows), BF)
        k = parts[SLOT : 2 * SLOT]
        one3 = (iota((rest, rows), 0) < 3).astype(F32)
        kn[at_pad, :] = jnp.concatenate([k, k, one3], axis=0).T.astype(BF)
        one = (iota((SLOT, rows), 0) == head_width).astype(F32)
        vt[:, at_pad] = (parts[2 * SLOT :] + one).astype(BF)

    def top(x):
        return jnp.max(x.reshape(x.shape[0] // 8, 8, BLK), axis=0)

    @pl.loop(0, blocks // GANG)
    def _(pair):
        blocks_now = [GANG * pair + i for i in range(GANG)]
        at_q = [units_at(PER * b, PER) for b in blocks_now]
        near = [units_at(PER * b - 1 + PAD // UNIT, NEAR) for b in blocks_now]
        x = [dot(kn[n, :], qaug[1, :, q]) + tile[...] for n, q in zip(near, at_q)]
        x = [
            jnp.where(meets(PER * b * UNIT - UNIT, NEAR * UNIT, bound_ref[:, units_at(PER * b + PAD // UNIT, PER)]), v, MASKED)
            for b, v in zip(blocks_now, x)
        ]
        m = [jnp.max(top(v), axis=0, keepdims=True) for v in x]
        p = [jnp.exp2(v - w).astype(BF) for v, w in zip(x, m)]
        out = [dot(vt[:, n], v) for n, v in zip(near, p)]
        for q, w, v in zip(at_q, m, out):
            acc[:, q] = v
            lse_ref[:, q] = w
            qaug[0, 2 * SLOT :, q] = three_rows(far[0] - w, rest).astype(BF)
            qaug[2, 2 * SLOT :, q] = three_rows(far[1] - w, rest).astype(BF)

    @pl.loop(0, blocks)
    def _(b):
        @pl.when(has_far(plan, b))
        def _():
            at_q = units_at(PER * b, PER)

            def scores(u, count, side, masked, part):
                x = dot(kn[units_at(u + PAD // UNIT, count), :], qaug[side, :, part_at(b, part)])
                if masked:
                    x = jnp.where(meets(u * UNIT, count * UNIT, bound_ref[:, part_at(b + PAD // BLK, part)]), x, MASKED)
                return x

            near_acc = acc[:, at_q]

            def add(u, count, side, masked, part):
                p = jnp.exp2(scores(u, count, side, masked, part)).astype(BF)
                acc[:, part_at(b, part)] += dot(vt[:, units_at(u + PAD // UNIT, count)], p)

            far_sweep(plan, b, add, 0, 2, False)
            sums = acc[head_width : head_width + 1, at_q]
            over = jnp.max(jnp.where(sums < 2.0**60, 0.0, 1.0))

            @pl.when(over > 0.5)
            def _():
                top_ref[...] = jnp.zeros_like(top_ref)

                def half_of(part):
                    return slice(None) if part is None else slice(part * BLK // 2, (part + 1) * BLK // 2)

                def first(u, count, side, masked, part):
                    x = scores(u, count, side, masked, part)
                    best = jnp.max(x.reshape(x.shape[0] // 8, 8, x.shape[1]), axis=0)
                    top_ref[:, half_of(part)] = jnp.maximum(top_ref[:, half_of(part)], best)

                far_sweep(plan, b, first, 0, 2, False)
                m = jnp.max(top_ref[...], axis=0, keepdims=True)
                acc[:, at_q] = near_acc * jnp.exp2(-m)
                lse_ref[:, at_q] += m

                def second(u, count, side, masked, part):
                    p = jnp.exp2(scores(u, count, side, masked, part) - m[:, half_of(part)]).astype(BF)
                    acc[:, part_at(b, part)] += dot(vt[:, units_at(u + PAD // UNIT, count)], p)

                far_sweep(plan, b, second, 0, 2, False)

    @pl.loop(0, chunks)
    def _(c):
        at = pl.ds(pl.multiple_of(c * rows, rows), rows)
        total_p = acc[head_width : head_width + 1, at]
        out = acc[:, at] / total_p
        o_ref[:, pl.ds(pl.multiple_of(c * rows + UNIT, UNIT), rows)] = out.astype(BF)
        tail_ref[c] = fold_rows(out[MAIN : MAIN + 4], 4).astype(BF)
        of_ref[:, at] = out[: of_ref.shape[0]]
        lse_ref[:, at] = lse_ref[:, at] + jnp.log2(total_p)


def attend_forward(qkv, bounds, plan, table, head_width):
    chunks, packed_rows, rows = qkv.shape
    total = chunks * rows
    vm = pltpu.VMEM
    return pl.pallas_call(
        functools.partial(fwd_kernel, head_width=head_width),
        out_shape=(
            jax.ShapeDtypeStruct((SLOT, total + 2 * UNIT), BF),
            jax.ShapeDtypeStruct((chunks, 16, rows // 4), BF),
            jax.ShapeDtypeStruct((40, total), F32),
            jax.ShapeDtypeStruct((1, total), F32),
        ),
        in_specs=[pl.BlockSpec(memory_space=pltpu.SMEM)] + [pl.BlockSpec()] * 3,
        scratch_shapes=[
            vm((3, DEPTH, total), BF),
            vm((total + 2 * PAD, DEPTH), BF),
            vm((SLOT, total + 2 * PAD), BF),
            vm((NEAR * UNIT, BLK), F32),
            vm((8, BLK), F32),
            vm((SLOT, total), F32),
        ],
        compiler_params=pltpu.CompilerParams(vmem_limit_bytes=62 * 2**20),
        name="attend_forward",
    )(plan, qkv, table, bounds)


def bwd_kernel(plan, qkv_ref, do_ref, tail_ref, of_ref, lse_ref, table_ref, bound_ref, dqkv_ref, dtab_ref,
               qaug, kn, kt, vn, dot_t, qn, don, tile, dq, band, ends, dv_acc, dk_acc, *, head_width):
    chunks, packed_rows, rows = qkv_ref.shape
    total = chunks * rows
    blocks = total // BLK
    span = table_ref.shape[1]
    table = pick_row(table_ref, lax.axis_index("head"))
    pick = spread_cols(packed_rows, 3, SLOT, head_width)
    scale = LOG2E / math.sqrt(head_width)
    back = 1.0 / math.sqrt(head_width)
    rest = DEPTH - 2 * SLOT
    bias_near(table, tile, False)
    for edge in (slice(0, PAD), slice(PAD + total, 2 * PAD + total)):
        for s in range(3):
            qaug[s, :, edge] = jnp.zeros((DEPTH, PAD), BF)
        dot_t[:, edge] = jnp.zeros((DEPTH, PAD), BF)
        qn[edge, :] = jnp.zeros((PAD, DEPTH), BF)
        don[edge, :] = jnp.zeros((PAD, DEPTH), BF)

    @pl.loop(0, chunks)
    def _(c):
        at = pl.ds(pl.multiple_of(c * rows, rows), rows)
        at_pad = pl.ds(pl.multiple_of(c * rows + PAD, UNIT), rows)
        parts = dot(pick, qkv_ref[c])
        q, k, v = parts[:SLOT], parts[SLOT : 2 * SLOT], parts[2 * SLOT :]
        qs = q * scale
        hi = qs.astype(BF)
        lo = (qs - hi.astype(F32)).astype(BF)
        lse = lse_ref[:, at]
        for s, shift in enumerate((table[:, :1] * LOG2E, 0.0, table[:, span - 1 :] * LOG2E)):
            qaug[s, :SLOT, at_pad] = hi
            qaug[s, SLOT : 2 * SLOT, at_pad] = lo
            qaug[s, 2 * SLOT :, at_pad] = three_rows(shift - lse, rest).astype(BF)
        one3 = (iota((rest, rows), 0) < 3).astype(F32)
        row48 = iota((SLOT, rows), 0)
        none = jnp.zeros((rest, rows), F32)
        empty = jnp.zeros((SLOT, rows), F32)
        kn[at, :] = jnp.concatenate([k, k, one3], axis=0).T.astype(BF)
        kt[:, at] = k.astype(BF)
        vn[at, :] = jnp.concatenate([v, empty, one3], axis=0).T.astype(BF)
        tail = unfold_rows(tail_ref[c].astype(F32))
        do = jnp.concatenate([do_ref[c].astype(F32), tail, jnp.zeros((SLOT - MAIN - 4, rows), F32)], axis=0)
        centre = jnp.sum(do[: of_ref.shape[0]] * of_ref[:, at], axis=0, keepdims=True)
        dot_t[:SLOT, at_pad] = do.astype(BF)
        dot_t[SLOT : 2 * SLOT, at_pad] = empty.astype(BF)
        dot_t[2 * SLOT :, at_pad] = three_rows(-centre, rest).astype(BF)
        qn[at_pad, :] = jnp.concatenate([q + (row48 == head_width).astype(F32), empty, none], axis=0).T.astype(BF)
        don[at_pad, :] = jnp.concatenate([do, empty, none], axis=0).T.astype(BF)

    dq[...] = jnp.zeros_like(dq)
    band[...] = jnp.zeros_like(band)
    ends[...] = jnp.zeros_like(ends)

    @pl.loop(0, blocks // GANG)
    def _(pair):
        width = NEAR * UNIT
        wide = width + (GANG - 1) * BLK
        blocks_now = [GANG * pair + i for i in range(GANG)]
        at_k = [units_at(PER * b, PER) for b in blocks_now]
        near = [units_at(PER * b - 1 + PAD // UNIT, NEAR) for b in blocks_now]
        x = [dot(kn[k, :], qaug[1, :, n]) + tile[...] for k, n in zip(at_k, near)]
        dp = [dot(vn[k, :], dot_t[:, n]) for k, n in zip(at_k, near)]
        p = [jnp.where(meets(b * BLK, BLK, bound_ref[:, n]), jnp.exp2(v), 0.0) for b, n, v in zip(blocks_now, near, x)]
        dsb = [(v * w).astype(BF) for v, w in zip(p, dp)]
        dv = [dot(v.astype(BF), don[n, :]) for n, v in zip(near, p)]
        dk = [dot(v, qn[n, :]) for n, v in zip(near, dsb)]
        part = [dot(kt[:, k], v) for k, v in zip(at_k, dsb)]
        for k, v, w in zip(at_k, dv, dk):
            dv_acc[k, :] = v
            dk_acc[k, :] = w
        gap = [jnp.zeros((SLOT, BLK), F32)]
        whole = [jnp.concatenate(gap * i + [v] + gap * (GANG - 1 - i), axis=1) for i, v in enumerate(part)]
        lines = [v.astype(F32) for v in dsb]
        dq[:, units_at(GANG * PER * pair - 1 + PAD // UNIT, wide // UNIT)] += functools.reduce(jnp.add, whole)
        band[...] += functools.reduce(jnp.add, lines)

    @pl.loop(0, blocks)
    def _(b):
        @pl.when(has_far(plan, b))
        def _():
            def far(u, count, side, masked, part):
                at_k = part_at(b, part)
                at_q = units_at(u + PAD // UNIT, count)
                p = jnp.exp2(dot(kn[at_k, :], qaug[side, :, at_q]))
                if masked:
                    first_key = b * BLK + (0 if part is None else part * BLK // 2)
                    p = jnp.where(meets(first_key, at_k.size, bound_ref[:, at_q]), p, 0.0)
                dsb = (p * dot(vn[at_k, :], dot_t[:, at_q])).astype(BF)
                dq[:, at_q] += dot(kt[:, at_k], dsb)
                dv_acc[at_k, :] += dot(p.astype(BF), don[at_q, :])
                dk = dot(dsb, qn[at_q, :])
                dk_acc[at_k, :] += dk
                ends[side // 2] += jnp.sum(dk.reshape(dk.shape[0] // 8, 8, DEPTH), axis=0)

            far_sweep(plan, b, far, 2, 0, True)

    def take(part, lanes):
        row, lane = iota((packed_rows, lanes), 0), iota((packed_rows, lanes), 1)
        return ((row - head_width * part == lane) & (lane < head_width)).astype(F32).astype(BF)

    @pl.loop(0, chunks)
    def _(c):
        at = pl.ds(pl.multiple_of(c * rows, rows), rows)
        at_pad = pl.ds(pl.multiple_of(c * rows + PAD, UNIT), rows)
        packed = dot(take(0, SLOT), (dq[:, at_pad] * back).astype(BF))
        packed += dot(take(1, DEPTH), (dk_acc[at, :] * back).astype(BF), NT)
        packed += dot(take(2, DEPTH), dv_acc[at, :].astype(BF), NT)
        dqkv_ref[c] = packed.astype(BF)

    flip = (iota((UNIT, UNIT), 0) + iota((UNIT, UNIT), 1) == UNIT - 1).astype(F32)
    half = span // 2
    lane = iota((8, span), 1)
    column = iota((8, DEPTH), 1) == head_width
    out = jnp.zeros((8, span), F32)
    far_sum = [jnp.where(column, ends[i], 0.0) for i in range(2)]
    for d in range(-PER, PER + 1):
        part = jnp.zeros((UNIT, UNIT), F32)
        for r in range(PER):
            c = r + d + 1
            if 0 <= c < NEAR:
                part = part + band[r * UNIT : (r + 1) * UNIT, c * UNIT : (c + 1) * UNIT]
        if abs(d) > 1:
            far_sum[0 if d > 0 else 1] += jnp.sum(part.reshape(UNIT // 8, 8, UNIT), axis=0)
            continue
        turned = lax.dot_general(flip, part, NN, precision=lax.Precision.HIGHEST, preferred_element_type=F32)
        wide = jnp.concatenate([turned, jnp.zeros_like(turned)], axis=1)
        skewed = pltpu.roll(wide, 0, 1, stride=1, stride_axis=0)
        line = jnp.sum(skewed.reshape(UNIT // 8, 8, 2 * UNIT), axis=0)
        offset = UNIT - 1 - d * UNIT - iota((span, 2 * UNIT), 1)
        hot = (jnp.clip(offset, -half, half - 1) + half == iota((span, 2 * UNIT), 0)).astype(F32)
        out += lax.dot_general(line, hot, NT, precision=lax.Precision.HIGHEST, preferred_element_type=F32)
    out += jnp.where(lane == 0, jnp.sum(far_sum[0], axis=1, keepdims=True), 0.0)
    out += jnp.where(lane == span - 1, jnp.sum(far_sum[1], axis=1, keepdims=True), 0.0)
    out = jnp.sum(out, axis=0, keepdims=True)
    dtab_ref[...] = out


def attend_backward(qkv, do, tail, of, lse, bounds, plan, table, head_width):
    chunks, packed_rows, rows = qkv.shape
    total = chunks * rows
    padded = total + 2 * PAD
    span = table.shape[1]
    vm = pltpu.VMEM
    return pl.pallas_call(
        functools.partial(bwd_kernel, head_width=head_width),
        out_shape=(
            jax.ShapeDtypeStruct((chunks, packed_rows, rows), BF),
            jax.ShapeDtypeStruct((1, span), F32),
        ),
        in_specs=[pl.BlockSpec(memory_space=pltpu.SMEM)] + [pl.BlockSpec()] * 7,
        scratch_shapes=[
            vm((3, DEPTH, padded), BF),
            vm((total, DEPTH), BF),
            vm((SLOT, total), BF),
            vm((total, DEPTH), BF),
            vm((DEPTH, padded), BF),
            vm((padded, DEPTH), BF),
            vm((padded, DEPTH), BF),
            vm((BLK, NEAR * UNIT), F32),
            vm((SLOT, padded), F32),
            vm((BLK, NEAR * UNIT), F32),
            vm((2, 8, DEPTH), F32),
            vm((total, DEPTH), F32),
            vm((total, DEPTH), F32),
        ],
        compiler_params=pltpu.CompilerParams(vmem_limit_bytes=62 * 2**20),
        name="attend_backward",
    )(plan, qkv, do, tail, of, lse, table, bounds)

VEC = types.SimpleNamespace(
    first_gain=0, first_shift=1, first_up_bias=2, first_down_bias=3, mix_gain=4, mix_shift=5, mix_output_bias=6, filter_gain=7,
    filter_shift=8, pointwise_in_bias=9, batch_gain=10, batch_shift=11, pointwise_out_bias=12, second_gain=13, second_shift=14,
    second_up_bias=15, second_down_bias=16, final_gain=17, final_shift=18,
)
VEC_ROWS = 24
EPSILON = 1e-05
HALO = 64
TILE = 128
PIECE = 256
STEP = 1024


def col(cols_ref, i, size):
    return cols_ref[:size, i : i + 1]


def eye(n):
    return (iota((n, n), 0) == iota((n, n), 1)).astype(F32).astype(BF)


def flipped(mat):
    return dot(eye(mat.shape[1]), mat, NT).astype(BF)


def exact(a, b, dims=NN):
    return lax.dot_general(a, b, dims, precision=lax.Precision.HIGHEST, preferred_element_type=F32)


def folded(values):
    part = values[:, :TILE]
    for at in range(TILE, values.shape[1], TILE):
        part = part + values[:, at : at + TILE]
    return part


def row_sums(values):
    return exact(jnp.ones((8, TILE), F32), values, NT)


def norm(x):
    m = jnp.mean(x, axis=0, keepdims=True)
    c = x - m
    inv = lax.rsqrt(jnp.mean(c * c, axis=0, keepdims=True) + EPSILON)
    return c * inv, inv


def norm_back(e, n, inv, gain):
    ea = e * gain
    return inv * (ea - jnp.mean(ea, axis=0, keepdims=True) - n * jnp.mean(ea * n, axis=0, keepdims=True))


def sigmoid(v):
    return 0.5 + 0.5 * jnp.tanh(0.5 * v)


def ones_row(rows, lanes):
    return (iota((rows, lanes), 0) == 0).astype(F32).astype(BF)


def open_rows(frames_ref, up_ref, down_ref, mix_ref, x1_ref, h2_ref, qkv_ref, cols_ref, packed_rows, ship):
    width, rows = frames_ref.shape
    hidden = up_ref.shape[1]
    heads = qkv_ref.shape[0]
    up_t = flipped(up_ref[...])
    mix_t = dot(spread_cols(mix_ref.shape[1], heads, packed_rows, mix_ref.shape[1] // heads), mix_ref[...], NT).astype(BF)

    @pl.loop(0, rows // PIECE)
    def _(c):
        at = pl.ds(pl.multiple_of(c * PIECE, PIECE), PIECE)
        x0 = frames_ref[:, at].astype(F32)
        n, _ = norm(x0)
        h1 = (n * col(cols_ref, VEC.first_gain, width) + col(cols_ref, VEC.first_shift, width)).astype(BF)
        a1 = dot(up_t, h1) + col(cols_ref, VEC.first_up_bias, hidden)
        s1 = (a1 * sigmoid(a1)).astype(BF)
        x1 = x0 + 0.5 * (dot(down_ref[...], s1) + col(cols_ref, VEC.first_down_bias, width))
        x1_ref[:, at] = x1
        n, _ = norm(x1)
        h2 = (n * col(cols_ref, VEC.mix_gain, width) + col(cols_ref, VEC.mix_shift, width)).astype(BF)
        h2_ref[:, at] = h2
        qkv = dot(mix_t, h2).astype(BF)
        for h in range(heads):
            qkv_ref[h, :, at] = qkv[h * packed_rows : (h + 1) * packed_rows]
        ship(c)


def open_segments(len_ref, bound_ref, plan_ref, ext_ref, line):
    rows = ext_ref.shape[1] - TILE
    group = bound_ref.shape[1] - 2 * PAD
    slots = len_ref.shape[1]
    lengths = jnp.broadcast_to(len_ref[...].astype(F32), (8, slots))
    row, column = iota((slots, slots), 0), iota((slots, slots), 1)
    ends = exact((column <= row).astype(F32), lengths, NT)[:, :1].astype(jnp.int32)
    own_len = exact((column == row).astype(F32), lengths, NT)[:, :1].astype(jnp.int32)
    ends_row = exact(lengths, (row <= column).astype(F32))[:1].astype(jnp.int32)
    plan_ref[...] = block_plan(ends, ends_row, group)
    line[...] = jnp.full_like(line, -1)
    for edge in (slice(0, PAD), slice(PAD + group, 2 * PAD + group)):
        bound_ref[:, edge] = jnp.where(iota((2, PAD), 0) == 0, 1 << 20, -1)

    @pl.loop(0, group // 512)
    def _(c):
        at = pl.multiple_of(c * 512, 512)
        seg, first, stop = segment_rows(ends, own_len, iota((1, 512), 1) + at, group)
        line[:, pl.ds(at + TILE, 512)] = seg
        bound_ref[0:1, pl.ds(at + PAD, 512)] = first
        bound_ref[1:2, pl.ds(at + PAD, 512)] = stop

    first = pl.multiple_of(lax.axis_index("head") * rows, TILE)
    ext_ref[:, :rows] = line[:, pl.ds(first + TILE, rows)]
    left = line[:, pl.ds(first, TILE)]
    right = line[:, pl.ds(first + TILE + rows, TILE)]
    ext_ref[:, rows:] = jnp.where(iota((1, TILE), 1) < HALO, right, left)


def split_heads(heads, head_width):
    size = heads * head_width
    row, column = iota((size, size), 0), iota((size, size), 1)
    hit = jnp.zeros((size, size), jnp.bool_)
    for h in range(heads):
        f = column - head_width * h
        mine = (f >= 0) & (f < head_width)
        hit = hit | (mine & (f < MAIN) & (row == MAIN * h + f)) | (mine & (f >= MAIN) & (row == MAIN * heads + 4 * h + f - MAIN))
    return hit.astype(F32).astype(BF)


def conv_masks(mask_ref, ext_ref):
    seg = jnp.broadcast_to(ext_ref[...], (8, ext_ref.shape[1]))
    lanes = seg.shape[1]
    reach = mask_ref.shape[0] // 2
    for i in range(mask_ref.shape[0]):
        mask_ref[i] = (pltpu.roll(seg, (reach - i) % lanes, 1) == seg).astype(F32)


def filter_kernel(x1_ref, x1l_ref, x1r_ref, o_ref, tail_ref, cols_ref, ext_ref, out_ref, pw_ref, taps_ref,
                  x2_ref, oc_ref, u_ref, y_ref, stat_ref, wide, mask, live_ref, h3s, n_ref, inv_ref, value_ref, gate_ref, *, head_width, slot_count, arrive):
    width, rows = x1_ref.shape
    lanes = rows + TILE
    heads = o_ref.shape[0]
    taps = taps_ref.shape[0]
    out_t = flipped(out_ref[...])
    pw_t = flipped(pw_ref[...])
    gather = split_heads(heads, head_width)
    seg = ext_ref[...]
    live = (seg >= 0) & (seg < slot_count)
    live_ref[...] = live.astype(F32)
    conv_masks(mask, ext_ref)
    wide_taps = taps_ref[...].astype(F32).T
    arrive()

    near = iota((1, TILE), 1) < HALO

    def extended(own, left, right):
        edge = jnp.where(near, right.astype(F32), left.astype(F32)).astype(own.dtype)
        return jnp.concatenate([own, edge], axis=1)

    x1 = extended(x1_ref[...], x1l_ref[...], x1r_ref[...])
    main = [extended(o_ref[h, :MAIN, TILE : TILE + rows], o_ref[h, :MAIN, :TILE], o_ref[h, :MAIN, TILE + rows :]) for h in range(heads)]
    tails = []
    for h in range(heads):
        left, right = (o_ref[h, MAIN:, at].astype(F32)[:4] for at in (slice(0, TILE), slice(TILE + rows, rows + 2 * TILE)))
        tails.append(extended(unfold_rows(tail_ref[h].astype(F32)), left, right))
    o = jnp.concatenate(main + [jnp.concatenate(tails, axis=0).astype(BF)], axis=0)
    oc = dot(gather, o, TN).astype(BF)
    x2 = x1 + (dot(out_t, oc) + col(cols_ref, VEC.mix_output_bias, width))
    n, inv = norm(x2)
    h3 = (n * col(cols_ref, VEC.filter_gain, width) + col(cols_ref, VEC.filter_shift, width)).astype(BF)
    g = dot(pw_t, h3) + col(cols_ref, VEC.pointwise_in_bias, 2 * width)
    gate = sigmoid(g[width:])
    u = jnp.where(live_ref[...] > 0.5, g[:width] * gate, 0.0).astype(BF)
    n_ref[...] = n[:, :rows]
    inv_ref[...] = inv[:, :rows]
    h3s[:width, :] = h3[:, :rows]
    value_ref[...] = g[:width, :rows]
    gate_ref[...] = gate[:, :rows]
    oc_ref[:width, :] = oc[:, :rows]
    x2_ref[...] = x2
    u_ref[...] = u
    wide[...] = u.astype(F32)

    own = (live & (iota((1, lanes), 1) < rows)).astype(F32)
    count = jnp.sum(own, axis=1, keepdims=True)
    safe = jnp.maximum(count, 1.0)
    for r in range(width // 8):
        sl = slice(8 * r, 8 * r + 8)
        u8 = wide[sl, :]
        acc = jnp.zeros((8, lanes), F32)
        for k in range(taps):
            moved = pltpu.roll(u8, (taps // 2 - k) % lanes, 1)
            acc = acc + wide_taps[sl, k : k + 1] * (moved * mask[k])
        y_ref[sl, :] = acc
    y = y_ref[...]
    part = folded(y * own)
    mean = exact(part, jnp.ones((TILE, TILE), F32)) / safe
    dev = (y - jnp.concatenate([mean] * (lanes // TILE), axis=1)) * own
    stat_ref[...] = two_rows(row_sums(part)[:1] / safe, row_sums(folded(dev * dev))[:1], count)


def two_rows(a, b, extra):
    rest = a.shape[1] - TILE
    tail = pad_lanes(jnp.concatenate([a[:, TILE:], b[:, TILE:]], axis=0))
    spot = (iota((2, TILE), 0) == 0) & (iota((2, TILE), 1) == rest)
    return jnp.concatenate([a[:, :TILE], b[:, :TILE], jnp.where(spot, extra, tail)], axis=0)


def all_rows(ref, width):
    rest = width - TILE
    values = ref[...]
    a = jnp.concatenate([values[:, 0, :], values[:, 2, :rest]], axis=1)
    b = jnp.concatenate([values[:, 1, :], values[:, 3, :rest]], axis=1)
    return a, b, values[:, 2, rest : rest + 1]


def total_stats(stats_ref, width):
    mean_of, spread_of, n = all_rows(stats_ref, width)
    count = jnp.sum(n, axis=0, keepdims=True)
    mean = jnp.sum(n * mean_of, axis=0, keepdims=True) / count
    gap = mean_of - mean
    spread = jnp.sum(spread_of + n * gap * gap, axis=0, keepdims=True)
    inv = lax.rsqrt(spread / count + EPSILON)
    table = jnp.concatenate([mean, inv, jnp.broadcast_to(count, (1, width)), jnp.zeros((5, width), F32)], axis=0).T
    return table[:, 0:1], table[:, 1:2], table[:, 2:3]


def second_kernel(x2_ref, y_ref, stats_ref, cot_ref, cotl_ref, cotr_ref, cols_ref, pwo_ref, up_ref, down_ref,
                  out_ref, dx3_ref, e_ref, sums_ref, pack_ref, small_ref,
                  h4s, das, s4s, dfs, ws, dcs, *, arrive, leave):
    width, rows = out_ref.shape
    hidden = up_ref.shape[1]
    pwo_t = flipped(pwo_ref[...])
    up_t = flipped(up_ref[...])
    down = flipped(down_ref[...])
    arrive()
    mean, inv_b, _ = total_stats(stats_ref, width)
    bgain = col(cols_ref, VEC.batch_gain, width)

    near = iota((1, TILE), 1) < HALO
    edge = jnp.where(near, cotr_ref[...].astype(F32), cotl_ref[...].astype(F32))
    cot = jnp.concatenate([cot_ref[...].astype(F32), edge], axis=1)
    zh = (y_ref[...] - mean) * inv_b
    z = zh * bgain + col(cols_ref, VEC.batch_shift, width)
    sig_z = sigmoid(z)
    w = (z * sig_z).astype(BF)
    x3 = x2_ref[...] + (dot(pwo_t, w) + col(cols_ref, VEC.pointwise_out_bias, width))
    n4, inv4 = norm(x3)
    h4 = (n4 * col(cols_ref, VEC.second_gain, width) + col(cols_ref, VEC.second_shift, width)).astype(BF)
    a4 = dot(up_t, h4) + col(cols_ref, VEC.second_up_bias, hidden)
    sig = sigmoid(a4)
    s4 = (a4 * sig).astype(BF)
    x4 = x3 + 0.5 * (dot(down_ref[...], s4) + col(cols_ref, VEC.second_down_bias, width))
    nf, invf = norm(x4)
    fgain = col(cols_ref, VEC.final_gain, width)
    dx4 = norm_back(cot, nf, invf, fgain)
    df = (0.5 * dx4).astype(BF)
    da = (dot(down, df) * (sig * (1.0 + a4 * (1.0 - sig)))).astype(BF)
    dh = dot(up_ref[...], da)
    dx3 = dx4 + norm_back(dh, n4, inv4, col(cols_ref, VEC.second_gain, width))
    dc = dx3.astype(BF)
    dz = dot(pwo_ref[...], dc) * (sig_z * (1.0 + z * (1.0 - sig_z)))
    e = dz * bgain
    e_ref[...] = e
    sums_ref[...] = two_rows(row_sums(folded(e[:, :rows]))[:1], row_sums(folded((e * zh)[:, :rows]))[:1], 0.0)
    leave()

    out_ref[...] = (nf * fgain + col(cols_ref, VEC.final_shift, width))[:, :rows].astype(BF)
    dx3_ref[...] = dx3[:, :rows]
    h4s[...] = h4[:, :rows]
    das[...] = da[:, :rows]
    s4s[:hidden, :] = s4[:, :rows]
    dfs[...] = df[:, :rows]
    ws[:width, :] = w[:, :rows]
    dcs[...] = dc[:, :rows]
    totals = [row_sums(folded(v[:, :rows]))[:1] for v in (dh * n4, dh, cot * nf, cot, dz * zh, dz)]
    s4s[hidden:, :] = ones_row(16, rows)
    ws[width:, :] = ones_row(16, rows)
    up_grad = dot(h4s[...], das[...], NT)
    up_bias = dot(ones_row(16, rows), das[...], NT)
    down_grad = dot(dfs[...], s4s[...], NT)
    pw_grad = dot(ws[...], dcs[...], NT)
    down_bias = exact(jnp.ones((8, rows), F32), dfs[...].astype(F32), NT)
    put_ff(pack_ref, up_grad, down_grad, 0)
    tall = 9 * width
    pack_ref[tall : tall + width, :] = pw_grad[:width, :TILE].astype(BF)
    pack_ref[tall + width : tall + 2 * width, :] = pad_lanes(pw_grad[:width, TILE:]).astype(BF)
    small_ref[...] = stack_rows(
        [totals[0], totals[1], up_bias[:1], down_bias[:1], totals[2], totals[3], totals[4], totals[5], pw_grad[width : width + 1]],
        small_ref.shape)


def pad_lanes(mat, lanes=TILE):
    if mat.shape[1] == lanes:
        return mat
    return jnp.concatenate([mat, jnp.zeros((mat.shape[0], lanes - mat.shape[1]), mat.dtype)], axis=1)


def stack_rows(rows, shape):
    parts = [pad_lanes(r, shape[1]) for r in rows]
    parts.append(jnp.zeros((shape[0] - len(rows), shape[1]), F32))
    return jnp.concatenate(parts, axis=0)


def put_ff(pack_ref, up_grad, down_grad_t, at):
    width, hidden = up_grad.shape
    whole = hidden // TILE
    for i in range(whole):
        pack_ref[at + i * width : at + (i + 1) * width, :] = up_grad[:, i * TILE : (i + 1) * TILE].astype(BF)
        j = whole + i
        pack_ref[at + j * width : at + (j + 1) * width, :] = down_grad_t[:, i * TILE : (i + 1) * TILE].astype(BF)
    rest = jnp.concatenate([up_grad[:, whole * TILE : hidden], down_grad_t[:, whole * TILE : hidden]], axis=1)
    pack_ref[at + 2 * whole * width : at + (2 * whole + 1) * width, :] = rest.astype(BF)


def unfilter_kernel(e_ref, y_ref, stats_ref, sums_ref, u_ref, dx3_ref, ocs, cols_ref, ext_ref, pw_ref, taps_ref,
                    out_ref, dx2_ref, do_ref, pack_ref, small_ref, tapg_ref,
                    dyw, du_s, mask, prod, h3s, dgs, dms, gains, live_ref, n_ref, inv_ref, value_ref, gate_ref, tail_ref, *, head_width, ship, arrive):
    width, rows = dx3_ref.shape
    lanes = rows + TILE
    heads = do_ref.shape[0]
    taps = taps_ref.shape[0]
    tap_cols = taps_ref[...].astype(F32).T
    out_w = dot(split_heads(heads, head_width), out_ref[...]).astype(BF)
    gains[...] = jnp.zeros_like(gains)
    fgain = col(cols_ref, VEC.filter_gain, width)
    mean, inv_b, count = total_stats(stats_ref, width)
    arrive()
    one_of, two_of, _ = all_rows(sums_ref, width)
    sums = jnp.concatenate([jnp.sum(one_of, axis=0, keepdims=True), jnp.sum(two_of, axis=0, keepdims=True), jnp.zeros((6, width), F32)], axis=0).T
    s1, s2 = sums[:, 0:1], sums[:, 1:2]
    seg = ext_ref[...]
    live = live_ref[...]
    zh = (y_ref[...] - mean) * inv_b
    dy = inv_b * (e_ref[...] - live * ((s1 + zh * s2) / count))
    dyw[...] = jnp.where(seg >= 0, dy, 0.0).astype(BF).astype(F32)

    for r in range(width // 8):
        sl = slice(8 * r, 8 * r + 8)
        dy8 = dyw[sl, :]
        u8 = u_ref[16 * (r // 2) : 16 * (r // 2) + 16, :rows].astype(F32)[8 * (r % 2) : 8 * (r % 2) + 8]
        acc = jnp.zeros((8, rows), F32)
        for k in range(taps):
            moved = pltpu.roll(dy8, (k - taps // 2) % lanes, 1)[:, :rows] * mask[taps - k][:, :rows]
            acc = acc + tap_cols[sl, k : k + 1] * moved
            hit = moved * u8
            prod[k, sl, :] = folded(hit)
        du_s[sl, :] = acc

    @pl.loop(0, rows // PIECE)
    def _(c):
        at = pl.ds(pl.multiple_of(c * PIECE, PIECE), PIECE)
        n, inv = n_ref[:, at], inv_ref[:, at]
        gate = gate_ref[:, at]
        t = live_ref[:, at] * du_s[:, at] * gate
        dg = jnp.concatenate([t, t * value_ref[:, at] * (1.0 - gate)], axis=0).astype(BF)
        dh = dot(pw_ref[...], dg)
        dx2 = dx3_ref[:, at] + norm_back(dh, n, inv, fgain)
        dx2_ref[:, at] = dx2
        dm = dx2.astype(BF)
        do = dot(out_w, dm)
        for h in range(heads):
            do_ref[h, :, at] = do[h * MAIN : (h + 1) * MAIN].astype(BF)
        tail_ref[:, at] = do[heads * MAIN :]
        ship(c)
        dgs[:, at] = dg
        dms[:, at] = dm
        for i, v in enumerate((dh * n, dh)):
            gains[i] += folded(v)

    ship(rows // PIECE)
    whole = prod[...].reshape(taps * width, TILE)
    hi = whole.astype(BF)
    lo = (whole - hi.astype(F32)).astype(BF)
    ones = jnp.ones((8, TILE), BF)
    lines = dot(ones, hi, NT) + dot(ones, lo, NT)
    for k in range(taps):
        tapg_ref[k : k + 1, :] = lines[:1, k * width : (k + 1) * width]

    h3s[width:, :] = ones_row(16, rows)
    ocs[width:, :] = ones_row(16, rows)
    pw_grad = dot(h3s[...], dgs[...], NT)
    out_grad = dot(ocs[...], dms[...], NT)
    at = 0
    for lo in range(0, 2 * width, TILE):
        pack_ref[at : at + width, :] = pad_lanes(pw_grad[:width, lo : min(lo + TILE, 2 * width)]).astype(BF)
        at += width
    for lo in range(0, width, TILE):
        pack_ref[at : at + width, :] = pad_lanes(out_grad[:width, lo : min(lo + TILE, width)]).astype(BF)
        at += width
    small_ref[...] = stack_rows(
        [row_sums(gains[0])[:1], row_sums(gains[1])[:1], pw_grad[width : width + 1], out_grad[width : width + 1]], small_ref.shape)


def close_kernel(frames_ref, x1_ref, h2_ref, dx2_ref, dqkv_ref, dtab_ref, cols_ref, up_ref, down_ref, mix_ref,
                 grad_ref, pack_ref, h1s, das, s1s, dfs, dqs, gains, *, mixed):
    width, rows = frames_ref.shape
    hidden = up_ref.shape[1]
    heads, packed_rows, _ = dqkv_ref.shape
    up_t = flipped(up_ref[...])
    down = flipped(down_ref[...])
    hot = spread_cols(mix_ref.shape[1], heads, packed_rows, mix_ref.shape[1] // heads)
    mix_w = dot(mix_ref[...], hot, NT).astype(BF)
    gains[...] = jnp.zeros_like(gains)
    mgain = col(cols_ref, VEC.mix_gain, width)
    fgain = col(cols_ref, VEC.first_gain, width)

    @pl.loop(0, rows // STEP)
    def _(c):
        at = pl.ds(pl.multiple_of(c * STEP, STEP), STEP)
        dq = jnp.concatenate([dqkv_ref[h, :, at] for h in range(heads)], axis=0)
        dqs[:, at] = dq
        dh2 = dot(mix_w, dq)
        n2, inv2 = norm(x1_ref[:, at])
        dx1 = dx2_ref[:, at] + norm_back(dh2, n2, inv2, mgain)
        x0 = frames_ref[:, at].astype(F32)
        n1, inv1 = norm(x0)
        h1 = (n1 * fgain + col(cols_ref, VEC.first_shift, width)).astype(BF)
        a1 = dot(up_t, h1) + col(cols_ref, VEC.first_up_bias, hidden)
        sig = sigmoid(a1)
        s1s[:, at] = (a1 * sig).astype(BF)
        df = (0.5 * dx1).astype(BF)
        da = (dot(down, df) * (sig * (1.0 + a1 * (1.0 - sig)))).astype(BF)
        dh1 = dot(up_ref[...], da)
        grad_ref[:, at] = dx1 + norm_back(dh1, n1, inv1, fgain)
        h1s[:, at] = h1
        das[:, at] = da
        dfs[:, at] = df
        for i, v in enumerate((dh1 * n1, dh1, dh2 * n2, dh2)):
            gains[i] += folded(v)

    mix_grad = dot(dot(h2_ref[...], dqs[...], NT).astype(BF), hot)
    at = 0
    for lo in range(0, mix_grad.shape[1], TILE):
        pack_ref[at : at + width, :] = pad_lanes(mix_grad[:, lo : min(lo + TILE, mix_grad.shape[1])]).astype(BF)
        at += width
    mixed()
    up_grad = dot(h1s[...], das[...], NT)
    up_bias = dot(ones_row(16, rows), das[...], NT)
    down_grad = dot(dfs[...], s1s[...], NT)
    down_bias = exact(jnp.ones((8, rows), F32), dfs[...].astype(F32), NT)
    put_ff(pack_ref, up_grad, down_grad, at)
    at += (2 * (hidden // TILE) + 1) * width
    totals = [row_sums(gains[i])[:1] for i in range(4)]
    small = stack_rows([totals[0], totals[1], up_bias[:1], down_bias[:1], totals[2], totals[3]], (16, 5 * TILE))
    at = put_small(pack_ref, small, at)
    span = dtab_ref.shape[1]
    table = jnp.where(iota((16, span), 0) == lax.axis_index("head"), dtab_ref[...], 0.0)
    pack_ref[at : at + 16, :] = table.astype(BF)
    if at + 16 < pack_ref.shape[0]:
        pack_ref[at + 16 :, :] = jnp.zeros((pack_ref.shape[0] - at - 16, TILE), BF)


def put_small(pack_ref, small, at):
    for lo in range(0, small.shape[1], TILE):
        pack_ref[at : at + small.shape[0], :] = small[:, lo : lo + TILE].astype(BF)
        at += small.shape[0]
    return at


def put_taps(pack_ref, tapg, at):
    taps = tapg.shape[0]
    pack_ref[at : at + taps, :] = tapg[:, :TILE].astype(BF)
    pack_ref[at + taps : at + 2 * taps, :] = pad_lanes(tapg[:, TILE:]).astype(BF)
    return at + 2 * taps


def unpack_kernel(pack_ref, out_ref, grad_ref, *refs, layout):
    refs[0][...] = out_ref[...]
    refs[1][...] = grad_ref[...]
    out_refs = refs[2:]
    given = Weights(*out_refs)

    def wide(at, rows, lanes):
        parts = [pack_ref[at + i * rows : at + (i + 1) * rows, :].astype(F32) for i in range(-(-lanes // TILE))]
        return jnp.concatenate(parts, axis=1)[:, :lanes]

    for at, up_ref, down_ref in ((layout.first, given.first_up, given.first_down), (layout.second, given.second_up, given.second_down)):
        width, hidden = up_ref.shape
        whole = hidden // TILE
        half = hidden - whole * TILE
        piece = lambda i: pack_ref[at + i * width : at + (i + 1) * width, :].astype(F32)
        rest = piece(2 * whole)
        up_ref[...] = jnp.concatenate([piece(i) for i in range(whole)] + [rest[:, :half]], axis=1)
        down_ref[...] = jnp.concatenate([piece(whole + i) for i in range(whole)] + [rest[:, half:]], axis=1)
    for ref, at in ((given.mix_inputs, layout.mix_inputs), (given.pointwise_in, layout.pointwise_in), (given.mix_output, layout.mix_output),
                    (given.pointwise_out, layout.pointwise_out), (given.depthwise_taps, layout.taps)):
        ref[...] = wide(at, *ref.shape)
    given.position_bias[...] = pack_ref[layout.table : layout.table + 16, :].astype(F32)[: given.position_bias.shape[0]]
    late = wide(layout.small_late, 16, 5 * TILE)
    early = wide(layout.small, 32, 5 * TILE)
    late_rows = (
        given.first_gain, given.first_shift, given.first_up_bias, given.first_down_bias, given.mix_gain, given.mix_shift,
    )
    second_rows = (
        given.second_gain, given.second_shift, given.second_up_bias, given.second_down_bias, given.final_gain, given.final_shift,
        given.batch_gain, given.batch_shift, given.pointwise_out_bias,
    )
    filter_rows = (given.filter_gain, given.filter_shift, given.pointwise_in_bias, given.mix_output_bias)
    for small, first, refs in ((late, 0, late_rows), (early, 0, second_rows), (early, 16, filter_rows)):
        for row, ref in enumerate(refs, first):
            ref[...] = small[row : row + 1, : ref.shape[0]].reshape(ref.shape)


@dataclasses.dataclass
class Weights:
    first_gain: object
    first_shift: object
    first_up: object
    first_up_bias: object
    first_down: object
    first_down_bias: object
    mix_gain: object
    mix_shift: object
    mix_inputs: object
    position_bias: object
    mix_output: object
    mix_output_bias: object
    filter_gain: object
    filter_shift: object
    pointwise_in: object
    pointwise_in_bias: object
    depthwise_taps: object
    batch_gain: object
    batch_shift: object
    pointwise_out: object
    pointwise_out_bias: object
    second_gain: object
    second_shift: object
    second_up: object
    second_up_bias: object
    second_down: object
    second_down_bias: object
    final_gain: object
    final_shift: object


def pack_layout(width, hidden, mix_width, taps, devices):
    ff = (2 * (hidden // TILE) + 1) * width
    chunks = lambda lanes: -(-lanes // TILE) * width
    unit = 16 * devices
    whole = lambda rows: -(-rows // unit) * unit
    at = types.SimpleNamespace(second=0, pointwise_out=ff)
    at.pointwise_in = ff + chunks(width)
    at.mix_output = at.pointwise_in + chunks(2 * width)
    at.taps = at.mix_output + chunks(width)
    at.small = at.taps + 2 * taps
    at.late = at.mix_inputs = whole(at.small + 32 * 5)
    at.last = at.late + chunks(mix_width) // unit * unit
    at.first = at.mix_inputs + chunks(mix_width)
    at.small_late = at.first + ff
    at.table = at.small_late + 16 * 5
    at.rows = at.late + whole(at.table + 16 - at.late)
    return at


MESH = pl.DeviceIdType.MESH


def meet(peers):
    barrier = pltpu.get_barrier_semaphore()
    for peer in peers:
        pl.semaphore_signal(barrier, inc=1, device_id=peer, device_id_type=MESH)
    pl.semaphore_wait(barrier, len(peers))


def head_peers(n):
    me = lax.axis_index("head")
    return me, [{"head": lax.rem(me + s, n)} for s in range(1, n)], [lax.rem(me + s, n) for s in range(1, n)]


def opening_kernel(frames_ref, len_ref, up_ref, down_ref, mix_ref, *refs, packed_rows, n):
    count = len(VEC.__dict__)
    vec_refs, refs = refs[:count], refs[count:]
    (cot_ref, x1_ref, h2_ref, cols_ref, bound_ref, plan_ref, ext_ref, all_ref, x1l_ref, x1r_ref, cotl_ref, cotr_ref,
     qkv, line, send, recv, local, hsend, hrecv) = refs
    me, peers, ids = head_peers(n)
    rows = cot_ref.shape[1]
    barrier = pltpu.get_barrier_semaphore()
    for peer in peers:
        pl.semaphore_signal(barrier, inc=1, device_id=peer, device_id_type=MESH)
    vecs = [ref[...].astype(F32).reshape(1, ref.shape[0]) for ref in vec_refs]
    cols_ref[...] = stack_rows(vecs, (VEC_ROWS, up_ref.shape[1])).T
    pl.semaphore_wait(barrier, len(peers))

    def piece(c, s):
        at = pl.ds(pl.multiple_of(c * PIECE, PIECE), PIECE)
        return pltpu.make_async_remote_copy(src_ref=qkv.at[ids[s], :, at], dst_ref=all_ref.at[me, :, at], send_sem=send.at[c, s],
                                            recv_sem=recv.at[c, s], device_id=peers[s], device_id_type=MESH)

    def ship(c):
        for s in range(n - 1):
            piece(c, s).start()

    open_rows(frames_ref, up_ref, down_ref, mix_ref, x1_ref, h2_ref, qkv, cols_ref, packed_rows, ship)
    own = pltpu.make_async_copy(qkv.at[me], all_ref.at[me], local)
    own.start()

    def edge(i, src, dst, head):
        return pltpu.make_async_remote_copy(src_ref=src, dst_ref=dst, send_sem=hsend.at[i], recv_sem=hrecv.at[i],
                                            device_id={"head": head}, device_id_type=MESH)

    up = lax.rem(me + 1, n)
    down = lax.rem(me + n - 1, n)
    last, start = pl.ds(rows - TILE, TILE), pl.ds(0, TILE)
    to_right = [edge(0, x1_ref.at[:, last], x1l_ref, up), edge(1, cot_ref.at[:, last], cotl_ref, up)]
    to_left = [edge(2, x1_ref.at[:, start], x1r_ref, down), edge(3, cot_ref.at[:, start], cotr_ref, down)]

    @pl.when(me < n - 1)
    def _():
        for c in to_right:
            c.start()

    @pl.when(me > 0)
    def _():
        for c in to_left:
            c.start()

    open_segments(len_ref, bound_ref, plan_ref, ext_ref, line)
    own.wait()

    @pl.loop(0, rows // PIECE)
    def _(c):
        for s in range(n - 1):
            piece(c, s).wait()

    @pl.when(me < n - 1)
    def _():
        for c in to_right:
            c.wait_send()
        for c in to_left:
            c.wait_recv()

    @pl.when(me > 0)
    def _():
        for c in to_left:
            c.wait_send()
        for c in to_right:
            c.wait_recv()


def everyone(n_tm, n_head):
    me = lax.axis_index("tm") * n_head + lax.axis_index("head")

    def for_all(act):
        for step in [s for i in range(1, n_head // 2 + 1) for s in {n_head - i, i}] + [0]:
            pl.loop(0 if step else 1, n_tm)(functools.partial(act, step))

    def place(along_head, along_tm):
        return {"tm": lax.rem(lax.axis_index("tm") + along_tm, n_tm), "head": lax.rem(lax.axis_index("head") + along_head, n_head)}

    return me, for_all, place


def tell(src_ref, all_ref, send, recv, n_tm, n_head):
    me, for_all, place = everyone(n_tm, n_head)

    def copy(h, t):
        return pltpu.make_async_remote_copy(src_ref=src_ref, dst_ref=all_ref.at[me], send_sem=send.at[h, t], recv_sem=recv.at[h, t],
                                            device_id=place(h, t), device_id_type=MESH)

    def start():
        for_all(lambda h, t: copy(h, t).start())
        all_ref[me] = src_ref[...]

    def end():
        for_all(lambda h, t: copy(h, t).wait())

    return start, end


def load_all(sources, targets, sems):
    copies = [pltpu.make_async_copy(src, dst, sems.at[i]) for i, (src, dst) in enumerate(zip(sources, targets))]
    for copy in copies:
        copy.start()
    return copies


def middle_kernel(*refs, n_tm, n_head, head_width, slot_count, layout):
    o_ref, o_tail, sources, refs = refs[0], refs[1], refs[2:16], refs[16:]
    (out_ref, dx2_ref, do_all, do_tails, pack_ref), refs = refs[:5], refs[5:]
    loaded, refs = refs[:14], refs[14:]
    (x1_ref, x1l_ref, x1r_ref, cot_ref, cotl_ref, cotr_ref, cols_ref, ext_ref, mixo_ref, pwi_ref, taps_ref, pwo_ref, up_ref,
     down_ref) = loaded
    (o_own, x2, oc, u, y, stat, stats, dx3, e, sums, all_sums, do, wide, mask, live,
     h4s, das, s4s, dfs, ws, dcs, dyw, du, prod, h3s, dgs, dms, gains2, smalld, smalle, tapg,
     n3, inv3, value3, gate3, tail_own, tail_wide, tail), refs = refs[:38], refs[38:]
    (load_sems, send_o, recv_o, local_o, send_a, recv_a, send_b, recv_b, send_d, recv_d, local_d) = refs
    me, peers, ids = head_peers(n_head)
    _, for_all, place = everyone(n_tm, n_head)
    barrier = pltpu.get_barrier_semaphore()
    rows = x1_ref.shape[1]
    for_all(lambda h, t: pl.semaphore_signal(barrier, inc=1, device_id=place(h, t), device_id_type=MESH))
    loads = load_all(sources, loaded, load_sems)
    pl.semaphore_wait(barrier, n_tm * n_head - 1)

    def parts(p):
        first = pl.multiple_of(p * rows, TILE)
        mine = o_own.at[me]
        low, high = pl.ds(0, MAIN), pl.ds(MAIN, SLOT - MAIN)
        left, right = pl.ds(0, TILE), pl.ds(rows + TILE, TILE)
        return (
            (o_ref.at[low, pl.ds(first, rows + 2 * TILE)], mine.at[low]),
            (o_tail.at[p], tail_own.at[me]),
            (o_ref.at[high, pl.ds(first, TILE)], mine.at[high, left]),
            (o_ref.at[high, pl.ds(pl.multiple_of(first + rows + TILE, TILE), TILE)], mine.at[high, right]),
        )

    copies = [
        pltpu.make_async_remote_copy(src_ref=src, dst_ref=dst, send_sem=send_o.at[s, i], recv_sem=recv_o.at[s, i],
                                     device_id=peer, device_id_type=MESH)
        for s, (peer, p) in enumerate(zip(peers, ids)) for i, (src, dst) in enumerate(parts(p))
    ]
    for copy in copies:
        copy.start()
    own = [pltpu.make_async_copy(src, dst, local_o.at[i]) for i, (src, dst) in enumerate(parts(me))]
    for copy in own:
        copy.start()
    for load in loads:
        load.wait()

    def arrive():
        for copy in own + copies:
            copy.wait()

    filter_kernel(x1_ref, x1l_ref, x1r_ref, o_own, tail_own, cols_ref, ext_ref, mixo_ref, pwi_ref, taps_ref, x2, oc, u, y, stat, wide, mask, live,
                  h3s, n3, inv3, value3, gate3, head_width=head_width, slot_count=slot_count, arrive=arrive)
    stats_out, stats_in = tell(stat, stats, send_a, recv_a, n_tm, n_head)
    sums_out, sums_in = tell(sums, all_sums, send_b, recv_b, n_tm, n_head)
    stats_out()
    second_kernel(x2, y, stats, cot_ref, cotl_ref, cotr_ref, cols_ref, pwo_ref, up_ref, down_ref,
                  out_ref, dx3, e, sums, pack_ref, smalld, h4s, das, s4s, dfs, ws, dcs, arrive=stats_in, leave=sums_out)

    def piece(c, s):
        at = pl.ds(pl.multiple_of(c * PIECE, PIECE), PIECE)
        return pltpu.make_async_remote_copy(src_ref=do.at[ids[s], :, at], dst_ref=do_all.at[me, :, at], send_sem=send_d.at[c, s],
                                            recv_sem=recv_d.at[c, s], device_id=peers[s], device_id_type=MESH)

    def ending(s):
        return pltpu.make_async_remote_copy(src_ref=tail.at[ids[s]], dst_ref=do_tails.at[me], send_sem=send_d.at[rows // PIECE, s],
                                            recv_sem=recv_d.at[rows // PIECE, s], device_id=peers[s], device_id_type=MESH)

    def ship(c):
        if isinstance(c, int):
            for h in range(n_head):
                tail[h] = fold_rows(tail_wide[4 * h : 4 * h + 4, :], 4).astype(BF)
        for s in range(n_head - 1):
            (ending(s) if isinstance(c, int) else piece(c, s)).start()

    unfilter_kernel(e, y, stats, all_sums, u, dx3, oc, cols_ref, ext_ref, pwi_ref, taps_ref, mixo_ref,
                    dx2_ref, do, pack_ref.at[pl.ds(layout.pointwise_in, layout.taps - layout.pointwise_in)], smalle, tapg, dyw, du, mask, prod, h3s, dgs, dms, gains2, live, n3, inv3, value3, gate3, tail_wide,
                    head_width=head_width, ship=ship, arrive=sums_in)
    own = [pltpu.make_async_copy(do.at[me], do_all.at[me], local_d.at[0]), pltpu.make_async_copy(tail.at[me], do_tails.at[me], local_d.at[1])]
    for copy in own:
        copy.start()
    end = put_taps(pack_ref, tapg[...], layout.taps)
    end = put_small(pack_ref, jnp.concatenate([smalld[...], smalle[...]], axis=0), end)
    if end < pack_ref.shape[0]:
        pack_ref[end:, :] = jnp.zeros((pack_ref.shape[0] - end, TILE), BF)
    for copy in own:
        copy.wait()
    for s in range(n_head - 1):
        ending(s).wait()

    @pl.loop(0, rows // PIECE)
    def _(c):
        for s in range(n_head - 1):
            piece(c, s).wait()


def sum_scratch(count, n_tm, n_head):
    half = count // 2
    big = half // (n_tm // 2)
    shapes = [(half, TILE), (half, TILE), (n_tm // 2, big, TILE), (big, TILE), (n_head, big // n_head, TILE), (big, TILE), (half, TILE)]
    return [pltpu.VMEM(shape, BF) for shape in shapes]


def gradient_sum(src_ref, out_ref, first, scratch, sems, local, n_tm, n_head):
    got0, half, got1, part1, got2, part2, whole = scratch
    tm, head = lax.axis_index("tm"), lax.axis_index("head")
    n_chip = n_tm // 2
    chip, core = tm // 2, lax.rem(tm, 2)
    size = src_ref.shape[0] // 2
    big = size // n_chip
    small = big // n_head
    sibling = {"tm": chip * 2 + 1 - core}

    def rows(i, count, base=0):
        return pl.ds(pl.multiple_of(base + i * count, 16), count)

    def send(src, dst, phase, s, peer):
        return pltpu.make_async_remote_copy(src_ref=src, dst_ref=dst, send_sem=sems.at[2 * phase, s], recv_sem=sems.at[2 * phase + 1, s],
                                            device_id=peer, device_id_type=MESH)

    def chip_peer(s):
        return lax.rem(chip + s, n_chip)

    def head_peer(s):
        return lax.rem(head + s, n_head)

    def zero():
        return send(src_ref.at[rows(1 - core, size)], got0, 0, 0, sibling)

    def one(s):
        return send(half.at[rows(chip_peer(s), big)], got1.at[s], 1, s, {"tm": chip_peer(s) * 2 + core})

    def two(s):
        return send(part1.at[rows(head_peer(s), small)], got2.at[s], 2, s, {"head": head_peer(s)})

    def three(s):
        at = part2.at[rows(head, small)]
        return send(at, at, 3, s, {"head": head_peer(s)})

    def four(s):
        return send(part2, whole.at[rows(chip, big)], 4, s, {"tm": chip_peer(s) * 2 + core})

    def five():
        return send(whole, out_ref.at[rows(core, size, first)], 5, 0, sibling)

    def keep():
        return pltpu.make_async_copy(whole, out_ref.at[rows(core, size, first)], local)

    def added(got, n):
        total = got[0].astype(F32)
        for s in range(1, n):
            total = total + got[s].astype(F32)
        return total.astype(BF)

    def step0():
        zero().start()

    def step1():
        zero().wait()
        half[...] = (src_ref[rows(core, size), :].astype(F32) + got0[...].astype(F32)).astype(BF)
        pl.loop(1, n_chip)(lambda s: one(s).start())
        got1[0] = half[rows(chip, big), :]

    def step2():
        pl.loop(1, n_chip)(lambda s: one(s).wait())
        part1[...] = added(got1, n_chip)
        pl.loop(1, n_head)(lambda s: two(s).start())
        got2[0] = part1[rows(head, small), :]

    def step3():
        pl.loop(1, n_head)(lambda s: two(s).wait())
        part2[rows(head, small), :] = added(got2, n_head)
        pl.loop(1, n_head)(lambda s: three(s).start())

    def step4():
        pl.loop(1, n_head)(lambda s: three(s).wait())
        pl.loop(1, n_chip)(lambda s: four(s).start())
        whole[rows(chip, big), :] = part2[...]

    def step5():
        pl.loop(1, n_chip)(lambda s: four(s).wait())
        five().start()
        keep().start()

    def step6():
        keep().wait()
        five().wait()

    return step0, step1, step2, step3, step4, step5, step6


def return_kernel(src_ref, dst_ref, send, recv, *, n):
    me, peers, ids = head_peers(n)
    meet(peers)
    copies = [
        pltpu.make_async_remote_copy(src_ref=src_ref.at[p], dst_ref=dst_ref.at[me], send_sem=send.at[s], recv_sem=recv.at[s],
                                     device_id=peer, device_id_type=MESH)
        for s, (peer, p) in enumerate(zip(peers, ids))
    ]
    for copy in copies:
        copy.start()
    for copy in copies:
        copy.wait()


def final_kernel(*refs, n_tm, n_head, parts):
    dqkv_ref, others_ref, sources, refs = refs[0], refs[1], refs[2:12], refs[12:]
    (grad_ref, total_ref), loaded, refs = refs[:2], refs[2:12], refs[12:]
    early_ref, frames_ref, x1_ref, h2_ref, dx2_ref, dtab_ref, cols_ref, up_ref, down_ref, mix_ref = loaded
    (dqkv, late, h1s, das, s1s, dfs, dqs, gains), refs = refs[:8], refs[8:]
    sum_refs = [refs[7 * i : 7 * i + 7] for i in range(3)]
    load_sems, load_q, sum_sems, sum_local = refs[21:]
    me, peers, ids = head_peers(n_head)
    tm = lax.axis_index("tm")
    rows = x1_ref.shape[1]
    barrier = pltpu.get_barrier_semaphore()
    for peer in peers:
        pl.semaphore_signal(barrier, inc=1, device_id=peer, device_id_type=MESH)

    @pl.loop(1, n_tm)
    def _(s):
        pl.semaphore_signal(barrier, inc=1, device_id={"tm": lax.rem(tm + s, n_tm)}, device_id_type=MESH)

    loads = load_all(sources, loaded, load_sems)
    own = pltpu.make_async_copy(dqkv_ref.at[me], dqkv.at[me], load_q.at[0])
    loads += [own] + [pltpu.make_async_copy(others_ref.at[p], dqkv.at[p], load_q.at[1 + s]) for s, p in enumerate(ids)]
    for load in loads[-n_head:]:
        load.start()
    pl.semaphore_wait(barrier, n_head + n_tm - 2)

    for load in loads:
        load.wait()
    late_at, last_at, end = parts

    def summed(i, src, first):
        return gradient_sum(src, total_ref, first, sum_refs[i], sum_sems.at[i], sum_local.at[i], n_tm, n_head)

    early = summed(0, early_ref, 0)
    last = summed(2, late.at[pl.ds(last_at - late_at, end - last_at)], last_at)
    late_sum = summed(1, late.at[pl.ds(0, last_at - late_at)], late_at) if last_at > late_at else [lambda: None] * 7
    early[0]()
    early[1]()

    def mixed():
        late_sum[0]()

    close_kernel(frames_ref, x1_ref, h2_ref, dx2_ref, dqkv, dtab_ref, cols_ref, up_ref, down_ref, mix_ref,
                 grad_ref, late, h1s, das, s1s, dfs, dqs, gains, mixed=mixed)
    for step in (last[0], late_sum[1], last[1], early[2], late_sum[2], last[2], early[3], late_sum[3], last[3], early[4], late_sum[4],
                 last[4], early[5], late_sum[5], last[5], early[6], late_sum[6], last[6]):
        step()


VMEM_MIB = 62


def body(
    frames, lengths, first_gain, first_shift, first_up, first_up_bias, first_down, first_down_bias, mix_gain, mix_shift,
    mix_inputs, position_bias, mix_output, mix_output_bias, filter_gain, filter_shift, pointwise_in, pointwise_in_bias,
    depthwise_taps, batch_gain, batch_shift, pointwise_out, pointwise_out_bias, second_gain, second_shift, second_up,
    second_up_bias, second_down, second_down_bias, final_gain, final_shift, cotangent,
):
    weights = Weights(
        first_gain, first_shift, first_up, first_up_bias, first_down, first_down_bias, mix_gain, mix_shift, mix_inputs, position_bias,
        mix_output, mix_output_bias, filter_gain, filter_shift, pointwise_in, pointwise_in_bias, depthwise_taps, batch_gain,
        batch_shift, pointwise_out, pointwise_out_bias, second_gain, second_shift, second_up, second_up_bias, second_down,
        second_down_bias, final_gain, final_shift)
    rows, width = frames.shape
    hidden = first_up.shape[1]
    n_head, n_tm = lax.axis_size("head"), lax.axis_size("tm")
    heads, span = position_bias.shape
    head_width = width // heads
    packed_rows = -(-3 * head_width // 16) * 16
    group = rows * n_head
    lanes = rows + TILE
    slots = lengths.shape[1]
    taps = depthwise_taps.shape[0]
    layout = pack_layout(width, hidden, mix_inputs.shape[1], taps, n_tm * n_head)

    vectors = tuple(getattr(weights, name) for name in VEC.__dict__)
    frames_t, cot_t, first_down_t, second_down_t = frames.T, cotangent.T, first_down.T, second_down.T
    vm, dma, hbm = pltpu.VMEM, pltpu.SemaphoreType.DMA, pl.BlockSpec(memory_space=pl.ANY)
    steps = rows // PIECE
    piece_sems = dma((steps, n_head - 1))

    def comm_call(kernel, name, collective_id, ins, in_hbm, outs, out_hbm, scratch):
        return pl.pallas_call(
            kernel,
            out_shape=tuple(jax.ShapeDtypeStruct(s, t) for s, t in outs),
            in_specs=[hbm if i in in_hbm else pl.BlockSpec() for i in range(len(ins))],
            out_specs=tuple(hbm if i in out_hbm else pl.BlockSpec() for i in range(len(outs))),
            scratch_shapes=scratch,
            compiler_params=pltpu.CompilerParams(collective_id=collective_id, has_side_effects=True, vmem_limit_bytes=VMEM_MIB * 2**20),
            name=name,
        )(*ins)

    ins = (frames_t, lengths, first_up, first_down_t, mix_inputs) + vectors + (cot_t,)
    x1, h2, cols, bounds, plan, ext, qkv_all, x1l, x1r, cotl, cotr = comm_call(
        functools.partial(opening_kernel, packed_rows=packed_rows, n=n_head), "opening", 1, ins, (len(ins) - 1,),
        [((width, rows), F32), ((width, rows), BF), ((hidden, VEC_ROWS), F32), ((2, group + 2 * PAD), jnp.int32),
         ((group // BLK, 128), jnp.int32), ((1, lanes), jnp.int32), ((n_head, packed_rows, rows), BF),
         ((width, TILE), F32), ((width, TILE), F32), ((width, TILE), BF), ((width, TILE), BF)], range(6, 11),
        [vm((n_head, packed_rows, rows), BF), vm((1, group + 2 * TILE), jnp.int32), piece_sems, piece_sems, dma, dma((4,)), dma((4,))])
    o, o_tail, of, lse = attend_forward(qkv_all, bounds, plan, position_bias, head_width)
    everyone_sems = dma((n_head, n_tm))
    ins = (x1, x1l, x1r, cot_t, cotl, cotr, cols, ext, mix_output, pointwise_in, depthwise_taps, pointwise_out, second_up, second_down_t)
    out, dx2, do_all, do_tails, pack = comm_call(
        functools.partial(middle_kernel, n_tm=n_tm, n_head=n_head, head_width=head_width, slot_count=slots, layout=layout),
        "middle", 2, (o, o_tail) + ins, range(len(ins) + 2),
        [((width, rows), BF), ((width, rows), F32), ((n_head, MAIN, rows), BF), ((n_head, 16, rows // 4), BF), ((layout.late, TILE), BF)],
        (2, 3),
        [vm(a.shape, a.dtype) for a in ins] + [
            vm((n_head, SLOT, rows + 2 * TILE), BF), vm((width, lanes), F32), vm((width + 16, rows), BF), vm((width, lanes), BF),
            vm((width, lanes), F32), vm((4, TILE), F32), vm((n_tm * n_head, 4, TILE), F32), vm((width, rows), F32),
            vm((width, lanes), F32), vm((4, TILE), F32), vm((n_tm * n_head, 4, TILE), F32), vm((n_head, MAIN, rows), BF),
            vm((width, lanes), F32), vm((taps + 1, 8, lanes), F32), vm((1, lanes), F32),
            vm((width, rows), BF), vm((hidden, rows), BF), vm((hidden + 16, rows), BF), vm((width, rows), BF),
            vm((width + 16, rows), BF), vm((width, rows), BF),
            vm((width, lanes), F32), vm((width, rows), F32), vm((taps, width, TILE), F32), vm((width + 16, rows), BF),
            vm((2 * width, rows), BF), vm((width, rows), BF), vm((2, width, TILE), F32),
            vm((16, 5 * TILE), F32), vm((16, 5 * TILE), F32), vm((taps, width), F32),
            vm((width, rows), F32), vm((1, rows), F32), vm((width, rows), F32), vm((width, rows), F32),
            vm((n_head, 16, rows // 4), BF), vm((4 * n_head, rows), F32), vm((n_head, 16, rows // 4), BF),
            dma((len(ins),)), dma((n_head - 1, 4)), dma((n_head - 1, 4)), dma((4,)), everyone_sems, everyone_sems, everyone_sems, everyone_sems,
            dma((steps + 1, n_head - 1)), dma((steps + 1, n_head - 1)), dma((2,)),
        ])
    dqkv, dtab = attend_backward(qkv_all, do_all, do_tails, of, lse, bounds, plan, position_bias, head_width)
    (others,) = comm_call(functools.partial(return_kernel, n=n_head), "return_gradients", 4, (dqkv,), (0,),
                          [(dqkv.shape, BF)], (0,), [dma((n_head - 1,)), dma((n_head - 1,))])
    parts = (layout.late, layout.last, layout.rows)
    sizes = (layout.late, max(layout.last - layout.late, 16 * n_tm * n_head), layout.rows - layout.last)
    ins = (pack, frames_t, x1, h2, dx2, dtab, cols, first_up, first_down_t, mix_inputs)
    grad, total = comm_call(
        functools.partial(final_kernel, n_tm=n_tm, n_head=n_head, parts=parts), "final", 3, (dqkv, others) + ins, range(len(ins) + 2),
        [((width, rows), F32), ((layout.rows, TILE), BF)], (1,),
        [vm(a.shape, a.dtype) for a in ins] + [
            vm((n_head, packed_rows, rows), BF), vm((layout.rows - layout.late, TILE), BF),
            vm((width, rows), BF), vm((hidden, rows), BF), vm((hidden, rows), BF), vm((width, rows), BF),
            vm((n_head * packed_rows, rows), BF), vm((4, width, TILE), F32),
            *[s for size in sizes for s in sum_scratch(size, n_tm, n_head)],
            dma((len(ins),)), dma((n_head,)), dma((3, 12, max(n_tm // 2, n_head))), dma((3,)),
        ])
    shapes = Weights(**{n: w.shape for n, w in weights.__dict__.items()})
    shapes.first_down = shapes.second_down = first_down_t.shape
    results = [((width, rows), BF), ((width, rows), F32)] + [(s, F32) for s in shapes.__dict__.values()]
    out, grad, *summed = pl.pallas_call(
        functools.partial(unpack_kernel, layout=layout),
        out_shape=tuple(jax.ShapeDtypeStruct(s, t) for s, t in results),
        compiler_params=pltpu.CompilerParams(vmem_limit_bytes=VMEM_MIB * 2**20),
        name="unpack",
    )(total, out, grad)
    summed = Weights(*summed)
    summed.first_down, summed.second_down = summed.first_down.T, summed.second_down.T
    return (out.T, grad.T) + tuple(summed.__dict__.values())


def solution(mesh):
    rows = P(("tm", "head"), None)
    placed = (rows, P("tm", None)) + (P(),) * 29 + (rows,)
    return jax.shard_map(body, mesh=mesh, in_specs=placed, out_specs=(rows, rows) + (P(),) * 29, check_vma=False)
```

```python
import dataclasses
import functools
import math
import types

import jax
import jax.numpy as jnp
from jax import lax
from jax.experimental import pallas as pl
from jax.experimental.pallas import tpu as pltpu
from jax.sharding import PartitionSpec as P

BF = jnp.bfloat16
F32 = jnp.float32
LOG2E = math.log2(math.e)
BLK = 512
UNIT = 128
PER = BLK // UNIT
NEAR = PER + 2
PAD = 8 * UNIT
SLOT = 48
MAIN = 32
DEPTH = 128
MASKED = -1e30
GANG = 4
NN = (((1,), (0,)), ((), ()))
NT = (((1,), (1,)), ((), ()))
TN = (((0,), (0,)), ((), ()))


def dot(a, b, dims=NN):
    return lax.dot_general(a, b, dims, preferred_element_type=F32)


def iota(shape, dim):
    return lax.broadcasted_iota(jnp.int32, shape, dim)


def spread_cols(width, slots, slot_rows, used):
    row, column = iota((slots * slot_rows, width), 0), iota((slots * slot_rows, width), 1)
    hit = jnp.zeros((slots * slot_rows, width), jnp.bool_)
    for s in range(slots):
        f = row - slot_rows * s
        hit = hit | ((f >= 0) & (f < used) & (column == used * s + f))
    return hit.astype(F32).astype(BF)


def split3(v):
    hi = v.astype(BF).astype(F32)
    r1 = v - hi
    mid = r1.astype(BF).astype(F32)
    return hi, mid, r1 - mid


def three_rows(v, rows):
    a, b, e = split3(v)
    row = iota((rows, v.shape[1]), 0)
    return jnp.where(row == 0, a, jnp.where(row == 1, b, jnp.where(row == 2, e, 0.0)))


def pick_row(ref, index):
    values = ref[...].astype(F32)
    return jnp.sum(jnp.where(iota(values.shape, 0) == index, values, 0.0), axis=0, keepdims=True)


def bias_square(table, d):
    span = table.shape[1]
    half = span // 2
    lanes = 2 * UNIT
    u = iota((span, lanes), 1)
    u = jnp.where(u < UNIT, u, u - lanes)
    ids = jnp.clip(-UNIT * d - u, -half, half - 1) + half
    hot = (ids == iota((span, lanes), 0)).astype(F32).astype(BF)
    line = dot(jnp.broadcast_to(table, (UNIT, span)).astype(BF), hot) * LOG2E
    return pltpu.roll(line, 0, 1, stride=1, stride_axis=0)[:, :UNIT]


def bias_near(table, tile, keys_near):
    span = table.shape[1]
    squares = {d: bias_square(table, d) for d in (-1, 0, 1)}
    low = jnp.broadcast_to(table[:, :1] * LOG2E, (UNIT, UNIT))
    high = jnp.broadcast_to(table[:, span - 1 :] * LOG2E, (UNIT, UNIT))
    for r in range(tile.shape[0] // UNIT):
        for c in range(tile.shape[1] // UNIT):
            d = c - (r - 1) if keys_near else (c - 1) - r
            part = squares[d] if abs(d) < 2 else (low if d > 0 else high)
            tile[r * UNIT : (r + 1) * UNIT, c * UNIT : (c + 1) * UNIT] = part


def units_at(u, count):
    return pl.ds(pl.multiple_of(u * UNIT, UNIT), count * UNIT)


def far_windows(low, plain, edge, step, side, up, fine):
    sign = 1 if up else -1

    def run(at, times, size, masked):
        def one(i, carry):
            near = at + sign * i * size
            step(near if up else near - size, size, side, masked)
            return carry

        lax.fori_loop(0, times, one, 0)
        return at + sign * times * size

    at = edge if plain is None else run(edge, sign * (plain - edge) // 8, 8, False)
    left = sign * (low - at)
    tail = lax.rem(left, 8)
    more = tail > (6 if fine else 4)
    at = run(at, left // 8 + more.astype(jnp.int32), 8, True)
    tail = jnp.where(more, 0, tail)
    four = tail > (2 if fine else 0)
    at = run(at, four.astype(jnp.int32), 4, True)
    if fine:
        run(at, (tail - jnp.where(four, 4, 0) > 0).astype(jnp.int32), 2, True)


def far_sweep(plan, block, step, before, after, fine):
    low, plain_low, plain_high, high, low_half, high_half = [plan[block, i] for i in range(6)]
    start, stop = PER * block - 1, PER * block + PER + 1
    for whole, part in ((True, None), (False, 0)):
        @pl.when((low_half == 0) if whole else (low_half != 0))
        def _():
            far_windows(low, plain_low if whole else None, start, functools.partial(step, part=part), before, False, fine)

    for whole, part in ((True, None), (False, 1)):
        @pl.when((high_half == 0) if whole else (high_half != 0))
        def _():
            far_windows(high, plain_high if whole else None, stop, functools.partial(step, part=part), after, True, fine)


def fold_rows(four, pieces):
    size = four.shape[1] // pieces
    return jnp.concatenate([four[:, i * size : (i + 1) * size] for i in range(pieces)], axis=0)


def unfold_rows(folded):
    return jnp.concatenate([folded[i : i + 4, :] for i in range(0, folded.shape[0], 4)], axis=1)


def part_at(block, part):
    if part is None:
        return units_at(PER * block, PER)
    return units_at(PER * block + part * (PER // 2), PER // 2)


def has_far(plan, block):
    return (plan[block, 0] < PER * block - 1) | (plan[block, 3] > PER * block + PER + 1)


def segment_rows(ends, lengths, place, total):
    slots = ends.shape[0]
    before = ends <= jnp.broadcast_to(place, (slots, place.shape[1]))
    seg = jnp.sum(before.astype(jnp.int32), axis=0, keepdims=True)
    first = jnp.sum(jnp.where(before, lengths, 0), axis=0, keepdims=True)
    stop = jnp.min(jnp.where(before, total, ends), axis=0, keepdims=True)
    return seg, first, stop


def block_plan(ends, ends_row, total):
    slots = ends.shape[0]
    blocks, units = total // BLK, total // UNIT

    def along(place):
        return jnp.sum((ends <= jnp.broadcast_to(place, (slots, 128))).astype(jnp.int32), axis=0, keepdims=True)

    def down(place):
        return jnp.sum((jnp.broadcast_to(ends_row, (blocks, slots)) <= place).astype(F32), axis=1, keepdims=True).astype(jnp.int32)

    unit = iota((1, 128), 1)
    u_first, u_last = along(unit * UNIT), along(unit * UNIT + UNIT - 1)
    b = iota((blocks, 1), 0)
    first, last = down(b * BLK), down(b * BLK + BLK - 1)
    low_half = (down(b * BLK + BLK // 2) != first).astype(jnp.int32)
    high_half = (down(b * BLK + BLK // 2 - 1) != last).astype(jnp.int32)
    start, stop = PER * b - 1, PER * b + PER + 1
    inside = unit < units

    def count(hit):
        return jnp.sum((hit & inside).astype(F32), axis=1, keepdims=True).astype(jnp.int32)

    low = jnp.minimum(count(u_last < first), start)
    high = jnp.maximum(units - count(u_first > last), stop)
    plain_low = start - count((unit < start) & (u_first == last))
    plain_high = stop + count((unit >= stop) & (u_last == first))
    lane = iota((blocks, 128), 1)
    out = jnp.zeros((blocks, 128), jnp.int32)
    for i, v in enumerate((low, plain_low, plain_high, high, low_half, high_half)):
        out = jnp.where(lane == i, v, out)
    return out


def meets(first_key, rows, bounds):
    key = iota((rows, bounds.shape[1]), 0)
    return (key >= bounds[0:1, :] - first_key) & (key < bounds[1:2, :] - first_key)


def fwd_kernel(plan, qkv_ref, table_ref, bound_ref, o_ref, tail_ref, of_ref, lse_ref, qaug, kn, vt, tile, top_ref, acc, *, head_width):
    chunks, packed_rows, rows = qkv_ref.shape
    total = chunks * rows
    blocks = total // BLK
    span = table_ref.shape[1]
    table = pick_row(table_ref, lax.axis_index("head"))
    far = (table[:, :1] * LOG2E, table[:, span - 1 :] * LOG2E)
    pick = spread_cols(packed_rows, 3, SLOT, head_width)
    scale = LOG2E / math.sqrt(head_width)
    o_ref[:, :UNIT] = jnp.zeros((SLOT, UNIT), BF)
    o_ref[:, UNIT + total :] = jnp.zeros((SLOT, UNIT), BF)
    for edge in (slice(0, PAD), slice(PAD + total, 2 * PAD + total)):
        kn[edge, :] = jnp.zeros((PAD, DEPTH), BF)
        vt[:, edge] = jnp.zeros((SLOT, PAD), BF)
    bias_near(table, tile, True)
    rest = DEPTH - 2 * SLOT

    @pl.loop(0, chunks)
    def _(c):
        at = pl.ds(pl.multiple_of(c * rows, rows), rows)
        at_pad = pl.ds(pl.multiple_of(c * rows + PAD, UNIT), rows)
        parts = dot(pick, qkv_ref[c])
        q = parts[:SLOT] * scale
        hi = q.astype(BF)
        lo = (q - hi.astype(F32)).astype(BF)
        for s in range(3):
            qaug[s, :SLOT, at] = hi
            qaug[s, SLOT : 2 * SLOT, at] = lo
            qaug[s, 2 * SLOT :, at] = jnp.zeros((rest, rows), BF)
        k = parts[SLOT : 2 * SLOT]
        one3 = (iota((rest, rows), 0) < 3).astype(F32)
        kn[at_pad, :] = jnp.concatenate([k, k, one3], axis=0).T.astype(BF)
        one = (iota((SLOT, rows), 0) == head_width).astype(F32)
        vt[:, at_pad] = (parts[2 * SLOT :] + one).astype(BF)

    def top(x):
        return jnp.max(x.reshape(x.shape[0] // 8, 8, BLK), axis=0)

    @pl.loop(0, blocks // GANG)
    def _(pair):
        blocks_now = [GANG * pair + i for i in range(GANG)]
        at_q = [units_at(PER * b, PER) for b in blocks_now]
        near = [units_at(PER * b - 1 + PAD // UNIT, NEAR) for b in blocks_now]
        x = [dot(kn[n, :], qaug[1, :, q]) + tile[...] for n, q in zip(near, at_q)]
        x = [
            jnp.where(meets(PER * b * UNIT - UNIT, NEAR * UNIT, bound_ref[:, units_at(PER * b + PAD // UNIT, PER)]), v, MASKED)
            for b, v in zip(blocks_now, x)
        ]
        m = [jnp.max(top(v), axis=0, keepdims=True) for v in x]
        p = [jnp.exp2(v - w).astype(BF) for v, w in zip(x, m)]
        out = [dot(vt[:, n], v) for n, v in zip(near, p)]
        for q, w, v in zip(at_q, m, out):
            acc[:, q] = v
            lse_ref[:, q] = w
            qaug[0, 2 * SLOT :, q] = three_rows(far[0] - w, rest).astype(BF)
            qaug[2, 2 * SLOT :, q] = three_rows(far[1] - w, rest).astype(BF)

    @pl.loop(0, blocks)
    def _(b):
        @pl.when(has_far(plan, b))
        def _():
            at_q = units_at(PER * b, PER)

            def scores(u, count, side, masked, part):
                x = dot(kn[units_at(u + PAD // UNIT, count), :], qaug[side, :, part_at(b, part)])
                if masked:
                    x = jnp.where(meets(u * UNIT, count * UNIT, bound_ref[:, part_at(b + PAD // BLK, part)]), x, MASKED)
                return x

            near_acc = acc[:, at_q]

            def add(u, count, side, masked, part):
                p = jnp.exp2(scores(u, count, side, masked, part)).astype(BF)
                acc[:, part_at(b, part)] += dot(vt[:, units_at(u + PAD // UNIT, count)], p)

            far_sweep(plan, b, add, 0, 2, False)
            sums = acc[head_width : head_width + 1, at_q]
            over = jnp.max(jnp.where(sums < 2.0**60, 0.0, 1.0))

            @pl.when(over > 0.5)
            def _():
                top_ref[...] = jnp.zeros_like(top_ref)

                def half_of(part):
                    return slice(None) if part is None else slice(part * BLK // 2, (part + 1) * BLK // 2)

                def first(u, count, side, masked, part):
                    x = scores(u, count, side, masked, part)
                    best = jnp.max(x.reshape(x.shape[0] // 8, 8, x.shape[1]), axis=0)
                    top_ref[:, half_of(part)] = jnp.maximum(top_ref[:, half_of(part)], best)

                far_sweep(plan, b, first, 0, 2, False)
                m = jnp.max(top_ref[...], axis=0, keepdims=True)
                acc[:, at_q] = near_acc * jnp.exp2(-m)
                lse_ref[:, at_q] += m

                def second(u, count, side, masked, part):
                    p = jnp.exp2(scores(u, count, side, masked, part) - m[:, half_of(part)]).astype(BF)
                    acc[:, part_at(b, part)] += dot(vt[:, units_at(u + PAD // UNIT, count)], p)

                far_sweep(plan, b, second, 0, 2, False)

    @pl.loop(0, chunks)
    def _(c):
        at = pl.ds(pl.multiple_of(c * rows, rows), rows)
        total_p = acc[head_width : head_width + 1, at]
        out = acc[:, at] / total_p
        o_ref[:, pl.ds(pl.multiple_of(c * rows + UNIT, UNIT), rows)] = out.astype(BF)
        tail_ref[c] = fold_rows(out[MAIN : MAIN + 4], 4).astype(BF)
        of_ref[:, at] = out[: of_ref.shape[0]]
        lse_ref[:, at] = lse_ref[:, at] + jnp.log2(total_p)


def attend_forward(qkv, bounds, plan, table, head_width):
    chunks, packed_rows, rows = qkv.shape
    total = chunks * rows
    vm = pltpu.VMEM
    return pl.pallas_call(
        functools.partial(fwd_kernel, head_width=head_width),
        out_shape=(
            jax.ShapeDtypeStruct((SLOT, total + 2 * UNIT), BF),
            jax.ShapeDtypeStruct((chunks, 16, rows // 4), BF),
            jax.ShapeDtypeStruct((40, total), F32),
            jax.ShapeDtypeStruct((1, total), F32),
        ),
        in_specs=[pl.BlockSpec(memory_space=pltpu.SMEM)] + [pl.BlockSpec()] * 3,
        scratch_shapes=[
            vm((3, DEPTH, total), BF),
            vm((total + 2 * PAD, DEPTH), BF),
            vm((SLOT, total + 2 * PAD), BF),
            vm((NEAR * UNIT, BLK), F32),
            vm((8, BLK), F32),
            vm((SLOT, total), F32),
        ],
        compiler_params=pltpu.CompilerParams(vmem_limit_bytes=62 * 2**20),
        name="attend_forward",
    )(plan, qkv, table, bounds)


def bwd_kernel(plan, qkv_ref, do_ref, tail_ref, of_ref, lse_ref, table_ref, bound_ref, dqkv_ref, dtab_ref,
               qaug, kn, kt, vn, dot_t, qn, don, tile, dq, band, ends, dv_acc, dk_acc, *, head_width):
    chunks, packed_rows, rows = qkv_ref.shape
    total = chunks * rows
    blocks = total // BLK
    span = table_ref.shape[1]
    table = pick_row(table_ref, lax.axis_index("head"))
    pick = spread_cols(packed_rows, 3, SLOT, head_width)
    scale = LOG2E / math.sqrt(head_width)
    back = 1.0 / math.sqrt(head_width)
    rest = DEPTH - 2 * SLOT
    bias_near(table, tile, False)
    for edge in (slice(0, PAD), slice(PAD + total, 2 * PAD + total)):
        for s in range(3):
            qaug[s, :, edge] = jnp.zeros((DEPTH, PAD), BF)
        dot_t[:, edge] = jnp.zeros((DEPTH, PAD), BF)
        qn[edge, :] = jnp.zeros((PAD, DEPTH), BF)
        don[edge, :] = jnp.zeros((PAD, DEPTH), BF)

    @pl.loop(0, chunks)
    def _(c):
        at = pl.ds(pl.multiple_of(c * rows, rows), rows)
        at_pad = pl.ds(pl.multiple_of(c * rows + PAD, UNIT), rows)
        parts = dot(pick, qkv_ref[c])
        q, k, v = parts[:SLOT], parts[SLOT : 2 * SLOT], parts[2 * SLOT :]
        qs = q * scale
        hi = qs.astype(BF)
        lo = (qs - hi.astype(F32)).astype(BF)
        lse = lse_ref[:, at]
        for s, shift in enumerate((table[:, :1] * LOG2E, 0.0, table[:, span - 1 :] * LOG2E)):
            qaug[s, :SLOT, at_pad] = hi
            qaug[s, SLOT : 2 * SLOT, at_pad] = lo
            qaug[s, 2 * SLOT :, at_pad] = three_rows(shift - lse, rest).astype(BF)
        one3 = (iota((rest, rows), 0) < 3).astype(F32)
        row48 = iota((SLOT, rows), 0)
        none = jnp.zeros((rest, rows), F32)
        empty = jnp.zeros((SLOT, rows), F32)
        kn[at, :] = jnp.concatenate([k, k, one3], axis=0).T.astype(BF)
        kt[:, at] = k.astype(BF)
        vn[at, :] = jnp.concatenate([v, empty, one3], axis=0).T.astype(BF)
        tail = unfold_rows(tail_ref[c].astype(F32))
        do = jnp.concatenate([do_ref[c].astype(F32), tail, jnp.zeros((SLOT - MAIN - 4, rows), F32)], axis=0)
        centre = jnp.sum(do[: of_ref.shape[0]] * of_ref[:, at], axis=0, keepdims=True)
        dot_t[:SLOT, at_pad] = do.astype(BF)
        dot_t[SLOT : 2 * SLOT, at_pad] = empty.astype(BF)
        dot_t[2 * SLOT :, at_pad] = three_rows(-centre, rest).astype(BF)
        qn[at_pad, :] = jnp.concatenate([q + (row48 == head_width).astype(F32), empty, none], axis=0).T.astype(BF)
        don[at_pad, :] = jnp.concatenate([do, empty, none], axis=0).T.astype(BF)

    dq[...] = jnp.zeros_like(dq)
    band[...] = jnp.zeros_like(band)
    ends[...] = jnp.zeros_like(ends)

    @pl.loop(0, blocks // GANG)
    def _(pair):
        width = NEAR * UNIT
        wide = width + (GANG - 1) * BLK
        blocks_now = [GANG * pair + i for i in range(GANG)]
        at_k = [units_at(PER * b, PER) for b in blocks_now]
        near = [units_at(PER * b - 1 + PAD // UNIT, NEAR) for b in blocks_now]
        x = [dot(kn[k, :], qaug[1, :, n]) + tile[...] for k, n in zip(at_k, near)]
        dp = [dot(vn[k, :], dot_t[:, n]) for k, n in zip(at_k, near)]
        p = [jnp.where(meets(b * BLK, BLK, bound_ref[:, n]), jnp.exp2(v), 0.0) for b, n, v in zip(blocks_now, near, x)]
        dsb = [(v * w).astype(BF) for v, w in zip(p, dp)]
        dv = [dot(v.astype(BF), don[n, :]) for n, v in zip(near, p)]
        dk = [dot(v, qn[n, :]) for n, v in zip(near, dsb)]
        part = [dot(kt[:, k], v) for k, v in zip(at_k, dsb)]
        for k, v, w in zip(at_k, dv, dk):
            dv_acc[k, :] = v
            dk_acc[k, :] = w
        gap = [jnp.zeros((SLOT, BLK), F32)]
        whole = [jnp.concatenate(gap * i + [v] + gap * (GANG - 1 - i), axis=1) for i, v in enumerate(part)]
        lines = [v.astype(F32) for v in dsb]
        dq[:, units_at(GANG * PER * pair - 1 + PAD // UNIT, wide // UNIT)] += functools.reduce(jnp.add, whole)
        band[...] += functools.reduce(jnp.add, lines)

    @pl.loop(0, blocks)
    def _(b):
        @pl.when(has_far(plan, b))
        def _():
            def far(u, count, side, masked, part):
                at_k = part_at(b, part)
                at_q = units_at(u + PAD // UNIT, count)
                p = jnp.exp2(dot(kn[at_k, :], qaug[side, :, at_q]))
                if masked:
                    first_key = b * BLK + (0 if part is None else part * BLK // 2)
                    p = jnp.where(meets(first_key, at_k.size, bound_ref[:, at_q]), p, 0.0)
                dsb = (p * dot(vn[at_k, :], dot_t[:, at_q])).astype(BF)
                dq[:, at_q] += dot(kt[:, at_k], dsb)
                dv_acc[at_k, :] += dot(p.astype(BF), don[at_q, :])
                dk = dot(dsb, qn[at_q, :])
                dk_acc[at_k, :] += dk
                ends[side // 2] += jnp.sum(dk.reshape(dk.shape[0] // 8, 8, DEPTH), axis=0)

            far_sweep(plan, b, far, 2, 0, True)

    def take(part, lanes):
        row, lane = iota((packed_rows, lanes), 0), iota((packed_rows, lanes), 1)
        return ((row - head_width * part == lane) & (lane < head_width)).astype(F32).astype(BF)

    @pl.loop(0, chunks)
    def _(c):
        at = pl.ds(pl.multiple_of(c * rows, rows), rows)
        at_pad = pl.ds(pl.multiple_of(c * rows + PAD, UNIT), rows)
        packed = dot(take(0, SLOT), (dq[:, at_pad] * back).astype(BF))
        packed += dot(take(1, DEPTH), (dk_acc[at, :] * back).astype(BF), NT)
        packed += dot(take(2, DEPTH), dv_acc[at, :].astype(BF), NT)
        dqkv_ref[c] = packed.astype(BF)

    flip = (iota((UNIT, UNIT), 0) + iota((UNIT, UNIT), 1) == UNIT - 1).astype(F32)
    half = span // 2
    lane = iota((8, span), 1)
    column = iota((8, DEPTH), 1) == head_width
    out = jnp.zeros((8, span), F32)
    far_sum = [jnp.where(column, ends[i], 0.0) for i in range(2)]
    for d in range(-PER, PER + 1):
        part = jnp.zeros((UNIT, UNIT), F32)
        for r in range(PER):
            c = r + d + 1
            if 0 <= c < NEAR:
                part = part + band[r * UNIT : (r + 1) * UNIT, c * UNIT : (c + 1) * UNIT]
        if abs(d) > 1:
            far_sum[0 if d > 0 else 1] += jnp.sum(part.reshape(UNIT // 8, 8, UNIT), axis=0)
            continue
        turned = lax.dot_general(flip, part, NN, precision=lax.Precision.HIGHEST, preferred_element_type=F32)
        wide = jnp.concatenate([turned, jnp.zeros_like(turned)], axis=1)
        skewed = pltpu.roll(wide, 0, 1, stride=1, stride_axis=0)
        line = jnp.sum(skewed.reshape(UNIT // 8, 8, 2 * UNIT), axis=0)
        offset = UNIT - 1 - d * UNIT - iota((span, 2 * UNIT), 1)
        hot = (jnp.clip(offset, -half, half - 1) + half == iota((span, 2 * UNIT), 0)).astype(F32)
        out += lax.dot_general(line, hot, NT, precision=lax.Precision.HIGHEST, preferred_element_type=F32)
    out += jnp.where(lane == 0, jnp.sum(far_sum[0], axis=1, keepdims=True), 0.0)
    out += jnp.where(lane == span - 1, jnp.sum(far_sum[1], axis=1, keepdims=True), 0.0)
    out = jnp.sum(out, axis=0, keepdims=True)
    dtab_ref[...] = out


def attend_backward(qkv, do, tail, of, lse, bounds, plan, table, head_width):
    chunks, packed_rows, rows = qkv.shape
    total = chunks * rows
    padded = total + 2 * PAD
    span = table.shape[1]
    vm = pltpu.VMEM
    return pl.pallas_call(
        functools.partial(bwd_kernel, head_width=head_width),
        out_shape=(
            jax.ShapeDtypeStruct((chunks, packed_rows, rows), BF),
            jax.ShapeDtypeStruct((1, span), F32),
        ),
        in_specs=[pl.BlockSpec(memory_space=pltpu.SMEM)] + [pl.BlockSpec()] * 7,
        scratch_shapes=[
            vm((3, DEPTH, padded), BF),
            vm((total, DEPTH), BF),
            vm((SLOT, total), BF),
            vm((total, DEPTH), BF),
            vm((DEPTH, padded), BF),
            vm((padded, DEPTH), BF),
            vm((padded, DEPTH), BF),
            vm((BLK, NEAR * UNIT), F32),
            vm((SLOT, padded), F32),
            vm((BLK, NEAR * UNIT), F32),
            vm((2, 8, DEPTH), F32),
            vm((total, DEPTH), F32),
            vm((total, DEPTH), F32),
        ],
        compiler_params=pltpu.CompilerParams(vmem_limit_bytes=62 * 2**20),
        name="attend_backward",
    )(plan, qkv, do, tail, of, lse, table, bounds)

VEC = types.SimpleNamespace(
    first_gain=0, first_shift=1, first_up_bias=2, first_down_bias=3, mix_gain=4, mix_shift=5, mix_output_bias=6, filter_gain=7,
    filter_shift=8, pointwise_in_bias=9, batch_gain=10, batch_shift=11, pointwise_out_bias=12, second_gain=13, second_shift=14,
    second_up_bias=15, second_down_bias=16, final_gain=17, final_shift=18,
)
VEC_ROWS = 24
EPSILON = 1e-05
HALO = 64
TILE = 128
PIECE = 256
PART = 512
STEP = 1024


def col(cols_ref, i, size):
    return cols_ref[:size, i : i + 1]


def eye(n):
    return (iota((n, n), 0) == iota((n, n), 1)).astype(F32).astype(BF)


def flipped(mat):
    return dot(eye(mat.shape[1]), mat, NT).astype(BF)


def exact(a, b, dims=NN):
    return lax.dot_general(a, b, dims, precision=lax.Precision.HIGHEST, preferred_element_type=F32)


def folded(values):
    part = values[:, :TILE]
    for at in range(TILE, values.shape[1], TILE):
        part = part + values[:, at : at + TILE]
    return part


def row_sums(values):
    return exact(jnp.ones((8, TILE), F32), values, NT)


def many_row_sums(parts):
    size = parts[0].shape[0]
    lines = row_sums(jnp.concatenate(parts, axis=0))
    return [lines[:1, i * size : (i + 1) * size] for i in range(len(parts))]


def norm(x):
    m = jnp.mean(x, axis=0, keepdims=True)
    c = x - m
    inv = lax.rsqrt(jnp.mean(c * c, axis=0, keepdims=True) + EPSILON)
    return c * inv, inv


def norm_back(e, n, inv, gain):
    ea = e * gain
    return inv * (ea - jnp.mean(ea, axis=0, keepdims=True) - n * jnp.mean(ea * n, axis=0, keepdims=True))


def sigmoid(v):
    return 0.5 + 0.5 * jnp.tanh(0.5 * v)


def ones_row(rows, lanes):
    return (iota((rows, lanes), 0) == 0).astype(F32).astype(BF)


def open_rows(frames_ref, up_ref, down_ref, mix_ref, x1_ref, h2_ref, qkv_ref, cols_ref, packed_rows, ship):
    width, rows = frames_ref.shape
    hidden = up_ref.shape[1]
    heads = qkv_ref.shape[0]
    up_t = flipped(up_ref[...])
    mix_t = dot(spread_cols(mix_ref.shape[1], heads, packed_rows, mix_ref.shape[1] // heads), mix_ref[...], NT).astype(BF)

    @pl.loop(0, rows // PIECE)
    def _(c):
        at = pl.ds(pl.multiple_of(c * PIECE, PIECE), PIECE)
        x0 = frames_ref[:, at].astype(F32)
        n, _ = norm(x0)
        h1 = (n * col(cols_ref, VEC.first_gain, width) + col(cols_ref, VEC.first_shift, width)).astype(BF)
        a1 = dot(up_t, h1) + col(cols_ref, VEC.first_up_bias, hidden)
        s1 = (a1 * sigmoid(a1)).astype(BF)
        x1 = x0 + 0.5 * (dot(down_ref[...], s1) + col(cols_ref, VEC.first_down_bias, width))
        x1_ref[:, at] = x1
        n, _ = norm(x1)
        h2 = (n * col(cols_ref, VEC.mix_gain, width) + col(cols_ref, VEC.mix_shift, width)).astype(BF)
        h2_ref[:, at] = h2
        qkv = dot(mix_t, h2).astype(BF)
        for h in range(heads):
            qkv_ref[h, :, at] = qkv[h * packed_rows : (h + 1) * packed_rows]
        ship(c)


def open_segments(len_ref, bound_ref, plan_ref, ext_ref, line):
    rows = ext_ref.shape[1] - TILE
    group = bound_ref.shape[1] - 2 * PAD
    slots = len_ref.shape[1]
    lengths = jnp.broadcast_to(len_ref[...].astype(F32), (8, slots))
    row, column = iota((slots, slots), 0), iota((slots, slots), 1)
    ends = exact((column <= row).astype(F32), lengths, NT)[:, :1].astype(jnp.int32)
    own_len = exact((column == row).astype(F32), lengths, NT)[:, :1].astype(jnp.int32)
    ends_row = exact(lengths, (row <= column).astype(F32))[:1].astype(jnp.int32)
    plan_ref[...] = block_plan(ends, ends_row, group)
    line[...] = jnp.full_like(line, -1)
    for edge in (slice(0, PAD), slice(PAD + group, 2 * PAD + group)):
        bound_ref[:, edge] = jnp.where(iota((2, PAD), 0) == 0, 1 << 20, -1)

    @pl.loop(0, group // 512)
    def _(c):
        at = pl.multiple_of(c * 512, 512)
        seg, first, stop = segment_rows(ends, own_len, iota((1, 512), 1) + at, group)
        line[:, pl.ds(at + TILE, 512)] = seg
        bound_ref[0:1, pl.ds(at + PAD, 512)] = first
        bound_ref[1:2, pl.ds(at + PAD, 512)] = stop

    first = pl.multiple_of(lax.axis_index("head") * rows, TILE)
    ext_ref[:, :rows] = line[:, pl.ds(first + TILE, rows)]
    left = line[:, pl.ds(first, TILE)]
    right = line[:, pl.ds(first + TILE + rows, TILE)]
    ext_ref[:, rows:] = jnp.where(iota((1, TILE), 1) < HALO, right, left)


def split_heads(heads, head_width):
    size = heads * head_width
    row, column = iota((size, size), 0), iota((size, size), 1)
    hit = jnp.zeros((size, size), jnp.bool_)
    for h in range(heads):
        f = column - head_width * h
        mine = (f >= 0) & (f < head_width)
        hit = hit | (mine & (f < MAIN) & (row == MAIN * h + f)) | (mine & (f >= MAIN) & (row == MAIN * heads + 4 * h + f - MAIN))
    return hit.astype(F32).astype(BF)


def conv_masks(mask_ref, ext_ref):
    seg = jnp.broadcast_to(ext_ref[...], (8, ext_ref.shape[1]))
    lanes = seg.shape[1]
    reach = mask_ref.shape[0] // 2
    for i in range(mask_ref.shape[0]):
        mask_ref[i] = (pltpu.roll(seg, (reach - i) % lanes, 1) == seg).astype(F32)


def filter_kernel(x1_ref, x1l_ref, x1r_ref, o_ref, tail_ref, cols_ref, ext_ref, out_ref, pw_ref, taps_ref,
                  x2_ref, oc_ref, u_ref, y_ref, stat_ref, wide, mask, live_ref, h3s, n_ref, inv_ref, value_ref, gate_ref, *, head_width, slot_count, arrive):
    width, rows = x1_ref.shape
    lanes = rows + TILE
    heads = o_ref.shape[0]
    taps = taps_ref.shape[0]
    out_t = flipped(out_ref[...])
    pw_t = flipped(pw_ref[...])
    gather = split_heads(heads, head_width)
    seg = ext_ref[...]
    live = (seg >= 0) & (seg < slot_count)
    live_ref[...] = live.astype(F32)
    conv_masks(mask, ext_ref)
    wide_taps = taps_ref[...].astype(F32).T
    arrive()

    near = iota((1, TILE), 1) < HALO

    def extended(own, left, right):
        edge = jnp.where(near, right.astype(F32), left.astype(F32)).astype(own.dtype)
        return jnp.concatenate([own, edge], axis=1)

    x1 = extended(x1_ref[...], x1l_ref[...], x1r_ref[...])
    main = [extended(o_ref[h, :MAIN, TILE : TILE + rows], o_ref[h, :MAIN, :TILE], o_ref[h, :MAIN, TILE + rows :]) for h in range(heads)]
    tails = []
    for h in range(heads):
        left, right = (o_ref[h, MAIN:, at].astype(F32)[:4] for at in (slice(0, TILE), slice(TILE + rows, rows + 2 * TILE)))
        tails.append(extended(unfold_rows(tail_ref[h].astype(F32)), left, right))
    o = jnp.concatenate(main + [jnp.concatenate(tails, axis=0).astype(BF)], axis=0)
    oc = dot(gather, o, TN).astype(BF)
    x2 = x1 + (dot(out_t, oc) + col(cols_ref, VEC.mix_output_bias, width))
    n, inv = norm(x2)
    h3 = (n * col(cols_ref, VEC.filter_gain, width) + col(cols_ref, VEC.filter_shift, width)).astype(BF)
    g = dot(pw_t, h3) + col(cols_ref, VEC.pointwise_in_bias, 2 * width)
    gate = sigmoid(g[width:])
    u = jnp.where(live_ref[...] > 0.5, g[:width] * gate, 0.0).astype(BF)
    n_ref[...] = n[:, :rows]
    inv_ref[...] = inv[:, :rows]
    h3s[:width, :] = h3[:, :rows]
    value_ref[...] = g[:width, :rows]
    gate_ref[...] = gate[:, :rows]
    oc_ref[:width, :] = oc[:, :rows]
    x2_ref[...] = x2
    u_ref[...] = u
    wide[...] = u.astype(F32)

    own = (live & (iota((1, lanes), 1) < rows)).astype(F32)
    count = jnp.sum(own, axis=1, keepdims=True)
    safe = jnp.maximum(count, 1.0)
    for r in range(width // 8):
        sl = slice(8 * r, 8 * r + 8)
        u8 = wide[sl, :]
        acc = jnp.zeros((8, lanes), F32)
        for k in range(taps):
            moved = pltpu.roll(u8, (taps // 2 - k) % lanes, 1)
            acc = acc + wide_taps[sl, k : k + 1] * (moved * mask[k])
        y_ref[sl, :] = acc
    y = y_ref[...]
    part = folded(y * own)
    mean = exact(part, jnp.ones((TILE, TILE), F32)) / safe
    dev = (y - jnp.concatenate([mean] * (lanes // TILE), axis=1)) * own
    mean_row, spread_row = many_row_sums([part, folded(dev * dev)])
    stat_ref[...] = two_rows(mean_row / safe, spread_row, count)


def two_rows(a, b, extra):
    rest = a.shape[1] - TILE
    tail = pad_lanes(jnp.concatenate([a[:, TILE:], b[:, TILE:]], axis=0))
    spot = (iota((2, TILE), 0) == 0) & (iota((2, TILE), 1) == rest)
    return jnp.concatenate([a[:, :TILE], b[:, :TILE], jnp.where(spot, extra, tail)], axis=0)


def all_rows(ref, width):
    rest = width - TILE
    values = ref[...]
    a = jnp.concatenate([values[:, 0, :], values[:, 2, :rest]], axis=1)
    b = jnp.concatenate([values[:, 1, :], values[:, 3, :rest]], axis=1)
    return a, b, values[:, 2, rest : rest + 1]


def total_stats(stats_ref, width):
    mean_of, spread_of, n = all_rows(stats_ref, width)
    count = jnp.sum(n, axis=0, keepdims=True)
    mean = jnp.sum(n * mean_of, axis=0, keepdims=True) / count
    gap = mean_of - mean
    spread = jnp.sum(spread_of + n * gap * gap, axis=0, keepdims=True)
    inv = lax.rsqrt(spread / count + EPSILON)
    table = jnp.concatenate([mean, inv, jnp.broadcast_to(count, (1, width)), jnp.zeros((5, width), F32)], axis=0).T
    return table[:, 0:1], table[:, 1:2], table[:, 2:3]


def second_kernel(x2_ref, y_ref, stats_ref, cot_ref, cotl_ref, cotr_ref, cols_ref, pwo_ref, up_ref, down_ref,
                  out_ref, dx3_ref, e_ref, sums_ref, pack_ref, small_ref,
                  h4s, das, s4s, dfs, ws, dcs, *, arrive, leave):
    width, rows = out_ref.shape
    hidden = up_ref.shape[1]
    pwo_t = flipped(pwo_ref[...])
    up_t = flipped(up_ref[...])
    down = flipped(down_ref[...])
    arrive()
    mean, inv_b, _ = total_stats(stats_ref, width)
    bgain = col(cols_ref, VEC.batch_gain, width)

    near = iota((1, TILE), 1) < HALO
    edge = jnp.where(near, cotr_ref[...].astype(F32), cotl_ref[...].astype(F32))
    cot = jnp.concatenate([cot_ref[...].astype(F32), edge], axis=1)
    zh = (y_ref[...] - mean) * inv_b
    z = zh * bgain + col(cols_ref, VEC.batch_shift, width)
    sig_z = sigmoid(z)
    w = (z * sig_z).astype(BF)
    x3 = x2_ref[...] + (dot(pwo_t, w) + col(cols_ref, VEC.pointwise_out_bias, width))
    n4, inv4 = norm(x3)
    h4 = (n4 * col(cols_ref, VEC.second_gain, width) + col(cols_ref, VEC.second_shift, width)).astype(BF)
    a4 = dot(up_t, h4) + col(cols_ref, VEC.second_up_bias, hidden)
    sig = sigmoid(a4)
    s4 = (a4 * sig).astype(BF)
    x4 = x3 + 0.5 * (dot(down_ref[...], s4) + col(cols_ref, VEC.second_down_bias, width))
    nf, invf = norm(x4)
    fgain = col(cols_ref, VEC.final_gain, width)
    dx4 = norm_back(cot, nf, invf, fgain)
    df = (0.5 * dx4).astype(BF)
    da = (dot(down, df) * (sig * (1.0 + a4 * (1.0 - sig)))).astype(BF)
    dh = dot(up_ref[...], da)
    dx3 = dx4 + norm_back(dh, n4, inv4, col(cols_ref, VEC.second_gain, width))
    dc = dx3.astype(BF)
    dz = dot(pwo_ref[...], dc) * (sig_z * (1.0 + z * (1.0 - sig_z)))
    e = dz * bgain
    e_ref[...] = e
    sums_ref[...] = two_rows(*many_row_sums([folded(e[:, :rows]), folded((e * zh)[:, :rows])]), 0.0)
    leave()

    out_ref[...] = (nf * fgain + col(cols_ref, VEC.final_shift, width))[:, :rows].astype(BF)
    dx3_ref[...] = dx3[:, :rows]
    h4s[...] = h4[:, :rows]
    das[...] = da[:, :rows]
    s4s[:hidden, :] = s4[:, :rows]
    dfs[...] = df[:, :rows]
    ws[:width, :] = w[:, :rows]
    dcs[...] = dc[:, :rows]
    totals = many_row_sums([folded(v[:, :rows]) for v in (dh * n4, dh, cot * nf, cot, dz * zh, dz)])
    s4s[hidden:, :] = ones_row(16, rows)
    ws[width:, :] = ones_row(16, rows)
    up_grad = dot(h4s[...], das[...], NT)
    up_bias = dot(ones_row(16, rows), das[...], NT)
    down_grad = dot(dfs[...], s4s[...], NT)
    pw_grad = dot(ws[...], dcs[...], NT)
    down_bias = dot(ones_row(16, rows), dfs[...], NT)
    put_ff(pack_ref, up_grad, down_grad, 0)
    tall = 9 * width
    pack_ref[tall : tall + width, :] = pw_grad[:width, :TILE].astype(BF)
    pack_ref[tall + width : tall + 2 * width, :] = pad_lanes(pw_grad[:width, TILE:]).astype(BF)
    small_ref[...] = stack_rows(
        [totals[0], totals[1], up_bias[:1], down_bias[:1], totals[2], totals[3], totals[4], totals[5], pw_grad[width : width + 1]],
        small_ref.shape)


def pad_lanes(mat, lanes=TILE):
    if mat.shape[1] == lanes:
        return mat
    return jnp.concatenate([mat, jnp.zeros((mat.shape[0], lanes - mat.shape[1]), mat.dtype)], axis=1)


def stack_rows(rows, shape):
    parts = [pad_lanes(r, shape[1]) for r in rows]
    parts.append(jnp.zeros((shape[0] - len(rows), shape[1]), F32))
    return jnp.concatenate(parts, axis=0)


def put_ff(pack_ref, up_grad, down_grad_t, at):
    width, hidden = up_grad.shape
    whole = hidden // TILE
    for i in range(whole):
        pack_ref[at + i * width : at + (i + 1) * width, :] = up_grad[:, i * TILE : (i + 1) * TILE].astype(BF)
        j = whole + i
        pack_ref[at + j * width : at + (j + 1) * width, :] = down_grad_t[:, i * TILE : (i + 1) * TILE].astype(BF)
    rest = jnp.concatenate([up_grad[:, whole * TILE : hidden], down_grad_t[:, whole * TILE : hidden]], axis=1)
    pack_ref[at + 2 * whole * width : at + (2 * whole + 1) * width, :] = rest.astype(BF)


def unfilter_kernel(e_ref, y_ref, stats_ref, sums_ref, u_ref, dx3_ref, ocs, cols_ref, ext_ref, pw_ref, taps_ref,
                    out_ref, dx2_ref, do_ref, pack_ref, small_ref, tapg_ref,
                    dyw, du_s, mask, prod, h3s, dgs, dms, gains, live_ref, n_ref, inv_ref, value_ref, gate_ref, tail_ref, *, head_width, ship, arrive):
    width, rows = dx3_ref.shape
    lanes = rows + TILE
    heads = do_ref.shape[0]
    taps = taps_ref.shape[0]
    tap_cols = taps_ref[...].astype(F32).T
    out_w = dot(split_heads(heads, head_width), out_ref[...]).astype(BF)
    gains[...] = jnp.zeros_like(gains)
    fgain = col(cols_ref, VEC.filter_gain, width)
    mean, inv_b, count = total_stats(stats_ref, width)
    arrive()
    one_of, two_of, _ = all_rows(sums_ref, width)
    sums = jnp.concatenate([jnp.sum(one_of, axis=0, keepdims=True), jnp.sum(two_of, axis=0, keepdims=True), jnp.zeros((6, width), F32)], axis=0).T
    s1, s2 = sums[:, 0:1], sums[:, 1:2]
    seg = ext_ref[...]
    live = live_ref[...]
    zh = (y_ref[...] - mean) * inv_b
    dy = inv_b * (e_ref[...] - live * ((s1 + zh * s2) / count))
    dyw[...] = jnp.where(seg >= 0, dy, 0.0).astype(BF).astype(F32)

    for r in range(width // 8):
        sl = slice(8 * r, 8 * r + 8)
        dy8 = dyw[sl, :]
        u8 = u_ref[16 * (r // 2) : 16 * (r // 2) + 16, :rows].astype(F32)[8 * (r % 2) : 8 * (r % 2) + 8]
        acc = jnp.zeros((8, rows), F32)
        for k in range(taps):
            moved = pltpu.roll(dy8, (k - taps // 2) % lanes, 1)[:, :rows] * mask[taps - k][:, :rows]
            acc = acc + tap_cols[sl, k : k + 1] * moved
            hit = moved * u8
            prod[k, sl, :] = folded(hit)
        du_s[sl, :] = acc

    @pl.loop(0, rows // PART)
    def _(c):
        at = pl.ds(pl.multiple_of(c * PART, PART), PART)
        n, inv = n_ref[:, at], inv_ref[:, at]
        gate = gate_ref[:, at]
        t = live_ref[:, at] * du_s[:, at] * gate
        dg = jnp.concatenate([t, t * value_ref[:, at] * (1.0 - gate)], axis=0).astype(BF)
        dh = dot(pw_ref[...], dg)
        dx2 = dx3_ref[:, at] + norm_back(dh, n, inv, fgain)
        dx2_ref[:, at] = dx2
        dm = dx2.astype(BF)
        do = dot(out_w, dm)
        for h in range(heads):
            do_ref[h, :, at] = do[h * MAIN : (h + 1) * MAIN].astype(BF)
        tail_ref[:, at] = do[heads * MAIN :]
        ship(c)
        dgs[:, at] = dg
        dms[:, at] = dm
        for i, v in enumerate((dh * n, dh)):
            gains[i] += folded(v)

    ship(rows // PART)
    whole = prod[...].reshape(taps * width, TILE)
    hi = whole.astype(BF)
    lo = (whole - hi.astype(F32)).astype(BF)
    ones = jnp.ones((8, TILE), BF)
    lines = dot(ones, hi, NT) + dot(ones, lo, NT)
    for k in range(taps):
        tapg_ref[k : k + 1, :] = lines[:1, k * width : (k + 1) * width]

    h3s[width:, :] = ones_row(16, rows)
    ocs[width:, :] = ones_row(16, rows)
    pw_grad = dot(h3s[...], dgs[...], NT)
    out_grad = dot(ocs[...], dms[...], NT)
    at = 0
    for lo in range(0, 2 * width, TILE):
        pack_ref[at : at + width, :] = pad_lanes(pw_grad[:width, lo : min(lo + TILE, 2 * width)]).astype(BF)
        at += width
    for lo in range(0, width, TILE):
        pack_ref[at : at + width, :] = pad_lanes(out_grad[:width, lo : min(lo + TILE, width)]).astype(BF)
        at += width
    small_ref[...] = stack_rows(
        [row_sums(gains[0])[:1], row_sums(gains[1])[:1], pw_grad[width : width + 1], out_grad[width : width + 1]], small_ref.shape)


def close_kernel(frames_ref, x1_ref, h2_ref, dx2_ref, dqkv_ref, dtab_ref, cols_ref, up_ref, down_ref, mix_ref,
                 grad_ref, pack_ref, h1s, das, s1s, dfs, dqs, gains, *, mixed):
    width, rows = frames_ref.shape
    hidden = up_ref.shape[1]
    heads, packed_rows, _ = dqkv_ref.shape
    up_t = flipped(up_ref[...])
    down = flipped(down_ref[...])
    hot = spread_cols(mix_ref.shape[1], heads, packed_rows, mix_ref.shape[1] // heads)
    mix_w = dot(mix_ref[...], hot, NT).astype(BF)
    gains[...] = jnp.zeros_like(gains)
    mgain = col(cols_ref, VEC.mix_gain, width)
    fgain = col(cols_ref, VEC.first_gain, width)

    @pl.loop(0, rows // STEP)
    def _(c):
        at = pl.ds(pl.multiple_of(c * STEP, STEP), STEP)
        dq = jnp.concatenate([dqkv_ref[h, :, at] for h in range(heads)], axis=0)
        dqs[:, at] = dq
        dh2 = dot(mix_w, dq)
        n2, inv2 = norm(x1_ref[:, at])
        dx1 = dx2_ref[:, at] + norm_back(dh2, n2, inv2, mgain)
        x0 = frames_ref[:, at].astype(F32)
        n1, inv1 = norm(x0)
        h1 = (n1 * fgain + col(cols_ref, VEC.first_shift, width)).astype(BF)
        a1 = dot(up_t, h1) + col(cols_ref, VEC.first_up_bias, hidden)
        sig = sigmoid(a1)
        s1s[:, at] = (a1 * sig).astype(BF)
        df = (0.5 * dx1).astype(BF)
        da = (dot(down, df) * (sig * (1.0 + a1 * (1.0 - sig)))).astype(BF)
        dh1 = dot(up_ref[...], da)
        grad_ref[:, at] = dx1 + norm_back(dh1, n1, inv1, fgain)
        h1s[:, at] = h1
        das[:, at] = da
        dfs[:, at] = df
        for i, v in enumerate((dh1 * n1, dh1, dh2 * n2, dh2)):
            gains[i] += folded(v)

    mix_grad = dot(dot(h2_ref[...], dqs[...], NT).astype(BF), hot)
    at = 0
    for lo in range(0, mix_grad.shape[1], TILE):
        pack_ref[at : at + width, :] = pad_lanes(mix_grad[:, lo : min(lo + TILE, mix_grad.shape[1])]).astype(BF)
        at += width
    mixed()
    up_grad = dot(h1s[...], das[...], NT)
    up_bias = dot(ones_row(16, rows), das[...], NT)
    down_grad = dot(dfs[...], s1s[...], NT)
    down_bias = dot(ones_row(16, rows), dfs[...], NT)
    put_ff(pack_ref, up_grad, down_grad, at)
    at += (2 * (hidden // TILE) + 1) * width
    totals = many_row_sums([gains[i] for i in range(4)])
    small = stack_rows([totals[0], totals[1], up_bias[:1], down_bias[:1], totals[2], totals[3]], (16, 5 * TILE))
    at = put_small(pack_ref, small, at)
    span = dtab_ref.shape[1]
    table = jnp.where(iota((16, span), 0) == lax.axis_index("head"), dtab_ref[...], 0.0)
    pack_ref[at : at + 16, :] = table.astype(BF)
    if at + 16 < pack_ref.shape[0]:
        pack_ref[at + 16 :, :] = jnp.zeros((pack_ref.shape[0] - at - 16, TILE), BF)


def put_small(pack_ref, small, at):
    for lo in range(0, small.shape[1], TILE):
        pack_ref[at : at + small.shape[0], :] = small[:, lo : lo + TILE].astype(BF)
        at += small.shape[0]
    return at


def put_taps(pack_ref, tapg, at):
    taps = tapg.shape[0]
    pack_ref[at : at + taps, :] = tapg[:, :TILE].astype(BF)
    pack_ref[at + taps : at + 2 * taps, :] = pad_lanes(tapg[:, TILE:]).astype(BF)
    return at + 2 * taps


def unpack_kernel(pack_ref, out_ref, grad_ref, *refs, layout):
    refs[0][...] = out_ref[...]
    refs[1][...] = grad_ref[...]
    out_refs = refs[2:]
    given = Weights(*out_refs)

    def wide(at, rows, lanes):
        parts = [pack_ref[at + i * rows : at + (i + 1) * rows, :].astype(F32) for i in range(-(-lanes // TILE))]
        return jnp.concatenate(parts, axis=1)[:, :lanes]

    for at, up_ref, down_ref in ((layout.first, given.first_up, given.first_down), (layout.second, given.second_up, given.second_down)):
        width, hidden = up_ref.shape
        whole = hidden // TILE
        half = hidden - whole * TILE
        piece = lambda i: pack_ref[at + i * width : at + (i + 1) * width, :].astype(F32)
        rest = piece(2 * whole)
        up_ref[...] = jnp.concatenate([piece(i) for i in range(whole)] + [rest[:, :half]], axis=1)
        down_ref[...] = jnp.concatenate([piece(whole + i) for i in range(whole)] + [rest[:, half:]], axis=1)
    for ref, at in ((given.mix_inputs, layout.mix_inputs), (given.pointwise_in, layout.pointwise_in), (given.mix_output, layout.mix_output),
                    (given.pointwise_out, layout.pointwise_out), (given.depthwise_taps, layout.taps)):
        ref[...] = wide(at, *ref.shape)
    given.position_bias[...] = pack_ref[layout.table : layout.table + 16, :].astype(F32)[: given.position_bias.shape[0]]
    late = wide(layout.small_late, 16, 5 * TILE)
    early = wide(layout.small, 32, 5 * TILE)
    late_rows = (
        given.first_gain, given.first_shift, given.first_up_bias, given.first_down_bias, given.mix_gain, given.mix_shift,
    )
    second_rows = (
        given.second_gain, given.second_shift, given.second_up_bias, given.second_down_bias, given.final_gain, given.final_shift,
        given.batch_gain, given.batch_shift, given.pointwise_out_bias,
    )
    filter_rows = (given.filter_gain, given.filter_shift, given.pointwise_in_bias, given.mix_output_bias)
    for small, first, refs in ((late, 0, late_rows), (early, 0, second_rows), (early, 16, filter_rows)):
        for row, ref in enumerate(refs, first):
            ref[...] = small[row : row + 1, : ref.shape[0]].reshape(ref.shape)


@dataclasses.dataclass
class Weights:
    first_gain: object
    first_shift: object
    first_up: object
    first_up_bias: object
    first_down: object
    first_down_bias: object
    mix_gain: object
    mix_shift: object
    mix_inputs: object
    position_bias: object
    mix_output: object
    mix_output_bias: object
    filter_gain: object
    filter_shift: object
    pointwise_in: object
    pointwise_in_bias: object
    depthwise_taps: object
    batch_gain: object
    batch_shift: object
    pointwise_out: object
    pointwise_out_bias: object
    second_gain: object
    second_shift: object
    second_up: object
    second_up_bias: object
    second_down: object
    second_down_bias: object
    final_gain: object
    final_shift: object


def pack_layout(width, hidden, mix_width, taps, devices):
    ff = (2 * (hidden // TILE) + 1) * width
    chunks = lambda lanes: -(-lanes // TILE) * width
    unit = 16 * devices
    whole = lambda rows: -(-rows // unit) * unit
    at = types.SimpleNamespace(second=0, pointwise_out=ff)
    at.pointwise_in = ff + chunks(width)
    at.mix_output = at.pointwise_in + chunks(2 * width)
    at.taps = at.mix_output + chunks(width)
    at.small = at.taps + 2 * taps
    at.late = at.mix_inputs = whole(at.small + 32 * 5)
    at.last = at.late + chunks(mix_width) // unit * unit
    at.first = at.mix_inputs + chunks(mix_width)
    at.small_late = at.first + ff
    at.table = at.small_late + 16 * 5
    at.rows = at.late + whole(at.table + 16 - at.late)
    return at


MESH = pl.DeviceIdType.MESH


def meet(peers):
    barrier = pltpu.get_barrier_semaphore()
    for peer in peers:
        pl.semaphore_signal(barrier, inc=1, device_id=peer, device_id_type=MESH)
    pl.semaphore_wait(barrier, len(peers))


def head_peers(n):
    me = lax.axis_index("head")
    return me, [{"head": lax.rem(me + s, n)} for s in range(1, n)], [lax.rem(me + s, n) for s in range(1, n)]


def opening_kernel(frames_ref, len_ref, up_ref, down_ref, mix_ref, *refs, packed_rows, n):
    count = len(VEC.__dict__)
    vec_refs, refs = refs[:count], refs[count:]
    (cot_ref, x1_ref, h2_ref, cols_ref, bound_ref, plan_ref, ext_ref, all_ref, x1l_ref, x1r_ref, cotl_ref, cotr_ref,
     qkv, line, send, recv, local, hsend, hrecv) = refs
    me, peers, ids = head_peers(n)
    rows = cot_ref.shape[1]
    barrier = pltpu.get_barrier_semaphore()
    for peer in peers:
        pl.semaphore_signal(barrier, inc=1, device_id=peer, device_id_type=MESH)
    vecs = [ref[...].astype(F32).reshape(1, ref.shape[0]) for ref in vec_refs]
    cols_ref[...] = stack_rows(vecs, (VEC_ROWS, up_ref.shape[1])).T
    pl.semaphore_wait(barrier, len(peers))

    def piece(c, s):
        at = pl.ds(pl.multiple_of(c * PIECE, PIECE), PIECE)
        return pltpu.make_async_remote_copy(src_ref=qkv.at[ids[s], :, at], dst_ref=all_ref.at[me, :, at], send_sem=send.at[c, s],
                                            recv_sem=recv.at[c, s], device_id=peers[s], device_id_type=MESH)

    def ship(c):
        for s in range(n - 1):
            piece(c, s).start()

    open_rows(frames_ref, up_ref, down_ref, mix_ref, x1_ref, h2_ref, qkv, cols_ref, packed_rows, ship)
    own = pltpu.make_async_copy(qkv.at[me], all_ref.at[me], local)
    own.start()

    def edge(i, src, dst, head):
        return pltpu.make_async_remote_copy(src_ref=src, dst_ref=dst, send_sem=hsend.at[i], recv_sem=hrecv.at[i],
                                            device_id={"head": head}, device_id_type=MESH)

    up = lax.rem(me + 1, n)
    down = lax.rem(me + n - 1, n)
    last, start = pl.ds(rows - TILE, TILE), pl.ds(0, TILE)
    to_right = [edge(0, x1_ref.at[:, last], x1l_ref, up), edge(1, cot_ref.at[:, last], cotl_ref, up)]
    to_left = [edge(2, x1_ref.at[:, start], x1r_ref, down), edge(3, cot_ref.at[:, start], cotr_ref, down)]

    @pl.when(me < n - 1)
    def _():
        for c in to_right:
            c.start()

    @pl.when(me > 0)
    def _():
        for c in to_left:
            c.start()

    open_segments(len_ref, bound_ref, plan_ref, ext_ref, line)
    own.wait()

    @pl.loop(0, rows // PIECE)
    def _(c):
        for s in range(n - 1):
            piece(c, s).wait()

    @pl.when(me < n - 1)
    def _():
        for c in to_right:
            c.wait_send()
        for c in to_left:
            c.wait_recv()

    @pl.when(me > 0)
    def _():
        for c in to_left:
            c.wait_send()
        for c in to_right:
            c.wait_recv()


def everyone(n_tm, n_head):
    me = lax.axis_index("tm") * n_head + lax.axis_index("head")

    def for_all(act):
        for step in [s for i in range(1, n_head // 2 + 1) for s in {n_head - i, i}] + [0]:
            pl.loop(0 if step else 1, n_tm)(functools.partial(act, step))

    def place(along_head, along_tm):
        return {"tm": lax.rem(lax.axis_index("tm") + along_tm, n_tm), "head": lax.rem(lax.axis_index("head") + along_head, n_head)}

    return me, for_all, place


def tell(src_ref, all_ref, send, recv, n_tm, n_head):
    me, for_all, place = everyone(n_tm, n_head)

    def copy(h, t):
        return pltpu.make_async_remote_copy(src_ref=src_ref, dst_ref=all_ref.at[me], send_sem=send.at[h, t], recv_sem=recv.at[h, t],
                                            device_id=place(h, t), device_id_type=MESH)

    def start():
        for_all(lambda h, t: copy(h, t).start())
        all_ref[me] = src_ref[...]

    def end():
        for_all(lambda h, t: copy(h, t).wait())

    return start, end


def load_all(sources, targets, sems):
    copies = [pltpu.make_async_copy(src, dst, sems.at[i]) for i, (src, dst) in enumerate(zip(sources, targets))]
    for copy in copies:
        copy.start()
    return copies


def middle_kernel(*refs, n_tm, n_head, head_width, slot_count, layout):
    o_ref, o_tail, sources, refs = refs[0], refs[1], refs[2:16], refs[16:]
    (out_ref, dx2_ref, do_all, do_tails, pack_ref), refs = refs[:5], refs[5:]
    loaded, refs = refs[:14], refs[14:]
    (x1_ref, x1l_ref, x1r_ref, cot_ref, cotl_ref, cotr_ref, cols_ref, ext_ref, mixo_ref, pwi_ref, taps_ref, pwo_ref, up_ref,
     down_ref) = loaded
    (o_own, x2, oc, u, y, stat, stats, dx3, e, sums, all_sums, do, wide, mask, live,
     h4s, das, s4s, dfs, ws, dcs, dyw, du, prod, h3s, dgs, dms, gains2, smalld, smalle, tapg,
     n3, inv3, value3, gate3, tail_own, tail_wide, tail), refs = refs[:38], refs[38:]
    (load_sems, send_o, recv_o, local_o, send_a, recv_a, send_b, recv_b, send_d, recv_d, local_d) = refs
    me, peers, ids = head_peers(n_head)
    _, for_all, place = everyone(n_tm, n_head)
    barrier = pltpu.get_barrier_semaphore()
    rows = x1_ref.shape[1]
    for_all(lambda h, t: pl.semaphore_signal(barrier, inc=1, device_id=place(h, t), device_id_type=MESH))
    loads = load_all(sources, loaded, load_sems)
    pl.semaphore_wait(barrier, n_tm * n_head - 1)

    def parts(p):
        first = pl.multiple_of(p * rows, TILE)
        mine = o_own.at[me]
        low, high = pl.ds(0, MAIN), pl.ds(MAIN, SLOT - MAIN)
        left, right = pl.ds(0, TILE), pl.ds(rows + TILE, TILE)
        return (
            (o_ref.at[low, pl.ds(first, rows + 2 * TILE)], mine.at[low]),
            (o_tail.at[p], tail_own.at[me]),
            (o_ref.at[high, pl.ds(first, TILE)], mine.at[high, left]),
            (o_ref.at[high, pl.ds(pl.multiple_of(first + rows + TILE, TILE), TILE)], mine.at[high, right]),
        )

    copies = [
        pltpu.make_async_remote_copy(src_ref=src, dst_ref=dst, send_sem=send_o.at[s, i], recv_sem=recv_o.at[s, i],
                                     device_id=peer, device_id_type=MESH)
        for s, (peer, p) in enumerate(zip(peers, ids)) for i, (src, dst) in enumerate(parts(p))
    ]
    for copy in copies:
        copy.start()
    own = [pltpu.make_async_copy(src, dst, local_o.at[i]) for i, (src, dst) in enumerate(parts(me))]
    for copy in own:
        copy.start()
    for load in loads:
        load.wait()

    def arrive():
        for copy in own + copies:
            copy.wait()

    filter_kernel(x1_ref, x1l_ref, x1r_ref, o_own, tail_own, cols_ref, ext_ref, mixo_ref, pwi_ref, taps_ref, x2, oc, u, y, stat, wide, mask, live,
                  h3s, n3, inv3, value3, gate3, head_width=head_width, slot_count=slot_count, arrive=arrive)
    stats_out, stats_in = tell(stat, stats, send_a, recv_a, n_tm, n_head)
    sums_out, sums_in = tell(sums, all_sums, send_b, recv_b, n_tm, n_head)
    stats_out()
    second_kernel(x2, y, stats, cot_ref, cotl_ref, cotr_ref, cols_ref, pwo_ref, up_ref, down_ref,
                  out_ref, dx3, e, sums, pack_ref, smalld, h4s, das, s4s, dfs, ws, dcs, arrive=stats_in, leave=sums_out)

    def piece(c, s):
        at = pl.ds(pl.multiple_of(c * PART, PART), PART)
        return pltpu.make_async_remote_copy(src_ref=do.at[ids[s], :, at], dst_ref=do_all.at[me, :, at], send_sem=send_d.at[c, s],
                                            recv_sem=recv_d.at[c, s], device_id=peers[s], device_id_type=MESH)

    def ending(s):
        return pltpu.make_async_remote_copy(src_ref=tail.at[ids[s]], dst_ref=do_tails.at[me], send_sem=send_d.at[rows // PART, s],
                                            recv_sem=recv_d.at[rows // PART, s], device_id=peers[s], device_id_type=MESH)

    def ship(c):
        if isinstance(c, int):
            for h in range(n_head):
                tail[h] = fold_rows(tail_wide[4 * h : 4 * h + 4, :], 4).astype(BF)
        for s in range(n_head - 1):
            (ending(s) if isinstance(c, int) else piece(c, s)).start()

    unfilter_kernel(e, y, stats, all_sums, u, dx3, oc, cols_ref, ext_ref, pwi_ref, taps_ref, mixo_ref,
                    dx2_ref, do, pack_ref.at[pl.ds(layout.pointwise_in, layout.taps - layout.pointwise_in)], smalle, tapg, dyw, du, mask, prod, h3s, dgs, dms, gains2, live, n3, inv3, value3, gate3, tail_wide,
                    head_width=head_width, ship=ship, arrive=sums_in)
    own = [pltpu.make_async_copy(do.at[me], do_all.at[me], local_d.at[0]), pltpu.make_async_copy(tail.at[me], do_tails.at[me], local_d.at[1])]
    for copy in own:
        copy.start()
    end = put_taps(pack_ref, tapg[...], layout.taps)
    end = put_small(pack_ref, jnp.concatenate([smalld[...], smalle[...]], axis=0), end)
    if end < pack_ref.shape[0]:
        pack_ref[end:, :] = jnp.zeros((pack_ref.shape[0] - end, TILE), BF)
    for copy in own:
        copy.wait()
    for s in range(n_head - 1):
        ending(s).wait()

    @pl.loop(0, rows // PART)
    def _(c):
        for s in range(n_head - 1):
            piece(c, s).wait()


def sum_scratch(count, n_tm, n_head):
    half = count // 2
    big = half // (n_tm // 2)
    shapes = [(half, TILE), (half, TILE), (n_tm // 2, big, TILE), (big, TILE), (n_head, big // n_head, TILE), (big, TILE), (half, TILE)]
    return [pltpu.VMEM(shape, BF) for shape in shapes]


def gradient_sum(src_ref, out_ref, first, scratch, sems, local, n_tm, n_head):
    got0, half, got1, part1, got2, part2, whole = scratch
    tm, head = lax.axis_index("tm"), lax.axis_index("head")
    n_chip = n_tm // 2
    chip, core = tm // 2, lax.rem(tm, 2)
    size = src_ref.shape[0] // 2
    big = size // n_chip
    small = big // n_head
    sibling = {"tm": chip * 2 + 1 - core}

    def rows(i, count, base=0):
        return pl.ds(pl.multiple_of(base + i * count, 16), count)

    def send(src, dst, phase, s, peer):
        return pltpu.make_async_remote_copy(src_ref=src, dst_ref=dst, send_sem=sems.at[2 * phase, s], recv_sem=sems.at[2 * phase + 1, s],
                                            device_id=peer, device_id_type=MESH)

    def chip_peer(s):
        return lax.rem(chip + s, n_chip)

    def head_peer(s):
        return lax.rem(head + s, n_head)

    def zero():
        return send(src_ref.at[rows(1 - core, size)], got0, 0, 0, sibling)

    def one(s):
        return send(half.at[rows(chip_peer(s), big)], got1.at[s], 1, s, {"tm": chip_peer(s) * 2 + core})

    def two(s):
        return send(part1.at[rows(head_peer(s), small)], got2.at[s], 2, s, {"head": head_peer(s)})

    def three(s):
        at = part2.at[rows(head, small)]
        return send(at, at, 3, s, {"head": head_peer(s)})

    def four(s):
        return send(part2, whole.at[rows(chip, big)], 4, s, {"tm": chip_peer(s) * 2 + core})

    def five():
        return send(whole, out_ref.at[rows(core, size, first)], 5, 0, sibling)

    def keep():
        return pltpu.make_async_copy(whole, out_ref.at[rows(core, size, first)], local)

    def added(got, n):
        total = got[0].astype(F32)
        for s in range(1, n):
            total = total + got[s].astype(F32)
        return total.astype(BF)

    def step0():
        zero().start()

    def step1():
        zero().wait()
        half[...] = (src_ref[rows(core, size), :].astype(F32) + got0[...].astype(F32)).astype(BF)
        pl.loop(1, n_chip)(lambda s: one(s).start())
        got1[0] = half[rows(chip, big), :]

    def step2():
        pl.loop(1, n_chip)(lambda s: one(s).wait())
        part1[...] = added(got1, n_chip)
        pl.loop(1, n_head)(lambda s: two(s).start())
        got2[0] = part1[rows(head, small), :]

    def step3():
        pl.loop(1, n_head)(lambda s: two(s).wait())
        part2[rows(head, small), :] = added(got2, n_head)
        pl.loop(1, n_head)(lambda s: three(s).start())

    def step4():
        pl.loop(1, n_head)(lambda s: three(s).wait())
        pl.loop(1, n_chip)(lambda s: four(s).start())
        whole[rows(chip, big), :] = part2[...]

    def step5():
        pl.loop(1, n_chip)(lambda s: four(s).wait())
        five().start()
        keep().start()

    def step6():
        keep().wait()
        five().wait()

    return step0, step1, step2, step3, step4, step5, step6


def return_kernel(src_ref, dst_ref, send, recv, *, n):
    me, peers, ids = head_peers(n)
    meet(peers)
    copies = [
        pltpu.make_async_remote_copy(src_ref=src_ref.at[p], dst_ref=dst_ref.at[me], send_sem=send.at[s], recv_sem=recv.at[s],
                                     device_id=peer, device_id_type=MESH)
        for s, (peer, p) in enumerate(zip(peers, ids))
    ]
    for copy in copies:
        copy.start()
    for copy in copies:
        copy.wait()


def final_kernel(*refs, n_tm, n_head, parts):
    dqkv_ref, others_ref, sources, refs = refs[0], refs[1], refs[2:12], refs[12:]
    (grad_ref, total_ref), loaded, refs = refs[:2], refs[2:12], refs[12:]
    early_ref, frames_ref, x1_ref, h2_ref, dx2_ref, dtab_ref, cols_ref, up_ref, down_ref, mix_ref = loaded
    (dqkv, late, h1s, das, s1s, dfs, dqs, gains), refs = refs[:8], refs[8:]
    sum_refs = [refs[7 * i : 7 * i + 7] for i in range(3)]
    load_sems, load_q, sum_sems, sum_local = refs[21:]
    me, peers, ids = head_peers(n_head)
    tm = lax.axis_index("tm")
    rows = x1_ref.shape[1]
    barrier = pltpu.get_barrier_semaphore()
    for peer in peers:
        pl.semaphore_signal(barrier, inc=1, device_id=peer, device_id_type=MESH)

    @pl.loop(1, n_tm)
    def _(s):
        pl.semaphore_signal(barrier, inc=1, device_id={"tm": lax.rem(tm + s, n_tm)}, device_id_type=MESH)

    loads = load_all(sources, loaded, load_sems)
    own = pltpu.make_async_copy(dqkv_ref.at[me], dqkv.at[me], load_q.at[0])
    loads += [own] + [pltpu.make_async_copy(others_ref.at[p], dqkv.at[p], load_q.at[1 + s]) for s, p in enumerate(ids)]
    for load in loads[-n_head:]:
        load.start()
    pl.semaphore_wait(barrier, n_head + n_tm - 2)

    for load in loads:
        load.wait()
    late_at, last_at, end = parts

    def summed(i, src, first):
        return gradient_sum(src, total_ref, first, sum_refs[i], sum_sems.at[i], sum_local.at[i], n_tm, n_head)

    early = summed(0, early_ref, 0)
    last = summed(2, late.at[pl.ds(last_at - late_at, end - last_at)], last_at)
    late_sum = summed(1, late.at[pl.ds(0, last_at - late_at)], late_at) if last_at > late_at else [lambda: None] * 7
    early[0]()
    early[1]()

    def mixed():
        late_sum[0]()

    close_kernel(frames_ref, x1_ref, h2_ref, dx2_ref, dqkv, dtab_ref, cols_ref, up_ref, down_ref, mix_ref,
                 grad_ref, late, h1s, das, s1s, dfs, dqs, gains, mixed=mixed)
    for step in (last[0], late_sum[1], last[1], early[2], late_sum[2], last[2], early[3], late_sum[3], last[3], early[4], late_sum[4],
                 last[4], early[5], late_sum[5], last[5], early[6], late_sum[6], last[6]):
        step()


VMEM_MIB = 62


def body(
    frames, lengths, first_gain, first_shift, first_up, first_up_bias, first_down, first_down_bias, mix_gain, mix_shift,
    mix_inputs, position_bias, mix_output, mix_output_bias, filter_gain, filter_shift, pointwise_in, pointwise_in_bias,
    depthwise_taps, batch_gain, batch_shift, pointwise_out, pointwise_out_bias, second_gain, second_shift, second_up,
    second_up_bias, second_down, second_down_bias, final_gain, final_shift, cotangent,
):
    weights = Weights(
        first_gain, first_shift, first_up, first_up_bias, first_down, first_down_bias, mix_gain, mix_shift, mix_inputs, position_bias,
        mix_output, mix_output_bias, filter_gain, filter_shift, pointwise_in, pointwise_in_bias, depthwise_taps, batch_gain,
        batch_shift, pointwise_out, pointwise_out_bias, second_gain, second_shift, second_up, second_up_bias, second_down,
        second_down_bias, final_gain, final_shift)
    rows, width = frames.shape
    hidden = first_up.shape[1]
    n_head, n_tm = lax.axis_size("head"), lax.axis_size("tm")
    heads, span = position_bias.shape
    head_width = width // heads
    packed_rows = -(-3 * head_width // 16) * 16
    group = rows * n_head
    lanes = rows + TILE
    slots = lengths.shape[1]
    taps = depthwise_taps.shape[0]
    layout = pack_layout(width, hidden, mix_inputs.shape[1], taps, n_tm * n_head)

    vectors = tuple(getattr(weights, name) for name in VEC.__dict__)
    frames_t, cot_t, first_down_t, second_down_t = frames.T, cotangent.T, first_down.T, second_down.T
    vm, dma, hbm = pltpu.VMEM, pltpu.SemaphoreType.DMA, pl.BlockSpec(memory_space=pl.ANY)
    steps = rows // PIECE
    piece_sems = dma((steps, n_head - 1))

    def comm_call(kernel, name, collective_id, ins, in_hbm, outs, out_hbm, scratch):
        return pl.pallas_call(
            kernel,
            out_shape=tuple(jax.ShapeDtypeStruct(s, t) for s, t in outs),
            in_specs=[hbm if i in in_hbm else pl.BlockSpec() for i in range(len(ins))],
            out_specs=tuple(hbm if i in out_hbm else pl.BlockSpec() for i in range(len(outs))),
            scratch_shapes=scratch,
            compiler_params=pltpu.CompilerParams(collective_id=collective_id, has_side_effects=True, vmem_limit_bytes=VMEM_MIB * 2**20),
            name=name,
        )(*ins)

    ins = (frames_t, lengths, first_up, first_down_t, mix_inputs) + vectors + (cot_t,)
    x1, h2, cols, bounds, plan, ext, qkv_all, x1l, x1r, cotl, cotr = comm_call(
        functools.partial(opening_kernel, packed_rows=packed_rows, n=n_head), "opening", 1, ins, (len(ins) - 1,),
        [((width, rows), F32), ((width, rows), BF), ((hidden, VEC_ROWS), F32), ((2, group + 2 * PAD), jnp.int32),
         ((group // BLK, 128), jnp.int32), ((1, lanes), jnp.int32), ((n_head, packed_rows, rows), BF),
         ((width, TILE), F32), ((width, TILE), F32), ((width, TILE), BF), ((width, TILE), BF)], range(6, 11),
        [vm((n_head, packed_rows, rows), BF), vm((1, group + 2 * TILE), jnp.int32), piece_sems, piece_sems, dma, dma((4,)), dma((4,))])
    o, o_tail, of, lse = attend_forward(qkv_all, bounds, plan, position_bias, head_width)
    everyone_sems = dma((n_head, n_tm))
    ins = (x1, x1l, x1r, cot_t, cotl, cotr, cols, ext, mix_output, pointwise_in, depthwise_taps, pointwise_out, second_up, second_down_t)
    out, dx2, do_all, do_tails, pack = comm_call(
        functools.partial(middle_kernel, n_tm=n_tm, n_head=n_head, head_width=head_width, slot_count=slots, layout=layout),
        "middle", 2, (o, o_tail) + ins, range(len(ins) + 2),
        [((width, rows), BF), ((width, rows), F32), ((n_head, MAIN, rows), BF), ((n_head, 16, rows // 4), BF), ((layout.late, TILE), BF)],
        (2, 3),
        [vm(a.shape, a.dtype) for a in ins] + [
            vm((n_head, SLOT, rows + 2 * TILE), BF), vm((width, lanes), F32), vm((width + 16, rows), BF), vm((width, lanes), BF),
            vm((width, lanes), F32), vm((4, TILE), F32), vm((n_tm * n_head, 4, TILE), F32), vm((width, rows), F32),
            vm((width, lanes), F32), vm((4, TILE), F32), vm((n_tm * n_head, 4, TILE), F32), vm((n_head, MAIN, rows), BF),
            vm((width, lanes), F32), vm((taps + 1, 8, lanes), F32), vm((1, lanes), F32),
            vm((width, rows), BF), vm((hidden, rows), BF), vm((hidden + 16, rows), BF), vm((width, rows), BF),
            vm((width + 16, rows), BF), vm((width, rows), BF),
            vm((width, lanes), F32), vm((width, rows), F32), vm((taps, width, TILE), F32), vm((width + 16, rows), BF),
            vm((2 * width, rows), BF), vm((width, rows), BF), vm((2, width, TILE), F32),
            vm((16, 5 * TILE), F32), vm((16, 5 * TILE), F32), vm((taps, width), F32),
            vm((width, rows), F32), vm((1, rows), F32), vm((width, rows), F32), vm((width, rows), F32),
            vm((n_head, 16, rows // 4), BF), vm((4 * n_head, rows), F32), vm((n_head, 16, rows // 4), BF),
            dma((len(ins),)), dma((n_head - 1, 4)), dma((n_head - 1, 4)), dma((4,)), everyone_sems, everyone_sems, everyone_sems, everyone_sems,
            dma((rows // PART + 1, n_head - 1)), dma((rows // PART + 1, n_head - 1)), dma((2,)),
        ])
    dqkv, dtab = attend_backward(qkv_all, do_all, do_tails, of, lse, bounds, plan, position_bias, head_width)
    (others,) = comm_call(functools.partial(return_kernel, n=n_head), "return_gradients", 4, (dqkv,), (0,),
                          [(dqkv.shape, BF)], (0,), [dma((n_head - 1,)), dma((n_head - 1,))])
    parts = (layout.late, layout.last, layout.rows)
    sizes = (layout.late, max(layout.last - layout.late, 16 * n_tm * n_head), layout.rows - layout.last)
    ins = (pack, frames_t, x1, h2, dx2, dtab, cols, first_up, first_down_t, mix_inputs)
    grad, total = comm_call(
        functools.partial(final_kernel, n_tm=n_tm, n_head=n_head, parts=parts), "final", 3, (dqkv, others) + ins, range(len(ins) + 2),
        [((width, rows), F32), ((layout.rows, TILE), BF)], (1,),
        [vm(a.shape, a.dtype) for a in ins] + [
            vm((n_head, packed_rows, rows), BF), vm((layout.rows - layout.late, TILE), BF),
            vm((width, rows), BF), vm((hidden, rows), BF), vm((hidden, rows), BF), vm((width, rows), BF),
            vm((n_head * packed_rows, rows), BF), vm((4, width, TILE), F32),
            *[s for size in sizes for s in sum_scratch(size, n_tm, n_head)],
            dma((len(ins),)), dma((n_head,)), dma((3, 12, max(n_tm // 2, n_head))), dma((3,)),
        ])
    shapes = Weights(**{n: w.shape for n, w in weights.__dict__.items()})
    shapes.first_down = shapes.second_down = first_down_t.shape
    results = [((width, rows), BF), ((width, rows), F32)] + [(s, F32) for s in shapes.__dict__.values()]
    out, grad, *summed = pl.pallas_call(
        functools.partial(unpack_kernel, layout=layout),
        out_shape=tuple(jax.ShapeDtypeStruct(s, t) for s, t in results),
        compiler_params=pltpu.CompilerParams(vmem_limit_bytes=VMEM_MIB * 2**20),
        name="unpack",
    )(total, out, grad)
    summed = Weights(*summed)
    summed.first_down, summed.second_down = summed.first_down.T, summed.second_down.T
    return (out.T, grad.T) + tuple(summed.__dict__.values())


def solution(mesh):
    rows = P(("tm", "head"), None)
    placed = (rows, P("tm", None)) + (P(),) * 29 + (rows,)
    return jax.shard_map(body, mesh=mesh, in_specs=placed, out_specs=(rows, rows) + (P(),) * 29, check_vma=False)
```

```python
import dataclasses
import functools
import math
import types

import jax
import jax.numpy as jnp
from jax import lax
from jax.experimental import pallas as pl
from jax.experimental.pallas import tpu as pltpu
from jax.sharding import PartitionSpec as P

BF = jnp.bfloat16
F32 = jnp.float32
LOG2E = math.log2(math.e)
BLK = 512
UNIT = 128
PER = BLK // UNIT
NEAR = PER + 2
PAD = 8 * UNIT
SLOT = 48
MAIN = 32
DEPTH = 128
MASKED = -1e30
GANG = 4
NN = (((1,), (0,)), ((), ()))
NT = (((1,), (1,)), ((), ()))
TN = (((0,), (0,)), ((), ()))


def dot(a, b, dims=NN):
    return lax.dot_general(a, b, dims, preferred_element_type=F32)


def iota(shape, dim):
    return lax.broadcasted_iota(jnp.int32, shape, dim)


def spread_cols(width, slots, slot_rows, used):
    row, column = iota((slots * slot_rows, width), 0), iota((slots * slot_rows, width), 1)
    hit = jnp.zeros((slots * slot_rows, width), jnp.bool_)
    for s in range(slots):
        f = row - slot_rows * s
        hit = hit | ((f >= 0) & (f < used) & (column == used * s + f))
    return hit.astype(F32).astype(BF)


def split3(v):
    hi = v.astype(BF).astype(F32)
    r1 = v - hi
    mid = r1.astype(BF).astype(F32)
    return hi, mid, r1 - mid


def three_rows(v, rows):
    a, b, e = split3(v)
    row = iota((rows, v.shape[1]), 0)
    return jnp.where(row == 0, a, jnp.where(row == 1, b, jnp.where(row == 2, e, 0.0)))


def pick_row(ref, index):
    values = ref[...].astype(F32)
    return jnp.sum(jnp.where(iota(values.shape, 0) == index, values, 0.0), axis=0, keepdims=True)


def bias_square(table, d):
    span = table.shape[1]
    half = span // 2
    lanes = 2 * UNIT
    u = iota((span, lanes), 1)
    u = jnp.where(u < UNIT, u, u - lanes)
    ids = jnp.clip(-UNIT * d - u, -half, half - 1) + half
    hot = (ids == iota((span, lanes), 0)).astype(F32).astype(BF)
    line = dot(jnp.broadcast_to(table, (UNIT, span)).astype(BF), hot) * LOG2E
    return pltpu.roll(line, 0, 1, stride=1, stride_axis=0)[:, :UNIT]


def bias_near(table, tile, keys_near):
    span = table.shape[1]
    squares = {d: bias_square(table, d) for d in (-1, 0, 1)}
    low = jnp.broadcast_to(table[:, :1] * LOG2E, (UNIT, UNIT))
    high = jnp.broadcast_to(table[:, span - 1 :] * LOG2E, (UNIT, UNIT))
    for r in range(tile.shape[0] // UNIT):
        for c in range(tile.shape[1] // UNIT):
            d = c - (r - 1) if keys_near else (c - 1) - r
            part = squares[d] if abs(d) < 2 else (low if d > 0 else high)
            tile[r * UNIT : (r + 1) * UNIT, c * UNIT : (c + 1) * UNIT] = part


def units_at(u, count):
    return pl.ds(pl.multiple_of(u * UNIT, UNIT), count * UNIT)


def far_windows(low, plain, edge, step, side, up, fine):
    sign = 1 if up else -1

    def run(at, times, size, masked):
        def one(i, carry):
            near = at + sign * i * size
            step(near if up else near - size, size, side, masked)
            return carry

        lax.fori_loop(0, times, one, 0)
        return at + sign * times * size

    at = edge if plain is None else run(edge, sign * (plain - edge) // 8, 8, False)
    left = sign * (low - at)
    tail = lax.rem(left, 8)
    more = tail > (6 if fine else 4)
    at = run(at, left // 8 + more.astype(jnp.int32), 8, True)
    tail = jnp.where(more, 0, tail)
    four = tail > (2 if fine else 0)
    at = run(at, four.astype(jnp.int32), 4, True)
    if fine:
        run(at, (tail - jnp.where(four, 4, 0) > 0).astype(jnp.int32), 2, True)


def far_sweep(plan, block, step, before, after, fine):
    low, plain_low, plain_high, high, low_half, high_half = [plan[block, i] for i in range(6)]
    start, stop = PER * block - 1, PER * block + PER + 1
    for whole, part in ((True, None), (False, 0)):
        @pl.when((low_half == 0) if whole else (low_half != 0))
        def _():
            far_windows(low, plain_low if whole else None, start, functools.partial(step, part=part), before, False, fine)

    for whole, part in ((True, None), (False, 1)):
        @pl.when((high_half == 0) if whole else (high_half != 0))
        def _():
            far_windows(high, plain_high if whole else None, stop, functools.partial(step, part=part), after, True, fine)


def fold_rows(four, pieces):
    size = four.shape[1] // pieces
    return jnp.concatenate([four[:, i * size : (i + 1) * size] for i in range(pieces)], axis=0)


def unfold_rows(folded):
    return jnp.concatenate([folded[i : i + 4, :] for i in range(0, folded.shape[0], 4)], axis=1)


def part_at(block, part):
    if part is None:
        return units_at(PER * block, PER)
    return units_at(PER * block + part * (PER // 2), PER // 2)


def has_far(plan, block):
    return (plan[block, 0] < PER * block - 1) | (plan[block, 3] > PER * block + PER + 1)


def segment_rows(ends, lengths, place, total):
    slots = ends.shape[0]
    before = ends <= jnp.broadcast_to(place, (slots, place.shape[1]))
    seg = jnp.sum(before.astype(jnp.int32), axis=0, keepdims=True)
    first = jnp.sum(jnp.where(before, lengths, 0), axis=0, keepdims=True)
    stop = jnp.min(jnp.where(before, total, ends), axis=0, keepdims=True)
    return seg, first, stop


def block_plan(ends, ends_row, total):
    slots = ends.shape[0]
    blocks, units = total // BLK, total // UNIT

    def along(place):
        return jnp.sum((ends <= jnp.broadcast_to(place, (slots, 128))).astype(jnp.int32), axis=0, keepdims=True)

    def down(place):
        return jnp.sum((jnp.broadcast_to(ends_row, (blocks, slots)) <= place).astype(F32), axis=1, keepdims=True).astype(jnp.int32)

    unit = iota((1, 128), 1)
    u_first, u_last = along(unit * UNIT), along(unit * UNIT + UNIT - 1)
    b = iota((blocks, 1), 0)
    first, last = down(b * BLK), down(b * BLK + BLK - 1)
    low_half = (down(b * BLK + BLK // 2) != first).astype(jnp.int32)
    high_half = (down(b * BLK + BLK // 2 - 1) != last).astype(jnp.int32)
    start, stop = PER * b - 1, PER * b + PER + 1
    inside = unit < units

    def count(hit):
        return jnp.sum((hit & inside).astype(F32), axis=1, keepdims=True).astype(jnp.int32)

    low = jnp.minimum(count(u_last < first), start)
    high = jnp.maximum(units - count(u_first > last), stop)
    plain_low = start - count((unit < start) & (u_first == last))
    plain_high = stop + count((unit >= stop) & (u_last == first))
    lane = iota((blocks, 128), 1)
    out = jnp.zeros((blocks, 128), jnp.int32)
    for i, v in enumerate((low, plain_low, plain_high, high, low_half, high_half)):
        out = jnp.where(lane == i, v, out)
    return out


def meets(first_key, rows, bounds):
    key = iota((rows, bounds.shape[1]), 0)
    return (key >= bounds[0:1, :] - first_key) & (key < bounds[1:2, :] - first_key)


def fwd_kernel(plan, qkv_ref, table_ref, bound_ref, o_ref, tail_ref, of_ref, lse_ref, qaug, kn, vt, tile, top_ref, acc, *, head_width):
    chunks, packed_rows, rows = qkv_ref.shape
    total = chunks * rows
    blocks = total // BLK
    span = table_ref.shape[1]
    table = pick_row(table_ref, lax.axis_index("head"))
    far = (table[:, :1] * LOG2E, table[:, span - 1 :] * LOG2E)
    pick = spread_cols(packed_rows, 3, SLOT, head_width)
    scale = LOG2E / math.sqrt(head_width)
    o_ref[:, :UNIT] = jnp.zeros((SLOT, UNIT), BF)
    o_ref[:, UNIT + total :] = jnp.zeros((SLOT, UNIT), BF)
    for edge in (slice(0, PAD), slice(PAD + total, 2 * PAD + total)):
        kn[edge, :] = jnp.zeros((PAD, DEPTH), BF)
        vt[:, edge] = jnp.zeros((SLOT, PAD), BF)
    bias_near(table, tile, True)
    rest = DEPTH - 2 * SLOT

    @pl.loop(0, chunks)
    def _(c):
        at = pl.ds(pl.multiple_of(c * rows, rows), rows)
        at_pad = pl.ds(pl.multiple_of(c * rows + PAD, UNIT), rows)
        parts = dot(pick, qkv_ref[c])
        q = parts[:SLOT] * scale
        hi = q.astype(BF)
        lo = (q - hi.astype(F32)).astype(BF)
        for s in range(3):
            qaug[s, :SLOT, at] = hi
            qaug[s, SLOT : 2 * SLOT, at] = lo
            qaug[s, 2 * SLOT :, at] = jnp.zeros((rest, rows), BF)
        k = parts[SLOT : 2 * SLOT]
        one3 = (iota((rest, rows), 0) < 3).astype(F32)
        kn[at_pad, :] = jnp.concatenate([k, k, one3], axis=0).T.astype(BF)
        one = (iota((SLOT, rows), 0) == head_width).astype(F32)
        vt[:, at_pad] = (parts[2 * SLOT :] + one).astype(BF)

    def top(x):
        return jnp.max(x.reshape(x.shape[0] // 8, 8, BLK), axis=0)

    @pl.loop(0, blocks // GANG)
    def _(pair):
        blocks_now = [GANG * pair + i for i in range(GANG)]
        at_q = [units_at(PER * b, PER) for b in blocks_now]
        near = [units_at(PER * b - 1 + PAD // UNIT, NEAR) for b in blocks_now]
        x = [dot(kn[n, :], qaug[1, :, q]) + tile[...] for n, q in zip(near, at_q)]
        x = [
            jnp.where(meets(PER * b * UNIT - UNIT, NEAR * UNIT, bound_ref[:, units_at(PER * b + PAD // UNIT, PER)]), v, MASKED)
            for b, v in zip(blocks_now, x)
        ]
        m = [jnp.max(top(v), axis=0, keepdims=True) for v in x]
        p = [jnp.exp2(v - w).astype(BF) for v, w in zip(x, m)]
        out = [dot(vt[:, n], v) for n, v in zip(near, p)]
        for q, w, v in zip(at_q, m, out):
            acc[:, q] = v
            lse_ref[:, q] = w
            qaug[0, 2 * SLOT :, q] = three_rows(far[0] - w, rest).astype(BF)
            qaug[2, 2 * SLOT :, q] = three_rows(far[1] - w, rest).astype(BF)

    @pl.loop(0, blocks)
    def _(b):
        @pl.when(has_far(plan, b))
        def _():
            at_q = units_at(PER * b, PER)

            def scores(u, count, side, masked, part):
                x = dot(kn[units_at(u + PAD // UNIT, count), :], qaug[side, :, part_at(b, part)])
                if masked:
                    x = jnp.where(meets(u * UNIT, count * UNIT, bound_ref[:, part_at(b + PAD // BLK, part)]), x, MASKED)
                return x

            near_acc = acc[:, at_q]

            def add(u, count, side, masked, part):
                p = jnp.exp2(scores(u, count, side, masked, part)).astype(BF)
                acc[:, part_at(b, part)] += dot(vt[:, units_at(u + PAD // UNIT, count)], p)

            far_sweep(plan, b, add, 0, 2, False)
            sums = acc[head_width : head_width + 1, at_q]
            over = jnp.max(jnp.where(sums < 2.0**60, 0.0, 1.0))

            @pl.when(over > 0.5)
            def _():
                top_ref[...] = jnp.zeros_like(top_ref)

                def half_of(part):
                    return slice(None) if part is None else slice(part * BLK // 2, (part + 1) * BLK // 2)

                def first(u, count, side, masked, part):
                    x = scores(u, count, side, masked, part)
                    best = jnp.max(x.reshape(x.shape[0] // 8, 8, x.shape[1]), axis=0)
                    top_ref[:, half_of(part)] = jnp.maximum(top_ref[:, half_of(part)], best)

                far_sweep(plan, b, first, 0, 2, False)
                m = jnp.max(top_ref[...], axis=0, keepdims=True)
                acc[:, at_q] = near_acc * jnp.exp2(-m)
                lse_ref[:, at_q] += m

                def second(u, count, side, masked, part):
                    p = jnp.exp2(scores(u, count, side, masked, part) - m[:, half_of(part)]).astype(BF)
                    acc[:, part_at(b, part)] += dot(vt[:, units_at(u + PAD // UNIT, count)], p)

                far_sweep(plan, b, second, 0, 2, False)

    @pl.loop(0, chunks)
    def _(c):
        at = pl.ds(pl.multiple_of(c * rows, rows), rows)
        total_p = acc[head_width : head_width + 1, at]
        out = acc[:, at] / total_p
        o_ref[:, pl.ds(pl.multiple_of(c * rows + UNIT, UNIT), rows)] = out.astype(BF)
        tail_ref[c] = fold_rows(out[MAIN : MAIN + 4], 4).astype(BF)
        of_ref[:, at] = out[: of_ref.shape[0]]
        lse_ref[:, at] = lse_ref[:, at] + jnp.log2(total_p)


def attend_forward(qkv, bounds, plan, table, head_width):
    chunks, packed_rows, rows = qkv.shape
    total = chunks * rows
    vm = pltpu.VMEM
    return pl.pallas_call(
        functools.partial(fwd_kernel, head_width=head_width),
        out_shape=(
            jax.ShapeDtypeStruct((SLOT, total + 2 * UNIT), BF),
            jax.ShapeDtypeStruct((chunks, 16, rows // 4), BF),
            jax.ShapeDtypeStruct((40, total), F32),
            jax.ShapeDtypeStruct((1, total), F32),
        ),
        in_specs=[pl.BlockSpec(memory_space=pltpu.SMEM)] + [pl.BlockSpec()] * 3,
        scratch_shapes=[
            vm((3, DEPTH, total), BF),
            vm((total + 2 * PAD, DEPTH), BF),
            vm((SLOT, total + 2 * PAD), BF),
            vm((NEAR * UNIT, BLK), F32),
            vm((8, BLK), F32),
            vm((SLOT, total), F32),
        ],
        compiler_params=pltpu.CompilerParams(vmem_limit_bytes=62 * 2**20),
        name="attend_forward",
    )(plan, qkv, table, bounds)


def bwd_kernel(plan, qkv_ref, do_ref, tail_ref, of_ref, lse_ref, table_ref, bound_ref, dqkv_ref, dtab_ref,
               qaug, kn, kt, vn, dot_t, qn, don, tile, dq, band, ends, dv_acc, dk_acc, *, head_width):
    chunks, packed_rows, rows = qkv_ref.shape
    total = chunks * rows
    blocks = total // BLK
    span = table_ref.shape[1]
    table = pick_row(table_ref, lax.axis_index("head"))
    pick = spread_cols(packed_rows, 3, SLOT, head_width)
    scale = LOG2E / math.sqrt(head_width)
    back = 1.0 / math.sqrt(head_width)
    rest = DEPTH - 2 * SLOT
    bias_near(table, tile, False)
    for edge in (slice(0, PAD), slice(PAD + total, 2 * PAD + total)):
        for s in range(3):
            qaug[s, :, edge] = jnp.zeros((DEPTH, PAD), BF)
        dot_t[:, edge] = jnp.zeros((DEPTH, PAD), BF)
        qn[edge, :] = jnp.zeros((PAD, DEPTH), BF)
        don[edge, :] = jnp.zeros((PAD, DEPTH), BF)

    @pl.loop(0, chunks)
    def _(c):
        at = pl.ds(pl.multiple_of(c * rows, rows), rows)
        at_pad = pl.ds(pl.multiple_of(c * rows + PAD, UNIT), rows)
        parts = dot(pick, qkv_ref[c])
        q, k, v = parts[:SLOT], parts[SLOT : 2 * SLOT], parts[2 * SLOT :]
        qs = q * scale
        hi = qs.astype(BF)
        lo = (qs - hi.astype(F32)).astype(BF)
        lse = lse_ref[:, at]
        for s, shift in enumerate((table[:, :1] * LOG2E, 0.0, table[:, span - 1 :] * LOG2E)):
            qaug[s, :SLOT, at_pad] = hi
            qaug[s, SLOT : 2 * SLOT, at_pad] = lo
            qaug[s, 2 * SLOT :, at_pad] = three_rows(shift - lse, rest).astype(BF)
        one3 = (iota((rest, rows), 0) < 3).astype(F32)
        row48 = iota((SLOT, rows), 0)
        none = jnp.zeros((rest, rows), F32)
        empty = jnp.zeros((SLOT, rows), F32)
        kn[at, :] = jnp.concatenate([k, k, one3], axis=0).T.astype(BF)
        kt[:, at] = k.astype(BF)
        vn[at, :] = jnp.concatenate([v, empty, one3], axis=0).T.astype(BF)
        tail = unfold_rows(tail_ref[c].astype(F32))
        do = jnp.concatenate([do_ref[c].astype(F32), tail, jnp.zeros((SLOT - MAIN - 4, rows), F32)], axis=0)
        centre = jnp.sum(do[: of_ref.shape[0]] * of_ref[:, at], axis=0, keepdims=True)
        dot_t[:SLOT, at_pad] = do.astype(BF)
        dot_t[SLOT : 2 * SLOT, at_pad] = empty.astype(BF)
        dot_t[2 * SLOT :, at_pad] = three_rows(-centre, rest).astype(BF)
        qn[at_pad, :] = jnp.concatenate([q + (row48 == head_width).astype(F32), empty, none], axis=0).T.astype(BF)
        don[at_pad, :] = jnp.concatenate([do, empty, none], axis=0).T.astype(BF)

    dq[...] = jnp.zeros_like(dq)
    band[...] = jnp.zeros_like(band)
    ends[...] = jnp.zeros_like(ends)

    @pl.loop(0, blocks // GANG)
    def _(pair):
        width = NEAR * UNIT
        wide = width + (GANG - 1) * BLK
        blocks_now = [GANG * pair + i for i in range(GANG)]
        at_k = [units_at(PER * b, PER) for b in blocks_now]
        near = [units_at(PER * b - 1 + PAD // UNIT, NEAR) for b in blocks_now]
        x = [dot(kn[k, :], qaug[1, :, n]) + tile[...] for k, n in zip(at_k, near)]
        dp = [dot(vn[k, :], dot_t[:, n]) for k, n in zip(at_k, near)]
        p = [jnp.where(meets(b * BLK, BLK, bound_ref[:, n]), jnp.exp2(v), 0.0) for b, n, v in zip(blocks_now, near, x)]
        dsb = [(v * w).astype(BF) for v, w in zip(p, dp)]
        dv = [dot(v.astype(BF), don[n, :]) for n, v in zip(near, p)]
        dk = [dot(v, qn[n, :]) for n, v in zip(near, dsb)]
        part = [dot(kt[:, k], v) for k, v in zip(at_k, dsb)]
        for k, v, w in zip(at_k, dv, dk):
            dv_acc[k, :] = v
            dk_acc[k, :] = w
        gap = [jnp.zeros((SLOT, BLK), F32)]
        whole = [jnp.concatenate(gap * i + [v] + gap * (GANG - 1 - i), axis=1) for i, v in enumerate(part)]
        lines = [v.astype(F32) for v in dsb]
        dq[:, units_at(GANG * PER * pair - 1 + PAD // UNIT, wide // UNIT)] += functools.reduce(jnp.add, whole)
        band[...] += functools.reduce(jnp.add, lines)

    @pl.loop(0, blocks)
    def _(b):
        @pl.when(has_far(plan, b))
        def _():
            def far(u, count, side, masked, part):
                at_k = part_at(b, part)
                at_q = units_at(u + PAD // UNIT, count)
                p = jnp.exp2(dot(kn[at_k, :], qaug[side, :, at_q]))
                if masked:
                    first_key = b * BLK + (0 if part is None else part * BLK // 2)
                    p = jnp.where(meets(first_key, at_k.size, bound_ref[:, at_q]), p, 0.0)
                dsb = (p * dot(vn[at_k, :], dot_t[:, at_q])).astype(BF)
                dq[:, at_q] += dot(kt[:, at_k], dsb)
                dv_acc[at_k, :] += dot(p.astype(BF), don[at_q, :])
                dk = dot(dsb, qn[at_q, :])
                dk_acc[at_k, :] += dk
                ends[side // 2] += jnp.sum(dk.reshape(dk.shape[0] // 8, 8, DEPTH), axis=0)

            far_sweep(plan, b, far, 2, 0, True)

    def take(part, lanes):
        row, lane = iota((packed_rows, lanes), 0), iota((packed_rows, lanes), 1)
        return ((row - head_width * part == lane) & (lane < head_width)).astype(F32).astype(BF)

    @pl.loop(0, chunks)
    def _(c):
        at = pl.ds(pl.multiple_of(c * rows, rows), rows)
        at_pad = pl.ds(pl.multiple_of(c * rows + PAD, UNIT), rows)
        packed = dot(take(0, SLOT), (dq[:, at_pad] * back).astype(BF))
        packed += dot(take(1, DEPTH), (dk_acc[at, :] * back).astype(BF), NT)
        packed += dot(take(2, DEPTH), dv_acc[at, :].astype(BF), NT)
        dqkv_ref[c] = packed.astype(BF)

    flip = (iota((UNIT, UNIT), 0) + iota((UNIT, UNIT), 1) == UNIT - 1).astype(F32)
    half = span // 2
    lane = iota((8, span), 1)
    column = iota((8, DEPTH), 1) == head_width
    out = jnp.zeros((8, span), F32)
    far_sum = [jnp.where(column, ends[i], 0.0) for i in range(2)]
    for d in range(-PER, PER + 1):
        part = jnp.zeros((UNIT, UNIT), F32)
        for r in range(PER):
            c = r + d + 1
            if 0 <= c < NEAR:
                part = part + band[r * UNIT : (r + 1) * UNIT, c * UNIT : (c + 1) * UNIT]
        if abs(d) > 1:
            far_sum[0 if d > 0 else 1] += jnp.sum(part.reshape(UNIT // 8, 8, UNIT), axis=0)
            continue
        turned = lax.dot_general(flip, part, NN, precision=lax.Precision.HIGHEST, preferred_element_type=F32)
        wide = jnp.concatenate([turned, jnp.zeros_like(turned)], axis=1)
        skewed = pltpu.roll(wide, 0, 1, stride=1, stride_axis=0)
        line = jnp.sum(skewed.reshape(UNIT // 8, 8, 2 * UNIT), axis=0)
        offset = UNIT - 1 - d * UNIT - iota((span, 2 * UNIT), 1)
        hot = (jnp.clip(offset, -half, half - 1) + half == iota((span, 2 * UNIT), 0)).astype(F32)
        out += lax.dot_general(line, hot, NT, precision=lax.Precision.HIGHEST, preferred_element_type=F32)
    out += jnp.where(lane == 0, jnp.sum(far_sum[0], axis=1, keepdims=True), 0.0)
    out += jnp.where(lane == span - 1, jnp.sum(far_sum[1], axis=1, keepdims=True), 0.0)
    out = jnp.sum(out, axis=0, keepdims=True)
    dtab_ref[...] = out


def attend_backward(qkv, do, tail, of, lse, bounds, plan, table, head_width):
    chunks, packed_rows, rows = qkv.shape
    total = chunks * rows
    padded = total + 2 * PAD
    span = table.shape[1]
    vm = pltpu.VMEM
    return pl.pallas_call(
        functools.partial(bwd_kernel, head_width=head_width),
        out_shape=(
            jax.ShapeDtypeStruct((chunks, packed_rows, rows), BF),
            jax.ShapeDtypeStruct((1, span), F32),
        ),
        in_specs=[pl.BlockSpec(memory_space=pltpu.SMEM)] + [pl.BlockSpec()] * 7,
        scratch_shapes=[
            vm((3, DEPTH, padded), BF),
            vm((total, DEPTH), BF),
            vm((SLOT, total), BF),
            vm((total, DEPTH), BF),
            vm((DEPTH, padded), BF),
            vm((padded, DEPTH), BF),
            vm((padded, DEPTH), BF),
            vm((BLK, NEAR * UNIT), F32),
            vm((SLOT, padded), F32),
            vm((BLK, NEAR * UNIT), F32),
            vm((2, 8, DEPTH), F32),
            vm((total, DEPTH), F32),
            vm((total, DEPTH), F32),
        ],
        compiler_params=pltpu.CompilerParams(vmem_limit_bytes=62 * 2**20),
        name="attend_backward",
    )(plan, qkv, do, tail, of, lse, table, bounds)

VEC = types.SimpleNamespace(
    first_gain=0, first_shift=1, first_up_bias=2, first_down_bias=3, mix_gain=4, mix_shift=5, mix_output_bias=6, filter_gain=7,
    filter_shift=8, pointwise_in_bias=9, batch_gain=10, batch_shift=11, pointwise_out_bias=12, second_gain=13, second_shift=14,
    second_up_bias=15, second_down_bias=16, final_gain=17, final_shift=18,
)
VEC_ROWS = 24
EPSILON = 1e-05
HALO = 64
TILE = 128
PIECE = 512
PART = 512
STEP = 1024


def col(cols_ref, i, size):
    return cols_ref[:size, i : i + 1]


def eye(n):
    return (iota((n, n), 0) == iota((n, n), 1)).astype(F32).astype(BF)


def flipped(mat):
    return dot(eye(mat.shape[1]), mat, NT).astype(BF)


def exact(a, b, dims=NN):
    return lax.dot_general(a, b, dims, precision=lax.Precision.HIGHEST, preferred_element_type=F32)


def folded(values):
    part = values[:, :TILE]
    for at in range(TILE, values.shape[1], TILE):
        part = part + values[:, at : at + TILE]
    return part


def row_sums(values):
    return exact(jnp.ones((8, TILE), F32), values, NT)


def many_row_sums(parts):
    size = parts[0].shape[0]
    lines = row_sums(jnp.concatenate(parts, axis=0))
    return [lines[:1, i * size : (i + 1) * size] for i in range(len(parts))]


def norm(x):
    m = jnp.mean(x, axis=0, keepdims=True)
    c = x - m
    inv = lax.rsqrt(jnp.mean(c * c, axis=0, keepdims=True) + EPSILON)
    return c * inv, inv


def norm_back(e, n, inv, gain):
    ea = e * gain
    return inv * (ea - jnp.mean(ea, axis=0, keepdims=True) - n * jnp.mean(ea * n, axis=0, keepdims=True))


def sigmoid(v):
    return 0.5 + 0.5 * jnp.tanh(0.5 * v)


def ones_row(rows, lanes):
    return (iota((rows, lanes), 0) == 0).astype(F32).astype(BF)


def open_rows(frames_ref, up_ref, down_ref, mix_ref, x1_ref, h2_ref, qkv_ref, cols_ref, packed_rows, ship):
    width, rows = frames_ref.shape
    hidden = up_ref.shape[1]
    heads = qkv_ref.shape[0]
    up_t = flipped(up_ref[...])
    mix_t = dot(spread_cols(mix_ref.shape[1], heads, packed_rows, mix_ref.shape[1] // heads), mix_ref[...], NT).astype(BF)

    @pl.loop(0, rows // PIECE)
    def _(c):
        at = pl.ds(pl.multiple_of(c * PIECE, PIECE), PIECE)
        x0 = frames_ref[:, at].astype(F32)
        n, _ = norm(x0)
        h1 = (n * col(cols_ref, VEC.first_gain, width) + col(cols_ref, VEC.first_shift, width)).astype(BF)
        a1 = dot(up_t, h1) + col(cols_ref, VEC.first_up_bias, hidden)
        s1 = (a1 * sigmoid(a1)).astype(BF)
        x1 = x0 + 0.5 * (dot(down_ref[...], s1) + col(cols_ref, VEC.first_down_bias, width))
        x1_ref[:, at] = x1
        n, _ = norm(x1)
        h2 = (n * col(cols_ref, VEC.mix_gain, width) + col(cols_ref, VEC.mix_shift, width)).astype(BF)
        h2_ref[:, at] = h2
        qkv = dot(mix_t, h2).astype(BF)
        for h in range(heads):
            qkv_ref[h, :, at] = qkv[h * packed_rows : (h + 1) * packed_rows]
        ship(c)


def open_segments(len_ref, bound_ref, plan_ref, ext_ref, line):
    rows = ext_ref.shape[1] - TILE
    group = bound_ref.shape[1] - 2 * PAD
    slots = len_ref.shape[1]
    lengths = jnp.broadcast_to(len_ref[...].astype(F32), (8, slots))
    row, column = iota((slots, slots), 0), iota((slots, slots), 1)
    ends = exact((column <= row).astype(F32), lengths, NT)[:, :1].astype(jnp.int32)
    own_len = exact((column == row).astype(F32), lengths, NT)[:, :1].astype(jnp.int32)
    ends_row = exact(lengths, (row <= column).astype(F32))[:1].astype(jnp.int32)
    plan_ref[...] = block_plan(ends, ends_row, group)
    line[...] = jnp.full_like(line, -1)
    for edge in (slice(0, PAD), slice(PAD + group, 2 * PAD + group)):
        bound_ref[:, edge] = jnp.where(iota((2, PAD), 0) == 0, 1 << 20, -1)

    @pl.loop(0, group // 512)
    def _(c):
        at = pl.multiple_of(c * 512, 512)
        seg, first, stop = segment_rows(ends, own_len, iota((1, 512), 1) + at, group)
        line[:, pl.ds(at + TILE, 512)] = seg
        bound_ref[0:1, pl.ds(at + PAD, 512)] = first
        bound_ref[1:2, pl.ds(at + PAD, 512)] = stop

    first = pl.multiple_of(lax.axis_index("head") * rows, TILE)
    ext_ref[:, :rows] = line[:, pl.ds(first + TILE, rows)]
    left = line[:, pl.ds(first, TILE)]
    right = line[:, pl.ds(first + TILE + rows, TILE)]
    ext_ref[:, rows:] = jnp.where(iota((1, TILE), 1) < HALO, right, left)


def split_heads(heads, head_width):
    size = heads * head_width
    row, column = iota((size, size), 0), iota((size, size), 1)
    hit = jnp.zeros((size, size), jnp.bool_)
    for h in range(heads):
        f = column - head_width * h
        mine = (f >= 0) & (f < head_width)
        hit = hit | (mine & (f < MAIN) & (row == MAIN * h + f)) | (mine & (f >= MAIN) & (row == MAIN * heads + 4 * h + f - MAIN))
    return hit.astype(F32).astype(BF)


def conv_masks(mask_ref, ext_ref):
    seg = jnp.broadcast_to(ext_ref[...], (8, ext_ref.shape[1]))
    lanes = seg.shape[1]
    reach = mask_ref.shape[0] // 2
    for i in range(mask_ref.shape[0]):
        mask_ref[i] = (pltpu.roll(seg, (reach - i) % lanes, 1) == seg).astype(F32)


def filter_kernel(x1_ref, x1l_ref, x1r_ref, o_ref, tail_ref, cols_ref, ext_ref, out_ref, pw_ref, taps_ref,
                  x2_ref, oc_ref, u_ref, y_ref, stat_ref, wide, mask, live_ref, h3s, n_ref, inv_ref, value_ref, gate_ref, *, head_width, slot_count, arrive):
    width, rows = x1_ref.shape
    lanes = rows + TILE
    heads = o_ref.shape[0]
    taps = taps_ref.shape[0]
    out_t = flipped(out_ref[...])
    pw_t = flipped(pw_ref[...])
    gather = split_heads(heads, head_width)
    seg = ext_ref[...]
    live = (seg >= 0) & (seg < slot_count)
    live_ref[...] = live.astype(F32)
    conv_masks(mask, ext_ref)
    wide_taps = taps_ref[...].astype(F32).T
    arrive()

    near = iota((1, TILE), 1) < HALO

    def extended(own, left, right):
        edge = jnp.where(near, right.astype(F32), left.astype(F32)).astype(own.dtype)
        return jnp.concatenate([own, edge], axis=1)

    x1 = extended(x1_ref[...], x1l_ref[...], x1r_ref[...])
    main = [extended(o_ref[h, :MAIN, TILE : TILE + rows], o_ref[h, :MAIN, :TILE], o_ref[h, :MAIN, TILE + rows :]) for h in range(heads)]
    tails = []
    for h in range(heads):
        left, right = (o_ref[h, MAIN:, at].astype(F32)[:4] for at in (slice(0, TILE), slice(TILE + rows, rows + 2 * TILE)))
        tails.append(extended(unfold_rows(tail_ref[h].astype(F32)), left, right))
    o = jnp.concatenate(main + [jnp.concatenate(tails, axis=0).astype(BF)], axis=0)
    oc = dot(gather, o, TN).astype(BF)
    x2 = x1 + (dot(out_t, oc) + col(cols_ref, VEC.mix_output_bias, width))
    n, inv = norm(x2)
    h3 = (n * col(cols_ref, VEC.filter_gain, width) + col(cols_ref, VEC.filter_shift, width)).astype(BF)
    g = dot(pw_t, h3) + col(cols_ref, VEC.pointwise_in_bias, 2 * width)
    gate = sigmoid(g[width:])
    u = jnp.where(live_ref[...] > 0.5, g[:width] * gate, 0.0).astype(BF)
    n_ref[...] = n[:, :rows]
    inv_ref[...] = inv[:, :rows]
    h3s[:width, :] = h3[:, :rows]
    value_ref[...] = g[:width, :rows]
    gate_ref[...] = gate[:, :rows]
    oc_ref[:width, :] = oc[:, :rows]
    x2_ref[...] = x2
    u_ref[...] = u
    wide[...] = u.astype(F32)

    own = (live & (iota((1, lanes), 1) < rows)).astype(F32)
    count = jnp.sum(own, axis=1, keepdims=True)
    safe = jnp.maximum(count, 1.0)
    for r in range(width // 8):
        sl = slice(8 * r, 8 * r + 8)
        u8 = wide[sl, :]
        acc = jnp.zeros((8, lanes), F32)
        for k in range(taps):
            moved = pltpu.roll(u8, (taps // 2 - k) % lanes, 1)
            acc = acc + wide_taps[sl, k : k + 1] * (moved * mask[k])
        y_ref[sl, :] = acc
    y = y_ref[...]
    part = folded(y * own)
    mean = exact(part, jnp.ones((TILE, TILE), F32)) / safe
    dev = (y - jnp.concatenate([mean] * (lanes // TILE), axis=1)) * own
    mean_row, spread_row = many_row_sums([part, folded(dev * dev)])
    stat_ref[...] = two_rows(mean_row / safe, spread_row, count)


def two_rows(a, b, extra):
    rest = a.shape[1] - TILE
    tail = pad_lanes(jnp.concatenate([a[:, TILE:], b[:, TILE:]], axis=0))
    spot = (iota((2, TILE), 0) == 0) & (iota((2, TILE), 1) == rest)
    return jnp.concatenate([a[:, :TILE], b[:, :TILE], jnp.where(spot, extra, tail)], axis=0)


def all_rows(ref, width):
    rest = width - TILE
    values = ref[...]
    a = jnp.concatenate([values[:, 0, :], values[:, 2, :rest]], axis=1)
    b = jnp.concatenate([values[:, 1, :], values[:, 3, :rest]], axis=1)
    return a, b, values[:, 2, rest : rest + 1]


def total_stats(stats_ref, width):
    mean_of, spread_of, n = all_rows(stats_ref, width)
    count = jnp.sum(n, axis=0, keepdims=True)
    mean = jnp.sum(n * mean_of, axis=0, keepdims=True) / count
    gap = mean_of - mean
    spread = jnp.sum(spread_of + n * gap * gap, axis=0, keepdims=True)
    inv = lax.rsqrt(spread / count + EPSILON)
    table = jnp.concatenate([mean, inv, jnp.broadcast_to(count, (1, width)), jnp.zeros((5, width), F32)], axis=0).T
    return table[:, 0:1], table[:, 1:2], table[:, 2:3]


def second_kernel(x2_ref, y_ref, stats_ref, cot_ref, cotl_ref, cotr_ref, cols_ref, pwo_ref, up_ref, down_ref,
                  out_ref, dx3_ref, e_ref, sums_ref, pack_ref, small_ref,
                  h4s, das, s4s, dfs, ws, dcs, *, arrive, leave):
    width, rows = out_ref.shape
    hidden = up_ref.shape[1]
    pwo_t = flipped(pwo_ref[...])
    up_t = flipped(up_ref[...])
    down = flipped(down_ref[...])
    arrive()
    mean, inv_b, _ = total_stats(stats_ref, width)
    bgain = col(cols_ref, VEC.batch_gain, width)

    near = iota((1, TILE), 1) < HALO
    edge = jnp.where(near, cotr_ref[...].astype(F32), cotl_ref[...].astype(F32))
    cot = jnp.concatenate([cot_ref[...].astype(F32), edge], axis=1)
    zh = (y_ref[...] - mean) * inv_b
    z = zh * bgain + col(cols_ref, VEC.batch_shift, width)
    sig_z = sigmoid(z)
    w = (z * sig_z).astype(BF)
    x3 = x2_ref[...] + (dot(pwo_t, w) + col(cols_ref, VEC.pointwise_out_bias, width))
    n4, inv4 = norm(x3)
    h4 = (n4 * col(cols_ref, VEC.second_gain, width) + col(cols_ref, VEC.second_shift, width)).astype(BF)
    a4 = dot(up_t, h4) + col(cols_ref, VEC.second_up_bias, hidden)
    sig = sigmoid(a4)
    s4 = (a4 * sig).astype(BF)
    x4 = x3 + 0.5 * (dot(down_ref[...], s4) + col(cols_ref, VEC.second_down_bias, width))
    nf, invf = norm(x4)
    fgain = col(cols_ref, VEC.final_gain, width)
    dx4 = norm_back(cot, nf, invf, fgain)
    df = (0.5 * dx4).astype(BF)
    da = (dot(down, df) * (sig * (1.0 + a4 * (1.0 - sig)))).astype(BF)
    dh = dot(up_ref[...], da)
    dx3 = dx4 + norm_back(dh, n4, inv4, col(cols_ref, VEC.second_gain, width))
    dc = dx3.astype(BF)
    dz = dot(pwo_ref[...], dc) * (sig_z * (1.0 + z * (1.0 - sig_z)))
    e = dz * bgain
    e_ref[...] = e
    sums_ref[...] = two_rows(*many_row_sums([folded(e[:, :rows]), folded((e * zh)[:, :rows])]), 0.0)
    leave()

    out_ref[...] = (nf * fgain + col(cols_ref, VEC.final_shift, width))[:, :rows].astype(BF)
    dx3_ref[...] = dx3[:, :rows]
    h4s[...] = h4[:, :rows]
    das[...] = da[:, :rows]
    s4s[:hidden, :] = s4[:, :rows]
    dfs[...] = df[:, :rows]
    ws[:width, :] = w[:, :rows]
    dcs[...] = dc[:, :rows]
    totals = many_row_sums([folded(v[:, :rows]) for v in (dh * n4, dh, cot * nf, cot, dz * zh, dz)])
    s4s[hidden:, :] = ones_row(16, rows)
    ws[width:, :] = ones_row(16, rows)
    up_grad = dot(h4s[...], das[...], NT)
    up_bias = dot(ones_row(16, rows), das[...], NT)
    down_grad = dot(dfs[...], s4s[...], NT)
    pw_grad = dot(ws[...], dcs[...], NT)
    down_bias = dot(ones_row(16, rows), dfs[...], NT)
    put_ff(pack_ref, up_grad, down_grad, 0)
    tall = 9 * width
    pack_ref[tall : tall + width, :] = pw_grad[:width, :TILE].astype(BF)
    pack_ref[tall + width : tall + 2 * width, :] = pad_lanes(pw_grad[:width, TILE:]).astype(BF)
    small_ref[...] = stack_rows(
        [totals[0], totals[1], up_bias[:1], down_bias[:1], totals[2], totals[3], totals[4], totals[5], pw_grad[width : width + 1]],
        small_ref.shape)


def pad_lanes(mat, lanes=TILE):
    if mat.shape[1] == lanes:
        return mat
    return jnp.concatenate([mat, jnp.zeros((mat.shape[0], lanes - mat.shape[1]), mat.dtype)], axis=1)


def stack_rows(rows, shape):
    parts = [pad_lanes(r, shape[1]) for r in rows]
    parts.append(jnp.zeros((shape[0] - len(rows), shape[1]), F32))
    return jnp.concatenate(parts, axis=0)


def put_ff(pack_ref, up_grad, down_grad_t, at):
    width, hidden = up_grad.shape
    whole = hidden // TILE
    for i in range(whole):
        pack_ref[at + i * width : at + (i + 1) * width, :] = up_grad[:, i * TILE : (i + 1) * TILE].astype(BF)
        j = whole + i
        pack_ref[at + j * width : at + (j + 1) * width, :] = down_grad_t[:, i * TILE : (i + 1) * TILE].astype(BF)
    rest = jnp.concatenate([up_grad[:, whole * TILE : hidden], down_grad_t[:, whole * TILE : hidden]], axis=1)
    pack_ref[at + 2 * whole * width : at + (2 * whole + 1) * width, :] = rest.astype(BF)


def unfilter_kernel(e_ref, y_ref, stats_ref, sums_ref, u_ref, dx3_ref, ocs, cols_ref, ext_ref, pw_ref, taps_ref,
                    out_ref, dx2_ref, do_ref, pack_ref, small_ref, tapg_ref,
                    dyw, du_s, mask, prod, h3s, dgs, dms, gains, live_ref, n_ref, inv_ref, value_ref, gate_ref, tail_ref, *, head_width, ship, arrive):
    width, rows = dx3_ref.shape
    lanes = rows + TILE
    heads = do_ref.shape[0]
    taps = taps_ref.shape[0]
    tap_cols = taps_ref[...].astype(F32).T
    out_w = dot(split_heads(heads, head_width), out_ref[...]).astype(BF)
    gains[...] = jnp.zeros_like(gains)
    fgain = col(cols_ref, VEC.filter_gain, width)
    mean, inv_b, count = total_stats(stats_ref, width)
    arrive()
    one_of, two_of, _ = all_rows(sums_ref, width)
    sums = jnp.concatenate([jnp.sum(one_of, axis=0, keepdims=True), jnp.sum(two_of, axis=0, keepdims=True), jnp.zeros((6, width), F32)], axis=0).T
    s1, s2 = sums[:, 0:1], sums[:, 1:2]
    seg = ext_ref[...]
    live = live_ref[...]
    zh = (y_ref[...] - mean) * inv_b
    dy = inv_b * (e_ref[...] - live * ((s1 + zh * s2) / count))
    dyw[...] = jnp.where(seg >= 0, dy, 0.0).astype(BF).astype(F32)

    for r in range(width // 8):
        sl = slice(8 * r, 8 * r + 8)
        dy8 = dyw[sl, :]
        u8 = u_ref[16 * (r // 2) : 16 * (r // 2) + 16, :rows].astype(F32)[8 * (r % 2) : 8 * (r % 2) + 8]
        acc = jnp.zeros((8, rows), F32)
        for k in range(taps):
            moved = pltpu.roll(dy8, (k - taps // 2) % lanes, 1)[:, :rows] * mask[taps - k][:, :rows]
            acc = acc + tap_cols[sl, k : k + 1] * moved
            hit = moved * u8
            prod[k, sl, :] = folded(hit)
        du_s[sl, :] = acc

    @pl.loop(0, rows // PART)
    def _(c):
        at = pl.ds(pl.multiple_of(c * PART, PART), PART)
        n, inv = n_ref[:, at], inv_ref[:, at]
        gate = gate_ref[:, at]
        t = live_ref[:, at] * du_s[:, at] * gate
        dg = jnp.concatenate([t, t * value_ref[:, at] * (1.0 - gate)], axis=0).astype(BF)
        dh = dot(pw_ref[...], dg)
        dx2 = dx3_ref[:, at] + norm_back(dh, n, inv, fgain)
        dx2_ref[:, at] = dx2
        dm = dx2.astype(BF)
        do = dot(out_w, dm)
        for h in range(heads):
            do_ref[h, :, at] = do[h * MAIN : (h + 1) * MAIN].astype(BF)
        tail_ref[:, at] = do[heads * MAIN :]
        ship(c)
        dgs[:, at] = dg
        dms[:, at] = dm
        for i, v in enumerate((dh * n, dh)):
            gains[i] += folded(v)

    ship(rows // PART)
    whole = prod[...].reshape(taps * width, TILE)
    hi = whole.astype(BF)
    lo = (whole - hi.astype(F32)).astype(BF)
    ones = jnp.ones((8, TILE), BF)
    lines = dot(ones, hi, NT) + dot(ones, lo, NT)
    for k in range(taps):
        tapg_ref[k : k + 1, :] = lines[:1, k * width : (k + 1) * width]

    h3s[width:, :] = ones_row(16, rows)
    ocs[width:, :] = ones_row(16, rows)
    pw_grad = dot(h3s[...], dgs[...], NT)
    out_grad = dot(ocs[...], dms[...], NT)
    at = 0
    for lo in range(0, 2 * width, TILE):
        pack_ref[at : at + width, :] = pad_lanes(pw_grad[:width, lo : min(lo + TILE, 2 * width)]).astype(BF)
        at += width
    for lo in range(0, width, TILE):
        pack_ref[at : at + width, :] = pad_lanes(out_grad[:width, lo : min(lo + TILE, width)]).astype(BF)
        at += width
    small_ref[...] = stack_rows(
        [row_sums(gains[0])[:1], row_sums(gains[1])[:1], pw_grad[width : width + 1], out_grad[width : width + 1]], small_ref.shape)


def close_kernel(frames_ref, x1_ref, h2_ref, dx2_ref, dqkv_ref, dtab_ref, cols_ref, up_ref, down_ref, mix_ref,
                 grad_ref, pack_ref, h1s, das, s1s, dfs, dqs, gains, *, mixed):
    width, rows = frames_ref.shape
    hidden = up_ref.shape[1]
    heads, packed_rows, _ = dqkv_ref.shape
    up_t = flipped(up_ref[...])
    down = flipped(down_ref[...])
    hot = spread_cols(mix_ref.shape[1], heads, packed_rows, mix_ref.shape[1] // heads)
    mix_w = dot(mix_ref[...], hot, NT).astype(BF)
    gains[...] = jnp.zeros_like(gains)
    mgain = col(cols_ref, VEC.mix_gain, width)
    fgain = col(cols_ref, VEC.first_gain, width)

    @pl.loop(0, rows // STEP)
    def _(c):
        at = pl.ds(pl.multiple_of(c * STEP, STEP), STEP)
        dq = jnp.concatenate([dqkv_ref[h, :, at] for h in range(heads)], axis=0)
        dqs[:, at] = dq
        dh2 = dot(mix_w, dq)
        n2, inv2 = norm(x1_ref[:, at])
        dx1 = dx2_ref[:, at] + norm_back(dh2, n2, inv2, mgain)
        x0 = frames_ref[:, at].astype(F32)
        n1, inv1 = norm(x0)
        h1 = (n1 * fgain + col(cols_ref, VEC.first_shift, width)).astype(BF)
        a1 = dot(up_t, h1) + col(cols_ref, VEC.first_up_bias, hidden)
        sig = sigmoid(a1)
        s1s[:, at] = (a1 * sig).astype(BF)
        df = (0.5 * dx1).astype(BF)
        da = (dot(down, df) * (sig * (1.0 + a1 * (1.0 - sig)))).astype(BF)
        dh1 = dot(up_ref[...], da)
        grad_ref[:, at] = dx1 + norm_back(dh1, n1, inv1, fgain)
        h1s[:, at] = h1
        das[:, at] = da
        dfs[:, at] = df
        for i, v in enumerate((dh1 * n1, dh1, dh2 * n2, dh2)):
            gains[i] += folded(v)

    mix_grad = dot(dot(h2_ref[...], dqs[...], NT).astype(BF), hot)
    at = 0
    for lo in range(0, mix_grad.shape[1], TILE):
        pack_ref[at : at + width, :] = pad_lanes(mix_grad[:, lo : min(lo + TILE, mix_grad.shape[1])]).astype(BF)
        at += width
    mixed()
    up_grad = dot(h1s[...], das[...], NT)
    up_bias = dot(ones_row(16, rows), das[...], NT)
    down_grad = dot(dfs[...], s1s[...], NT)
    down_bias = dot(ones_row(16, rows), dfs[...], NT)
    put_ff(pack_ref, up_grad, down_grad, at)
    at += (2 * (hidden // TILE) + 1) * width
    totals = many_row_sums([gains[i] for i in range(4)])
    small = stack_rows([totals[0], totals[1], up_bias[:1], down_bias[:1], totals[2], totals[3]], (16, 5 * TILE))
    at = put_small(pack_ref, small, at)
    span = dtab_ref.shape[1]
    table = jnp.where(iota((16, span), 0) == lax.axis_index("head"), dtab_ref[...], 0.0)
    pack_ref[at : at + 16, :] = table.astype(BF)
    if at + 16 < pack_ref.shape[0]:
        pack_ref[at + 16 :, :] = jnp.zeros((pack_ref.shape[0] - at - 16, TILE), BF)


def put_small(pack_ref, small, at):
    for lo in range(0, small.shape[1], TILE):
        pack_ref[at : at + small.shape[0], :] = small[:, lo : lo + TILE].astype(BF)
        at += small.shape[0]
    return at


def put_taps(pack_ref, tapg, at):
    taps = tapg.shape[0]
    pack_ref[at : at + taps, :] = tapg[:, :TILE].astype(BF)
    pack_ref[at + taps : at + 2 * taps, :] = pad_lanes(tapg[:, TILE:]).astype(BF)
    return at + 2 * taps


def unpack_kernel(pack_ref, out_ref, grad_ref, *refs, layout):
    refs[0][...] = out_ref[...]
    refs[1][...] = grad_ref[...]
    out_refs = refs[2:]
    given = Weights(*out_refs)

    def wide(at, rows, lanes):
        parts = [pack_ref[at + i * rows : at + (i + 1) * rows, :].astype(F32) for i in range(-(-lanes // TILE))]
        return jnp.concatenate(parts, axis=1)[:, :lanes]

    for at, up_ref, down_ref in ((layout.first, given.first_up, given.first_down), (layout.second, given.second_up, given.second_down)):
        width, hidden = up_ref.shape
        whole = hidden // TILE
        half = hidden - whole * TILE
        piece = lambda i: pack_ref[at + i * width : at + (i + 1) * width, :].astype(F32)
        rest = piece(2 * whole)
        up_ref[...] = jnp.concatenate([piece(i) for i in range(whole)] + [rest[:, :half]], axis=1)
        down_ref[...] = jnp.concatenate([piece(whole + i) for i in range(whole)] + [rest[:, half:]], axis=1)
    for ref, at in ((given.mix_inputs, layout.mix_inputs), (given.pointwise_in, layout.pointwise_in), (given.mix_output, layout.mix_output),
                    (given.pointwise_out, layout.pointwise_out), (given.depthwise_taps, layout.taps)):
        ref[...] = wide(at, *ref.shape)
    given.position_bias[...] = pack_ref[layout.table : layout.table + 16, :].astype(F32)[: given.position_bias.shape[0]]
    late = wide(layout.small_late, 16, 5 * TILE)
    early = wide(layout.small, 32, 5 * TILE)
    late_rows = (
        given.first_gain, given.first_shift, given.first_up_bias, given.first_down_bias, given.mix_gain, given.mix_shift,
    )
    second_rows = (
        given.second_gain, given.second_shift, given.second_up_bias, given.second_down_bias, given.final_gain, given.final_shift,
        given.batch_gain, given.batch_shift, given.pointwise_out_bias,
    )
    filter_rows = (given.filter_gain, given.filter_shift, given.pointwise_in_bias, given.mix_output_bias)
    for small, first, refs in ((late, 0, late_rows), (early, 0, second_rows), (early, 16, filter_rows)):
        for row, ref in enumerate(refs, first):
            ref[...] = small[row : row + 1, : ref.shape[0]].reshape(ref.shape)


@dataclasses.dataclass
class Weights:
    first_gain: object
    first_shift: object
    first_up: object
    first_up_bias: object
    first_down: object
    first_down_bias: object
    mix_gain: object
    mix_shift: object
    mix_inputs: object
    position_bias: object
    mix_output: object
    mix_output_bias: object
    filter_gain: object
    filter_shift: object
    pointwise_in: object
    pointwise_in_bias: object
    depthwise_taps: object
    batch_gain: object
    batch_shift: object
    pointwise_out: object
    pointwise_out_bias: object
    second_gain: object
    second_shift: object
    second_up: object
    second_up_bias: object
    second_down: object
    second_down_bias: object
    final_gain: object
    final_shift: object


def pack_layout(width, hidden, mix_width, taps, devices):
    ff = (2 * (hidden // TILE) + 1) * width
    chunks = lambda lanes: -(-lanes // TILE) * width
    unit = 16 * devices
    whole = lambda rows: -(-rows // unit) * unit
    at = types.SimpleNamespace(second=0, pointwise_out=ff)
    at.pointwise_in = ff + chunks(width)
    at.mix_output = at.pointwise_in + chunks(2 * width)
    at.taps = at.mix_output + chunks(width)
    at.small = at.taps + 2 * taps
    at.late = at.mix_inputs = whole(at.small + 32 * 5)
    at.last = at.late + chunks(mix_width) // unit * unit
    at.first = at.mix_inputs + chunks(mix_width)
    at.small_late = at.first + ff
    at.table = at.small_late + 16 * 5
    at.rows = at.late + whole(at.table + 16 - at.late)
    return at


MESH = pl.DeviceIdType.MESH


def meet(peers):
    barrier = pltpu.get_barrier_semaphore()
    for peer in peers:
        pl.semaphore_signal(barrier, inc=1, device_id=peer, device_id_type=MESH)
    pl.semaphore_wait(barrier, len(peers))


def head_peers(n):
    me = lax.axis_index("head")
    return me, [{"head": lax.rem(me + s, n)} for s in range(1, n)], [lax.rem(me + s, n) for s in range(1, n)]


def opening_kernel(frames_ref, len_ref, up_ref, down_ref, mix_ref, *refs, packed_rows, n):
    count = len(VEC.__dict__)
    vec_refs, refs = refs[:count], refs[count:]
    (cot_ref, x1_ref, h2_ref, cols_ref, bound_ref, plan_ref, ext_ref, all_ref, x1l_ref, x1r_ref, cotl_ref, cotr_ref,
     qkv, line, send, recv, local, hsend, hrecv) = refs
    me, peers, ids = head_peers(n)
    rows = cot_ref.shape[1]
    barrier = pltpu.get_barrier_semaphore()
    for peer in peers:
        pl.semaphore_signal(barrier, inc=1, device_id=peer, device_id_type=MESH)
    vecs = [ref[...].astype(F32).reshape(1, ref.shape[0]) for ref in vec_refs]
    cols_ref[...] = stack_rows(vecs, (VEC_ROWS, up_ref.shape[1])).T
    pl.semaphore_wait(barrier, len(peers))

    def piece(c, s):
        at = pl.ds(pl.multiple_of(c * PIECE, PIECE), PIECE)
        return pltpu.make_async_remote_copy(src_ref=qkv.at[ids[s], :, at], dst_ref=all_ref.at[me, :, at], send_sem=send.at[c, s],
                                            recv_sem=recv.at[c, s], device_id=peers[s], device_id_type=MESH)

    def ship(c):
        for s in range(n - 1):
            piece(c, s).start()

    open_rows(frames_ref, up_ref, down_ref, mix_ref, x1_ref, h2_ref, qkv, cols_ref, packed_rows, ship)
    own = pltpu.make_async_copy(qkv.at[me], all_ref.at[me], local)
    own.start()

    def edge(i, src, dst, head):
        return pltpu.make_async_remote_copy(src_ref=src, dst_ref=dst, send_sem=hsend.at[i], recv_sem=hrecv.at[i],
                                            device_id={"head": head}, device_id_type=MESH)

    up = lax.rem(me + 1, n)
    down = lax.rem(me + n - 1, n)
    last, start = pl.ds(rows - TILE, TILE), pl.ds(0, TILE)
    to_right = [edge(0, x1_ref.at[:, last], x1l_ref, up), edge(1, cot_ref.at[:, last], cotl_ref, up)]
    to_left = [edge(2, x1_ref.at[:, start], x1r_ref, down), edge(3, cot_ref.at[:, start], cotr_ref, down)]

    @pl.when(me < n - 1)
    def _():
        for c in to_right:
            c.start()

    @pl.when(me > 0)
    def _():
        for c in to_left:
            c.start()

    open_segments(len_ref, bound_ref, plan_ref, ext_ref, line)
    own.wait()

    @pl.loop(0, rows // PIECE)
    def _(c):
        for s in range(n - 1):
            piece(c, s).wait()

    @pl.when(me < n - 1)
    def _():
        for c in to_right:
            c.wait_send()
        for c in to_left:
            c.wait_recv()

    @pl.when(me > 0)
    def _():
        for c in to_left:
            c.wait_send()
        for c in to_right:
            c.wait_recv()


def everyone(n_tm, n_head):
    me = lax.axis_index("tm") * n_head + lax.axis_index("head")

    def for_all(act):
        for step in [s for i in range(1, n_head // 2 + 1) for s in {n_head - i, i}] + [0]:
            pl.loop(0 if step else 1, n_tm)(functools.partial(act, step))

    def place(along_head, along_tm):
        return {"tm": lax.rem(lax.axis_index("tm") + along_tm, n_tm), "head": lax.rem(lax.axis_index("head") + along_head, n_head)}

    return me, for_all, place


def tell(src_ref, all_ref, send, recv, n_tm, n_head):
    me, for_all, place = everyone(n_tm, n_head)

    def copy(h, t):
        return pltpu.make_async_remote_copy(src_ref=src_ref, dst_ref=all_ref.at[me], send_sem=send.at[h, t], recv_sem=recv.at[h, t],
                                            device_id=place(h, t), device_id_type=MESH)

    def start():
        for_all(lambda h, t: copy(h, t).start())
        all_ref[me] = src_ref[...]

    def end():
        for_all(lambda h, t: copy(h, t).wait())

    return start, end


def load_all(sources, targets, sems):
    copies = [pltpu.make_async_copy(src, dst, sems.at[i]) for i, (src, dst) in enumerate(zip(sources, targets))]
    for copy in copies:
        copy.start()
    return copies


def middle_kernel(*refs, n_tm, n_head, head_width, slot_count, layout):
    o_ref, o_tail, sources, refs = refs[0], refs[1], refs[2:16], refs[16:]
    (out_ref, dx2_ref, do_all, do_tails, pack_ref), refs = refs[:5], refs[5:]
    loaded, refs = refs[:14], refs[14:]
    (x1_ref, x1l_ref, x1r_ref, cot_ref, cotl_ref, cotr_ref, cols_ref, ext_ref, mixo_ref, pwi_ref, taps_ref, pwo_ref, up_ref,
     down_ref) = loaded
    (o_own, x2, oc, u, y, stat, stats, dx3, e, sums, all_sums, do, wide, mask, live,
     h4s, das, s4s, dfs, ws, dcs, dyw, du, prod, h3s, dgs, dms, gains2, smalld, smalle, tapg,
     n3, inv3, value3, gate3, tail_own, tail_wide, tail), refs = refs[:38], refs[38:]
    (load_sems, send_o, recv_o, local_o, send_a, recv_a, send_b, recv_b, send_d, recv_d, local_d) = refs
    me, peers, ids = head_peers(n_head)
    _, for_all, place = everyone(n_tm, n_head)
    barrier = pltpu.get_barrier_semaphore()
    rows = x1_ref.shape[1]
    for_all(lambda h, t: pl.semaphore_signal(barrier, inc=1, device_id=place(h, t), device_id_type=MESH))
    loads = load_all(sources, loaded, load_sems)
    pl.semaphore_wait(barrier, n_tm * n_head - 1)

    def parts(p):
        first = pl.multiple_of(p * rows, TILE)
        mine = o_own.at[me]
        low, high = pl.ds(0, MAIN), pl.ds(MAIN, SLOT - MAIN)
        left, right = pl.ds(0, TILE), pl.ds(rows + TILE, TILE)
        return (
            (o_ref.at[low, pl.ds(first, rows + 2 * TILE)], mine.at[low]),
            (o_tail.at[p], tail_own.at[me]),
            (o_ref.at[high, pl.ds(first, TILE)], mine.at[high, left]),
            (o_ref.at[high, pl.ds(pl.multiple_of(first + rows + TILE, TILE), TILE)], mine.at[high, right]),
        )

    copies = [
        pltpu.make_async_remote_copy(src_ref=src, dst_ref=dst, send_sem=send_o.at[s, i], recv_sem=recv_o.at[s, i],
                                     device_id=peer, device_id_type=MESH)
        for s, (peer, p) in enumerate(zip(peers, ids)) for i, (src, dst) in enumerate(parts(p))
    ]
    for copy in copies:
        copy.start()
    own = [pltpu.make_async_copy(src, dst, local_o.at[i]) for i, (src, dst) in enumerate(parts(me))]
    for copy in own:
        copy.start()
    for load in loads:
        load.wait()

    def arrive():
        for copy in own + copies:
            copy.wait()

    filter_kernel(x1_ref, x1l_ref, x1r_ref, o_own, tail_own, cols_ref, ext_ref, mixo_ref, pwi_ref, taps_ref, x2, oc, u, y, stat, wide, mask, live,
                  h3s, n3, inv3, value3, gate3, head_width=head_width, slot_count=slot_count, arrive=arrive)
    stats_out, stats_in = tell(stat, stats, send_a, recv_a, n_tm, n_head)
    sums_out, sums_in = tell(sums, all_sums, send_b, recv_b, n_tm, n_head)
    stats_out()
    second_kernel(x2, y, stats, cot_ref, cotl_ref, cotr_ref, cols_ref, pwo_ref, up_ref, down_ref,
                  out_ref, dx3, e, sums, pack_ref, smalld, h4s, das, s4s, dfs, ws, dcs, arrive=stats_in, leave=sums_out)

    def piece(c, s):
        at = pl.ds(pl.multiple_of(c * PART, PART), PART)
        return pltpu.make_async_remote_copy(src_ref=do.at[ids[s], :, at], dst_ref=do_all.at[me, :, at], send_sem=send_d.at[c, s],
                                            recv_sem=recv_d.at[c, s], device_id=peers[s], device_id_type=MESH)

    def ending(s):
        return pltpu.make_async_remote_copy(src_ref=tail.at[ids[s]], dst_ref=do_tails.at[me], send_sem=send_d.at[rows // PART, s],
                                            recv_sem=recv_d.at[rows // PART, s], device_id=peers[s], device_id_type=MESH)

    def ship(c):
        if isinstance(c, int):
            for h in range(n_head):
                tail[h] = fold_rows(tail_wide[4 * h : 4 * h + 4, :], 4).astype(BF)
        for s in range(n_head - 1):
            (ending(s) if isinstance(c, int) else piece(c, s)).start()

    unfilter_kernel(e, y, stats, all_sums, u, dx3, oc, cols_ref, ext_ref, pwi_ref, taps_ref, mixo_ref,
                    dx2_ref, do, pack_ref.at[pl.ds(layout.pointwise_in, layout.taps - layout.pointwise_in)], smalle, tapg, dyw, du, mask, prod, h3s, dgs, dms, gains2, live, n3, inv3, value3, gate3, tail_wide,
                    head_width=head_width, ship=ship, arrive=sums_in)
    own = [pltpu.make_async_copy(do.at[me], do_all.at[me], local_d.at[0]), pltpu.make_async_copy(tail.at[me], do_tails.at[me], local_d.at[1])]
    for copy in own:
        copy.start()
    end = put_taps(pack_ref, tapg[...], layout.taps)
    end = put_small(pack_ref, jnp.concatenate([smalld[...], smalle[...]], axis=0), end)
    if end < pack_ref.shape[0]:
        pack_ref[end:, :] = jnp.zeros((pack_ref.shape[0] - end, TILE), BF)
    for copy in own:
        copy.wait()
    for s in range(n_head - 1):
        ending(s).wait()

    @pl.loop(0, rows // PART)
    def _(c):
        for s in range(n_head - 1):
            piece(c, s).wait()


def sum_scratch(count, n_tm, n_head):
    half = count // 2
    big = half // (n_tm // 2)
    shapes = [(half, TILE), (half, TILE), (n_tm // 2, big, TILE), (big, TILE), (n_head, big // n_head, TILE), (big, TILE), (half, TILE)]
    return [pltpu.VMEM(shape, BF) for shape in shapes]


def gradient_sum(src_ref, out_ref, first, scratch, sems, local, n_tm, n_head):
    got0, half, got1, part1, got2, part2, whole = scratch
    tm, head = lax.axis_index("tm"), lax.axis_index("head")
    n_chip = n_tm // 2
    chip, core = tm // 2, lax.rem(tm, 2)
    size = src_ref.shape[0] // 2
    big = size // n_chip
    small = big // n_head
    sibling = {"tm": chip * 2 + 1 - core}

    def rows(i, count, base=0):
        return pl.ds(pl.multiple_of(base + i * count, 16), count)

    def send(src, dst, phase, s, peer):
        return pltpu.make_async_remote_copy(src_ref=src, dst_ref=dst, send_sem=sems.at[2 * phase, s], recv_sem=sems.at[2 * phase + 1, s],
                                            device_id=peer, device_id_type=MESH)

    def chip_peer(s):
        return lax.rem(chip + s, n_chip)

    def head_peer(s):
        return lax.rem(head + s, n_head)

    def zero():
        return send(src_ref.at[rows(1 - core, size)], got0, 0, 0, sibling)

    def one(s):
        return send(half.at[rows(chip_peer(s), big)], got1.at[s], 1, s, {"tm": chip_peer(s) * 2 + core})

    def two(s):
        return send(part1.at[rows(head_peer(s), small)], got2.at[s], 2, s, {"head": head_peer(s)})

    def three(s):
        at = part2.at[rows(head, small)]
        return send(at, at, 3, s, {"head": head_peer(s)})

    def four(s):
        return send(part2, whole.at[rows(chip, big)], 4, s, {"tm": chip_peer(s) * 2 + core})

    def five():
        return send(whole, out_ref.at[rows(core, size, first)], 5, 0, sibling)

    def keep():
        return pltpu.make_async_copy(whole, out_ref.at[rows(core, size, first)], local)

    def added(got, n):
        total = got[0].astype(F32)
        for s in range(1, n):
            total = total + got[s].astype(F32)
        return total.astype(BF)

    def step0():
        zero().start()

    def step1():
        zero().wait()
        half[...] = (src_ref[rows(core, size), :].astype(F32) + got0[...].astype(F32)).astype(BF)
        pl.loop(1, n_chip)(lambda s: one(s).start())
        got1[0] = half[rows(chip, big), :]

    def step2():
        pl.loop(1, n_chip)(lambda s: one(s).wait())
        part1[...] = added(got1, n_chip)
        pl.loop(1, n_head)(lambda s: two(s).start())
        got2[0] = part1[rows(head, small), :]

    def step3():
        pl.loop(1, n_head)(lambda s: two(s).wait())
        part2[rows(head, small), :] = added(got2, n_head)
        pl.loop(1, n_head)(lambda s: three(s).start())

    def step4():
        pl.loop(1, n_head)(lambda s: three(s).wait())
        pl.loop(1, n_chip)(lambda s: four(s).start())
        whole[rows(chip, big), :] = part2[...]

    def step5():
        pl.loop(1, n_chip)(lambda s: four(s).wait())
        five().start()
        keep().start()

    def step6():
        keep().wait()
        five().wait()

    return step0, step1, step2, step3, step4, step5, step6


def return_kernel(src_ref, dst_ref, send, recv, *, n):
    me, peers, ids = head_peers(n)
    meet(peers)
    copies = [
        pltpu.make_async_remote_copy(src_ref=src_ref.at[p], dst_ref=dst_ref.at[me], send_sem=send.at[s], recv_sem=recv.at[s],
                                     device_id=peer, device_id_type=MESH)
        for s, (peer, p) in enumerate(zip(peers, ids))
    ]
    for copy in copies:
        copy.start()
    for copy in copies:
        copy.wait()


def final_kernel(*refs, n_tm, n_head, parts):
    dqkv_ref, others_ref, sources, refs = refs[0], refs[1], refs[2:12], refs[12:]
    (grad_ref, total_ref), loaded, refs = refs[:2], refs[2:12], refs[12:]
    early_ref, frames_ref, x1_ref, h2_ref, dx2_ref, dtab_ref, cols_ref, up_ref, down_ref, mix_ref = loaded
    (dqkv, late, h1s, das, s1s, dfs, dqs, gains), refs = refs[:8], refs[8:]
    sum_refs = [refs[7 * i : 7 * i + 7] for i in range(3)]
    load_sems, load_q, sum_sems, sum_local = refs[21:]
    me, peers, ids = head_peers(n_head)
    tm = lax.axis_index("tm")
    rows = x1_ref.shape[1]
    barrier = pltpu.get_barrier_semaphore()
    for peer in peers:
        pl.semaphore_signal(barrier, inc=1, device_id=peer, device_id_type=MESH)

    @pl.loop(1, n_tm)
    def _(s):
        pl.semaphore_signal(barrier, inc=1, device_id={"tm": lax.rem(tm + s, n_tm)}, device_id_type=MESH)

    loads = load_all(sources, loaded, load_sems)
    own = pltpu.make_async_copy(dqkv_ref.at[me], dqkv.at[me], load_q.at[0])
    loads += [own] + [pltpu.make_async_copy(others_ref.at[p], dqkv.at[p], load_q.at[1 + s]) for s, p in enumerate(ids)]
    for load in loads[-n_head:]:
        load.start()
    pl.semaphore_wait(barrier, n_head + n_tm - 2)

    for load in loads:
        load.wait()
    late_at, last_at, end = parts

    def summed(i, src, first):
        return gradient_sum(src, total_ref, first, sum_refs[i], sum_sems.at[i], sum_local.at[i], n_tm, n_head)

    early = summed(0, early_ref, 0)
    last = summed(2, late.at[pl.ds(last_at - late_at, end - last_at)], last_at)
    late_sum = summed(1, late.at[pl.ds(0, last_at - late_at)], late_at) if last_at > late_at else [lambda: None] * 7
    early[0]()
    early[1]()

    def mixed():
        late_sum[0]()

    close_kernel(frames_ref, x1_ref, h2_ref, dx2_ref, dqkv, dtab_ref, cols_ref, up_ref, down_ref, mix_ref,
                 grad_ref, late, h1s, das, s1s, dfs, dqs, gains, mixed=mixed)
    for step in (last[0], late_sum[1], last[1], early[2], late_sum[2], last[2], early[3], late_sum[3], last[3], early[4], late_sum[4],
                 last[4], early[5], late_sum[5], last[5], early[6], late_sum[6], last[6]):
        step()


VMEM_MIB = 62


def body(
    frames, lengths, first_gain, first_shift, first_up, first_up_bias, first_down, first_down_bias, mix_gain, mix_shift,
    mix_inputs, position_bias, mix_output, mix_output_bias, filter_gain, filter_shift, pointwise_in, pointwise_in_bias,
    depthwise_taps, batch_gain, batch_shift, pointwise_out, pointwise_out_bias, second_gain, second_shift, second_up,
    second_up_bias, second_down, second_down_bias, final_gain, final_shift, cotangent,
):
    weights = Weights(
        first_gain, first_shift, first_up, first_up_bias, first_down, first_down_bias, mix_gain, mix_shift, mix_inputs, position_bias,
        mix_output, mix_output_bias, filter_gain, filter_shift, pointwise_in, pointwise_in_bias, depthwise_taps, batch_gain,
        batch_shift, pointwise_out, pointwise_out_bias, second_gain, second_shift, second_up, second_up_bias, second_down,
        second_down_bias, final_gain, final_shift)
    rows, width = frames.shape
    hidden = first_up.shape[1]
    n_head, n_tm = lax.axis_size("head"), lax.axis_size("tm")
    heads, span = position_bias.shape
    head_width = width // heads
    packed_rows = -(-3 * head_width // 16) * 16
    group = rows * n_head
    lanes = rows + TILE
    slots = lengths.shape[1]
    taps = depthwise_taps.shape[0]
    layout = pack_layout(width, hidden, mix_inputs.shape[1], taps, n_tm * n_head)

    vectors = tuple(getattr(weights, name) for name in VEC.__dict__)
    frames_t, cot_t, first_down_t, second_down_t = frames.T, cotangent.T, first_down.T, second_down.T
    vm, dma, hbm = pltpu.VMEM, pltpu.SemaphoreType.DMA, pl.BlockSpec(memory_space=pl.ANY)
    steps = rows // PIECE
    piece_sems = dma((steps, n_head - 1))

    def comm_call(kernel, name, collective_id, ins, in_hbm, outs, out_hbm, scratch):
        return pl.pallas_call(
            kernel,
            out_shape=tuple(jax.ShapeDtypeStruct(s, t) for s, t in outs),
            in_specs=[hbm if i in in_hbm else pl.BlockSpec() for i in range(len(ins))],
            out_specs=tuple(hbm if i in out_hbm else pl.BlockSpec() for i in range(len(outs))),
            scratch_shapes=scratch,
            compiler_params=pltpu.CompilerParams(collective_id=collective_id, has_side_effects=True, vmem_limit_bytes=VMEM_MIB * 2**20),
            name=name,
        )(*ins)

    ins = (frames_t, lengths, first_up, first_down_t, mix_inputs) + vectors + (cot_t,)
    x1, h2, cols, bounds, plan, ext, qkv_all, x1l, x1r, cotl, cotr = comm_call(
        functools.partial(opening_kernel, packed_rows=packed_rows, n=n_head), "opening", 1, ins, (len(ins) - 1,),
        [((width, rows), F32), ((width, rows), BF), ((hidden, VEC_ROWS), F32), ((2, group + 2 * PAD), jnp.int32),
         ((group // BLK, 128), jnp.int32), ((1, lanes), jnp.int32), ((n_head, packed_rows, rows), BF),
         ((width, TILE), F32), ((width, TILE), F32), ((width, TILE), BF), ((width, TILE), BF)], range(6, 11),
        [vm((n_head, packed_rows, rows), BF), vm((1, group + 2 * TILE), jnp.int32), piece_sems, piece_sems, dma, dma((4,)), dma((4,))])
    o, o_tail, of, lse = attend_forward(qkv_all, bounds, plan, position_bias, head_width)
    everyone_sems = dma((n_head, n_tm))
    ins = (x1, x1l, x1r, cot_t, cotl, cotr, cols, ext, mix_output, pointwise_in, depthwise_taps, pointwise_out, second_up, second_down_t)
    out, dx2, do_all, do_tails, pack = comm_call(
        functools.partial(middle_kernel, n_tm=n_tm, n_head=n_head, head_width=head_width, slot_count=slots, layout=layout),
        "middle", 2, (o, o_tail) + ins, range(len(ins) + 2),
        [((width, rows), BF), ((width, rows), F32), ((n_head, MAIN, rows), BF), ((n_head, 16, rows // 4), BF), ((layout.late, TILE), BF)],
        (2, 3),
        [vm(a.shape, a.dtype) for a in ins] + [
            vm((n_head, SLOT, rows + 2 * TILE), BF), vm((width, lanes), F32), vm((width + 16, rows), BF), vm((width, lanes), BF),
            vm((width, lanes), F32), vm((4, TILE), F32), vm((n_tm * n_head, 4, TILE), F32), vm((width, rows), F32),
            vm((width, lanes), F32), vm((4, TILE), F32), vm((n_tm * n_head, 4, TILE), F32), vm((n_head, MAIN, rows), BF),
            vm((width, lanes), F32), vm((taps + 1, 8, lanes), F32), vm((1, lanes), F32),
            vm((width, rows), BF), vm((hidden, rows), BF), vm((hidden + 16, rows), BF), vm((width, rows), BF),
            vm((width + 16, rows), BF), vm((width, rows), BF),
            vm((width, lanes), F32), vm((width, rows), F32), vm((taps, width, TILE), F32), vm((width + 16, rows), BF),
            vm((2 * width, rows), BF), vm((width, rows), BF), vm((2, width, TILE), F32),
            vm((16, 5 * TILE), F32), vm((16, 5 * TILE), F32), vm((taps, width), F32),
            vm((width, rows), F32), vm((1, rows), F32), vm((width, rows), F32), vm((width, rows), F32),
            vm((n_head, 16, rows // 4), BF), vm((4 * n_head, rows), F32), vm((n_head, 16, rows // 4), BF),
            dma((len(ins),)), dma((n_head - 1, 4)), dma((n_head - 1, 4)), dma((4,)), everyone_sems, everyone_sems, everyone_sems, everyone_sems,
            dma((rows // PART + 1, n_head - 1)), dma((rows // PART + 1, n_head - 1)), dma((2,)),
        ])
    dqkv, dtab = attend_backward(qkv_all, do_all, do_tails, of, lse, bounds, plan, position_bias, head_width)
    (others,) = comm_call(functools.partial(return_kernel, n=n_head), "return_gradients", 4, (dqkv,), (0,),
                          [(dqkv.shape, BF)], (0,), [dma((n_head - 1,)), dma((n_head - 1,))])
    parts = (layout.late, layout.last, layout.rows)
    sizes = (layout.late, max(layout.last - layout.late, 16 * n_tm * n_head), layout.rows - layout.last)
    ins = (pack, frames_t, x1, h2, dx2, dtab, cols, first_up, first_down_t, mix_inputs)
    grad, total = comm_call(
        functools.partial(final_kernel, n_tm=n_tm, n_head=n_head, parts=parts), "final", 3, (dqkv, others) + ins, range(len(ins) + 2),
        [((width, rows), F32), ((layout.rows, TILE), BF)], (1,),
        [vm(a.shape, a.dtype) for a in ins] + [
            vm((n_head, packed_rows, rows), BF), vm((layout.rows - layout.late, TILE), BF),
            vm((width, rows), BF), vm((hidden, rows), BF), vm((hidden, rows), BF), vm((width, rows), BF),
            vm((n_head * packed_rows, rows), BF), vm((4, width, TILE), F32),
            *[s for size in sizes for s in sum_scratch(size, n_tm, n_head)],
            dma((len(ins),)), dma((n_head,)), dma((3, 12, max(n_tm // 2, n_head))), dma((3,)),
        ])
    shapes = Weights(**{n: w.shape for n, w in weights.__dict__.items()})
    shapes.first_down = shapes.second_down = first_down_t.shape
    results = [((width, rows), BF), ((width, rows), F32)] + [(s, F32) for s in shapes.__dict__.values()]
    out, grad, *summed = pl.pallas_call(
        functools.partial(unpack_kernel, layout=layout),
        out_shape=tuple(jax.ShapeDtypeStruct(s, t) for s, t in results),
        compiler_params=pltpu.CompilerParams(vmem_limit_bytes=VMEM_MIB * 2**20),
        name="unpack",
    )(total, out, grad)
    summed = Weights(*summed)
    summed.first_down, summed.second_down = summed.first_down.T, summed.second_down.T
    return (out.T, grad.T) + tuple(summed.__dict__.values())


def solution(mesh):
    rows = P(("tm", "head"), None)
    placed = (rows, P("tm", None)) + (P(),) * 29 + (rows,)
    return jax.shard_map(body, mesh=mesh, in_specs=placed, out_specs=(rows, rows) + (P(),) * 29, check_vma=False)
```
